32 devices in a mesh: section: 2 (over core), dp: 8 (over z, x), rep: 2 (over y).
Axes of the slice: x: 2, y: 2, z: 4, core: 2. Of those that a mesh axis runs over, the one named last changes fastest.
Arguments:
- query_crops: bfloat16 [32, 256, 768], P(('dp', 'rep'), 'section'), may hold values from -5 to 5
- key_crops: bfloat16 [32, 256, 768], P(('dp', 'rep'), 'section'), may hold values from -5 to 5
- query_lengths: int32 [32], P(('dp', 'rep')), may hold values from 64 to 256, as said below
- key_lengths: int32 [32], P(('dp', 'rep')), may hold values from 64 to 256, as said below
- positive: int32 [32], P(('dp', 'rep')), may hold values from 0 to 31, as said below
- queue: bfloat16 [4096, 768], replicated, may hold values from -6 to 6
- qkv_weight: bfloat16 [2, 768, 2304], P('section'), may hold values from -0.21875 to 0.21875
- out_weight: bfloat16 [2, 768, 768], P('section'), may hold values from -0.875 to 0.875
- up_weight: bfloat16 [2, 768, 3072], P('section'), may hold values from -0.21875 to 0.21875
- down_weight: bfloat16 [2, 3072, 768], P('section'), may hold values from -0.109375 to 0.109375
- biases: bfloat16 [2, 5, 768], P('section'), may hold values from -1.25 to 1.25
- gains: bfloat16 [2, 2, 768], P('section'), may hold values from 0.5 to 1.5
- up_biases: bfloat16 [2, 3072], P('section'), may hold values from -1.25 to 1.25
- query_bias: bfloat16 [2, 768], P('section'), may hold values from -1.25 to 1.25
- key_qkv_weight: bfloat16 [2, 768, 2304], P('section'), may hold values from -0.21875 to 0.21875
- key_out_weight: bfloat16 [2, 768, 768], P('section'), may hold values from -0.875 to 0.875
- key_up_weight: bfloat16 [2, 768, 3072], P('section'), may hold values from -0.21875 to 0.21875
- key_down_weight: bfloat16 [2, 3072, 768], P('section'), may hold values from -0.109375 to 0.109375
- key_biases: bfloat16 [2, 6, 768], P('section'), may hold values from -1.25 to 1.25
- key_gains: bfloat16 [2, 2, 768], P('section'), may hold values from 0.5 to 1.5
- key_up_biases: bfloat16 [2, 3072], P('section'), may hold values from -1.25 to 1.25
Outputs:
- loss: float32 [1], replicated
- crops_grad: float32 [32, 256, 768], P(('dp', 'rep'), 'section')
- qkv_weight_grad: float32 [2, 768, 2304], P('section', ('dp', 'rep'))
- out_weight_grad: float32 [2, 768, 768], P('section', ('dp', 'rep'))
- up_weight_grad: float32 [2, 768, 3072], P('section', ('dp', 'rep'))
- down_weight_grad: float32 [2, 3072, 768], P('section', ('dp', 'rep'))
- biases_grad: float32 [2, 5, 768], P('section', None, ('dp', 'rep'))
- gains_grad: float32 [2, 2, 768], P('section', None, ('dp', 'rep'))
- up_biases_grad: float32 [2, 3072], P('section', ('dp', 'rep'))
- query_bias_grad: float32 [2, 768], P('section', ('dp', 'rep'))
The draws below stay inside these ranges and needn't reach their ends.
Inputs may be any that keep to these rules, and one draw needn't show every extreme that they name: `query_lengths`: some crop has exactly 256 real tokens and some exactly 64. `key_lengths`: some crop has exactly 256 real tokens and some exactly 64. A permutation: every key crop is the positive of exactly one query crop.
All inputs are finite; a program needn't handle non-finite values.
Results may differ from the reference program's by a relative error of at most 0.0095.
Values may be sent and summed in bfloat16 or wider, within the bound.
No kernel may reach another device: no remote copies, remote signals or barrier semaphores. Data moves between devices by JAX's collectives and lax.ppermute only.
A program may use at most 192 MiB of HBM per device.

```python
import math
import jax
import jax.numpy as jnp
from jax import lax

D = 768
H = 12
DH = 64
FF = 3072
SLOT = 256
QUEUE = 4096
CROPS = 32


def document_plan(key):
    documents = jax.random.normal(jax.random.fold_in(key, 101), (CROPS, D), jnp.float32)
    order = jax.random.permutation(jax.random.fold_in(key, 102), CROPS).astype(jnp.int32)
    return (documents, order)


def crop_lengths(key):
    lengths = jax.random.randint(jax.random.fold_in(key, 11), (CROPS,), SLOT // 4, SLOT + 1)
    longest = jax.random.randint(jax.random.fold_in(key, 12), (), 0, CROPS)
    shortest = (longest + 1 + jax.random.randint(jax.random.fold_in(key, 13), (), 0, CROPS - 1)) % CROPS
    return lengths.at[longest].set(SLOT).at[shortest].set(SLOT // 4).astype(jnp.int32)


def draw_query_crops(key, part):
    documents, order = document_plan(key)
    key = jax.random.fold_in(key, 1)
    noise = jax.random.normal(key, (CROPS, SLOT, D), jnp.float32)
    return jnp.clip(0.8 * documents[:, None, :] + 0.6 * noise, -5.0, 5.0).astype(jnp.bfloat16)


def draw_key_crops(key, part):
    documents, order = document_plan(key)
    key = jax.random.fold_in(key, 2)
    placed = jnp.zeros_like(documents).at[order].set(documents)
    noise = jax.random.normal(key, (CROPS, SLOT, D), jnp.float32)
    return jnp.clip(0.8 * placed[:, None, :] + 0.6 * noise, -5.0, 5.0).astype(jnp.bfloat16)


def draw_positive(key, part):
    documents, order = document_plan(key)
    return order


def draw_query_lengths(key, part):
    key = jax.random.fold_in(key, 3)
    return crop_lengths(key)


def draw_key_lengths(key, part):
    key = jax.random.fold_in(key, 4)
    return crop_lengths(key)


def levels(key, extent, split, smallest, top_value):
    gain = 1.0
    for dim, shards_of in split:
        steps = jax.random.uniform(jax.random.fold_in(jax.random.fold_in(key, 6), dim), (shards_of,), jnp.float32, smallest / len(split), top_value / len(split))
        gain = gain * jnp.repeat(jnp.exp(steps), extent[dim] // shards_of).reshape((-1,) + (1,) * (len(extent) - 1 - dim))
    return gain


def gaussian(stream_key, extent, spread, reach, cuts=(), held_as=jnp.bfloat16):
    factor_of = levels(stream_key, extent, cuts, -0.22, 0.18) if cuts else 1.0
    drawn = jax.random.normal(stream_key, extent, jnp.float32) * spread * factor_of
    return jnp.minimum(jnp.maximum(drawn, -reach), reach).astype(held_as)


def setup_inputs(seed: int = 0) -> dict:
    seeds = jax.random.split(jax.random.key(seed), 22)
    return {
        "query_crops": draw_query_crops(jax.random.fold_in(seeds[21], 71), 0),
        "key_crops": draw_key_crops(jax.random.fold_in(seeds[21], 71), 0),
        "query_lengths": draw_query_lengths(jax.random.fold_in(seeds[21], 71), 0),
        "key_lengths": draw_key_lengths(jax.random.fold_in(seeds[21], 71), 0),
        "positive": draw_positive(jax.random.fold_in(seeds[21], 71), 0),
        "queue": gaussian(seeds[5], (QUEUE, D), 1.0, 6.0),
        "qkv_weight": gaussian(seeds[6], (2, D, 3 * D), D ** -0.5, 0.21875, ((0, 2),)),
        "out_weight": gaussian(seeds[7], (2, D, D), (D // 16) ** -0.5, 0.875, ((0, 2),)),
        "up_weight": gaussian(seeds[8], (2, D, FF), D ** -0.5, 0.21875, ((0, 2),)),
        "down_weight": gaussian(seeds[9], (2, FF, D), FF ** -0.5, 0.109375, ((0, 2),)),
        "biases": gaussian(seeds[10], (2, 5, D), 0.2, 1.25, ((0, 2),)),
        "gains": jnp.clip(1.0 + 0.1 * jax.random.normal(seeds[11], (2, 2, D), jnp.float32), 0.5, 1.5).astype(jnp.bfloat16),
        "up_biases": gaussian(seeds[12], (2, FF), 0.2, 1.25, ((0, 2),)),
        "query_bias": gaussian(seeds[13], (2, D), 0.2, 1.25, ((0, 2),)),
        "key_qkv_weight": gaussian(seeds[14], (2, D, 3 * D), D ** -0.5, 0.21875, ((0, 2),)),
        "key_out_weight": gaussian(seeds[15], (2, D, D), (D // 16) ** -0.5, 0.875, ((0, 2),)),
        "key_up_weight": gaussian(seeds[16], (2, D, FF), D ** -0.5, 0.21875, ((0, 2),)),
        "key_down_weight": gaussian(seeds[17], (2, FF, D), FF ** -0.5, 0.109375, ((0, 2),)),
        "key_biases": gaussian(seeds[18], (2, 6, D), 0.2, 1.25, ((0, 2),)),
        "key_gains": jnp.clip(1.0 + 0.1 * jax.random.normal(seeds[19], (2, 2, D), jnp.float32), 0.5, 1.5).astype(jnp.bfloat16),
        "key_up_biases": gaussian(seeds[20], (2, FF), 0.2, 1.25, ((0, 2),)),
    }


masked_score = -1e+30
norm_eps = 1e-12
unit_eps = 1e-06
logit_divisor = 0.05

@jax.custom_vjp
def low(v):
    return lax.optimization_barrier(v.astype(jnp.bfloat16)).astype(jnp.float32)

@jax.custom_vjp
def low_back(v):
    return v

def low_keep(v):
    return (low(v), None)

def low_pass(kept, grad):
    return (grad,)

def back_keep(v):
    return (v, None)

def back_low(kept, grad):
    return (low(grad),)
low.defvjp(low_keep, low_pass)
low_back.defvjp(back_keep, back_low)

def highfidelity_matmul(left, right):
    return jnp.dot(left, right, preferred_element_type=jnp.float32, precision=lax.Precision.HIGHEST)

def norm_rows(value, gain_row, shift_row):
    row_mean = lax.optimization_barrier(jnp.mean(value, axis=-1, keepdims=True))
    centred = value - row_mean
    row_var = lax.optimization_barrier(jnp.mean(centred * centred, axis=-1, keepdims=True))
    return centred * lax.rsqrt(row_var + norm_eps) * gain_row + shift_row

def gelu_exact(value):
    return jax.nn.gelu(value, approximate=False)

def unit_rows(rows):
    return rows * lax.rsqrt(lax.optimization_barrier(jnp.sum(rows * rows, axis=-1, keepdims=True)) + unit_eps)

def encoder_layer(inputs, keep_mask, qkv_w, out_w, up_w, down_w, bias_rows, gain_rows, up_bias, query_b):
    crop_count, slot_count, model_width = inputs.shape
    flat_rows = inputs.reshape(crop_count * slot_count, model_width)
    qkv_bias = jnp.concatenate([query_b, jnp.zeros_like(query_b), bias_rows[0]])
    packed = low(low_back(highfidelity_matmul(flat_rows, qkv_w) + qkv_bias))
    packed = packed.reshape(crop_count, slot_count, 3, H, DH)
    query_heads = packed[:, :, 0]
    key_heads = packed[:, :, 1]
    value_heads = packed[:, :, 2]
    score_scale = 1.0 / math.sqrt(DH)
    raw_scores = jnp.einsum('cqhd,ckhd->chqk', query_heads, key_heads, precision=lax.Precision.HIGHEST) * score_scale
    scores = low_back(jnp.where(keep_mask[:, None, None, :], raw_scores, masked_score))
    row_top = lax.optimization_barrier(jnp.max(scores, axis=-1, keepdims=True))
    exponent = jnp.exp(scores - row_top)
    probabilities = exponent / lax.optimization_barrier(jnp.sum(exponent, axis=-1, keepdims=True))
    context = jnp.einsum('chqk,ckhd->cqhd', low(probabilities), value_heads, precision=lax.Precision.HIGHEST)
    context = low(low_back(context)).reshape(crop_count * slot_count, model_width)
    attended = low_back(highfidelity_matmul(context, out_w) + bias_rows[1])
    first_norm = low(norm_rows(flat_rows + attended, gain_rows[0], bias_rows[2]))
    up_rows = low_back(highfidelity_matmul(first_norm, up_w) + up_bias)
    hidden = low(gelu_exact(up_rows))
    down_rows = low_back(highfidelity_matmul(hidden, down_w) + bias_rows[3])
    output = norm_rows(first_norm + down_rows, gain_rows[1], bias_rows[4])
    return output.reshape(crop_count, slot_count, model_width)

def encode_block(block_values, block_keep, params):
    lower = [stacked[0] for stacked in params]
    upper = [stacked[1] for stacked in params]
    middle = low(low_back(encoder_layer(block_values, block_keep, lower[0], lower[1], lower[2], lower[3], lower[4], lower[5], lower[6], lower[7])))
    output = encoder_layer(middle, block_keep, upper[0], upper[1], upper[2], upper[3], upper[4], upper[5], upper[6], upper[7])
    weight_mask = block_keep.astype(jnp.float32)
    return lax.optimization_barrier(jnp.sum(output * weight_mask[:, :, None], axis=1)) / lax.optimization_barrier(jnp.sum(weight_mask, axis=1))[:, None]

def encode_all(crops_value, keep_mask, params):
    block_crops = math.gcd(CROPS, 16)
    block_count = CROPS // block_crops

    def one_block(block_pair):
        return encode_block(block_pair[0], block_pair[1], params)
    shaped = (crops_value.reshape(block_count, block_crops, SLOT, D), keep_mask.reshape(block_count, block_crops, SLOT))
    pooled = lax.map(jax.checkpoint(one_block), shaped)
    return pooled.reshape(CROPS, D)

def contrast(pooled, matching_cosine, memory_bank_directions):
    anchor_direction = unit_rows(pooled)
    matching_logit = lax.optimization_barrier(jnp.sum(anchor_direction * matching_cosine, axis=-1)) / logit_divisor
    distractor_logits = highfidelity_matmul(anchor_direction, memory_bank_directions.T) / logit_divisor
    row_top = jnp.maximum(matching_logit, lax.optimization_barrier(jnp.max(distractor_logits, axis=-1)))
    total = jnp.exp(matching_logit - row_top) + lax.optimization_barrier(jnp.sum(jnp.exp(distractor_logits - row_top[:, None]), axis=-1))
    return row_top + jnp.log(total) - matching_logit

def reference(query_crops, key_crops, query_lengths, key_lengths, positive, queue, qkv_weight, out_weight, up_weight, down_weight, biases, gains, up_biases, query_bias, key_qkv_weight, key_out_weight, key_up_weight, key_down_weight, key_biases, key_gains, key_up_biases):
    places = lax.broadcasted_iota(jnp.int32, (CROPS, SLOT), 1)
    query_keep = places < query_lengths.astype(jnp.int32)[:, None]
    key_keep = places < key_lengths.astype(jnp.int32)[:, None]
    key_params = tuple((array_in.astype(jnp.float32) for array_in in (key_qkv_weight, key_out_weight, key_up_weight, key_down_weight, key_biases[:, 1:], key_gains, key_up_biases, key_biases[:, 0])))
    key_unit = unit_rows(encode_all(key_crops.astype(jnp.float32), key_keep, key_params))
    matching_cosine = jnp.take(key_unit, positive.astype(jnp.int32), axis=0)
    memory_bank_directions = unit_rows(queue.astype(jnp.float32))
    query_params = tuple((array_in.astype(jnp.float32) for array_in in (qkv_weight, out_weight, up_weight, down_weight, biases, gains, up_biases, query_bias)))

    def objective(crops_value, params):
        pooled = encode_all(crops_value, query_keep, params)
        return jnp.mean(contrast(pooled, matching_cosine, memory_bank_directions))
    loss_value, pullback = jax.vjp(objective, query_crops.astype(jnp.float32), query_params)
    crops_grad, weight_grads = pullback(jnp.ones_like(loss_value))
    return (loss_value.reshape(1), crops_grad, weight_grads[0], weight_grads[1], weight_grads[2], weight_grads[3], weight_grads[4], weight_grads[5], weight_grads[6], weight_grads[7])
```

```python
import functools

import jax
import jax.numpy as jnp
from jax import lax
from jax.experimental import pallas as pl
from jax.experimental.pallas import tpu as pltpu
from jax.sharding import PartitionSpec as P

F32 = jnp.float32
BF = jnp.bfloat16
MASKED = -1e30
D = 768
FF = 3072
SLOTS = 256
PAIRS = 6
MIB = 2**20


def dot(a, b):
    return lax.dot_general(a, b, (((1,), (0,)), ((), ())), preferred_element_type=F32)


def dot_nt(a, b):
    return lax.dot_general(a, b, (((1,), (1,)), ((), ())), preferred_element_type=F32)


def dot_tn(a, b):
    return lax.dot_general(a, b, (((0,), (0,)), ((), ())), preferred_element_type=F32)


def gelu_parts(x, want_slope):
    ax = jnp.abs(x)
    t = pl.reciprocal(1.0 + (0.3275911 * 0.7071067811865476) * ax)
    e = jnp.exp(-0.5 * (x * x))
    poly = (0.5 * 1.061405429) * t + 0.5 * -1.453152027
    poly = poly * t + 0.5 * 1.421413741
    poly = poly * t + 0.5 * -0.284496736
    poly = poly * t + 0.5 * 0.254829592
    q = poly * t * e
    g = jnp.maximum(x, 0.0) - ax * q
    if not want_slope:
        return g, None
    return g, jnp.where(x >= 0, 1.0 - q, q) + (0.3989422804014327 * x) * e


def norm_parts(z):
    mean = jnp.mean(z, axis=-1, keepdims=True)
    c = z - mean
    var = jnp.mean(c * c, axis=-1, keepdims=True)
    r = lax.rsqrt(var + 1e-12)
    return c * r, r


def head_masks(scale):
    lane = lax.broadcasted_iota(jnp.int32, (1, 128), 1)
    low = jnp.where(lane < 64, scale, 0.0).astype(BF)
    high = jnp.where(lane < 64, 0.0, scale).astype(BF)
    return low, high


def stack_heads(pair, scale):
    low, high = head_masks(scale)
    return jnp.concatenate([pair * low, pair * high], axis=0)


def side_by_side(stacked):
    half = stacked.shape[0] // 2
    return jnp.concatenate([stacked[:half], stacked[half:]], axis=1)


class Copies:
    def __init__(self, sems):
        self.sems, self.used, self.open = sems, 0, []

    def make(self, src, dst):
        self.used += 1
        return pltpu.make_async_copy(src, dst, self.sems.at[self.used - 1])

    def fetch(self, src, dst):
        cp = self.make(src, dst)
        cp.start()
        return cp

    def pick(self, by_section, dst):
        if by_section[0] is by_section[1]:
            return self.fetch(by_section[0], dst)
        sem = self.sems.at[self.used]
        self.used += 1
        here = lax.axis_index("section")

        @pl.when(here == 0)
        def _():
            pltpu.make_async_copy(by_section[0], dst, sem).start()

        @pl.when(here != 0)
        def _():
            pltpu.make_async_copy(by_section[1], dst, sem).start()

        return pltpu.make_async_copy(by_section[0], dst, sem)

    def send(self, src, dst):
        self.open.append(self.fetch(src, dst))

    def drain(self):
        for cp in self.open:
            cp.wait()


def only_on(section, run):
    if section is None:
        run()
    else:
        pl.when(lax.axis_index("section") == section)(run)


VMEM = pl.BlockSpec(memory_space=pltpu.VMEM)
ANY = pl.BlockSpec(memory_space=pl.ANY)
SMEM = pl.BlockSpec(memory_space=pltpu.SMEM)
sd = jax.ShapeDtypeStruct


def call(kernel, name, outs, out_specs, ins, in_specs, scratch, flops, moved):
    return pl.pallas_call(
        kernel,
        out_shape=[sd(*o) for o in outs],
        in_specs=in_specs,
        out_specs=out_specs,
        scratch_shapes=[pltpu.VMEM(*s) for s in scratch] + [pltpu.SemaphoreType.DMA((64,))],
        compiler_params=pltpu.CompilerParams(vmem_limit_bytes=56 * MIB),
        cost_estimate=pl.CostEstimate(flops=flops, bytes_accessed=moved, transcendentals=0),
        name=name,
    )(*ins)


def saved_shapes(rows):
    crops = rows // SLOTS
    return [
        ((rows, 3 * D), BF),
        ((PAIRS * crops, 2 * SLOTS, SLOTS), BF),
        ((rows, D), BF),
        ((rows, D), BF),
        ((rows, 128), F32),
        ((rows, D), BF),
        ((rows, FF), BF),
        ((rows, FF), BF),
        ((rows, D), BF),
        ((rows, 128), F32),
    ]


def forward_kernel(rows, active, save, picks, lens, *refs):
    def run():
        forward_body(rows, save, picks, lens, *refs)

    only_on(active, run)


def forward_body(rows, save, picks, lens, *refs):
    crops = rows // SLOTS
    sources = [(refs[2 * i], refs[2 * i + 1]) if two else (refs[2 * i], refs[2 * i]) for i, two in enumerate(picks)]
    refs = refs[2 * len(picks) :]
    bqkv, bup, vecs, y_ref, pool_ref = refs[:5]
    refs = refs[5:]
    if save:
        (qkv_o, prob_o, ctx_o, n1_o, r1_o, first_o, hid_o, slope_o, n2_o, r2_o) = refs[:10]
        refs = refs[10:]
    (x, wqkv, wout, wup, wdown, ctx, zbuf, first, hid) = refs[:9]
    refs = refs[9:]
    if save:
        (qkv, prob, n1, r1, slope, n2, r2) = refs[:7]
        refs = refs[7:]
    copies = Copies(refs[0])
    got_x = copies.pick(sources[0], x)
    got_qkv = copies.pick(sources[1], wqkv)
    got_x.wait()
    got_qkv.wait()
    got_out = copies.pick(sources[2], wout)
    got_up = copies.pick(sources[3], wup)
    got_down = copies.pick(sources[4], wdown)
    keycol = lax.broadcasted_iota(jnp.int32, (1, SLOTS), 1)
    for i in range(3):
        thirds = []
        for j in range(3):
            cols = slice(D * j + 256 * i, D * j + 256 * (i + 1))
            part = (dot(x[...], wqkv[:, cols]) + bqkv[:, cols]).astype(BF)
            if save:
                qkv[:, cols] = part
            thirds.append(part)
        for c in range(crops):
            crop = slice(SLOTS * c, SLOTS * (c + 1))
            for pr in range(2):
                qp, kp, vp = [t[crop, 128 * pr : 128 * (pr + 1)] for t in thirds]
                scores = jnp.where(keycol < lens[c], dot_nt(stack_heads(qp, 0.125), kp), MASKED)
                e = jnp.exp(scores - jnp.max(scores, axis=-1, keepdims=True))
                p = (e * pl.reciprocal(jnp.sum(e, axis=-1, keepdims=True))).astype(BF)
                if save:
                    prob[PAIRS * c + 2 * i + pr] = p
                ctx[crop, 256 * i + 128 * pr : 256 * i + 128 * (pr + 1)] = dot(
                    side_by_side(p), stack_heads(vp, 1.0)
                ).astype(BF)
    if save:
        copies.send(qkv, qkv_o)
        copies.send(prob, prob_o)
        copies.send(ctx, ctx_o)
    got_out.wait()
    for j in range(3):
        cols = slice(256 * j, 256 * (j + 1))
        zbuf[:, cols] = x[:, cols].astype(F32) + dot(ctx[...], wout[:, cols]) + vecs[0:1, cols]
    block = 64
    steps = rows // block

    def first_norm(i, carry):
        at = pl.ds(pl.multiple_of(i * block, block), block)
        n, r = norm_parts(zbuf[at, :])
        f = (n * vecs[4:5] + vecs[1:2]).astype(BF)
        first[at, :] = f
        zbuf[at, :] = f.astype(F32) + vecs[2:3]
        if save:
            n1[at, :] = n.astype(BF)
            r1[at, :] = jnp.broadcast_to(r, (block, 128))
        return carry

    lax.fori_loop(0, steps, first_norm, 0, unroll=True)
    if save:
        copies.send(n1, n1_o)
        copies.send(r1, r1_o)
        copies.send(first, first_o)
    got_up.wait()
    got_down.wait()

    def down_part(k):
        cols = slice(512 * k, 512 * (k + 1))
        zbuf[...] += dot(hid[:, cols], wdown[cols, :])

    for i in range(12):
        cols = slice(256 * i, 256 * (i + 1))
        g, slope_part = gelu_parts(dot(first[...], wup[:, cols]) + bup[:, cols], save)
        hid[:, cols] = g.astype(BF)
        if save:
            slope[:, cols] = slope_part.astype(BF)
        if i % 2 and i > 2:
            down_part(i // 2 - 1)
    if save:
        copies.send(hid, hid_o)
        copies.send(slope, slope_o)
    down_part(5)
    pool_ref[...] = jnp.zeros_like(pool_ref)
    per_crop = SLOTS // block

    def second_norm(i, carry):
        at = pl.ds(pl.multiple_of(i * block, block), block)
        n, r = norm_parts(zbuf[at, :])
        f = n * vecs[5:6] + vecs[3:4]
        y_ref[at, :] = f.astype(BF)
        if save:
            n2[at, :] = n.astype(BF)
            r2[at, :] = jnp.broadcast_to(r, (block, 128))
        c = i // per_crop
        token = lax.broadcasted_iota(jnp.int32, (block, 1), 0) + (i % per_crop) * block
        part = jnp.sum(jnp.where(token < lens[c], f, 0.0), axis=0, keepdims=True)
        pool_ref[pl.ds(c, 1), :] += part / lens[c].astype(F32)
        return carry

    lax.fori_loop(0, steps, second_norm, 0, unroll=True)
    if save:
        copies.send(n2, n2_o)
        copies.send(r2, r2_o)
    copies.drain()


def forward(active, save, lens, x, weights, vectors):
    rows = x[0].shape[0]
    pairs = [x] + weights
    picks = [a is not b for a, b in pairs]
    flat = [a for pair in pairs for a in pair]
    outs = [((rows, D), BF), ((8, D), F32)]
    out_specs = [VMEM, VMEM]
    scratch = [
        ((rows, D), BF),
        ((D, 3 * D), BF),
        ((D, D), BF),
        ((D, FF), BF),
        ((FF, D), BF),
        ((rows, D), BF),
        ((rows, D), F32),
        ((rows, D), BF),
        ((rows, FF), BF),
    ]
    if save:
        kept = saved_shapes(rows)
        outs += kept
        out_specs += [ANY] * len(kept)
        scratch += [kept[i] for i in (0, 1, 3, 4, 7, 8, 9)]
    return call(
        functools.partial(forward_kernel, rows, active, save, picks),
        "layer_forward",
        outs,
        out_specs,
        [lens, *flat, *vectors],
        [SMEM] + [ANY] * len(flat) + [VMEM] * 3,
        scratch,
        rows * 15000000,
        16000000 + (15000000 if save else 0),
    )


def split3(v):
    hi = v.astype(BF)
    rest = v - hi.astype(F32)
    mid = rest.astype(BF)
    lo = (rest - mid.astype(F32)).astype(BF)
    return hi, mid, lo


def stack3(v):
    parts = split3(v)
    return jnp.concatenate(list(parts) + [jnp.zeros_like(parts[0])] * 5, axis=0)


def unstack3(rows, n):
    return rows[:n] + rows[n : 2 * n] + rows[2 * n : 3 * n]


def queue_norm_kernel(active, queue, inv_ref, sems):
    def run():
        def step(i, carry):
            at = pl.ds(pl.multiple_of(i * 512, 512), 512)
            v = queue[at, :].astype(F32)
            sq = v * v
            hi = sq.astype(BF)
            lo = (sq - hi.astype(F32)).astype(BF)
            ones = jnp.ones((8, D), BF)
            total = dot_nt(ones, hi) + dot_nt(ones, lo)
            inv_ref[:, at] = lax.rsqrt(total + 1e-6)
            return carry

        lax.fori_loop(0, queue.shape[0] // 512, step, 0)

    only_on(active, run)


def loss_kernel(active, crops, count, pooled, matched, queue, inv, grad_ref, loss_ref, sems):
    def run():
        v = pooled[:crops]
        r = lax.rsqrt(jnp.sum(v * v, axis=-1, keepdims=True) + 1e-6)
        u = v * r
        k = matched[:crops]
        near = jnp.sum(u * k, axis=-1, keepdims=True) * 20.0
        inv_row = inv[0:1]
        far = unstack3(dot_nt(stack3(u), queue[...]), crops) * (inv_row * 20.0)
        top = jnp.maximum(near, jnp.max(far, axis=-1, keepdims=True))
        e_near = jnp.exp(near - top)
        e_far = jnp.exp(far - top)
        total = e_near + jnp.sum(e_far, axis=-1, keepdims=True)
        share = 20.0 / (total * count)
        d_u = unstack3(dot(stack3(e_far * inv_row * share), queue[...]), crops)
        d_u = d_u + (e_near - total) * share * k
        grad = r * (d_u - u * jnp.sum(u * d_u, axis=-1, keepdims=True))
        grad_ref[...] = jnp.zeros_like(grad_ref)
        grad_ref[:crops] = grad
        lost = jnp.sum(top + jnp.log(total) - near, axis=0, keepdims=True) / count
        loss_ref[...] = jnp.broadcast_to(lost, loss_ref.shape)

    only_on(active, run)


def norm_back(dy, gain, n, r):
    dn = dy * gain
    return r * (dn - jnp.mean(dn, axis=-1, keepdims=True) - n * jnp.mean(dn * n, axis=-1, keepdims=True))


def column_sum(v):
    return jnp.sum(v, axis=0, keepdims=True)


ORDERS = {"x": (3, 2), "y": (2, 3), "z": (1, 0)}


def slot_owner(order, j, sizes):
    dp, rep = lax.axis_index("dp"), lax.axis_index("rep")
    if order == "x":
        jx, jy, jz = j // 8, j // 4 % 2, j % 4
    elif order == "y":
        jy, jx, jz = j // 8, j // 4 % 2, j % 4
    else:
        jz, jx, jy = j // 4, j // 2 % 2, j % 2
    flipped = jnp.bitwise_xor(dp, 2 * jz + jx) * 2 + jnp.bitwise_xor(rep, jy)
    return flipped


def ship(copies, grad, outs, order, fast):
    if not fast:
        copies.send(grad, outs[0])
        return
    size = grad.shape[0] // 16
    per = 16 // len(outs)
    for j in range(15, -1, -1):
        owner = slot_owner(order, j, None)
        at = pl.ds(pl.multiple_of(owner * size, 16), size)
        copies.send(grad.at[at, :], outs[j // per].at[j % per])


def shipped(shape, order, fast):
    if not fast:
        return [(shape, BF)]
    n = 4 if order == "z" else 2
    return [((16 // n, shape[0] // 16, shape[1]), BF)] * n


def back1_kernel(rows, active, pooled, order, fast, lens, *refs):
    def run():
        n_out = len(shipped((FF, D), order, fast))
        dy, n2, r2, hid_h, vecs, ddown_ref, dsum_ref, vec_ref = refs[:8]
        outs = refs[8 : 8 + n_out]
        hid, grad, sems = refs[8 + n_out :]
        copies = Copies(sems)
        got_hid = copies.fetch(hid_h, hid)
        vec_ref[...] = jnp.zeros_like(vec_ref)
        block = 64
        per_crop = SLOTS // block
        for i in range(rows // block):
            at = slice(block * i, block * (i + 1))
            c = i // per_crop
            if pooled:
                token = lax.broadcasted_iota(jnp.int32, (block, 1), 0) + (i % per_crop) * block
                grow = jnp.where(token < lens[c], 1.0 / lens[c].astype(F32), 0.0) * dy[c : c + 1]
            else:
                grow = dy[at].astype(F32)
            n = n2[at].astype(F32)
            ds = norm_back(grow, vecs[5:6], n, r2[at, 0:1])
            low = ds.astype(BF)
            dsum_ref[at] = ds
            ddown_ref[at] = low
            vec_ref[0:1] += column_sum(grow * n)
            vec_ref[1:2] += column_sum(grow)
            vec_ref[2:3] += column_sum(low.astype(F32))
        got_hid.wait()
        for i in range(12):
            cols = slice(256 * i, 256 * (i + 1))
            grad[cols, :] = dot_tn(hid[:, cols], ddown_ref[...]).astype(BF)
        ship(copies, grad, outs, order, fast)
        copies.drain()

    only_on(active, run)


def back1(active, pooled, order, fast, lens, dy, n2, r2, hid, vecs):
    rows = n2.shape[0]
    ships = shipped((FF, D), order, fast)
    return call(
        functools.partial(back1_kernel, rows, active, pooled, order, fast),
        "down_backward",
        [((rows, D), BF), ((rows, D), F32), ((8, D), F32)] + ships,
        [VMEM] * 3 + [ANY] * len(ships),
        [lens, dy, n2, r2, hid, vecs],
        [SMEM, VMEM, VMEM, VMEM, ANY, VMEM],
        [((rows, FF), BF), ((FF, D), BF)],
        rows * 2 * FF * D,
        12000000,
    )


def back2_kernel(rows, active, order, fast, *refs):
    def run():
        n_out = len(shipped((D, FF), order, fast))
        ddown, dsum2, first, n1, r1, slope_h, wdown_h, wup_h, vecs = refs[:9]
        datt_ref, dsum_ref, vec_ref, bup_ref = refs[9:13]
        outs = refs[13 : 13 + n_out]
        slope, wdown, wup, grad, acc, sems = refs[13 + n_out :]
        copies = Copies(sems)
        got = [copies.fetch(wdown_h, wdown), copies.fetch(slope_h, slope), copies.fetch(wup_h, wup)]
        vec_ref[...] = jnp.zeros_like(vec_ref)
        for cp in got:
            cp.wait()
        acc[...] = dsum2[...]
        for i in range(6):
            cols = slice(512 * i, 512 * (i + 1))
            up = (dot_nt(ddown[...], wdown[cols, :]) * slope[:, cols].astype(F32)).astype(BF)
            bup_ref[:, cols] = jnp.broadcast_to(column_sum(up.astype(F32)), (8, 512))
            acc[...] += dot_nt(up, wup[:, cols])
            grad[:, cols] = dot_tn(first[...], up).astype(BF)
        ship(copies, grad, outs, order, fast)
        block = 64
        for i in range(rows // block):
            at = slice(block * i, block * (i + 1))
            n = n1[at].astype(F32)
            dfirst = acc[at]
            ds = norm_back(dfirst, vecs[4:5], n, r1[at, 0:1])
            low = ds.astype(BF)
            dsum_ref[at] = ds
            datt_ref[at] = low
            vec_ref[0:1] += column_sum(dfirst * n)
            vec_ref[1:2] += column_sum(dfirst)
            vec_ref[2:3] += column_sum(low.astype(F32))
        copies.drain()

    only_on(active, run)


def back2(active, order, fast, ddown, dsum2, first, n1, r1, slope, wdown, wup, vecs):
    rows = n1.shape[0]
    ships = shipped((D, FF), order, fast)
    return call(
        functools.partial(back2_kernel, rows, active, order, fast),
        "up_backward",
        [((rows, D), BF), ((rows, D), F32), ((8, D), F32), ((8, FF), F32)] + ships,
        [VMEM] * 4 + [ANY] * len(ships),
        [ddown, dsum2, first, n1, r1, slope, wdown, wup, vecs],
        [VMEM] * 5 + [ANY] * 3 + [VMEM],
        [((rows, FF), BF), ((FF, D), BF), ((D, FF), BF), ((D, FF), BF), ((rows, D), F32)],
        rows * 6 * FF * D,
        24000000,
    )


QKV_CUT = 1152


def back3_kernel(rows, active, orders, fast, x_two, *refs):
    def run():
        n_out = len(shipped((D, D), orders[0], fast))
        n_a = len(shipped((D, QKV_CUT), orders[1], fast))
        n_b = len(shipped((D, QKV_CUT), orders[2], fast))
        x0, x1, datt, dsum1, ctx, qkv_h, prob_h, wout_h, wqkv_h = refs[:9]
        dx_ref, vec_ref = refs[9:11]
        outs = refs[11:]
        x, qkv, prob, wout, wqkv, grad_out, grad_a, grad_b, dqkv, sems = outs[n_out + n_a + n_b :]
        outs_o, outs_a, outs_b = outs[:n_out], outs[n_out : n_out + n_a], outs[n_out + n_a : n_out + n_a + n_b]
        copies = Copies(sems)
        got_out = copies.fetch(wout_h, wout)
        got_qkv = copies.fetch(qkv_h, qkv)
        got_prob = copies.fetch(prob_h, prob)
        got_x = copies.pick((x0, x1) if x_two else (x0, x0), x)
        got_w = copies.fetch(wqkv_h, wqkv)
        crops = rows // SLOTS
        got_out.wait()
        dctx = dot_nt(datt[...], wout[...]).astype(BF)
        grad_out[...] = dot_tn(ctx[...], datt[...]).astype(BF)
        ship(copies, grad_out, outs_o, orders[0], fast)
        got_qkv.wait()
        got_prob.wait()
        for c in range(crops):
            crop = slice(SLOTS * c, SLOTS * (c + 1))
            for pr in range(PAIRS):
                cols = [slice(D * j + 128 * pr, D * j + 128 * (pr + 1)) for j in range(3)]
                qp, kp, vp = [qkv[crop, t] for t in cols]
                dcs = stack_heads(dctx[crop, 128 * pr : 128 * (pr + 1)], 1.0)
                p = prob[PAIRS * c + pr]
                pf = p.astype(F32)
                weighted = pf * dot_nt(dcs, vp)
                ds = (weighted - pf * jnp.sum(weighted, axis=-1, keepdims=True)).astype(BF)
                dqkv[crop, cols[0]] = dot(side_by_side(ds), stack_heads(kp, 0.125)).astype(BF)
                dqkv[crop, cols[1]] = dot_tn(ds, stack_heads(qp, 0.125)).astype(BF)
                dqkv[crop, cols[2]] = dot_tn(p, dcs).astype(BF)
        vec_ref[...] = jnp.zeros_like(vec_ref)
        vec_ref[0:1] = column_sum(dqkv[:, :D].astype(F32))
        vec_ref[1:2] = column_sum(dqkv[:, 2 * D :].astype(F32))
        got_w.wait()
        for j in range(3):
            cols = slice(256 * j, 256 * (j + 1))
            dx_ref[:, cols] = (dot_nt(dqkv[...], wqkv[cols, :]) + dsum1[:, cols]).astype(BF)
        got_x.wait()
        for j in range(3):
            cols = slice(384 * j, 384 * (j + 1))
            grad_a[:, cols] = dot_tn(x[...], dqkv[:, cols]).astype(BF)
        ship(copies, grad_a, outs_a, orders[1], fast)
        for j in range(3):
            cols = slice(384 * j, 384 * (j + 1))
            grad_b[:, cols] = dot_tn(x[...], dqkv[:, QKV_CUT + 384 * j : QKV_CUT + 384 * (j + 1)]).astype(BF)
        ship(copies, grad_b, outs_b, orders[2], fast)
        copies.drain()

    only_on(active, run)


def back3(active, orders, fast, x, datt, dsum1, ctx, qkv, prob, wout, wqkv):
    rows = datt.shape[0]
    ship_o = shipped((D, D), orders[0], fast)
    ship_a = shipped((D, QKV_CUT), orders[1], fast)
    ship_b = shipped((D, QKV_CUT), orders[2], fast)
    crops = rows // SLOTS
    outs = call(
        functools.partial(back3_kernel, rows, active, orders, fast, x[0] is not x[1]),
        "attention_backward",
        [((rows, D), BF), ((8, D), F32)] + ship_o + ship_a + ship_b,
        [VMEM] * 2 + [ANY] * (len(ship_o) + len(ship_a) + len(ship_b)),
        [x[0], x[1], datt, dsum1, ctx, qkv, prob, wout, wqkv],
        [ANY] * 2 + [VMEM] * 3 + [ANY] * 4,
        [
            ((rows, D), BF),
            ((rows, 3 * D), BF),
            ((PAIRS * crops, 2 * SLOTS, SLOTS), BF),
            ((D, D), BF),
            ((D, 3 * D), BF),
            ((D, D), BF),
            ((D, QKV_CUT), BF),
            ((D, QKV_CUT), BF),
            ((rows, 3 * D), BF),
        ],
        rows * (8 * D * D * 2 + 10 * SLOTS * D),
        22000000,
    )
    a, b = 2 + len(ship_o), 2 + len(ship_o) + len(ship_a)
    return outs[0], outs[1], outs[2:a], outs[a:b], outs[b:]


AXES = ("section", "dp", "rep")


def swap(block, section, dp_flip, rep_flip):
    dps, reps = lax.axis_size("dp"), lax.axis_size("rep")
    sections = range(lax.axis_size("section")) if section is None else [section]
    route = [
        ((s * dps + d) * reps + r, (s * dps + (d ^ dp_flip)) * reps + (r ^ rep_flip))
        for s in sections
        for d in range(dps)
        for r in range(reps)
    ]
    return lax.ppermute(block, AXES, route)


def flips():
    out, bit = [], 1
    while bit < lax.axis_size("rep"):
        out.append((0, bit))
        bit *= 2
    bit = 1
    while bit < lax.axis_size("dp"):
        out.append((bit, 0))
        bit *= 2
    return out


def low(v):
    return v.astype(BF)


def wide(*terms):
    total = terms[0].astype(F32)
    for t in terms[1:]:
        total = total + t.astype(F32)
    return total


def scatter_sum(pieces, order, section):
    if order == "z":
        keep = [pieces[0]] + [swap(pieces[k], section, 2 * k, 0) for k in range(1, 4)]
        first = swap(low(wide(*[t[2:] for t in keep])), section, 1, 0)
        keep = [t[:2] for t in keep] + [first]
        second = swap(low(wide(*[t[1:] for t in keep])), section, 0, 1)
        return wide(*[t[0] for t in keep], second[0])
    flip1, flip2 = ((1, 0), (0, 1)) if order == "x" else ((0, 1), (1, 0))
    first = swap(pieces[1], section, *flip1)
    kept = pieces[0]
    second = swap(low(wide(kept[4:], first[4:])), section, *flip2)
    parts = [wide(kept[k], first[k], second[k]) for k in range(4)]
    others = [swap(low(parts[k]), section, 2 * k, 0) for k in range(1, 4)]
    return wide(parts[0], *others)


def body(
    query_crops,
    key_crops,
    query_lengths,
    key_lengths,
    positive,
    queue,
    qkv_weight,
    out_weight,
    up_weight,
    down_weight,
    biases,
    gains,
    up_biases,
    query_bias,
    key_qkv_weight,
    key_out_weight,
    key_up_weight,
    key_down_weight,
    key_biases,
    key_gains,
    key_up_biases,
):
    here, crops = query_crops.shape[0], query_crops.shape[0]
    rows = crops * SLOTS
    sections, dps, reps = [lax.axis_size(a) for a in AXES]
    fast = dps == 8 and reps == 2
    crop_all = crops * dps * reps
    section_index = lax.axis_index("section")
    on_first = section_index == 0
    dp, rep = lax.axis_index("dp"), lax.axis_index("rep")

    def gather_rows(block):
        other = lax.ppermute(block, "section", [(1, 0)])
        return jnp.concatenate([block, other], axis=1).reshape(rows, D)

    def vectors(bias_q, bias_rows, gain_rows, up_b):
        bias_rows = bias_rows.astype(F32)
        bqkv = jnp.concatenate([bias_q.astype(F32), jnp.zeros((D,), F32), bias_rows[0]])
        vecs = jnp.concatenate([bias_rows[1:5], gain_rows.astype(F32), jnp.zeros((2, D), F32)])
        return bqkv[None], up_b.astype(F32)[None], vecs

    query_vectors = vectors(query_bias[0], biases[0], gains[0], up_biases[0])
    key_vectors = vectors(key_biases[0, 0], key_biases[0, 1:], key_gains[0], key_up_biases[0])
    mixed_vectors = [jnp.where(on_first, a, b) for a, b in zip(query_vectors, key_vectors)]
    query_weights = [w[0] for w in (qkv_weight, out_weight, up_weight, down_weight)]
    key_weights = [w[0] for w in (key_qkv_weight, key_out_weight, key_up_weight, key_down_weight)]

    key_rows = gather_rows(key_crops)
    query_rows = gather_rows(query_crops)

    def relay(block, distance):
        return lax.ppermute(block, "section", [(0, 1)] if distance > 0 else [(1, 0)])

    key_middle, _ = forward(0, False, key_lengths, (key_rows, key_rows), [(w, w) for w in key_weights], key_vectors)
    inv = call(
        functools.partial(queue_norm_kernel, sections - 1),
        "queue_norm",
        [((8, queue.shape[0]), F32)],
        [VMEM],
        [queue],
        [VMEM],
        [],
        8 * queue.size,
        queue.size * 2,
    )[0]
    key_middle = relay(key_middle, 1)
    lens_mixed = jnp.where(on_first, query_lengths, key_lengths)
    query_middle, key_pooled = forward(
        None, False, lens_mixed, (query_rows, key_middle), list(zip(query_weights, key_weights)), mixed_vectors
    )
    query_middle = relay(query_middle, 1)
    inputs = (query_rows, query_middle)
    step = forward(None, True, query_lengths, inputs, [(w, w) for w in query_weights], query_vectors)
    query_pooled = step[1]
    qkv, prob, ctx, n1, r1, first, hid, slope, n2, r2 = step[2:]

    every_key = key_pooled[:crops]
    every_key = every_key * lax.rsqrt(jnp.sum(every_key * every_key, axis=-1, keepdims=True) + 1e-6)
    for flip in flips():
        every_key = jnp.concatenate([every_key, swap(every_key, None, *flip)], axis=0)
    place = dp * reps + rep
    matched = jnp.take(every_key, jnp.bitwise_xor(positive // crops, place) * crops + positive % crops, axis=0)
    matched = jnp.concatenate([matched, jnp.zeros((8 - crops, D), F32)], axis=0)

    pooled_grad, lost = call(
        functools.partial(loss_kernel, sections - 1, crops, crop_all),
        "contrast",
        [((8, D), F32), ((8, 128), F32)],
        [VMEM] * 2,
        [query_pooled, matched, queue, inv],
        [VMEM] * 4,
        [],
        16 * 2 * queue.size,
        queue.size * 2,
    )

    vecs = query_vectors[2]
    orders = ("x", "y", ("z", "x", "y"))

    def layer_back(active, pooled, dy):
        ddown, dsum2, vec_a, *grad_down = back1(active, pooled, orders[0], fast, query_lengths, dy, n2, r2, hid, vecs)
        datt, dsum1, vec_b, grad_bup, *grad_up = back2(
            active, orders[1], fast, ddown, dsum2, first, n1, r1, slope, query_weights[3], query_weights[2], vecs
        )
        dx, vec_c, grad_out, grad_qa, grad_qb = back3(
            active, orders[2], fast, inputs, datt, dsum1, ctx, qkv, prob, query_weights[1], query_weights[0]
        )
        small = jnp.concatenate(
            [
                vec_c[1:2],
                vec_b[2:3],
                vec_b[1:2],
                vec_a[2:3],
                vec_a[1:2],
                vec_b[0:1],
                vec_a[0:1],
                vec_c[0:1],
                grad_bup[0:1].reshape(FF // D, D),
            ],
            axis=0,
        )
        return dx, small, (grad_down, grad_up, grad_out, grad_qa, grad_qb)

    flat_orders = (orders[0], orders[1], *orders[2])
    last = sections - 1
    dmiddle, small_last, grads_last = layer_back(last, True, pooled_grad)
    dmiddle = relay(dmiddle, -1)
    dx, small_first, grads_first = layer_back(0, False, dmiddle)

    if fast:
        sums_last = [scatter_sum(g, o, last) for g, o in zip(grads_last, flat_orders)]
        sums_first = [scatter_sum(g, o, 0) for g, o in zip(grads_first, flat_orders)]
        totals = [jnp.where(on_first, a, b) for a, b in zip(sums_first, sums_last)]
    else:
        totals = [
            lax.psum_scatter(
                jnp.where(on_first, a[0], b[0]).astype(F32), ("dp", "rep"), scatter_dimension=0, tiled=True
            )
            for a, b in zip(grads_first, grads_last)
        ]
    grad_down, grad_up, grad_out, grad_qa, grad_qb = totals
    grad_qkv = jnp.concatenate([grad_qa, grad_qb], axis=1)

    small = jnp.where(on_first, small_first, small_last)
    loss_row = jnp.where(on_first, 0.0, jnp.concatenate([lost[0:1]] * (D // 128), axis=1))
    small = jnp.concatenate([small, loss_row], axis=0)
    for flip in flips():
        small = small + swap(small, None, *flip)
    loss_value = jnp.where(on_first, relay(small[12, :128], -1), small[12, :128])[:1]
    width = D // (dps * reps)
    mine = lax.dynamic_slice(small[:8], (0, place * width), (8, width))
    up_part = lax.dynamic_slice(small[8:12].reshape(FF), (place * (FF // (dps * reps)),), (FF // (dps * reps),))

    dx = dx.reshape(crops, SLOTS, D)
    half = SLOTS // sections
    crops_grad = jnp.where(on_first, dx[:, :half], lax.ppermute(dx[:, half:], "section", [(0, 1)])).astype(F32)
    return (
        loss_value,
        crops_grad,
        grad_qkv[None],
        grad_out[None],
        grad_up[None],
        grad_down[None],
        mine[None, :5],
        mine[None, 5:7],
        up_part[None],
        mine[None, 7],
    )


def solution(mesh):
    crop = P(("dp", "rep"), "section", None)
    per_crop = P(("dp", "rep"))
    layer3 = P("section", None, None)
    layer2 = P("section", None)
    placed = (
        (crop, crop, per_crop, per_crop, per_crop, P())
        + (layer3,) * 6
        + (layer2,) * 2
        + (layer3,) * 6
        + (layer2,)
    )
    shared3 = P("section", ("dp", "rep"), None)
    return jax.shard_map(
        body,
        mesh=mesh,
        in_specs=placed,
        out_specs=(
            P(),
            crop,
            shared3,
            shared3,
            shared3,
            shared3,
            P("section", None, ("dp", "rep")),
            P("section", None, ("dp", "rep")),
            P("section", ("dp", "rep")),
            P("section", ("dp", "rep")),
        ),
        check_vma=False,
    )
```

```python
import functools

import jax
import jax.numpy as jnp
from jax import lax
from jax.experimental import pallas as pl
from jax.experimental.pallas import tpu as pltpu
from jax.sharding import PartitionSpec as P

F32 = jnp.float32
BF = jnp.bfloat16
MASKED = -1e30
D = 768
FF = 3072
SLOTS = 256
PAIRS = 6
MIB = 2**20
SEMS = 96


def dot(a, b):
    return lax.dot_general(a, b, (((1,), (0,)), ((), ())), preferred_element_type=F32)


def dot_nt(a, b):
    return lax.dot_general(a, b, (((1,), (1,)), ((), ())), preferred_element_type=F32)


def dot_tn(a, b):
    return lax.dot_general(a, b, (((0,), (0,)), ((), ())), preferred_element_type=F32)


def gelu_parts(x, want_slope):
    ax = jnp.abs(x)
    t = pl.reciprocal(1.0 + (0.3275911 * 0.7071067811865476) * ax)
    e = jnp.exp(-0.5 * (x * x))
    poly = (0.5 * 1.061405429) * t + 0.5 * -1.453152027
    poly = poly * t + 0.5 * 1.421413741
    poly = poly * t + 0.5 * -0.284496736
    poly = poly * t + 0.5 * 0.254829592
    q = poly * t * e
    g = jnp.maximum(x, 0.0) - ax * q
    if not want_slope:
        return g, None
    return g, jnp.where(x >= 0, 1.0 - q, q) + (0.3989422804014327 * x) * e


def norm_parts(z):
    mean = jnp.mean(z, axis=-1, keepdims=True)
    c = z - mean
    var = jnp.mean(c * c, axis=-1, keepdims=True)
    r = lax.rsqrt(var + 1e-12)
    return c * r, r


def head_masks(scale):
    lane = lax.broadcasted_iota(jnp.int32, (1, 128), 1)
    low = jnp.where(lane < 64, scale, 0.0).astype(BF)
    high = jnp.where(lane < 64, 0.0, scale).astype(BF)
    return low, high


def stack_heads(pair, scale):
    low, high = head_masks(scale)
    return jnp.concatenate([pair * low, pair * high], axis=0)


def side_by_side(stacked):
    half = stacked.shape[0] // 2
    return jnp.concatenate([stacked[:half], stacked[half:]], axis=1)


class Copies:
    def __init__(self, sems):
        self.sems, self.used, self.open = sems, 0, []

    def make(self, src, dst):
        self.used += 1
        return pltpu.make_async_copy(src, dst, self.sems.at[self.used - 1])

    def fetch(self, src, dst):
        cp = self.make(src, dst)
        cp.start()
        return cp

    def pick(self, by_section, dst):
        if by_section[0] is by_section[1]:
            return self.fetch(by_section[0], dst)
        sem = self.sems.at[self.used]
        self.used += 1
        here = lax.axis_index("section")

        @pl.when(here == 0)
        def _():
            pltpu.make_async_copy(by_section[0], dst, sem).start()

        @pl.when(here != 0)
        def _():
            pltpu.make_async_copy(by_section[1], dst, sem).start()

        return pltpu.make_async_copy(by_section[0], dst, sem)

    def send(self, src, dst):
        self.open.append(self.fetch(src, dst))

    def drain(self):
        for cp in self.open:
            cp.wait()


def only_on(section, run):
    if section is None:
        run()
    else:
        pl.when(lax.axis_index("section") == section)(run)


VMEM = pl.BlockSpec(memory_space=pltpu.VMEM)
ANY = pl.BlockSpec(memory_space=pl.ANY)
SMEM = pl.BlockSpec(memory_space=pltpu.SMEM)
sd = jax.ShapeDtypeStruct


def call(kernel, name, outs, out_specs, ins, in_specs, scratch, flops, moved):
    return pl.pallas_call(
        kernel,
        out_shape=[sd(*o) for o in outs],
        in_specs=in_specs,
        out_specs=out_specs,
        scratch_shapes=[pltpu.VMEM(*s) for s in scratch] + [pltpu.SemaphoreType.DMA((SEMS,))],
        compiler_params=pltpu.CompilerParams(vmem_limit_bytes=56 * MIB),
        cost_estimate=pl.CostEstimate(flops=flops, bytes_accessed=moved, transcendentals=0),
        name=name,
    )(*ins)


def saved_shapes(rows):
    crops = rows // SLOTS
    return [
        ((rows, 3 * D), BF),
        ((PAIRS * crops, 2 * SLOTS, SLOTS), BF),
        ((rows, D), BF),
        ((rows, D), BF),
        ((rows, 128), F32),
        ((rows, D), BF),
        ((rows, FF), BF),
        ((rows, FF), BF),
        ((rows, D), BF),
        ((rows, 128), F32),
    ]


def fetch_rows(copies, refs, kinds, x):
    waits = []
    half = refs[0].shape[1] if "halves" in kinds else SLOTS // 2
    for c in range(x.shape[0] // SLOTS):
        for h in range(SLOTS // half):
            at = slice(SLOTS * c + half * h, SLOTS * c + half * (h + 1))
            options = []
            if "halves" in kinds:
                options.append(refs[h].at[c])
            if "whole" in kinds:
                options.append(refs[-1].at[at, :])
            waits.append(copies.pick((options[0], options[-1]), x.at[at, :]))
    return waits


def read_vectors(refs, key):
    if key:
        b, g, up = refs
        rows = b[0].astype(F32)
        rows = [rows[i : i + 1] for i in range(6)]
    else:
        b, g, up, q = refs
        rows = b[0].astype(F32)
        rows = [q[...].astype(F32)] + [rows[i : i + 1] for i in range(5)]
    gains = g[0].astype(F32)
    return rows + [gains[0:1], gains[1:2]], up[...].astype(F32)


def load_vectors(refs, kinds, vec, bup):
    sets = []
    for kind in kinds:
        n = 3 if kind == "key" else 4
        sets.append(read_vectors(refs[:n], kind == "key"))
        refs = refs[n:]
    here = lax.axis_index("section")
    for i in range(8):
        row = sets[0][0][i]
        if len(sets) == 2:
            row = jnp.where(here == 0, row, sets[1][0][i])
        vec[i : i + 1, :] = row
    up = sets[0][1]
    if len(sets) == 2:
        up = jnp.where(here == 0, up, sets[1][1])
    bup[...] = up


def forward_kernel(rows, active, save, x_kinds, sets, *refs):
    def run():
        forward_body(rows, save, x_kinds, sets, *refs)

    only_on(active, run)


def forward_body(rows, save, x_kinds, sets, *refs):
    crops = rows // SLOTS
    lens_refs, refs = refs[: len(sets)], refs[len(sets) :]
    here = lax.axis_index("section")
    if len(sets) == 2:
        lens = [jnp.where(here == 0, lens_refs[0][c], lens_refs[1][c]) for c in range(crops)]
    else:
        lens = [lens_refs[0][c] for c in range(crops)]
    n_x = (2 if "halves" in x_kinds else 0) + (1 if "whole" in x_kinds else 0)
    x_refs, refs = refs[:n_x], refs[n_x:]
    w_refs, refs = refs[: 4 * len(sets)], refs[4 * len(sets) :]
    n_v = sum(3 if k == "key" else 4 for k in sets)
    v_refs, refs = refs[:n_v], refs[n_v:]
    y_ref, pool_ref = refs[:2]
    refs = refs[2:]
    if save:
        (qkv_o, prob_o, ctx_o, n1_o, r1_o, first_o, hid_o, slope_o, n2_o, r2_o) = refs[:10]
        refs = refs[10:]
    (x, wqkv, wout, wup, wdown, ctx, zbuf, first, hid, vec, bup) = refs[:11]
    refs = refs[11:]
    if save:
        (qkv, prob, n1, r1, slope, n2, r2) = refs[:7]
        refs = refs[7:]
    copies = Copies(refs[0])
    got_x = fetch_rows(copies, x_refs, x_kinds, x)
    pairs = [(w_refs[i], w_refs[4 + i] if len(sets) == 2 else w_refs[i]) for i in range(4)]
    got_qkv = copies.pick(pairs[0], wqkv)
    load_vectors(v_refs, sets, vec, bup)
    for cp in got_x:
        cp.wait()
    got_qkv.wait()
    got_out = copies.pick(pairs[1], wout)
    got_up = copies.pick(pairs[2], wup)
    got_down = copies.pick(pairs[3], wdown)
    keycol = lax.broadcasted_iota(jnp.int32, (1, SLOTS), 1)
    gain1, gain2 = vec[6:7], vec[7:8]

    def heads(i, carry):
        thirds = []
        for j in range(3):
            cols = pl.ds(pl.multiple_of(D * j + 256 * i, 256), 256)
            part = dot(x[...], wqkv[:, cols])
            if j != 1:
                at = pl.ds(pl.multiple_of(256 * i, 256), 256)
                part = part + vec[j // 2 : j // 2 + 1, at]
            part = part.astype(BF)
            if save:
                qkv[:, cols] = part
            thirds.append(part)
        for c in range(crops):
            crop = slice(SLOTS * c, SLOTS * (c + 1))
            for pr in range(2):
                qp, kp, vp = [t[crop, 128 * pr : 128 * (pr + 1)] for t in thirds]
                scores = jnp.where(keycol < lens[c], dot_nt(stack_heads(qp, 0.125), kp), MASKED)
                e = jnp.exp(scores - jnp.max(scores, axis=-1, keepdims=True))
                p = (e * pl.reciprocal(jnp.sum(e, axis=-1, keepdims=True))).astype(BF)
                if save:
                    prob[PAIRS * c + 2 * i + pr] = p
                at = pl.ds(pl.multiple_of(256 * i + 128 * pr, 128), 128)
                ctx[crop, at] = dot(side_by_side(p), stack_heads(vp, 1.0)).astype(BF)
        return carry

    lax.fori_loop(0, 3, heads, 0)
    if save:
        copies.send(qkv, qkv_o)
        copies.send(prob, prob_o)
        copies.send(ctx, ctx_o)
    got_out.wait()
    for j in range(3):
        cols = slice(256 * j, 256 * (j + 1))
        zbuf[:, cols] = x[:, cols].astype(F32) + dot(ctx[...], wout[:, cols]) + vec[2:3, cols]
    block = 64
    steps = rows // block

    def first_norm(i, carry):
        at = pl.ds(pl.multiple_of(i * block, block), block)
        n, r = norm_parts(zbuf[at, :])
        f = (n * gain1 + vec[3:4]).astype(BF)
        first[at, :] = f
        zbuf[at, :] = f.astype(F32) + vec[4:5]
        if save:
            n1[at, :] = n.astype(BF)
            r1[at, :] = jnp.broadcast_to(r, (block, 128))
        return carry

    lax.fori_loop(0, steps, first_norm, 0, unroll=True)
    if save:
        copies.send(n1, n1_o)
        copies.send(r1, r1_o)
        copies.send(first, first_o)
    got_up.wait()
    got_down.wait()

    def down_part(k):
        cols = slice(512 * k, 512 * (k + 1))
        zbuf[...] += dot(hid[:, cols], wdown[cols, :])

    for i in range(12):
        cols = slice(256 * i, 256 * (i + 1))
        g, slope_part = gelu_parts(dot(first[...], wup[:, cols]) + bup[:, cols], save)
        hid[:, cols] = g.astype(BF)
        if save:
            slope[:, cols] = slope_part.astype(BF)
        if i % 2 and i > 2:
            down_part(i // 2 - 1)
    if save:
        copies.send(hid, hid_o)
        copies.send(slope, slope_o)
    down_part(5)
    pool_ref[...] = jnp.zeros_like(pool_ref)
    per_crop = SLOTS // block
    for i in range(steps):
        at = slice(i * block, (i + 1) * block)
        n, r = norm_parts(zbuf[at, :])
        f = n * gain2 + vec[5:6]
        y_ref[at, :] = f.astype(BF)
        if save:
            n2[at, :] = n.astype(BF)
            r2[at, :] = jnp.broadcast_to(r, (block, 128))
        c = i // per_crop
        token = lax.broadcasted_iota(jnp.int32, (block, 1), 0) + (i % per_crop) * block
        part = jnp.sum(jnp.where(token < lens[c], f, 0.0), axis=0, keepdims=True)
        pool_ref[c : c + 1, :] += part / lens[c].astype(F32)
    if save:
        copies.send(n2, n2_o)
        copies.send(r2, r2_o)
    copies.drain()


def forward(rows, active, save, halves, whole, encoders):
    x_kinds = (("halves",) if halves else ()) + (("whole",) if whole is not None else ())
    xs = list(halves or ()) + ([whole] if whole is not None else [])
    lens = [e[1] for e in encoders]
    weights = [w for e in encoders for w in e[2]]
    vectors = [v for e in encoders for v in e[3]]
    outs = [((rows, D), BF), ((8, D), F32)]
    out_specs = [VMEM, VMEM]
    scratch = [
        ((rows, D), BF),
        ((D, 3 * D), BF),
        ((D, D), BF),
        ((D, FF), BF),
        ((FF, D), BF),
        ((rows, D), BF),
        ((rows, D), F32),
        ((rows, D), BF),
        ((rows, FF), BF),
        ((8, D), F32),
        ((1, FF), F32),
    ]
    if save:
        kept = saved_shapes(rows)
        outs += kept
        out_specs += [ANY] * len(kept)
        scratch += [kept[i] for i in (0, 1, 3, 4, 7, 8, 9)]
    return call(
        functools.partial(forward_kernel, rows, active, save, x_kinds, [e[0] for e in encoders]),
        "layer_forward",
        outs,
        out_specs,
        [*lens, *xs, *weights, *vectors],
        [SMEM] * len(lens) + [ANY] * (len(xs) + len(weights)) + [VMEM] * len(vectors),
        scratch,
        rows * 15000000,
        16000000 + (15000000 if save else 0),
    )


def split3(v):
    hi = v.astype(BF)
    rest = v - hi.astype(F32)
    mid = rest.astype(BF)
    lo = (rest - mid.astype(F32)).astype(BF)
    return hi, mid, lo


def stack3(v):
    parts = split3(v)
    return jnp.concatenate(list(parts) + [jnp.zeros_like(parts[0])] * 5, axis=0)


def unstack3(rows, n):
    return rows[:n] + rows[n : 2 * n] + rows[2 * n : 3 * n]


def queue_norm_kernel(active, queue_h, inv_ref, queue, sems):
    def run():
        Copies(sems).fetch(queue_h, queue).wait()

        def step(i, carry):
            at = pl.ds(pl.multiple_of(i * 512, 512), 512)
            v = queue[at, :].astype(F32)
            sq = v * v
            hi = sq.astype(BF)
            lo = (sq - hi.astype(F32)).astype(BF)
            ones = jnp.ones((8, D), BF)
            total = dot_nt(ones, hi) + dot_nt(ones, lo)
            inv_ref[:, at] = lax.rsqrt(total + 1e-6)
            return carry

        lax.fori_loop(0, queue.shape[0] // 512, step, 0)

    only_on(active, run)


def loss_kernel(active, crops, count, pooled, matched, queue, inv, grad_ref, loss_ref, sems):
    def run():
        v = pooled[:crops]
        r = lax.rsqrt(jnp.sum(v * v, axis=-1, keepdims=True) + 1e-6)
        u = v * r
        k = matched[:crops]
        near = jnp.sum(u * k, axis=-1, keepdims=True) * 20.0
        inv_row = inv[0:1]
        far = unstack3(dot_nt(stack3(u), queue[...]), crops) * (inv_row * 20.0)
        top = jnp.maximum(near, jnp.max(far, axis=-1, keepdims=True))
        e_near = jnp.exp(near - top)
        e_far = jnp.exp(far - top)
        total = e_near + jnp.sum(e_far, axis=-1, keepdims=True)
        share = 20.0 / (total * count)
        d_u = unstack3(dot(stack3(e_far * inv_row * share), queue[...]), crops)
        d_u = d_u + (e_near - total) * share * k
        grad = r * (d_u - u * jnp.sum(u * d_u, axis=-1, keepdims=True))
        grad_ref[...] = jnp.zeros_like(grad_ref)
        grad_ref[:crops] = grad
        lost = jnp.sum(top + jnp.log(total) - near, axis=0, keepdims=True) / count
        loss_ref[...] = jnp.broadcast_to(lost, loss_ref.shape)

    only_on(active, run)


def norm_back(dy, gain, n, r):
    dn = dy * gain
    return r * (dn - jnp.mean(dn, axis=-1, keepdims=True) - n * jnp.mean(dn * n, axis=-1, keepdims=True))


def column_sum(v):
    return jnp.sum(v, axis=0, keepdims=True)


def fast_mesh():
    return lax.axis_size("dp") == 8 and lax.axis_size("rep") == 2


def place_bits():
    dp, rep = lax.axis_index("dp"), lax.axis_index("rep")
    return dp // 2, dp % 2, rep


def norm_backward_kernel(rows, active, pooled, lens, dy, n2, r2, gains, ddown_ref, dsum_ref, vec_ref, sems):
    def run():
        gain = gains[0].astype(F32)[1:2]
        vec_ref[...] = jnp.zeros_like(vec_ref)
        block = 64
        per_crop = SLOTS // block
        for i in range(rows // block):
            at = slice(block * i, block * (i + 1))
            c = i // per_crop
            if pooled:
                token = lax.broadcasted_iota(jnp.int32, (block, 1), 0) + (i % per_crop) * block
                grow = jnp.where(token < lens[c], 1.0 / lens[c].astype(F32), 0.0) * dy[c : c + 1]
            else:
                grow = dy[at].astype(F32)
            n = n2[at].astype(F32)
            ds = norm_back(grow, gain, n, r2[at, 0:1])
            low = ds.astype(BF)
            dsum_ref[at] = ds
            ddown_ref[at] = low
            vec_ref[0:1] += column_sum(grow * n)
            vec_ref[1:2] += column_sum(grow)
            vec_ref[2:3] += column_sum(low.astype(F32))

    only_on(active, run)


def norm_backward(active, pooled, lens, dy, n2, r2, gains):
    rows = n2.shape[0]
    return call(
        functools.partial(norm_backward_kernel, rows, active, pooled),
        "second_norm_backward",
        [((rows, D), BF), ((rows, D), F32), ((8, D), F32)],
        [VMEM] * 3,
        [lens, dy, n2, r2, gains],
        [SMEM] + [VMEM] * 4,
        [],
        rows * 30 * D,
        5000000,
    )


CHUNK = 512


def ffn_backward_kernel(rows, active, ddown, dsum2, n1, r1, gains, slope_h, wdown_h, wup_h, *refs):
    def run():
        datt_ref, dsum_ref, vec_ref, bup_ref, dup_h, slope, wdown, wup, acc, dup, sems = refs
        copies = Copies(sems)
        got = []
        for i in range(FF // CHUNK):
            cols = slice(CHUNK * i, CHUNK * (i + 1))
            got.append(
                [
                    copies.fetch(wdown_h.at[cols, :], wdown.at[cols, :]),
                    copies.fetch(slope_h.at[:, cols], slope.at[:, cols]),
                    copies.fetch(wup_h.at[:, cols], wup.at[:, cols]),
                ]
            )
        vec_ref[...] = jnp.zeros_like(vec_ref)
        acc[...] = dsum2[...]
        for i in range(FF // CHUNK):
            cols = slice(CHUNK * i, CHUNK * (i + 1))
            for cp in got[i]:
                cp.wait()
            up = (dot_nt(ddown[...], wdown[cols, :]) * slope[:, cols].astype(F32)).astype(BF)
            dup[:, cols] = up
            copies.send(dup.at[:, cols], dup_h.at[:, cols])
            bup_ref[:, cols] = jnp.broadcast_to(column_sum(up.astype(F32)), (8, CHUNK))
            acc[...] += dot_nt(up, wup[:, cols])
        gain = gains[0].astype(F32)[0:1]
        block = 64
        for i in range(rows // block):
            at = slice(block * i, block * (i + 1))
            n = n1[at].astype(F32)
            dfirst = acc[at]
            ds = norm_back(dfirst, gain, n, r1[at, 0:1])
            low = ds.astype(BF)
            dsum_ref[at] = ds
            datt_ref[at] = low
            vec_ref[0:1] += column_sum(dfirst * n)
            vec_ref[1:2] += column_sum(dfirst)
            vec_ref[2:3] += column_sum(low.astype(F32))
        copies.drain()

    only_on(active, run)


def ffn_backward(active, ddown, dsum2, n1, r1, gains, slope, wdown, wup):
    rows = n1.shape[0]
    return call(
        functools.partial(ffn_backward_kernel, rows, active),
        "ffn_backward",
        [((rows, D), BF), ((rows, D), F32), ((8, D), F32), ((8, FF), F32), ((rows, FF), BF)],
        [VMEM] * 4 + [ANY],
        [ddown, dsum2, n1, r1, gains, slope, wdown, wup],
        [VMEM] * 5 + [ANY] * 3,
        [((rows, FF), BF), ((FF, D), BF), ((D, FF), BF), ((rows, D), F32), ((rows, FF), BF)],
        rows * 4 * FF * D,
        24000000,
    )


def ffn_weights_kernel(rows, active, fast, *refs):
    def run():
        if fast:
            first_h, first_p, ddown_h, ddown_p, hid_h, dup_h, wup_h, wdown_h, bup_h, send, keep = refs[:11]
            first, ddown, hid, dup, gup, gdown, wup, wdown, bup, sems = refs[11:]
        else:
            first_h, ddown_h, hid_h, dup_h, up_o, down_o = refs[:6]
            first, ddown, hid, dup, gup, gdown, sems = refs[6:]
        copies = Copies(sems)
        own = slice(0, rows)
        got = [copies.fetch(first_h, first.at[own, :]), copies.fetch(ddown_h, ddown.at[own, :])]
        z, x, y = place_bits()
        parts = 4 if fast else FF // 384
        if fast:
            peer = slice(rows, 2 * rows)
            got += [copies.fetch(first_p, first.at[peer, :]), copies.fetch(ddown_p, ddown.at[peer, :])]
            got.append(copies.fetch(bup_h, bup))
        blocks = []
        for i in range(parts):
            here = slice(384 * i, 384 * (i + 1))
            there = pl.ds(pl.multiple_of(768 * i + 384 * x, 128), 384) if fast else here
            block = [
                copies.fetch(hid_h.at[:, there], hid.at[own, here]),
                copies.fetch(dup_h.at[:, there], dup.at[own, here]),
            ]
            if fast:
                block.append(copies.fetch(wup_h.at[:, there], wup.at[:, here]))
                block.append(copies.fetch(wdown_h.at[there, :], wdown.at[here, :]))
            blocks.append(block)
        for cp in got:
            cp.wait()
        for i in range(parts):
            here = slice(384 * i, 384 * (i + 1))
            for cp in blocks[i]:
                cp.wait()
            if fast:
                there = pl.ds(pl.multiple_of(768 * i + 384 * x, 128), 384)
                bias = bup[:, there].astype(F32)
                g, slope = gelu_parts(dot(first[peer, :], wup[:, here]) + bias, True)
                hid[peer, here] = g.astype(BF)
                dup[peer, here] = (dot_nt(ddown[peer, :], wdown[here, :]) * slope).astype(BF)
            gdown[here, :] = dot_tn(hid[:, here], ddown[...]).astype(BF)
            gup[:, here] = dot_tn(first[...], dup[:, here]).astype(BF)
        if not fast:
            copies.send(gup, up_o)
            copies.send(gdown, down_o)
        else:
            for jy in (1, 0):
                out = send if jy else keep
                for jz in (3, 2, 1, 0):
                    zz, yy = jnp.bitwise_xor(z, jz), jnp.bitwise_xor(y, jy)
                    for jx in range(2):
                        owner = (zz * 2 + jnp.bitwise_xor(x, jx)) * 2 + yy
                        at = pl.ds(pl.multiple_of(48 * owner, 16), 48)
                        for c in range(2):
                            copies.send(
                                gup.at[at, slice(768 * c, 768 * (c + 1))],
                                out.at[jz, slice(96 * jx + 48 * c, 96 * jx + 48 * (c + 1)), :],
                            )
                    at = pl.ds(pl.multiple_of(384 * zz + 192 * yy, 64), 192)
                    copies.send(gdown.at[at, :], out.at[jz, 192:384, :])
        copies.drain()

    only_on(active, run)


def ffn_weights(active, first, first_peer, ddown, ddown_peer, hid, dup, wup, wdown, bup):
    rows = first.shape[0]
    fast = fast_mesh()
    if fast:
        ins = [first, first_peer, ddown, ddown_peer, hid, dup, wup, wdown, bup]
        outs = [((4, 384, D), BF)] * 2
        tokens, units = 2 * rows, FF // 2
        extra = [((D, units), BF), ((units, D), BF), ((1, FF), BF)]
    else:
        ins = [first, ddown, hid, dup]
        outs = [((D, FF), BF), ((FF, D), BF)]
        tokens, units, extra = rows, FF, []
    return call(
        functools.partial(ffn_weights_kernel, rows, active, fast),
        "ffn_weights",
        outs,
        [ANY] * 2,
        ins,
        [ANY] * len(ins),
        [
            ((tokens, D), BF),
            ((tokens, D), BF),
            ((tokens, units), BF),
            ((tokens, units), BF),
            ((D, units), BF),
            ((units, D), BF),
        ]
        + extra,
        rows * 6 * FF * D,
        20000000,
    )


def attention_backward_kernel(rows, active, datt, dsum1, qkv_h, prob_h, wout_h, wqkv_h, *refs):
    def run():
        dx_ref, vec_ref, dqkv_o, qkv, prob, wout, wqkv, dqkv, sems = refs
        copies = Copies(sems)
        got_out = copies.fetch(wout_h, wout)
        got_qkv = copies.fetch(qkv_h, qkv)
        got_prob = copies.fetch(prob_h, prob)
        got_w = copies.fetch(wqkv_h, wqkv)
        got_out.wait()
        dctx = dot_nt(datt[...], wout[...]).astype(BF)
        got_qkv.wait()
        got_prob.wait()
        for c in range(rows // SLOTS):
            crop = slice(SLOTS * c, SLOTS * (c + 1))
            for pr in range(PAIRS):
                cols = [slice(D * j + 128 * pr, D * j + 128 * (pr + 1)) for j in range(3)]
                qp, kp, vp = [qkv[crop, t] for t in cols]
                dcs = stack_heads(dctx[crop, 128 * pr : 128 * (pr + 1)], 1.0)
                p = prob[PAIRS * c + pr]
                pf = p.astype(F32)
                weighted = pf * dot_nt(dcs, vp)
                ds = (weighted - pf * jnp.sum(weighted, axis=-1, keepdims=True)).astype(BF)
                dqkv[crop, cols[0]] = dot(side_by_side(ds), stack_heads(kp, 0.125)).astype(BF)
                dqkv[crop, cols[1]] = dot_tn(ds, stack_heads(qp, 0.125)).astype(BF)
                dqkv[crop, cols[2]] = dot_tn(p, dcs).astype(BF)
        copies.send(dqkv, dqkv_o)
        vec_ref[...] = jnp.zeros_like(vec_ref)
        vec_ref[0:1] = column_sum(dqkv[:, :D].astype(F32))
        vec_ref[1:2] = column_sum(dqkv[:, 2 * D :].astype(F32))
        got_w.wait()
        for j in range(3):
            cols = slice(256 * j, 256 * (j + 1))
            dx_ref[:, cols] = (dot_nt(dqkv[...], wqkv[cols, :]) + dsum1[:, cols]).astype(BF)
        copies.drain()

    only_on(active, run)


def attention_backward(active, datt, dsum1, qkv, prob, wout, wqkv):
    rows = datt.shape[0]
    return call(
        functools.partial(attention_backward_kernel, rows, active),
        "attention_backward",
        [((rows, D), BF), ((8, D), F32), ((rows, 3 * D), BF)],
        [VMEM] * 2 + [ANY],
        [datt, dsum1, qkv, prob, wout, wqkv],
        [VMEM] * 2 + [ANY] * 4,
        [(qkv.shape, BF), (prob.shape, BF), (wout.shape, BF), (wqkv.shape, BF), (qkv.shape, BF)],
        rows * (4 * D * D * 2 + 10 * SLOTS * D),
        22000000,
    )


def attention_weights_kernel(rows, active, fast, x_kinds, *refs):
    def run():
        n_x = len(x_kinds) + 1
        x_refs = refs[:n_x]
        ctx_h, datt_h, dqkv_h, out_a, out_b, x, ctx, datt, dqkv, gqkv, gout, sems = refs[n_x:]
        copies = Copies(sems)
        got = [copies.fetch(ctx_h, ctx), copies.fetch(datt_h, datt)]
        got_x = fetch_rows(copies, x_refs, x_kinds, x)
        got_x.append(copies.fetch(dqkv_h, dqkv))
        for cp in got:
            cp.wait()
        gout[...] = dot_tn(ctx[...], datt[...]).astype(BF)
        for cp in got_x:
            cp.wait()
        for j in range(6):
            cols = slice(384 * j, 384 * (j + 1))
            gqkv[:, cols] = dot_tn(x[...], dqkv[:, cols]).astype(BF)
        if not fast:
            copies.send(gqkv, out_a)
            copies.send(gout, out_b)
        else:
            z, xx, y = place_bits()
            for j in range(15, -1, -1):
                jx, jy, jz = j // 8, j // 4 % 2, j % 4
                owner = (jnp.bitwise_xor(z, jz) * 2 + jnp.bitwise_xor(xx, jx)) * 2 + jnp.bitwise_xor(y, jy)
                at = pl.ds(pl.multiple_of(48 * owner, 16), 48)
                out = (out_b if jx else out_a).at[j % 8]
                for t in range(3):
                    copies.send(gqkv.at[at, slice(D * t, D * (t + 1))], out.at[48 * t : 48 * (t + 1), :])
                copies.send(gout.at[at, :], out.at[144:192, :])
        copies.drain()

    only_on(active, run)


def attention_weights(active, halves, whole, ctx, datt, dqkv):
    rows = ctx.shape[0]
    fast = fast_mesh()
    x_kinds = ("halves", "whole")
    outs = [((8, 192, D), BF)] * 2 if fast else [((D, 3 * D), BF), ((D, D), BF)]
    ins = [*halves, whole, ctx, datt, dqkv]
    return call(
        functools.partial(attention_weights_kernel, rows, active, fast, x_kinds),
        "attention_weights",
        outs,
        [ANY] * 2,
        ins,
        [ANY] * len(ins),
        [((rows, D), BF)] * 3 + [((rows, 3 * D), BF), ((D, 3 * D), BF), ((D, D), BF)],
        rows * 8 * D * D,
        12000000,
    )


AXES = ("section", "dp", "rep")


def swap(block, section, dp_flip, rep_flip):
    dps, reps = lax.axis_size("dp"), lax.axis_size("rep")
    sections = range(lax.axis_size("section")) if section is None else [section]
    route = [
        ((s * dps + d) * reps + r, (s * dps + (d ^ dp_flip)) * reps + (r ^ rep_flip))
        for s in sections
        for d in range(dps)
        for r in range(reps)
    ]
    return lax.ppermute(block, AXES, route)


def flips():
    out, bit = [], 1
    while bit < lax.axis_size("rep"):
        out.append((0, bit))
        bit *= 2
    bit = 1
    while bit < lax.axis_size("dp"):
        out.append((bit, 0))
        bit *= 2
    return out


def low(v):
    return v.astype(BF)


def wide(*terms):
    total = terms[0].astype(F32)
    for t in terms[1:]:
        total = total + t.astype(F32)
    return total


def attention_sum(keep, send, section):
    first = swap(send, section, 1, 0)
    second = swap(low(wide(keep[4:], first[4:])), section, 0, 1)
    parts = [wide(keep[k], first[k], second[k]) for k in range(4)]
    others = [swap(low(parts[k]), section, 2 * k, 0) for k in range(1, 4)]
    return wide(parts[0], *others)


def ffn_sum(keep, send, section):
    first = swap(send, section, 0, 1)
    parts = [wide(keep[k], first[k]) for k in range(4)]
    others = [swap(low(parts[k]), section, 2 * k, 0) for k in range(1, 4)]
    return wide(parts[0], *others)


def body(
    query_crops,
    key_crops,
    query_lengths,
    key_lengths,
    positive,
    queue,
    qkv_weight,
    out_weight,
    up_weight,
    down_weight,
    biases,
    gains,
    up_biases,
    query_bias,
    key_qkv_weight,
    key_out_weight,
    key_up_weight,
    key_down_weight,
    key_biases,
    key_gains,
    key_up_biases,
):
    crops = query_crops.shape[0]
    rows = crops * SLOTS
    sections, dps, reps = [lax.axis_size(a) for a in AXES]
    fast = fast_mesh()
    crop_all = crops * dps * reps
    on_first = lax.axis_index("section") == 0
    dp, rep = lax.axis_index("dp"), lax.axis_index("rep")
    last = sections - 1

    def relay(block, distance):
        return lax.ppermute(block, "section", [(0, 1)] if distance > 0 else [(1, 0)])

    key_halves = (key_crops, relay(key_crops, -1))
    query_halves = (query_crops, relay(query_crops, -1))
    query_weights = [w[0] for w in (qkv_weight, out_weight, up_weight, down_weight)]
    key_weights = [w[0] for w in (key_qkv_weight, key_out_weight, key_up_weight, key_down_weight)]
    query_encoder = ("query", query_lengths, query_weights, (biases, gains, up_biases, query_bias))
    key_encoder = ("key", key_lengths, key_weights, (key_biases, key_gains, key_up_biases))

    key_middle, _ = forward(rows, 0, False, key_halves, None, [key_encoder])
    inv = call(
        functools.partial(queue_norm_kernel, last),
        "queue_norm",
        [((8, queue.shape[0]), F32)],
        [VMEM],
        [queue],
        [ANY],
        [(queue.shape, BF)],
        8 * queue.size,
        queue.size * 2,
    )[0]
    key_middle, inv = lax.optimization_barrier((key_middle, inv))
    key_middle = relay(key_middle, 1)
    query_middle, key_pooled = forward(rows, None, False, query_halves, key_middle, [query_encoder, key_encoder])
    query_middle = relay(query_middle, 1)

    every_key = key_pooled[:crops]
    every_key = every_key * lax.rsqrt(jnp.sum(every_key * every_key, axis=-1, keepdims=True) + 1e-6)
    near_flips = [(0, 1), (1, 0), (1, 1)]
    if fast:
        every_key = jnp.concatenate([every_key] + [swap(every_key, None, *f) for f in near_flips], axis=0)
    step = forward(rows, None, True, query_halves, query_middle, [query_encoder])
    query_pooled = step[1]
    qkv, prob, ctx, n1, r1, first, hid, slope, n2, r2 = step[2:]

    if fast:
        every_key, query_pooled = lax.optimization_barrier((every_key, query_pooled))
        every_key = jnp.concatenate([every_key] + [swap(every_key, None, 2 * k, 0) for k in range(1, 4)], axis=0)
    else:
        for flip in flips():
            every_key = jnp.concatenate([every_key, swap(every_key, None, *flip)], axis=0)
    place = dp * reps + rep
    matched = jnp.take(every_key, jnp.bitwise_xor(positive // crops, place) * crops + positive % crops, axis=0)
    matched = jnp.concatenate([matched, jnp.zeros((8 - crops, D), F32)], axis=0)
    first_peer = swap(first, None, 1, 0) if fast else None

    pooled_grad, lost = call(
        functools.partial(loss_kernel, last, crops, crop_all),
        "contrast",
        [((8, D), F32), ((8, 128), F32)],
        [VMEM] * 2,
        [query_pooled, matched, queue, inv],
        [VMEM] * 4,
        [],
        16 * 2 * queue.size,
        queue.size * 2,
    )

    def ffn_part(active, pooled, dy):
        ddown, dsum2, vec_a = norm_backward(active, pooled, query_lengths, dy, n2, r2, gains)
        ddown_peer = swap(ddown, active, 1, 0) if fast else None
        datt, dsum1, vec_b, grad_bup, dup = ffn_backward(
            active, ddown, dsum2, n1, r1, gains, slope, query_weights[3], query_weights[2]
        )
        return ddown, ddown_peer, dup, datt, dsum1, vec_a, vec_b, grad_bup

    def ffn_grads(active, ddown, ddown_peer, dup):
        return ffn_weights(
            active, first, first_peer, ddown, ddown_peer, hid, dup, query_weights[2], query_weights[3], up_biases
        )

    def attention_part(active, datt, dsum1):
        return attention_backward(active, datt, dsum1, qkv, prob, query_weights[1], query_weights[0])

    def attention_grads(active, datt, dqkv):
        return attention_weights(active, query_halves, query_middle, ctx, datt, dqkv)

    def small_rows(vec_a, vec_b, vec_c, grad_bup):
        picked = [vec_c[1:2], vec_b[2:3], vec_b[1:2], vec_a[2:3], vec_a[1:2], vec_b[0:1], vec_a[0:1], vec_c[0:1]]
        return jnp.concatenate(picked + [grad_bup[0:1].reshape(FF // D, D)], axis=0)

    ddown, ddown_peer, dup, datt, dsum1, vec_a, vec_b, grad_bup = ffn_part(last, True, pooled_grad)
    dmiddle, vec_c, dqkv = attention_part(last, datt, dsum1)
    small_last = small_rows(vec_a, vec_b, vec_c, grad_bup)
    dmiddle = relay(dmiddle, -1)
    attention_last = attention_grads(last, datt, dqkv)
    ffn_last = ffn_grads(last, ddown, ddown_peer, dup)

    ddown, ddown_peer, dup, datt, dsum1, vec_a, vec_b, grad_bup = ffn_part(0, False, dmiddle)
    ffn_first = ffn_grads(0, ddown, ddown_peer, dup)
    dx, vec_c, dqkv = attention_part(0, datt, dsum1)
    small_first = small_rows(vec_a, vec_b, vec_c, grad_bup)
    attention_first = attention_grads(0, datt, dqkv)

    if fast:
        attention_total = [attention_sum(*attention_first, 0), attention_sum(*attention_last, last)]
        ffn_total = [ffn_sum(ffn_first[1], ffn_first[0], 0), ffn_sum(ffn_last[1], ffn_last[0], last)]
        attention_total = jnp.where(on_first, *attention_total)
        ffn_total = jnp.where(on_first, *ffn_total)
        grad_qkv = jnp.concatenate([attention_total[48 * t : 48 * (t + 1)] for t in range(3)], axis=1)
        grad_out = attention_total[144:]
        grad_down = ffn_total[192:]

        def joined(rows96):
            return jnp.concatenate([rows96[:48], rows96[48:96]], axis=1).reshape(48, 4, 384)

        own = joined(ffn_total[:96])
        peer = swap(joined(ffn_total[96:192]), None, 1, 0)
        even = dp % 2 == 0
        grad_up = jnp.stack([jnp.where(even, own, peer), jnp.where(even, peer, own)], axis=2).reshape(48, FF)
    else:
        totals = [
            lax.psum_scatter(jnp.where(on_first, a, b).astype(F32), ("dp", "rep"), scatter_dimension=0, tiled=True)
            for a, b in zip([*ffn_first, *attention_first], [*ffn_last, *attention_last])
        ]
        grad_up, grad_down, grad_qkv, grad_out = totals

    small = jnp.where(on_first, small_first, small_last)
    loss_row = jnp.where(on_first, 0.0, jnp.concatenate([lost[0:1]] * (D // 128), axis=1))
    small = jnp.concatenate([small, loss_row], axis=0)
    for flip in flips():
        small = small + swap(small, None, *flip)
    loss_value = jnp.where(on_first, relay(small[12, :128], -1), small[12, :128])[:1]
    width = D // (dps * reps)
    mine = lax.dynamic_slice(small[:8], (0, place * width), (8, width))
    up_part = lax.dynamic_slice(small[8:12].reshape(FF), (place * (FF // (dps * reps)),), (FF // (dps * reps),))

    dx = dx.reshape(crops, SLOTS, D)
    half = SLOTS // sections
    crops_grad = jnp.where(on_first, dx[:, :half], lax.ppermute(dx[:, half:], "section", [(0, 1)])).astype(F32)
    return (
        loss_value,
        crops_grad,
        grad_qkv[None],
        grad_out[None],
        grad_up[None],
        grad_down[None],
        mine[None, :5],
        mine[None, 5:7],
        up_part[None],
        mine[None, 7],
    )


def solution(mesh):
    crop = P(("dp", "rep"), "section", None)
    per_crop = P(("dp", "rep"))
    layer3 = P("section", None, None)
    layer2 = P("section", None)
    placed = (
        (crop, crop, per_crop, per_crop, per_crop, P())
        + (layer3,) * 6
        + (layer2,) * 2
        + (layer3,) * 6
        + (layer2,)
    )
    shared3 = P("section", ("dp", "rep"), None)
    return jax.shard_map(
        body,
        mesh=mesh,
        in_specs=placed,
        out_specs=(
            P(),
            crop,
            shared3,
            shared3,
            shared3,
            shared3,
            P("section", None, ("dp", "rep")),
            P("section", None, ("dp", "rep")),
            P("section", ("dp", "rep")),
            P("section", ("dp", "rep")),
        ),
        check_vma=False,
    )
```

```python
import functools

import jax
import jax.numpy as jnp
from jax import lax
from jax.experimental import pallas as pl
from jax.experimental.pallas import tpu as pltpu
from jax.sharding import PartitionSpec as P

F32 = jnp.float32
BF = jnp.bfloat16
MASKED = -1e30
D = 768
FF = 3072
SLOTS = 256
PAIRS = 6
MIB = 2**20
SEMS = 96


def dot(a, b):
    return lax.dot_general(a, b, (((1,), (0,)), ((), ())), preferred_element_type=F32)


def dot_nt(a, b):
    return lax.dot_general(a, b, (((1,), (1,)), ((), ())), preferred_element_type=F32)


def dot_tn(a, b):
    return lax.dot_general(a, b, (((0,), (0,)), ((), ())), preferred_element_type=F32)


def gelu_parts(x, want_slope):
    ax = jnp.abs(x)
    t = pl.reciprocal(1.0 + (0.3275911 * 0.7071067811865476) * ax)
    e = jnp.exp(-0.5 * (x * x))
    poly = (0.5 * 1.061405429) * t + 0.5 * -1.453152027
    poly = poly * t + 0.5 * 1.421413741
    poly = poly * t + 0.5 * -0.284496736
    poly = poly * t + 0.5 * 0.254829592
    q = poly * t * e
    g = jnp.maximum(x, 0.0) - ax * q
    if not want_slope:
        return g, None
    return g, jnp.where(x >= 0, 1.0 - q, q) + (0.3989422804014327 * x) * e


def norm_parts(z):
    mean = jnp.mean(z, axis=-1, keepdims=True)
    c = z - mean
    var = jnp.mean(c * c, axis=-1, keepdims=True)
    r = lax.rsqrt(var + 1e-12)
    return c * r, r


def head_masks(scale):
    lane = lax.broadcasted_iota(jnp.int32, (1, 128), 1)
    low = jnp.where(lane < 64, scale, 0.0).astype(BF)
    high = jnp.where(lane < 64, 0.0, scale).astype(BF)
    return low, high


def stack_heads(pair, scale):
    low, high = head_masks(scale)
    return jnp.concatenate([pair * low, pair * high], axis=0)


def side_by_side(stacked):
    half = stacked.shape[0] // 2
    return jnp.concatenate([stacked[:half], stacked[half:]], axis=1)


class Copies:
    def __init__(self, sems):
        self.sems, self.used, self.open = sems, 0, []

    def make(self, src, dst):
        self.used += 1
        return pltpu.make_async_copy(src, dst, self.sems.at[self.used - 1])

    def fetch(self, src, dst):
        cp = self.make(src, dst)
        cp.start()
        return cp

    def pick(self, by_section, dst):
        if by_section[0] is by_section[1]:
            return self.fetch(by_section[0], dst)
        sem = self.sems.at[self.used]
        self.used += 1
        here = lax.axis_index("section")

        @pl.when(here == 0)
        def _():
            pltpu.make_async_copy(by_section[0], dst, sem).start()

        @pl.when(here != 0)
        def _():
            pltpu.make_async_copy(by_section[1], dst, sem).start()

        return pltpu.make_async_copy(by_section[0], dst, sem)

    def send(self, src, dst):
        self.open.append(self.fetch(src, dst))

    def drain(self):
        for cp in self.open:
            cp.wait()


def only_on(section, run):
    if section is None:
        run()
    else:
        pl.when(lax.axis_index("section") == section)(run)


VMEM = pl.BlockSpec(memory_space=pltpu.VMEM)
ANY = pl.BlockSpec(memory_space=pl.ANY)
SMEM = pl.BlockSpec(memory_space=pltpu.SMEM)
sd = jax.ShapeDtypeStruct


def call(kernel, name, outs, out_specs, ins, in_specs, scratch, flops, moved):
    return pl.pallas_call(
        kernel,
        out_shape=[sd(*o) for o in outs],
        in_specs=in_specs,
        out_specs=out_specs,
        scratch_shapes=[pltpu.VMEM(*s) for s in scratch] + [pltpu.SemaphoreType.DMA((SEMS,))],
        compiler_params=pltpu.CompilerParams(vmem_limit_bytes=56 * MIB),
        cost_estimate=pl.CostEstimate(flops=flops, bytes_accessed=moved, transcendentals=0),
        name=name,
    )(*ins)


def saved_shapes(rows):
    crops = rows // SLOTS
    return [
        ((rows, 3 * D), BF),
        ((PAIRS * crops, 2 * SLOTS, SLOTS), BF),
        ((rows, D), BF),
        ((rows, D), BF),
        ((rows, 128), F32),
        ((rows, D), BF),
        ((rows, FF), BF),
        ((rows, FF), BF),
        ((rows, D), BF),
        ((rows, 128), F32),
    ]


def fetch_rows(copies, refs, kinds, x):
    waits = []
    half = refs[0].shape[1] if "halves" in kinds else SLOTS // 2
    for c in range(x.shape[0] // SLOTS):
        for h in range(SLOTS // half):
            at = slice(SLOTS * c + half * h, SLOTS * c + half * (h + 1))
            options = []
            if "halves" in kinds:
                options.append(refs[h].at[c])
            if "whole" in kinds:
                options.append(refs[-1].at[at, :])
            waits.append(copies.pick((options[0], options[-1]), x.at[at, :]))
    return waits


def read_vectors(refs, key):
    if key:
        b, g, up = refs
        rows = b[0].astype(F32)
        rows = [rows[i : i + 1] for i in range(6)]
    else:
        b, g, up, q = refs
        rows = b[0].astype(F32)
        rows = [q[...].astype(F32)] + [rows[i : i + 1] for i in range(5)]
    gains = g[0].astype(F32)
    return rows + [gains[0:1], gains[1:2]], up[...].astype(F32)


def load_vectors(refs, kinds, vec, bup):
    sets = []
    for kind in kinds:
        n = 3 if kind == "key" else 4
        sets.append(read_vectors(refs[:n], kind == "key"))
        refs = refs[n:]
    here = lax.axis_index("section")
    for i in range(8):
        row = sets[0][0][i]
        if len(sets) == 2:
            row = jnp.where(here == 0, row, sets[1][0][i])
        vec[i : i + 1, :] = row
    up = sets[0][1]
    if len(sets) == 2:
        up = jnp.where(here == 0, up, sets[1][1])
    bup[...] = up


def forward_kernel(rows, active, save, x_kinds, sets, *refs):
    def run():
        forward_body(rows, save, x_kinds, sets, *refs)

    only_on(active, run)


def forward_body(rows, save, x_kinds, sets, *refs):
    crops = rows // SLOTS
    lens_refs, refs = refs[: len(sets)], refs[len(sets) :]
    here = lax.axis_index("section")
    if len(sets) == 2:
        lens = [jnp.where(here == 0, lens_refs[0][c], lens_refs[1][c]) for c in range(crops)]
    else:
        lens = [lens_refs[0][c] for c in range(crops)]
    n_x = (2 if "halves" in x_kinds else 0) + (1 if "whole" in x_kinds else 0)
    x_refs, refs = refs[:n_x], refs[n_x:]
    w_refs, refs = refs[: 4 * len(sets)], refs[4 * len(sets) :]
    n_v = sum(3 if k == "key" else 4 for k in sets)
    v_refs, refs = refs[:n_v], refs[n_v:]
    y_ref, pool_ref = refs[:2]
    refs = refs[2:]
    if save:
        (qkv_o, prob_o, ctx_o, n1_o, r1_o, first_o, hid_o, slope_o, n2_o, r2_o) = refs[:10]
        refs = refs[10:]
    (x, wqkv, wout, wup, wdown, ctx, zbuf, first, hid, vec, bup) = refs[:11]
    refs = refs[11:]
    if save:
        (qkv, prob, n1, r1, slope, n2, r2) = refs[:7]
        refs = refs[7:]
    copies = Copies(refs[0])
    got_x = fetch_rows(copies, x_refs, x_kinds, x)
    pairs = [(w_refs[i], w_refs[4 + i] if len(sets) == 2 else w_refs[i]) for i in range(4)]
    got_qkv = copies.pick(pairs[0], wqkv)
    load_vectors(v_refs, sets, vec, bup)
    for cp in got_x:
        cp.wait()
    got_qkv.wait()
    got_out = copies.pick(pairs[1], wout)
    got_up = copies.pick(pairs[2], wup)
    got_down = copies.pick(pairs[3], wdown)
    keycol = lax.broadcasted_iota(jnp.int32, (1, SLOTS), 1)
    gain1, gain2 = vec[6:7], vec[7:8]

    def heads(i, carry):
        thirds = []
        for j in range(3):
            cols = pl.ds(pl.multiple_of(D * j + 256 * i, 256), 256)
            part = dot(x[...], wqkv[:, cols])
            if j != 1:
                at = pl.ds(pl.multiple_of(256 * i, 256), 256)
                part = part + vec[j // 2 : j // 2 + 1, at]
            part = part.astype(BF)
            if save:
                qkv[:, cols] = part
            thirds.append(part)
        for c in range(crops):
            crop = slice(SLOTS * c, SLOTS * (c + 1))
            for pr in range(2):
                qp, kp, vp = [t[crop, 128 * pr : 128 * (pr + 1)] for t in thirds]
                scores = jnp.where(keycol < lens[c], dot_nt(stack_heads(qp, 0.125), kp), MASKED)
                e = jnp.exp(scores - jnp.max(scores, axis=-1, keepdims=True))
                p = (e * pl.reciprocal(jnp.sum(e, axis=-1, keepdims=True))).astype(BF)
                if save:
                    prob[PAIRS * c + 2 * i + pr] = p
                at = pl.ds(pl.multiple_of(256 * i + 128 * pr, 128), 128)
                ctx[crop, at] = dot(side_by_side(p), stack_heads(vp, 1.0)).astype(BF)
        return carry

    lax.fori_loop(0, 3, heads, 0)
    if save:
        copies.send(qkv, qkv_o)
        copies.send(prob, prob_o)
        copies.send(ctx, ctx_o)
    got_out.wait()
    for j in range(3):
        cols = slice(256 * j, 256 * (j + 1))
        zbuf[:, cols] = x[:, cols].astype(F32) + dot(ctx[...], wout[:, cols]) + vec[2:3, cols]
    block = 64
    steps = rows // block

    def first_norm(i, carry):
        at = pl.ds(pl.multiple_of(i * block, block), block)
        n, r = norm_parts(zbuf[at, :])
        f = (n * gain1 + vec[3:4]).astype(BF)
        first[at, :] = f
        zbuf[at, :] = f.astype(F32) + vec[4:5]
        if save:
            n1[at, :] = n.astype(BF)
            r1[at, :] = jnp.broadcast_to(r, (block, 128))
        return carry

    lax.fori_loop(0, steps, first_norm, 0, unroll=True)
    if save:
        copies.send(n1, n1_o)
        copies.send(r1, r1_o)
        copies.send(first, first_o)
    got_up.wait()
    got_down.wait()

    def down_part(k):
        cols = slice(512 * k, 512 * (k + 1))
        zbuf[...] += dot(hid[:, cols], wdown[cols, :])

    for i in range(12):
        cols = slice(256 * i, 256 * (i + 1))
        g, slope_part = gelu_parts(dot(first[...], wup[:, cols]) + bup[:, cols], save)
        hid[:, cols] = g.astype(BF)
        if save:
            slope[:, cols] = slope_part.astype(BF)
        if i % 2 and i > 2:
            down_part(i // 2 - 1)
    if save:
        copies.send(hid, hid_o)
        copies.send(slope, slope_o)
    down_part(5)
    pool_ref[...] = jnp.zeros_like(pool_ref)
    per_crop = SLOTS // block
    for i in range(steps):
        at = slice(i * block, (i + 1) * block)
        n, r = norm_parts(zbuf[at, :])
        f = n * gain2 + vec[5:6]
        y_ref[at, :] = f.astype(BF)
        if save:
            n2[at, :] = n.astype(BF)
            r2[at, :] = jnp.broadcast_to(r, (block, 128))
        c = i // per_crop
        token = lax.broadcasted_iota(jnp.int32, (block, 1), 0) + (i % per_crop) * block
        part = jnp.sum(jnp.where(token < lens[c], f, 0.0), axis=0, keepdims=True)
        pool_ref[c : c + 1, :] += part / lens[c].astype(F32)
    pooled = pool_ref[:crops]
    pool_ref[crops : 2 * crops] = pooled * lax.rsqrt(jnp.sum(pooled * pooled, axis=-1, keepdims=True) + 1e-6)
    if save:
        copies.send(n2, n2_o)
        copies.send(r2, r2_o)
    copies.drain()


def forward(rows, active, save, halves, whole, encoders):
    x_kinds = (("halves",) if halves else ()) + (("whole",) if whole is not None else ())
    xs = list(halves or ()) + ([whole] if whole is not None else [])
    lens = [e[1] for e in encoders]
    weights = [w for e in encoders for w in e[2]]
    vectors = [v for e in encoders for v in e[3]]
    outs = [((rows, D), BF), ((8, D), F32)]
    out_specs = [VMEM, VMEM]
    scratch = [
        ((rows, D), BF),
        ((D, 3 * D), BF),
        ((D, D), BF),
        ((D, FF), BF),
        ((FF, D), BF),
        ((rows, D), BF),
        ((rows, D), F32),
        ((rows, D), BF),
        ((rows, FF), BF),
        ((8, D), F32),
        ((1, FF), F32),
    ]
    if save:
        kept = saved_shapes(rows)
        outs += kept
        out_specs += [ANY] * len(kept)
        scratch += [kept[i] for i in (0, 1, 3, 4, 7, 8, 9)]
    return call(
        functools.partial(forward_kernel, rows, active, save, x_kinds, [e[0] for e in encoders]),
        "layer_forward",
        outs,
        out_specs,
        [*lens, *xs, *weights, *vectors],
        [SMEM] * len(lens) + [ANY] * (len(xs) + len(weights)) + [VMEM] * len(vectors),
        scratch,
        rows * 15000000,
        16000000 + (15000000 if save else 0),
    )


def split3(v):
    hi = v.astype(BF)
    rest = v - hi.astype(F32)
    mid = rest.astype(BF)
    lo = (rest - mid.astype(F32)).astype(BF)
    return hi, mid, lo


def stack3(v):
    parts = split3(v)
    return jnp.concatenate(list(parts) + [jnp.zeros_like(parts[0])] * 5, axis=0)


def unstack3(rows, n):
    return rows[:n] + rows[n : 2 * n] + rows[2 * n : 3 * n]


def queue_norm_kernel(active, queue_h, inv_ref, queue, sems):
    def run():
        Copies(sems).fetch(queue_h, queue).wait()

        def step(i, carry):
            at = pl.ds(pl.multiple_of(i * 512, 512), 512)
            v = queue[at, :].astype(F32)
            sq = v * v
            hi = sq.astype(BF)
            lo = (sq - hi.astype(F32)).astype(BF)
            ones = jnp.ones((8, D), BF)
            total = dot_nt(ones, hi) + dot_nt(ones, lo)
            inv_ref[:, at] = lax.rsqrt(total + 1e-6)
            return carry

        lax.fori_loop(0, queue.shape[0] // 512, step, 0)

    only_on(active, run)


def loss_kernel(active, crops, count, pooled, matched, queue, inv, grad_ref, loss_ref, sems):
    def run():
        v = pooled[:crops]
        r = lax.rsqrt(jnp.sum(v * v, axis=-1, keepdims=True) + 1e-6)
        u = v * r
        k = matched[:crops]
        near = jnp.sum(u * k, axis=-1, keepdims=True) * 20.0
        inv_row = inv[0:1]
        far = unstack3(dot_nt(stack3(u), queue[...]), crops) * (inv_row * 20.0)
        top = jnp.maximum(near, jnp.max(far, axis=-1, keepdims=True))
        e_near = jnp.exp(near - top)
        e_far = jnp.exp(far - top)
        total = e_near + jnp.sum(e_far, axis=-1, keepdims=True)
        share = 20.0 / (total * count)
        d_u = unstack3(dot(stack3(e_far * inv_row * share), queue[...]), crops)
        d_u = d_u + (e_near - total) * share * k
        grad = r * (d_u - u * jnp.sum(u * d_u, axis=-1, keepdims=True))
        grad_ref[...] = jnp.zeros_like(grad_ref)
        grad_ref[:crops] = grad
        lost = jnp.sum(top + jnp.log(total) - near, axis=0, keepdims=True) / count
        loss_ref[...] = jnp.broadcast_to(lost, loss_ref.shape)

    only_on(active, run)


def norm_back(dy, gain, n, r):
    dn = dy * gain
    return r * (dn - jnp.mean(dn, axis=-1, keepdims=True) - n * jnp.mean(dn * n, axis=-1, keepdims=True))


def column_sum(v):
    return jnp.sum(v, axis=0, keepdims=True)


def fast_mesh():
    return lax.axis_size("dp") == 8 and lax.axis_size("rep") == 2


def place_bits():
    dp, rep = lax.axis_index("dp"), lax.axis_index("rep")
    return dp // 2, dp % 2, rep


def norm_backward_kernel(rows, active, pooled, lens, dy, n2, r2, gains, ddown_ref, dsum_ref, vec_ref, sems):
    def run():
        gain = gains[0].astype(F32)[1:2]
        vec_ref[...] = jnp.zeros_like(vec_ref)
        block = 64
        per_crop = SLOTS // block
        for i in range(rows // block):
            at = slice(block * i, block * (i + 1))
            c = i // per_crop
            if pooled:
                token = lax.broadcasted_iota(jnp.int32, (block, 1), 0) + (i % per_crop) * block
                grow = jnp.where(token < lens[c], 1.0 / lens[c].astype(F32), 0.0) * dy[c : c + 1]
            else:
                grow = dy[at].astype(F32)
            n = n2[at].astype(F32)
            ds = norm_back(grow, gain, n, r2[at, 0:1])
            low = ds.astype(BF)
            dsum_ref[at] = ds
            ddown_ref[at] = low
            vec_ref[0:1] += column_sum(grow * n)
            vec_ref[1:2] += column_sum(grow)
            vec_ref[2:3] += column_sum(low.astype(F32))

    only_on(active, run)


def norm_backward(active, pooled, lens, dy, n2, r2, gains):
    rows = n2.shape[0]
    return call(
        functools.partial(norm_backward_kernel, rows, active, pooled),
        "second_norm_backward",
        [((rows, D), BF), ((rows, D), F32), ((8, D), F32)],
        [VMEM] * 3,
        [lens, dy, n2, r2, gains],
        [SMEM] + [VMEM] * 4,
        [],
        rows * 30 * D,
        5000000,
    )


CHUNK = 512


def ffn_backward_kernel(rows, active, ddown, dsum2, n1, r1, gains, slope_h, wdown_h, wup_h, *refs):
    def run():
        datt_ref, dsum_ref, vec_ref, bup_ref, dup_h, slope, wdown, wup, acc, dup, sems = refs
        copies = Copies(sems)
        got = []
        for i in range(FF // CHUNK):
            cols = slice(CHUNK * i, CHUNK * (i + 1))
            got.append(
                [
                    copies.fetch(wdown_h.at[cols, :], wdown.at[cols, :]),
                    copies.fetch(slope_h.at[:, cols], slope.at[:, cols]),
                    copies.fetch(wup_h.at[:, cols], wup.at[:, cols]),
                ]
            )
        vec_ref[...] = jnp.zeros_like(vec_ref)
        acc[...] = dsum2[...]
        for i in range(FF // CHUNK):
            cols = slice(CHUNK * i, CHUNK * (i + 1))
            for cp in got[i]:
                cp.wait()
            up = (dot_nt(ddown[...], wdown[cols, :]) * slope[:, cols].astype(F32)).astype(BF)
            dup[:, cols] = up
            copies.send(dup.at[:, cols], dup_h.at[:, cols])
            bup_ref[:, cols] = jnp.broadcast_to(column_sum(up.astype(F32)), (8, CHUNK))
            acc[...] += dot_nt(up, wup[:, cols])
        gain = gains[0].astype(F32)[0:1]
        block = 64
        for i in range(rows // block):
            at = slice(block * i, block * (i + 1))
            n = n1[at].astype(F32)
            dfirst = acc[at]
            ds = norm_back(dfirst, gain, n, r1[at, 0:1])
            low = ds.astype(BF)
            dsum_ref[at] = ds
            datt_ref[at] = low
            vec_ref[0:1] += column_sum(dfirst * n)
            vec_ref[1:2] += column_sum(dfirst)
            vec_ref[2:3] += column_sum(low.astype(F32))
        copies.drain()

    only_on(active, run)


def ffn_backward(active, ddown, dsum2, n1, r1, gains, slope, wdown, wup):
    rows = n1.shape[0]
    return call(
        functools.partial(ffn_backward_kernel, rows, active),
        "ffn_backward",
        [((rows, D), BF), ((rows, D), F32), ((8, D), F32), ((8, FF), F32), ((rows, FF), BF)],
        [VMEM] * 4 + [ANY],
        [ddown, dsum2, n1, r1, gains, slope, wdown, wup],
        [VMEM] * 5 + [ANY] * 3,
        [((rows, FF), BF), ((FF, D), BF), ((D, FF), BF), ((rows, D), F32), ((rows, FF), BF)],
        rows * 4 * FF * D,
        24000000,
    )


def ffn_weights_kernel(rows, active, fast, *refs):
    def run():
        if fast:
            first_h, first_p, ddown_h, ddown_p, hid_h, dup_h, wup_h, wdown_h, bup_h, send, keep = refs[:11]
            first, ddown, hid, dup, gup, gdown, wup, wdown, bup, sems = refs[11:]
        else:
            first_h, ddown_h, hid_h, dup_h, up_o, down_o = refs[:6]
            first, ddown, hid, dup, gup, gdown, sems = refs[6:]
        copies = Copies(sems)
        own = slice(0, rows)
        got = [copies.fetch(first_h, first.at[own, :]), copies.fetch(ddown_h, ddown.at[own, :])]
        z, x, y = place_bits()
        parts = 4 if fast else FF // 384
        if fast:
            peer = slice(rows, 2 * rows)
            got += [copies.fetch(first_p, first.at[peer, :]), copies.fetch(ddown_p, ddown.at[peer, :])]
            got.append(copies.fetch(bup_h, bup))
        blocks = []
        for i in range(parts):
            here = slice(384 * i, 384 * (i + 1))
            there = pl.ds(pl.multiple_of(768 * i + 384 * x, 128), 384) if fast else here
            block = [
                copies.fetch(hid_h.at[:, there], hid.at[own, here]),
                copies.fetch(dup_h.at[:, there], dup.at[own, here]),
            ]
            if fast:
                block.append(copies.fetch(wup_h.at[:, there], wup.at[:, here]))
                block.append(copies.fetch(wdown_h.at[there, :], wdown.at[here, :]))
            blocks.append(block)
        for cp in got:
            cp.wait()
        for i in range(parts):
            here = slice(384 * i, 384 * (i + 1))
            for cp in blocks[i]:
                cp.wait()
            if fast:
                there = pl.ds(pl.multiple_of(768 * i + 384 * x, 128), 384)
                bias = bup[:, there].astype(F32)
                g, slope = gelu_parts(dot(first[peer, :], wup[:, here]) + bias, True)
                hid[peer, here] = g.astype(BF)
                dup[peer, here] = (dot_nt(ddown[peer, :], wdown[here, :]) * slope).astype(BF)
            gdown[here, :] = dot_tn(hid[:, here], ddown[...]).astype(BF)
            gup[:, here] = dot_tn(first[...], dup[:, here]).astype(BF)
        if not fast:
            copies.send(gup, up_o)
            copies.send(gdown, down_o)
        else:
            for jy in (1, 0):
                out = send if jy else keep
                for jz in (3, 2, 1, 0):
                    zz, yy = jnp.bitwise_xor(z, jz), jnp.bitwise_xor(y, jy)
                    for jx in range(2):
                        owner = (zz * 2 + jnp.bitwise_xor(x, jx)) * 2 + yy
                        at = pl.ds(pl.multiple_of(48 * owner, 16), 48)
                        for c in range(2):
                            copies.send(
                                gup.at[at, slice(768 * c, 768 * (c + 1))],
                                out.at[jz, slice(96 * jx + 48 * c, 96 * jx + 48 * (c + 1)), :],
                            )
                    at = pl.ds(pl.multiple_of(384 * zz + 192 * yy, 64), 192)
                    copies.send(gdown.at[at, :], out.at[jz, 192:384, :])
        copies.drain()

    only_on(active, run)


def ffn_weights(active, first, first_peer, ddown, ddown_peer, hid, dup, wup, wdown, bup):
    rows = first.shape[0]
    fast = fast_mesh()
    if fast:
        ins = [first, first_peer, ddown, ddown_peer, hid, dup, wup, wdown, bup]
        outs = [((4, 384, D), BF)] * 2
        tokens, units = 2 * rows, FF // 2
        extra = [((D, units), BF), ((units, D), BF), ((1, FF), BF)]
    else:
        ins = [first, ddown, hid, dup]
        outs = [((D, FF), BF), ((FF, D), BF)]
        tokens, units, extra = rows, FF, []
    return call(
        functools.partial(ffn_weights_kernel, rows, active, fast),
        "ffn_weights",
        outs,
        [ANY] * 2,
        ins,
        [ANY] * len(ins),
        [
            ((tokens, D), BF),
            ((tokens, D), BF),
            ((tokens, units), BF),
            ((tokens, units), BF),
            ((D, units), BF),
            ((units, D), BF),
        ]
        + extra,
        rows * 6 * FF * D,
        20000000,
    )


def attention_backward_kernel(rows, active, datt, dsum1, qkv_h, prob_h, wout_h, wqkv_h, *refs):
    def run():
        dx_ref, vec_ref, dqkv_o, qkv, prob, wout, wqkv, dqkv, sems = refs
        copies = Copies(sems)
        got_out = copies.fetch(wout_h, wout)
        got_qkv = copies.fetch(qkv_h, qkv)
        got_prob = copies.fetch(prob_h, prob)
        got_w = copies.fetch(wqkv_h, wqkv)
        got_out.wait()
        dctx = dot_nt(datt[...], wout[...]).astype(BF)
        got_qkv.wait()
        got_prob.wait()
        for c in range(rows // SLOTS):
            crop = slice(SLOTS * c, SLOTS * (c + 1))
            for pr in range(PAIRS):
                cols = [slice(D * j + 128 * pr, D * j + 128 * (pr + 1)) for j in range(3)]
                qp, kp, vp = [qkv[crop, t] for t in cols]
                dcs = stack_heads(dctx[crop, 128 * pr : 128 * (pr + 1)], 1.0)
                p = prob[PAIRS * c + pr]
                pf = p.astype(F32)
                weighted = pf * dot_nt(dcs, vp)
                ds = (weighted - pf * jnp.sum(weighted, axis=-1, keepdims=True)).astype(BF)
                dqkv[crop, cols[0]] = dot(side_by_side(ds), stack_heads(kp, 0.125)).astype(BF)
                dqkv[crop, cols[1]] = dot_tn(ds, stack_heads(qp, 0.125)).astype(BF)
                dqkv[crop, cols[2]] = dot_tn(p, dcs).astype(BF)
        copies.send(dqkv, dqkv_o)
        vec_ref[...] = jnp.zeros_like(vec_ref)
        vec_ref[0:1] = column_sum(dqkv[:, :D].astype(F32))
        vec_ref[1:2] = column_sum(dqkv[:, 2 * D :].astype(F32))
        got_w.wait()
        for j in range(3):
            cols = slice(256 * j, 256 * (j + 1))
            dx_ref[:, cols] = (dot_nt(dqkv[...], wqkv[cols, :]) + dsum1[:, cols]).astype(BF)
        copies.drain()

    only_on(active, run)


def attention_backward(active, datt, dsum1, qkv, prob, wout, wqkv):
    rows = datt.shape[0]
    return call(
        functools.partial(attention_backward_kernel, rows, active),
        "attention_backward",
        [((rows, D), BF), ((8, D), F32), ((rows, 3 * D), BF)],
        [VMEM] * 2 + [ANY],
        [datt, dsum1, qkv, prob, wout, wqkv],
        [VMEM] * 2 + [ANY] * 4,
        [(qkv.shape, BF), (prob.shape, BF), (wout.shape, BF), (wqkv.shape, BF), (qkv.shape, BF)],
        rows * (4 * D * D * 2 + 10 * SLOTS * D),
        22000000,
    )


def attention_weights_kernel(rows, active, fast, x_kinds, *refs):
    def run():
        n_x = len(x_kinds) + 1
        x_refs = refs[:n_x]
        if fast:
            vec_a, vec_b, vec_c, bup, lost, *refs_ = refs[n_x:]
            ctx_h, datt_h, dqkv_h, out_a, out_b, x, ctx, datt, dqkv, gqkv, gout, tail, sems = refs_
        else:
            ctx_h, datt_h, dqkv_h, out_a, out_b, x, ctx, datt, dqkv, gqkv, gout, sems = refs[n_x:]
        copies = Copies(sems)
        got = [copies.fetch(ctx_h, ctx), copies.fetch(datt_h, datt)]
        got_x = fetch_rows(copies, x_refs, x_kinds, x)
        got_x.append(copies.fetch(dqkv_h, dqkv))
        for cp in got:
            cp.wait()
        gout[...] = dot_tn(ctx[...], datt[...]).astype(BF)
        for cp in got_x:
            cp.wait()
        for j in range(6):
            cols = slice(384 * j, 384 * (j + 1))
            gqkv[:, cols] = dot_tn(x[...], dqkv[:, cols]).astype(BF)
        if not fast:
            copies.send(gqkv, out_a)
            copies.send(gout, out_b)
        else:
            z, xx, y = place_bits()
            picked = [vec_c[1:2], vec_b[2:3], vec_b[1:2], vec_a[2:3], vec_a[1:2], vec_b[0:1], vec_a[0:1], vec_c[0:1]]
            small = jnp.concatenate([p[...] for p in picked], axis=0)
            row = lax.broadcasted_iota(jnp.int32, (8, D), 0)
            lane = lax.broadcasted_iota(jnp.int32, (8, D), 1) - 3 * ((z * 2 + xx) * 2 + y)
            terms = [jnp.broadcast_to(t.astype(F32)[0:1, 0:1], (8, D)) for t in split3(lost[...])]
            lost_row = sum(jnp.where(lane == i, t, 0.0) for i, t in enumerate(terms))
            for j in range(16):
                jx, jy, jz = j // 8, j // 4 % 2, j % 4
                owner = (jnp.bitwise_xor(z, jz) * 2 + jnp.bitwise_xor(xx, jx)) * 2 + jnp.bitwise_xor(y, jy)
                head = pltpu.roll(small, D - 48 * owner, 1)
                ups = pltpu.roll(bup[...], FF - 192 * owner, 1)[:, :D]
                other = jnp.where(row == 0, ups, jnp.where(row == 1, lost_row, 0.0))
                tail[j] = jnp.concatenate([head, other], axis=0).astype(BF)
            for j in range(15, -1, -1):
                jx, jy, jz = j // 8, j // 4 % 2, j % 4
                owner = (jnp.bitwise_xor(z, jz) * 2 + jnp.bitwise_xor(xx, jx)) * 2 + jnp.bitwise_xor(y, jy)
                at = pl.ds(pl.multiple_of(48 * owner, 16), 48)
                out = (out_b if jx else out_a).at[j % 8]
                for t in range(3):
                    copies.send(gqkv.at[at, slice(D * t, D * (t + 1))], out.at[48 * t : 48 * (t + 1), :])
                copies.send(gout.at[at, :], out.at[144:192, :])
                copies.send(tail.at[j], out.at[192:208, :])
        copies.drain()

    only_on(active, run)


def attention_weights(active, halves, whole, ctx, datt, dqkv, small):
    rows = ctx.shape[0]
    fast = fast_mesh()
    x_kinds = ("halves", "whole")
    outs = [((8, 208, D), BF)] * 2 if fast else [((D, 3 * D), BF), ((D, D), BF)]
    ins = [*halves, whole, *(small if fast else ()), ctx, datt, dqkv]
    in_specs = [ANY] * 3 + [VMEM] * (5 if fast else 0) + [ANY] * 3
    return call(
        functools.partial(attention_weights_kernel, rows, active, fast, x_kinds),
        "attention_weights",
        outs,
        [ANY] * 2,
        ins,
        in_specs,
        [((rows, D), BF)] * 3
        + [((rows, 3 * D), BF), ((D, 3 * D), BF), ((D, D), BF)]
        + ([((16, 16, D), BF)] if fast else []),
        rows * 8 * D * D,
        12000000,
    )


AXES = ("section", "dp", "rep")


def swap(block, section, dp_flip, rep_flip):
    dps, reps = lax.axis_size("dp"), lax.axis_size("rep")
    sections = range(lax.axis_size("section")) if section is None else [section]
    route = [
        ((s * dps + d) * reps + r, (s * dps + (d ^ dp_flip)) * reps + (r ^ rep_flip))
        for s in sections
        for d in range(dps)
        for r in range(reps)
    ]
    return lax.ppermute(block, AXES, route)


def flips():
    out, bit = [], 1
    while bit < lax.axis_size("rep"):
        out.append((0, bit))
        bit *= 2
    bit = 1
    while bit < lax.axis_size("dp"):
        out.append((bit, 0))
        bit *= 2
    return out


def add_rows(pieces, dst, at, count):
    def step(i, carry):
        here = pl.ds(pl.multiple_of(i * 16, 16), 16)
        total = pieces[0][here, :].astype(F32)
        for p in pieces[1:]:
            total = total + p[here, :].astype(F32)
        dst[pl.ds(pl.multiple_of(at + i * 16, 16), 16), :] = total.astype(dst.dtype)
        return carry

    lax.fori_loop(0, count // 16, step, 0, unroll=2 if count % 32 == 0 else 1)


def partial_kernel(active, slots, joined, n_in, rows, *refs):
    def run():
        ins, outs = refs[:n_in], refs[n_in : n_in + (1 if joined else len(slots))]
        held, made, sems = refs[-3:]
        copies = Copies(sems)
        got = [[copies.fetch(r.at[k], held.at[i, t]) for t, r in enumerate(ins)] for i, k in enumerate(slots)]
        for i in range(len(slots)):
            for cp in got[i]:
                cp.wait()
            add_rows([held.at[i, t] for t in range(n_in)], made.at[i], 0, rows)
            copies.send(made.at[i], outs[0].at[i] if joined else outs[i])
        copies.drain()

    only_on(active, run)


def partial_sums(active, slots, joined, ins):
    shape = ins[0].shape[1:]
    n = len(slots)
    outs = [((n, *shape), BF)] if joined else [(shape, BF)] * n
    made = call(
        functools.partial(partial_kernel, active, slots, joined, len(ins), shape[0]),
        "partial_sums",
        outs,
        [ANY] * len(outs),
        list(ins),
        [ANY] * len(ins),
        [((n, len(ins), *shape), BF), ((n, *shape), BF)],
        n * len(ins) * shape[0] * shape[1],
        2 * n * (len(ins) + 1) * shape[0] * shape[1],
    )
    return made[0] if joined else made


def fetch_terms(copies, refs, n_slotted, held):
    half = len(refs) // 2
    got = []
    for t in range(half):
        pair = (refs[t], refs[half + t])
        if t < n_slotted:
            pair = tuple(r.at[0] for r in pair)
        got.append(copies.pick(pair, held.at[t]))
    for cp in got:
        cp.wait()
    return [held.at[t] for t in range(half)]


def attention_total_kernel(*refs):
    qkv_o, out_o, bias_o, gain_o, query_o, up_o, loss_o, held, total, sems = refs[12:]
    terms = fetch_terms(Copies(sems), refs[:12], 3, held)
    add_rows(terms, total, 0, 208)
    for t in range(3):
        qkv_o[:, D * t : D * (t + 1)] = total[48 * t : 48 * (t + 1), :]
    out_o[...] = total[144:192, :]
    bias_o[...] = total[192:197, :48]
    gain_o[...] = total[197:199, :48]
    query_o[...] = total[199:200, :48]
    up_o[...] = total[200:201, :192]
    loss_o[...] = jnp.broadcast_to(jnp.sum(total[201:202, :], axis=-1, keepdims=True), loss_o.shape)


def ffn_total_kernel(*refs):
    down_o, own_o, peer_o, held, total, sems = refs[10:]
    terms = fetch_terms(Copies(sems), refs[:10], 2, held)
    add_rows(terms, total, 0, 384)
    own_o[...] = total[0:96, :]
    peer_o[...] = total[96:192, :].astype(BF)
    down_o[...] = total[192:384, :]


def up_total_kernel(own, peer, up_o, sems):
    x = lax.axis_index("dp") % 2
    for c in range(2):
        for k in range(2):
            cols = slice(384 * k, 384 * (k + 1))
            at = 768 * (2 * c + k)
            up_o[:, pl.ds(pl.multiple_of(at + 384 * x, 128), 384)] = own[48 * c : 48 * (c + 1), cols]
            up_o[:, pl.ds(pl.multiple_of(at + 384 * (1 - x), 128), 384)] = peer[48 * c : 48 * (c + 1), cols].astype(F32)


def totals(kernel, name, ins, rows, outs, in_spec=ANY):
    terms = len(ins) // 2
    scratch = [((terms, rows, D), BF), ((rows, D), F32)] if rows else []
    return call(kernel, name, outs, [VMEM] * len(outs), ins, [in_spec] * len(ins), scratch, 1000000, 4000000)


def after(value, *others):
    return lax.optimization_barrier((value, others))[0]


def chip_sums(attention, ffn, last):
    (ka0, sa0), (ka1, sa1) = attention
    (kf0, sf0), (kf1, sf1) = ffn
    a1 = swap(sa1, last, 1, 0)
    f1 = swap(sf1, last, 0, 1)
    f0 = swap(sf0, 0, 0, 1)
    a0 = swap(sa0, 0, 1, 0)
    distances = (1, 2, 3)

    def over_z(parts, section):
        return [swap(p, section, 2 * k, 0) for k, p in zip(distances, parts)]

    s1 = partial_sums(last, (4, 5, 6, 7), True, [ka1, after(a1, ka0)])
    b1 = swap(s1, last, 0, 1)
    p1 = partial_sums(last, distances, False, [kf1, after(f1, s1)])
    g1 = over_z(p1, last)
    p0 = partial_sums(0, distances, False, [kf0, after(f0, *p1)])
    g0 = over_z(p0, 0)
    s0 = partial_sums(0, (4, 5, 6, 7), True, [ka0, after(a0, *p0)])
    b0 = swap(s0, 0, 0, 1)
    q1 = partial_sums(last, distances, False, [ka1, a1, after(b1, s0)])
    h1 = over_z(q1, last)
    q0 = partial_sums(0, distances, False, [ka0, a0, after(b0, *q1)])
    h0 = over_z(q0, 0)
    down, own, peer = totals(
        ffn_total_kernel,
        "ffn_total",
        [kf0, f0, *g0, kf1, after(f1, *q0), *g1],
        384,
        [((192, D), F32), ((96, D), F32), ((96, D), BF)],
    )
    peer = swap(peer, None, 1, 0)
    qkv, out, bias, gain, query, up_bias, loss = totals(
        attention_total_kernel,
        "attention_total",
        [ka0, a0, b0, *h0, ka1, after(a1, down), b1, *h1],
        208,
        [((48, 3 * D), F32), ((48, D), F32), ((5, 48), F32), ((2, 48), F32), ((1, 48), F32), ((1, 192), F32), ((8, 128), F32)],
    )
    (up,) = totals(up_total_kernel, "up_total", [own, peer], 0, [((48, FF), F32)], VMEM)
    return qkv, out, up, down, bias, gain, up_bias, query, loss


def body(
    query_crops,
    key_crops,
    query_lengths,
    key_lengths,
    positive,
    queue,
    qkv_weight,
    out_weight,
    up_weight,
    down_weight,
    biases,
    gains,
    up_biases,
    query_bias,
    key_qkv_weight,
    key_out_weight,
    key_up_weight,
    key_down_weight,
    key_biases,
    key_gains,
    key_up_biases,
):
    crops = query_crops.shape[0]
    rows = crops * SLOTS
    sections, dps, reps = [lax.axis_size(a) for a in AXES]
    fast = fast_mesh()
    crop_all = crops * dps * reps
    on_first = lax.axis_index("section") == 0
    dp, rep = lax.axis_index("dp"), lax.axis_index("rep")
    last = sections - 1

    def relay(block, distance):
        return lax.ppermute(block, "section", [(0, 1)] if distance > 0 else [(1, 0)])

    key_halves = (key_crops, relay(key_crops, -1))
    query_halves = (query_crops, relay(query_crops, -1))
    query_weights = [w[0] for w in (qkv_weight, out_weight, up_weight, down_weight)]
    key_weights = [w[0] for w in (key_qkv_weight, key_out_weight, key_up_weight, key_down_weight)]
    query_encoder = ("query", query_lengths, query_weights, (biases, gains, up_biases, query_bias))
    key_encoder = ("key", key_lengths, key_weights, (key_biases, key_gains, key_up_biases))

    key_middle, _ = forward(rows, 0, False, key_halves, None, [key_encoder])
    inv = call(
        functools.partial(queue_norm_kernel, last),
        "queue_norm",
        [((8, queue.shape[0]), F32)],
        [VMEM],
        [queue],
        [ANY],
        [(queue.shape, BF)],
        8 * queue.size,
        queue.size * 2,
    )[0]
    key_middle, inv = lax.optimization_barrier((key_middle, inv))
    key_middle = relay(key_middle, 1)
    query_middle, key_pooled = forward(rows, None, False, query_halves, key_middle, [query_encoder, key_encoder])
    query_middle = relay(query_middle, 1)

    every_key = key_pooled[crops : 2 * crops]
    near_flips = [(0, 1), (1, 0), (1, 1)]
    if fast:
        every_key = jnp.concatenate([every_key] + [swap(every_key, None, *f) for f in near_flips], axis=0)
    step = forward(rows, None, True, query_halves, query_middle, [query_encoder])
    query_pooled = step[1]
    qkv, prob, ctx, n1, r1, first, hid, slope, n2, r2 = step[2:]

    if fast:
        every_key, query_pooled = lax.optimization_barrier((every_key, query_pooled))
        every_key = jnp.concatenate([every_key] + [swap(every_key, None, 2 * k, 0) for k in range(1, 4)], axis=0)
    else:
        for flip in flips():
            every_key = jnp.concatenate([every_key, swap(every_key, None, *flip)], axis=0)
    place = dp * reps + rep
    matched = jnp.take(every_key, jnp.bitwise_xor(positive // crops, place) * crops + positive % crops, axis=0)
    matched = jnp.concatenate([matched, jnp.zeros((8 - crops, D), F32)], axis=0)
    first_peer = swap(first, None, 1, 0) if fast else None

    pooled_grad, lost = call(
        functools.partial(loss_kernel, last, crops, crop_all),
        "contrast",
        [((8, D), F32), ((8, 128), F32)],
        [VMEM] * 2,
        [query_pooled, matched, queue, inv],
        [VMEM] * 4,
        [],
        16 * 2 * queue.size,
        queue.size * 2,
    )

    def ffn_part(active, pooled, dy):
        ddown, dsum2, vec_a = norm_backward(active, pooled, query_lengths, dy, n2, r2, gains)
        ddown_peer = swap(ddown, active, 1, 0) if fast else None
        datt, dsum1, vec_b, grad_bup, dup = ffn_backward(
            active, ddown, dsum2, n1, r1, gains, slope, query_weights[3], query_weights[2]
        )
        return ddown, ddown_peer, dup, datt, dsum1, vec_a, vec_b, grad_bup

    def ffn_grads(active, ddown, ddown_peer, dup):
        return ffn_weights(
            active, first, first_peer, ddown, ddown_peer, hid, dup, query_weights[2], query_weights[3], up_biases
        )

    def attention_part(active, datt, dsum1):
        return attention_backward(active, datt, dsum1, qkv, prob, query_weights[1], query_weights[0])

    def attention_grads(active, datt, dqkv, small):
        return attention_weights(active, query_halves, query_middle, ctx, datt, dqkv, small)

    def small_rows(vec_a, vec_b, vec_c, grad_bup, lost):
        picked = [vec_c[1:2], vec_b[2:3], vec_b[1:2], vec_a[2:3], vec_a[1:2], vec_b[0:1], vec_a[0:1], vec_c[0:1]]
        lost_row = jnp.concatenate([lost[0:1]] * (D // 128), axis=1)
        return jnp.concatenate(picked + [grad_bup[0:1].reshape(FF // D, D), lost_row], axis=0)

    ddown, ddown_peer, dup, datt, dsum1, vec_a, vec_b, grad_bup = ffn_part(last, True, pooled_grad)
    dmiddle, vec_c, dqkv = attention_part(last, datt, dsum1)
    small_last = (vec_a, vec_b, vec_c, grad_bup, lost)
    dmiddle = relay(dmiddle, -1)
    attention_last = attention_grads(last, datt, dqkv, small_last)
    ffn_last = ffn_grads(last, ddown, ddown_peer, dup)

    ddown, ddown_peer, dup, datt, dsum1, vec_a, vec_b, grad_bup = ffn_part(0, False, after(dmiddle, *ffn_last))
    ffn_first = ffn_grads(0, ddown, ddown_peer, dup)
    dx, vec_c, dqkv = attention_part(0, after(datt, *ffn_first), dsum1)
    small_first = (vec_a, vec_b, vec_c, grad_bup, jnp.zeros_like(lost))
    attention_first = attention_grads(0, datt, dqkv, small_first)

    if fast:
        summed = chip_sums((attention_first, attention_last), (ffn_first[::-1], ffn_last[::-1]), last)
        grad_qkv, grad_out, grad_up, grad_down, bias, gain, up_part, query_part, loss_row = summed
        loss_row = loss_row[0]
    else:
        grad_up, grad_down, grad_qkv, grad_out = [
            lax.psum_scatter(jnp.where(on_first, a, b).astype(F32), ("dp", "rep"), scatter_dimension=0, tiled=True)
            for a, b in zip([*ffn_first, *attention_first], [*ffn_last, *attention_last])
        ]
        small = jnp.where(on_first, small_rows(*small_first), small_rows(*small_last))
        for flip in flips():
            small = small + swap(small, None, *flip)
        width, up_width = D // (dps * reps), FF // (dps * reps)
        mine = lax.dynamic_slice(small[:8], (0, place * width), (8, width))
        bias, gain, query_part = mine[:5], mine[5:7], mine[7:]
        up_part = lax.dynamic_slice(small[8:12].reshape(1, FF), (0, place * up_width), (1, up_width))
        loss_row = small[12, :128]
    loss_value = jnp.where(on_first, relay(loss_row, -1), loss_row)[:1]

    dx = dx.reshape(crops, SLOTS, D)
    half = SLOTS // sections
    crops_grad = jnp.where(on_first, dx[:, :half], relay(after(dx[:, half:], grad_down), 1)).astype(F32)
    return (
        loss_value,
        crops_grad,
        grad_qkv[None],
        grad_out[None],
        grad_up[None],
        grad_down[None],
        bias[None],
        gain[None],
        up_part,
        query_part,
    )


def solution(mesh):
    crop = P(("dp", "rep"), "section", None)
    per_crop = P(("dp", "rep"))
    layer3 = P("section", None, None)
    layer2 = P("section", None)
    placed = (
        (crop, crop, per_crop, per_crop, per_crop, P())
        + (layer3,) * 6
        + (layer2,) * 2
        + (layer3,) * 6
        + (layer2,)
    )
    shared3 = P("section", ("dp", "rep"), None)
    return jax.shard_map(
        body,
        mesh=mesh,
        in_specs=placed,
        out_specs=(
            P(),
            crop,
            shared3,
            shared3,
            shared3,
            shared3,
            P("section", None, ("dp", "rep")),
            P("section", None, ("dp", "rep")),
            P("section", ("dp", "rep")),
            P("section", ("dp", "rep")),
        ),
        check_vma=False,
    )
```

```python
import functools

import jax
import jax.numpy as jnp
from jax import lax
from jax.experimental import pallas as pl
from jax.experimental.pallas import tpu as pltpu
from jax.sharding import PartitionSpec as P

F32 = jnp.float32
BF = jnp.bfloat16
MASKED = -1e30
D = 768
FF = 3072
SLOTS = 256
PAIRS = 6
MIB = 2**20
SEMS = 96


def dot(a, b):
    return lax.dot_general(a, b, (((1,), (0,)), ((), ())), preferred_element_type=F32)


def dot_nt(a, b):
    return lax.dot_general(a, b, (((1,), (1,)), ((), ())), preferred_element_type=F32)


def dot_tn(a, b):
    return lax.dot_general(a, b, (((0,), (0,)), ((), ())), preferred_element_type=F32)


def gelu_parts(x, want_slope):
    share = 0.5 + 0.5 * lax.erf(x * 0.7071067811865476)
    if not want_slope:
        return x * share, None
    return x * share, share + (0.3989422804014327 * x) * jnp.exp(-0.5 * (x * x))


def norm_parts(z):
    mean = jnp.mean(z, axis=-1, keepdims=True)
    c = z - mean
    var = jnp.mean(c * c, axis=-1, keepdims=True)
    r = lax.rsqrt(var + 1e-12)
    return c * r, r


def head_masks(scale):
    lane = lax.broadcasted_iota(jnp.int32, (1, 128), 1)
    low = jnp.where(lane < 64, scale, 0.0).astype(BF)
    high = jnp.where(lane < 64, 0.0, scale).astype(BF)
    return low, high


def stack_heads(pair, scale):
    low, high = head_masks(scale)
    return jnp.concatenate([pair * low, pair * high], axis=0)


def side_by_side(stacked):
    half = stacked.shape[0] // 2
    return jnp.concatenate([stacked[:half], stacked[half:]], axis=1)


class Copies:
    def __init__(self, sems):
        self.sems, self.used, self.open = sems, 0, []

    def make(self, src, dst):
        self.used += 1
        return pltpu.make_async_copy(src, dst, self.sems.at[self.used - 1])

    def fetch(self, src, dst):
        cp = self.make(src, dst)
        cp.start()
        return cp

    def pick(self, by_section, dst):
        if by_section[0] is by_section[1]:
            return self.fetch(by_section[0], dst)
        sem = self.sems.at[self.used]
        self.used += 1
        here = lax.axis_index("section")

        @pl.when(here == 0)
        def _():
            pltpu.make_async_copy(by_section[0], dst, sem).start()

        @pl.when(here != 0)
        def _():
            pltpu.make_async_copy(by_section[1], dst, sem).start()

        return pltpu.make_async_copy(by_section[0], dst, sem)

    def send(self, src, dst):
        self.open.append(self.fetch(src, dst))

    def drain(self):
        for cp in self.open:
            cp.wait()


def only_on(section, run):
    if section is None:
        run()
    else:
        pl.when(lax.axis_index("section") == section)(run)


VMEM = pl.BlockSpec(memory_space=pltpu.VMEM)
ANY = pl.BlockSpec(memory_space=pl.ANY)
SMEM = pl.BlockSpec(memory_space=pltpu.SMEM)
sd = jax.ShapeDtypeStruct


def call(kernel, name, outs, out_specs, ins, in_specs, scratch, limit=56):
    return pl.pallas_call(
        kernel,
        out_shape=[sd(*o) for o in outs],
        in_specs=in_specs,
        out_specs=out_specs,
        scratch_shapes=[pltpu.VMEM(*s) for s in scratch] + [pltpu.SemaphoreType.DMA((SEMS,))],
        compiler_params=pltpu.CompilerParams(vmem_limit_bytes=limit * MIB),
        cost_estimate=pl.CostEstimate(flops=1000, bytes_accessed=1000, transcendentals=0),
        name=name,
    )(*ins)


def saved_shapes(rows):
    crops = rows // SLOTS
    return [
        ((rows, 3 * D), BF),
        ((PAIRS * crops, 2 * SLOTS, SLOTS), BF),
        ((2 * SLOTS, 128), F32),
        ((rows, D), BF),
        ((rows, D), BF),
        ((rows, 128), F32),
        ((rows, D), BF),
        ((rows, FF), BF),
        ((rows, FF), BF),
        ((rows, D), BF),
        ((rows, 128), F32),
    ]


def fetch_rows(copies, refs, kinds, x):
    waits = []
    half = refs[0].shape[1] if "halves" in kinds else SLOTS // 2
    for c in range(x.shape[0] // SLOTS):
        for h in range(SLOTS // half):
            at = slice(SLOTS * c + half * h, SLOTS * c + half * (h + 1))
            options = []
            if "halves" in kinds:
                options.append(refs[h].at[c])
            if "whole" in kinds:
                options.append(refs[-1].at[at, :])
            waits.append(copies.pick((options[0], options[-1]), x.at[at, :]))
    return waits


def read_vectors(refs, key):
    if key:
        b, g, up = refs
        rows = b[0].astype(F32)
        rows = [rows[i : i + 1] for i in range(6)]
    else:
        b, g, up, q = refs
        rows = b[0].astype(F32)
        rows = [q[...].astype(F32)] + [rows[i : i + 1] for i in range(5)]
    gains = g[0].astype(F32)
    return rows + [gains[0:1], gains[1:2]], up[...].astype(F32)


def load_vectors(refs, kinds, vec, bup):
    sets = []
    for kind in kinds:
        n = 3 if kind == "key" else 4
        sets.append(read_vectors(refs[:n], kind == "key"))
        refs = refs[n:]
    here = lax.axis_index("section")
    for i in range(8):
        row = sets[0][0][i]
        if len(sets) == 2:
            row = jnp.where(here == 0, row, sets[1][0][i])
        vec[i : i + 1, :] = row
    up = sets[0][1]
    if len(sets) == 2:
        up = jnp.where(here == 0, up, sets[1][1])
    bup[...] = up


def forward_kernel(rows, active, save, x_kinds, sets, *refs):
    def run():
        forward_body(rows, save, x_kinds, sets, *refs)

    only_on(active, run)


def forward_body(rows, save, x_kinds, sets, *refs):
    crops = rows // SLOTS
    lens_refs, refs = refs[: len(sets)], refs[len(sets) :]
    here = lax.axis_index("section")
    if len(sets) == 2:
        lens = [jnp.where(here == 0, lens_refs[0][c], lens_refs[1][c]) for c in range(crops)]
    else:
        lens = [lens_refs[0][c] for c in range(crops)]
    n_x = (2 if "halves" in x_kinds else 0) + (1 if "whole" in x_kinds else 0)
    x_refs, refs = refs[:n_x], refs[n_x:]
    w_refs, refs = refs[: 4 * len(sets)], refs[4 * len(sets) :]
    n_v = sum(3 if k == "key" else 4 for k in sets)
    v_refs, refs = refs[:n_v], refs[n_v:]
    y_ref, pool_ref = refs[:2]
    refs = refs[2:]
    if save:
        (qkv_o, prob_o, inv_o, ctx_o, n1_o, r1_o, first_o, hid_o, slope_o, n2_o, r2_o) = refs[:11]
        refs = refs[11:]
    (x, wqkv, wout, wup, wdown, ctx, zbuf, first, hid, vec, bup) = refs[:11]
    refs = refs[11:]
    if save:
        (qkv, prob, inv_all, n1, r1, slope, n2, r2) = refs[:8]
        refs = refs[8:]
        inv_all[...] = jnp.zeros_like(inv_all)
    copies = Copies(refs[0])
    got_x = fetch_rows(copies, x_refs, x_kinds, x)
    pairs = [(w_refs[i], w_refs[4 + i] if len(sets) == 2 else w_refs[i]) for i in range(4)]
    got_qkv = copies.pick(pairs[0], wqkv)
    load_vectors(v_refs, sets, vec, bup)
    for cp in got_x:
        cp.wait()
    got_qkv.wait()
    got_out = copies.pick(pairs[1], wout)
    got_up = copies.pick(pairs[2], wup)
    got_down = copies.pick(pairs[3], wdown)
    keycol = lax.broadcasted_iota(jnp.int32, (1, SLOTS), 1)
    lane = lax.broadcasted_iota(jnp.int32, (1, 128), 1)
    gain1, gain2 = vec[6:7], vec[7:8]

    def heads(i, carry):
        thirds = []
        for j in range(3):
            cols = pl.ds(pl.multiple_of(D * j + 256 * i, 256), 256)
            part = dot(x[...], wqkv[:, cols])
            if j != 1:
                at = pl.ds(pl.multiple_of(256 * i, 256), 256)
                part = part + vec[j // 2 : j // 2 + 1, at]
            part = part.astype(BF)
            if save:
                qkv[:, cols] = part
            thirds.append(part)
        for c in range(crops):
            crop = slice(SLOTS * c, SLOTS * (c + 1))
            for pr in range(2):
                qp, kp, vp = [t[crop, 128 * pr : 128 * (pr + 1)] for t in thirds]
                scores = jnp.where(keycol < lens[c], dot_nt(stack_heads(qp, 0.125), kp), MASKED)
                e = jnp.exp(scores - jnp.max(scores, axis=-1, keepdims=True))
                inv = pl.reciprocal(jnp.sum(e, axis=-1, keepdims=True))
                e = e.astype(BF)
                if save:
                    unit = PAIRS * c + 2 * i + pr
                    prob[unit] = e
                    inv_all[...] = jnp.where(lane == unit, inv, inv_all[...])
                at = pl.ds(pl.multiple_of(256 * i + 128 * pr, 128), 128)
                both = dot(e, vp) * inv
                ctx[crop, at] = jnp.where(lane < 64, both[:SLOTS], both[SLOTS:]).astype(BF)
        return carry

    lax.fori_loop(0, 3, heads, 0)
    if save:
        copies.send(qkv, qkv_o)
        copies.send(prob, prob_o)
        copies.send(inv_all, inv_o)
        copies.send(ctx, ctx_o)
    got_out.wait()
    for j in range(3):
        cols = slice(256 * j, 256 * (j + 1))
        zbuf[:, cols] = x[:, cols].astype(F32) + dot(ctx[...], wout[:, cols]) + vec[2:3, cols]
    block = 64
    steps = rows // block

    def first_norm(i, carry):
        at = pl.ds(pl.multiple_of(i * block, block), block)
        n, r = norm_parts(zbuf[at, :])
        f = (n * gain1 + vec[3:4]).astype(BF)
        first[at, :] = f
        zbuf[at, :] = f.astype(F32) + vec[4:5]
        if save:
            n1[at, :] = n.astype(BF)
            r1[at, :] = jnp.broadcast_to(r, (block, 128))
        return carry

    lax.fori_loop(0, steps, first_norm, 0, unroll=True)
    if save:
        copies.send(n1, n1_o)
        copies.send(r1, r1_o)
        copies.send(first, first_o)
    got_up.wait()
    got_down.wait()

    def down_part(k):
        cols = slice(512 * k, 512 * (k + 1))
        zbuf[...] += dot(hid[:, cols], wdown[cols, :])

    for i in range(12):
        cols = slice(256 * i, 256 * (i + 1))
        g, slope_part = gelu_parts(dot(first[...], wup[:, cols]) + bup[:, cols], save)
        hid[:, cols] = g.astype(BF)
        if save:
            slope[:, cols] = slope_part.astype(BF)
        if i % 2 and i > 2:
            down_part(i // 2 - 1)
    if save:
        copies.send(hid, hid_o)
        copies.send(slope, slope_o)
    down_part(5)
    pool_ref[...] = jnp.zeros_like(pool_ref)
    per_crop = SLOTS // block
    for i in range(steps):
        at = slice(i * block, (i + 1) * block)
        n, r = norm_parts(zbuf[at, :])
        f = n * gain2 + vec[5:6]
        y_ref[at, :] = f.astype(BF)
        if save:
            n2[at, :] = n.astype(BF)
            r2[at, :] = jnp.broadcast_to(r, (block, 128))
        c = i // per_crop
        token = lax.broadcasted_iota(jnp.int32, (block, 1), 0) + (i % per_crop) * block
        part = jnp.sum(jnp.where(token < lens[c], f, 0.0), axis=0, keepdims=True)
        pool_ref[c : c + 1, :] += part / lens[c].astype(F32)
    pooled = pool_ref[:crops]
    pool_ref[crops : 2 * crops] = pooled * lax.rsqrt(jnp.sum(pooled * pooled, axis=-1, keepdims=True) + 1e-6)
    if save:
        copies.send(n2, n2_o)
        copies.send(r2, r2_o)
    copies.drain()


def forward(rows, active, save, halves, whole, encoders):
    x_kinds = (("halves",) if halves else ()) + (("whole",) if whole is not None else ())
    xs = list(halves or ()) + ([whole] if whole is not None else [])
    lens = [e[1] for e in encoders]
    weights = [w for e in encoders for w in e[2]]
    vectors = [v for e in encoders for v in e[3]]
    outs = [((rows, D), BF), ((8, D), F32)]
    out_specs = [VMEM, VMEM]
    scratch = [
        ((rows, D), BF),
        ((D, 3 * D), BF),
        ((D, D), BF),
        ((D, FF), BF),
        ((FF, D), BF),
        ((rows, D), BF),
        ((rows, D), F32),
        ((rows, D), BF),
        ((rows, FF), BF),
        ((8, D), F32),
        ((1, FF), F32),
    ]
    if save:
        kept = saved_shapes(rows)
        outs += kept
        out_specs += [ANY] * len(kept)
        scratch += [kept[i] for i in (0, 1, 2, 4, 5, 8, 9, 10)]
    return call(
        functools.partial(forward_kernel, rows, active, save, x_kinds, [e[0] for e in encoders]),
        "layer_forward",
        outs,
        out_specs,
        [*lens, *xs, *weights, *vectors],
        [SMEM] * len(lens) + [ANY] * (len(xs) + len(weights)) + [VMEM] * len(vectors),
        scratch,
    )


def split3(v):
    hi = v.astype(BF)
    rest = v - hi.astype(F32)
    mid = rest.astype(BF)
    lo = (rest - mid.astype(F32)).astype(BF)
    return hi, mid, lo


def stack3(v):
    parts = split3(v)
    return jnp.concatenate(list(parts) + [jnp.zeros_like(parts[0])] * 5, axis=0)


def unstack3(rows, n):
    return rows[:n] + rows[n : 2 * n] + rows[2 * n : 3 * n]


def queue_norm_kernel(active, queue_h, inv_ref, queue, sems):
    def run():
        Copies(sems).fetch(queue_h, queue).wait()

        def step(i, carry):
            at = pl.ds(pl.multiple_of(i * 512, 512), 512)
            v = queue[at, :].astype(F32)
            sq = v * v
            hi = sq.astype(BF)
            lo = (sq - hi.astype(F32)).astype(BF)
            ones = jnp.ones((8, D), BF)
            total = dot_nt(ones, hi) + dot_nt(ones, lo)
            inv_ref[:, at] = lax.rsqrt(total + 1e-6)
            return carry

        lax.fori_loop(0, queue.shape[0] // 512, step, 0)

    only_on(active, run)


def loss_kernel(active, crops, count, pooled, matched, queue, inv, grad_ref, loss_ref, sems):
    def run():
        v = pooled[:crops]
        r = lax.rsqrt(jnp.sum(v * v, axis=-1, keepdims=True) + 1e-6)
        u = v * r
        k = matched[:crops]
        near = jnp.sum(u * k, axis=-1, keepdims=True) * 20.0
        inv_row = inv[0:1]
        far = unstack3(dot_nt(stack3(u), queue[...]), crops) * (inv_row * 20.0)
        top = jnp.maximum(near, jnp.max(far, axis=-1, keepdims=True))
        e_near = jnp.exp(near - top)
        e_far = jnp.exp(far - top)
        total = e_near + jnp.sum(e_far, axis=-1, keepdims=True)
        share = 20.0 / (total * count)
        d_u = unstack3(dot(stack3(e_far * inv_row * share), queue[...]), crops)
        d_u = d_u + (e_near - total) * share * k
        grad = r * (d_u - u * jnp.sum(u * d_u, axis=-1, keepdims=True))
        grad_ref[...] = jnp.zeros_like(grad_ref)
        grad_ref[:crops] = grad
        lost = jnp.sum(top + jnp.log(total) - near, axis=0, keepdims=True) / count
        loss_ref[...] = jnp.broadcast_to(lost, loss_ref.shape)

    only_on(active, run)


def norm_back(dy, gain, n, r):
    dn = dy * gain
    return r * (dn - jnp.mean(dn, axis=-1, keepdims=True) - n * jnp.mean(dn * n, axis=-1, keepdims=True))


def column_sum(v):
    return jnp.sum(v, axis=0, keepdims=True)


def fast_mesh():
    return lax.axis_size("dp") == 8 and lax.axis_size("rep") == 2


def place_bits():
    dp, rep = lax.axis_index("dp"), lax.axis_index("rep")
    return dp // 2, dp % 2, rep


CHUNK = 512


def data_backward_kernel(rows, active, pooled, lens, dy, gains, *refs):
    def run():
        n2_h, r2_h, wdown_h, slope_h, wup_h, n1_h, r1_h, wout_h, qkv_h, prob_h, inv_h, wqkv_h = refs[:12]
        vec, bup, ddown_o, dup_o, datt_o, dqkv_o, dx_o = refs[12:19]
        n2, r2, wdown, slope, wup, n1, r1, wout, qkv, prob, inv, wqkv = refs[19:31]
        acc, ddown, dup, datt, dqkv, dx, sems = refs[31:]
        copies = Copies(sems)
        got_n2, got_r2 = copies.fetch(n2_h, n2), copies.fetch(r2_h, r2)
        got = []
        for i in range(FF // CHUNK):
            cols = slice(CHUNK * i, CHUNK * (i + 1))
            got.append(
                [
                    copies.fetch(wdown_h.at[cols, :], wdown.at[cols, :]),
                    copies.fetch(slope_h.at[:, cols], slope.at[:, cols]),
                    copies.fetch(wup_h.at[:, cols], wup.at[:, cols]),
                ]
            )
        got_n1 = [copies.fetch(n1_h, n1), copies.fetch(r1_h, r1), copies.fetch(wout_h, wout)]
        got_qkv = [copies.fetch(qkv_h, qkv), copies.fetch(prob_h, prob), copies.fetch(inv_h, inv)]
        got_w = copies.fetch(wqkv_h, wqkv)
        vec[...] = jnp.zeros_like(vec)
        gain1, gain2 = gains[0].astype(F32)[0:1], gains[0].astype(F32)[1:2]
        block = 64
        per_crop = SLOTS // block
        got_n2.wait()
        got_r2.wait()
        for i in range(rows // block):
            at = slice(block * i, block * (i + 1))
            c = i // per_crop
            if pooled:
                token = lax.broadcasted_iota(jnp.int32, (block, 1), 0) + (i % per_crop) * block
                grow = jnp.where(token < lens[c], 1.0 / lens[c].astype(F32), 0.0) * dy[c : c + 1]
            else:
                grow = dy[at].astype(F32)
            n = n2[at].astype(F32)
            ds = norm_back(grow, gain2, n, r2[at, 0:1])
            low_ds = ds.astype(BF)
            acc[at] = ds
            ddown[at] = low_ds
            vec[0:1] += column_sum(grow * n)
            vec[1:2] += column_sum(grow)
            vec[2:3] += column_sum(low_ds.astype(F32))
        copies.send(ddown, ddown_o)
        for i in range(FF // CHUNK):
            cols = slice(CHUNK * i, CHUNK * (i + 1))
            for cp in got[i]:
                cp.wait()
            up = (dot_nt(ddown[...], wdown[cols, :]) * slope[:, cols].astype(F32)).astype(BF)
            dup[:, cols] = up
            copies.send(dup.at[:, cols], dup_o.at[:, cols])
            bup[:, cols] = jnp.broadcast_to(column_sum(up.astype(F32)), (8, CHUNK))
            acc[...] += dot_nt(up, wup[:, cols])
        for cp in got_n1:
            cp.wait()
        for i in range(rows // block):
            at = slice(block * i, block * (i + 1))
            n = n1[at].astype(F32)
            dfirst = acc[at]
            ds = norm_back(dfirst, gain1, n, r1[at, 0:1])
            low_ds = ds.astype(BF)
            acc[at] = ds
            datt[at] = low_ds
            vec[3:4] += column_sum(dfirst * n)
            vec[4:5] += column_sum(dfirst)
            vec[5:6] += column_sum(low_ds.astype(F32))
        copies.send(datt, datt_o)
        dctx = dot_nt(datt[...], wout[...]).astype(BF)
        for cp in got_qkv:
            cp.wait()
        for c in range(rows // SLOTS):
            crop = slice(SLOTS * c, SLOTS * (c + 1))
            for pr in range(PAIRS):
                cols = [slice(D * j + 128 * pr, D * j + 128 * (pr + 1)) for j in range(3)]
                unit = PAIRS * c + pr
                qp, kp, vp = [qkv[crop, t] for t in cols]
                dcs = stack_heads(dctx[crop, 128 * pr : 128 * (pr + 1)], 1.0)
                scale = inv[:, unit : unit + 1]
                e = prob[unit]
                pf = e.astype(F32) * scale
                weighted = pf * dot_nt(dcs, vp)
                ds = (weighted - pf * jnp.sum(weighted, axis=-1, keepdims=True)).astype(BF)
                dqkv[crop, cols[0]] = dot(side_by_side(ds), stack_heads(kp, 0.125)).astype(BF)
                dqkv[crop, cols[1]] = dot_tn(ds, stack_heads(qp, 0.125)).astype(BF)
                dqkv[crop, cols[2]] = dot_tn(e, (dcs * scale).astype(BF)).astype(BF)
        got_w.wait()
        for j in range(3):
            cols = slice(256 * j, 256 * (j + 1))
            dx[:, cols] = (dot_nt(dqkv[...], wqkv[cols, :]) + acc[:, cols]).astype(BF)
        copies.send(dx, dx_o)
        copies.send(dqkv, dqkv_o)
        vec[6:7] = column_sum(dqkv[:, :D].astype(F32))
        vec[7:8] = column_sum(dqkv[:, 2 * D :].astype(F32))
        copies.drain()

    only_on(active, run)


def data_backward(active, pooled, lens, dy, gains, n2, r2, wdown, slope, wup, n1, r1, wout, qkv, prob, inv, wqkv):
    rows = n1.shape[0]
    held = [n2, r2, wdown, slope, wup, n1, r1, wout, qkv, prob, inv, wqkv]
    wide_rows = ((rows, D), BF)
    return call(
        functools.partial(data_backward_kernel, rows, active, pooled),
        "data_backward",
        [((8, D), F32), ((8, FF), F32), wide_rows, ((rows, FF), BF), wide_rows, ((rows, 3 * D), BF), wide_rows],
        [VMEM] * 2 + [ANY] * 5,
        [lens, dy, gains, *held],
        [SMEM, VMEM, VMEM] + [ANY] * len(held),
        [(h.shape, h.dtype) for h in held]
        + [((rows, D), F32), wide_rows, ((rows, FF), BF), wide_rows, ((rows, 3 * D), BF), wide_rows],
    )


def ffn_weights_kernel(rows, active, fast, *refs):
    def run():
        if fast:
            first_h, first_p, ddown_h, ddown_p, hid_h, dup_h, wup_h, wdown_h, bup_h, send, keep = refs[:11]
            first, ddown, hid, dup, gup, gdown, wup, wdown, bup, sems = refs[11:]
        else:
            first_h, ddown_h, hid_h, dup_h, up_o, down_o = refs[:6]
            first, ddown, hid, dup, gup, gdown, sems = refs[6:]
        copies = Copies(sems)
        own = slice(0, rows)
        got = [copies.fetch(first_h, first.at[own, :]), copies.fetch(ddown_h, ddown.at[own, :])]
        z, x, y = place_bits()
        parts = 4 if fast else FF // 384
        if fast:
            peer = slice(rows, 2 * rows)
            got += [copies.fetch(first_p, first.at[peer, :]), copies.fetch(ddown_p, ddown.at[peer, :])]
            got.append(copies.fetch(bup_h, bup))
        blocks = []
        for i in range(parts):
            here = slice(384 * i, 384 * (i + 1))
            there = pl.ds(pl.multiple_of(768 * i + 384 * x, 128), 384) if fast else here
            block = [
                copies.fetch(hid_h.at[:, there], hid.at[own, here]),
                copies.fetch(dup_h.at[:, there], dup.at[own, here]),
            ]
            if fast:
                block.append(copies.fetch(wup_h.at[:, there], wup.at[:, here]))
                block.append(copies.fetch(wdown_h.at[there, :], wdown.at[here, :]))
            blocks.append(block)
        for cp in got:
            cp.wait()
        for i in range(parts):
            here = slice(384 * i, 384 * (i + 1))
            for cp in blocks[i]:
                cp.wait()
            if fast:
                there = pl.ds(pl.multiple_of(768 * i + 384 * x, 128), 384)
                bias = bup[:, there].astype(F32)
                g, slope = gelu_parts(dot(first[peer, :], wup[:, here]) + bias, True)
                hid[peer, here] = g.astype(BF)
                dup[peer, here] = (dot_nt(ddown[peer, :], wdown[here, :]) * slope).astype(BF)
            gdown[here, :] = dot_tn(hid[:, here], ddown[...]).astype(BF)
            if fast:
                for jy, out in ((1, send), (0, keep)):
                    at = pl.ds(pl.multiple_of(384 * i + 192 * jnp.bitwise_xor(y, jy), 64), 192)
                    copies.send(gdown.at[at, :], out.at[jnp.bitwise_xor(z, i), 192:384, :])
            gup[:, here] = dot_tn(first[...], dup[:, here]).astype(BF)
            if fast and i % 2:
                half = i // 2
                for jy, out in ((1, send), (0, keep)):
                    for jz in range(4):
                        for jx in range(2):
                            owner = (jnp.bitwise_xor(z, jz) * 2 + jnp.bitwise_xor(x, jx)) * 2 + jnp.bitwise_xor(y, jy)
                            at = pl.ds(pl.multiple_of(48 * owner, 16), 48)
                            to = slice(96 * jx + 48 * half, 96 * jx + 48 * (half + 1))
                            copies.send(gup.at[at, slice(D * half, D * (half + 1))], out.at[jz, to, :])
        if not fast:
            copies.send(gup, up_o)
            copies.send(gdown, down_o)
        copies.drain()

    only_on(active, run)


def ffn_weights(active, first, first_peer, ddown, ddown_peer, hid, dup, wup, wdown, bup):
    rows = first.shape[0]
    fast = fast_mesh()
    if fast:
        ins = [first, first_peer, ddown, ddown_peer, hid, dup, wup, wdown, bup]
        outs = [((4, 384, D), BF)] * 2
        tokens, units = 2 * rows, FF // 2
        extra = [((D, units), BF), ((units, D), BF), ((1, FF), BF)]
    else:
        ins = [first, ddown, hid, dup]
        outs = [((D, FF), BF), ((FF, D), BF)]
        tokens, units, extra = rows, FF, []
    return call(
        functools.partial(ffn_weights_kernel, rows, active, fast),
        "ffn_weights",
        outs,
        [ANY] * 2,
        ins,
        [ANY] * len(ins),
        [
            ((tokens, D), BF),
            ((tokens, D), BF),
            ((tokens, units), BF),
            ((tokens, units), BF),
            ((D, units), BF),
            ((units, D), BF),
        ]
        + extra,
    )


VECTOR_ROWS = (7, 5, 4, 2, 1, 3, 0, 6)


def attention_weights_kernel(rows, active, fast, x_kinds, *refs):
    def run():
        n_x = len(x_kinds) + 1
        x_refs = refs[:n_x]
        if fast:
            vec, bup, lost, *refs_ = refs[n_x:]
            ctx_h, datt_h, dqkv_h, out_a, out_b, x, ctx, datt, dqkv, gqkv, gout, tail, sems = refs_
        else:
            ctx_h, datt_h, dqkv_h, out_a, out_b, x, ctx, datt, dqkv, gqkv, gout, sems = refs[n_x:]
        copies = Copies(sems)
        got = [copies.fetch(ctx_h, ctx), copies.fetch(datt_h, datt)]
        got_x = fetch_rows(copies, x_refs, x_kinds, x)
        got_x.append(copies.fetch(dqkv_h, dqkv))
        if fast:
            z, xx, y = place_bits()
            small = jnp.concatenate([vec[k : k + 1] for k in VECTOR_ROWS], axis=0)
            row = lax.broadcasted_iota(jnp.int32, (8, D), 0)
            lane = lax.broadcasted_iota(jnp.int32, (8, D), 1) - 3 * ((z * 2 + xx) * 2 + y)
            terms = [jnp.broadcast_to(t.astype(F32)[0:1, 0:1], (8, D)) for t in split3(lost[...])]
            lost_row = sum(jnp.where(lane == i, t, 0.0) for i, t in enumerate(terms))

        def ship(part, to):
            for j in range(15, -1, -1):
                jx, jy, jz = j // 8, j // 4 % 2, j % 4
                owner = (jnp.bitwise_xor(z, jz) * 2 + jnp.bitwise_xor(xx, jx)) * 2 + jnp.bitwise_xor(y, jy)
                at = pl.ds(pl.multiple_of(48 * owner, 16), 48)
                copies.send(part.at[at, :], (out_b if jx else out_a).at[j % 8, to : to + 48, :])

        for cp in got:
            cp.wait()
        gout[...] = dot_tn(ctx[...], datt[...]).astype(BF)
        if fast:
            ship(gout, 144)
            for j in range(16):
                jx, jy, jz = j // 8, j // 4 % 2, j % 4
                owner = (jnp.bitwise_xor(z, jz) * 2 + jnp.bitwise_xor(xx, jx)) * 2 + jnp.bitwise_xor(y, jy)
                head = pltpu.roll(small, D - 48 * owner, 1)
                ups = pltpu.roll(bup[...], FF - 192 * owner, 1)[:, :D]
                other = jnp.where(row == 0, ups, jnp.where(row == 1, lost_row, 0.0))
                tail[j] = jnp.concatenate([head, other], axis=0).astype(BF)
                copies.send(tail.at[j], (out_b if jx else out_a).at[j % 8, 192:208, :])
        for cp in got_x:
            cp.wait()
        for t in range(3):
            for k in range(2):
                cols = slice(D * t + 384 * k, D * t + 384 * (k + 1))
                gqkv[:, cols] = dot_tn(x[...], dqkv[:, cols]).astype(BF)
            if fast:
                ship(gqkv.at[:, slice(D * t, D * (t + 1))], 48 * t)
        if not fast:
            copies.send(gqkv, out_a)
            copies.send(gout, out_b)
        copies.drain()

    only_on(active, run)


def attention_weights(active, halves, whole, ctx, datt, dqkv, small):
    rows = ctx.shape[0]
    fast = fast_mesh()
    x_kinds = ("halves", "whole")
    outs = [((8, 208, D), BF)] * 2 if fast else [((D, 3 * D), BF), ((D, D), BF)]
    ins = [*halves, whole, *(small if fast else ()), ctx, datt, dqkv]
    in_specs = [ANY] * 3 + [VMEM] * (3 if fast else 0) + [ANY] * 3
    return call(
        functools.partial(attention_weights_kernel, rows, active, fast, x_kinds),
        "attention_weights",
        outs,
        [ANY] * 2,
        ins,
        in_specs,
        [((rows, D), BF)] * 3
        + [((rows, 3 * D), BF), ((D, 3 * D), BF), ((D, D), BF)]
        + ([((16, 16, D), BF)] if fast else []),
    )


AXES = ("section", "dp", "rep")


def swap(block, section, dp_flip, rep_flip):
    dps, reps = lax.axis_size("dp"), lax.axis_size("rep")
    sections = range(lax.axis_size("section")) if section is None else [section]
    route = [
        ((s * dps + d) * reps + r, (s * dps + (d ^ dp_flip)) * reps + (r ^ rep_flip))
        for s in sections
        for d in range(dps)
        for r in range(reps)
    ]
    return lax.ppermute(block, AXES, route)


def flips():
    out, bit = [], 1
    while bit < lax.axis_size("rep"):
        out.append((0, bit))
        bit *= 2
    bit = 1
    while bit < lax.axis_size("dp"):
        out.append((bit, 0))
        bit *= 2
    return out


def add_rows(pieces, dst, at, count):
    def step(i, carry):
        here = pl.ds(pl.multiple_of(i * 16, 16), 16)
        total = pieces[0][here, :].astype(F32)
        for p in pieces[1:]:
            total = total + p[here, :].astype(F32)
        dst[pl.ds(pl.multiple_of(at + i * 16, 16), 16), :] = total.astype(dst.dtype)
        return carry

    lax.fori_loop(0, count // 16, step, 0, unroll=2 if count % 32 == 0 else 1)


def partial_kernel(active, slots, joined, n_in, rows, *refs):
    def run():
        ins, outs = refs[:n_in], refs[n_in : n_in + (1 if joined else len(slots))]
        held, made, sems = refs[-3:]
        copies = Copies(sems)
        got = [[copies.fetch(r.at[k], held.at[i, t]) for t, r in enumerate(ins)] for i, k in enumerate(slots)]
        for i in range(len(slots)):
            for cp in got[i]:
                cp.wait()
            add_rows([held.at[i, t] for t in range(n_in)], made.at[i], 0, rows)
            copies.send(made.at[i], outs[0].at[i] if joined else outs[i])
        copies.drain()

    only_on(active, run)


def partial_sums(active, slots, joined, ins):
    shape = ins[0].shape[1:]
    n = len(slots)
    outs = [((n, *shape), BF)] if joined else [(shape, BF)] * n
    made = call(
        functools.partial(partial_kernel, active, slots, joined, len(ins), shape[0]),
        "partial_sums",
        outs,
        [ANY] * len(outs),
        list(ins),
        [ANY] * len(ins),
        [((n, len(ins), *shape), BF), ((n, *shape), BF)],
        16,
    )
    return made[0] if joined else made


def fetch_terms(copies, refs, n_slotted, held):
    half = len(refs) // 2
    got = []
    for t in range(half):
        pair = (refs[t], refs[half + t])
        if t < n_slotted:
            pair = tuple(r.at[0] for r in pair)
        got.append(copies.pick(pair, held.at[t]))
    for cp in got:
        cp.wait()
    return [held.at[t] for t in range(half)]


def attention_total_kernel(*refs):
    qkv_o, out_o, bias_o, gain_o, query_o, up_o, loss_o, held, total, sems = refs[12:]
    terms = fetch_terms(Copies(sems), refs[:12], 3, held)
    add_rows(terms, total, 0, 208)
    for t in range(3):
        qkv_o[:, D * t : D * (t + 1)] = total[48 * t : 48 * (t + 1), :]
    out_o[...] = total[144:192, :]
    bias_o[...] = total[192:197, :48]
    gain_o[...] = total[197:199, :48]
    query_o[...] = total[199:200, :48]
    up_o[...] = total[200:201, :192]
    loss_o[...] = jnp.broadcast_to(jnp.sum(total[201:202, :], axis=-1, keepdims=True), loss_o.shape)


def ffn_total_kernel(*refs):
    down_o, own_o, peer_o, held, total, sems = refs[10:]
    terms = fetch_terms(Copies(sems), refs[:10], 2, held)
    add_rows(terms, total, 0, 384)
    own_o[...] = total[0:96, :]
    peer_o[...] = total[96:192, :].astype(BF)
    down_o[...] = total[192:384, :]


def up_total_kernel(own, peer, up_o, sems):
    x = lax.axis_index("dp") % 2
    for c in range(2):
        for k in range(2):
            cols = slice(384 * k, 384 * (k + 1))
            at = 768 * (2 * c + k)
            up_o[:, pl.ds(pl.multiple_of(at + 384 * x, 128), 384)] = own[48 * c : 48 * (c + 1), cols]
            up_o[:, pl.ds(pl.multiple_of(at + 384 * (1 - x), 128), 384)] = peer[48 * c : 48 * (c + 1), cols].astype(F32)


def totals(kernel, name, ins, rows, outs, in_spec=ANY):
    terms = len(ins) // 2
    scratch = [((terms, rows, D), BF), ((rows, D), F32)] if rows else []
    return call(kernel, name, outs, [VMEM] * len(outs), ins, [in_spec] * len(ins), scratch, 16)


def after(value, *others):
    return lax.optimization_barrier((value, others))[0]


def chip_sums(attention, ffn, last):
    (ka0, sa0), (ka1, sa1) = attention
    (kf0, sf0), (kf1, sf1) = ffn
    a1 = swap(sa1, last, 1, 0)
    f1 = swap(sf1, last, 0, 1)
    f0 = swap(sf0, 0, 0, 1)
    a0 = swap(sa0, 0, 1, 0)
    distances = (1, 2, 3)

    def over_z(parts, section):
        return [swap(p, section, 2 * k, 0) for k, p in zip(distances, parts)]

    s1 = partial_sums(last, (4, 5, 6, 7), True, [ka1, after(a1, ka0)])
    b1 = swap(s1, last, 0, 1)
    p1 = partial_sums(last, distances, False, [kf1, after(f1, s1)])
    g1 = over_z(p1, last)
    p0 = partial_sums(0, distances, False, [kf0, after(f0, *p1)])
    g0 = over_z(p0, 0)
    s0 = partial_sums(0, (4, 5, 6, 7), True, [ka0, after(a0, *p0)])
    b0 = swap(s0, 0, 0, 1)
    q1 = partial_sums(last, distances, False, [ka1, a1, after(b1, s0)])
    h1 = over_z(q1, last)
    q0 = partial_sums(0, distances, False, [ka0, a0, after(b0, *q1)])
    h0 = over_z(q0, 0)
    down, own, peer = totals(
        ffn_total_kernel,
        "ffn_total",
        [kf0, f0, *g0, kf1, after(f1, *q0), *g1],
        384,
        [((192, D), F32), ((96, D), F32), ((96, D), BF)],
    )
    peer = swap(peer, None, 1, 0)
    qkv, out, bias, gain, query, up_bias, loss = totals(
        attention_total_kernel,
        "attention_total",
        [ka0, a0, b0, *h0, ka1, after(a1, down), b1, *h1],
        208,
        [((48, 3 * D), F32), ((48, D), F32), ((5, 48), F32), ((2, 48), F32), ((1, 48), F32), ((1, 192), F32), ((8, 128), F32)],
    )
    (up,) = totals(up_total_kernel, "up_total", [own, peer], 0, [((48, FF), F32)], VMEM)
    return qkv, out, up, down, bias, gain, up_bias, query, loss


def body(
    query_crops,
    key_crops,
    query_lengths,
    key_lengths,
    positive,
    queue,
    qkv_weight,
    out_weight,
    up_weight,
    down_weight,
    biases,
    gains,
    up_biases,
    query_bias,
    key_qkv_weight,
    key_out_weight,
    key_up_weight,
    key_down_weight,
    key_biases,
    key_gains,
    key_up_biases,
):
    crops = query_crops.shape[0]
    rows = crops * SLOTS
    sections, dps, reps = [lax.axis_size(a) for a in AXES]
    fast = fast_mesh()
    crop_all = crops * dps * reps
    on_first = lax.axis_index("section") == 0
    dp, rep = lax.axis_index("dp"), lax.axis_index("rep")
    last = sections - 1

    def relay(block, distance):
        return lax.ppermute(block, "section", [(0, 1)] if distance > 0 else [(1, 0)])

    key_halves = (key_crops, relay(key_crops, -1))
    query_halves = (query_crops, relay(query_crops, -1))
    query_weights = [w[0] for w in (qkv_weight, out_weight, up_weight, down_weight)]
    key_weights = [w[0] for w in (key_qkv_weight, key_out_weight, key_up_weight, key_down_weight)]
    query_encoder = ("query", query_lengths, query_weights, (biases, gains, up_biases, query_bias))
    key_encoder = ("key", key_lengths, key_weights, (key_biases, key_gains, key_up_biases))

    key_middle, _ = forward(rows, 0, False, key_halves, None, [key_encoder])
    inv = call(
        functools.partial(queue_norm_kernel, last),
        "queue_norm",
        [((8, queue.shape[0]), F32)],
        [VMEM],
        [queue],
        [ANY],
        [(queue.shape, BF)],
    )[0]
    key_middle, inv = lax.optimization_barrier((key_middle, inv))
    key_middle = relay(key_middle, 1)
    query_middle, key_pooled = forward(rows, None, False, query_halves, key_middle, [query_encoder, key_encoder])
    query_middle = relay(query_middle, 1)

    every_key = key_pooled[crops : 2 * crops]
    near_flips = [(0, 1), (1, 0), (1, 1)]
    if fast:
        every_key = jnp.concatenate([every_key] + [swap(every_key, None, *f) for f in near_flips], axis=0)
    step = forward(rows, None, True, query_halves, query_middle, [query_encoder])
    query_pooled = step[1]
    qkv, prob, row_scale, ctx, n1, r1, first, hid, slope, n2, r2 = step[2:]

    if fast:
        every_key, query_pooled = lax.optimization_barrier((every_key, query_pooled))
        every_key = jnp.concatenate([every_key] + [swap(every_key, None, 2 * k, 0) for k in range(1, 4)], axis=0)
    else:
        for flip in flips():
            every_key = jnp.concatenate([every_key, swap(every_key, None, *flip)], axis=0)
    place = dp * reps + rep
    matched = jnp.take(every_key, jnp.bitwise_xor(positive // crops, place) * crops + positive % crops, axis=0)
    matched = jnp.concatenate([matched, jnp.zeros((8 - crops, D), F32)], axis=0)
    first_peer = swap(first, None, 1, 0) if fast else None

    pooled_grad, lost = call(
        functools.partial(loss_kernel, last, crops, crop_all),
        "contrast",
        [((8, D), F32), ((8, 128), F32)],
        [VMEM] * 2,
        [query_pooled, matched, queue, inv],
        [VMEM] * 4,
        [],
    )

    def data_part(active, pooled, dy):
        wqkv, wout, wup, wdown = query_weights
        vec, grad_bup, ddown, dup, datt, dqkv, dx = data_backward(
            active, pooled, query_lengths, dy, gains, n2, r2, wdown, slope, wup, n1, r1, wout, qkv, prob, row_scale, wqkv
        )
        ddown_peer = swap(ddown, active, 1, 0) if fast else None
        return vec, grad_bup, ddown, ddown_peer, dup, datt, dqkv, dx

    def weight_part(active, vec, grad_bup, ddown, ddown_peer, dup, datt, dqkv, term):
        attention = attention_weights(active, query_halves, query_middle, ctx, datt, dqkv, (vec, grad_bup, term))
        ffn = ffn_weights(
            active,
            after(first, *attention),
            first_peer,
            ddown,
            ddown_peer,
            hid,
            dup,
            query_weights[2],
            query_weights[3],
            up_biases,
        )
        return attention, ffn

    def small_rows(vec, grad_bup, term):
        picked = [vec[k : k + 1] for k in VECTOR_ROWS]
        lost_row = jnp.concatenate([term[0:1]] * (D // 128), axis=1)
        return jnp.concatenate(picked + [grad_bup[0:1].reshape(FF // D, D), lost_row], axis=0)

    *made_last, dmiddle = data_part(last, True, pooled_grad)
    dmiddle = relay(dmiddle, -1)
    attention_last, ffn_last = weight_part(last, *made_last, lost)
    *made_first, dx = data_part(0, False, after(dmiddle, *ffn_last))
    no_loss = jnp.zeros_like(lost)
    attention_first, ffn_first = weight_part(0, *made_first, no_loss)

    if fast:
        summed = chip_sums((attention_first, attention_last), (ffn_first[::-1], ffn_last[::-1]), last)
        grad_qkv, grad_out, grad_up, grad_down, bias, gain, up_part, query_part, loss_row = summed
        loss_row = loss_row[0]
    else:
        grad_up, grad_down, grad_qkv, grad_out = [
            lax.psum_scatter(jnp.where(on_first, a, b).astype(F32), ("dp", "rep"), scatter_dimension=0, tiled=True)
            for a, b in zip([*ffn_first, *attention_first], [*ffn_last, *attention_last])
        ]
        small = jnp.where(on_first, small_rows(*made_first[:2], no_loss), small_rows(*made_last[:2], lost))
        for flip in flips():
            small = small + swap(small, None, *flip)
        width, up_width = D // (dps * reps), FF // (dps * reps)
        mine = lax.dynamic_slice(small[:8], (0, place * width), (8, width))
        bias, gain, query_part = mine[:5], mine[5:7], mine[7:]
        up_part = lax.dynamic_slice(small[8:12].reshape(1, FF), (0, place * up_width), (1, up_width))
        loss_row = small[12, :128]
    loss_value = jnp.where(on_first, relay(loss_row, -1), loss_row)[:1]

    dx = dx.reshape(crops, SLOTS, D)
    half = SLOTS // sections
    crops_grad = jnp.where(on_first, dx[:, :half], relay(after(dx[:, half:], grad_down), 1)).astype(F32)
    return (
        loss_value,
        crops_grad,
        grad_qkv[None],
        grad_out[None],
        grad_up[None],
        grad_down[None],
        bias[None],
        gain[None],
        up_part,
        query_part,
    )


def solution(mesh):
    crop = P(("dp", "rep"), "section", None)
    per_crop = P(("dp", "rep"))
    layer3 = P("section", None, None)
    layer2 = P("section", None)
    placed = (
        (crop, crop, per_crop, per_crop, per_crop, P())
        + (layer3,) * 6
        + (layer2,) * 2
        + (layer3,) * 6
        + (layer2,)
    )
    shared3 = P("section", ("dp", "rep"), None)
    return jax.shard_map(
        body,
        mesh=mesh,
        in_specs=placed,
        out_specs=(
            P(),
            crop,
            shared3,
            shared3,
            shared3,
            shared3,
            P("section", None, ("dp", "rep")),
            P("section", None, ("dp", "rep")),
            P("section", ("dp", "rep")),
            P("section", ("dp", "rep")),
        ),
        check_vma=False,
    )
```

```python
import functools

import jax
import jax.numpy as jnp
from jax import lax
from jax.experimental import pallas as pl
from jax.experimental.pallas import tpu as pltpu
from jax.sharding import PartitionSpec as P

F32 = jnp.float32
BF = jnp.bfloat16
MASKED = -1e30
D = 768
FF = 3072
SLOTS = 256
PAIRS = 6
MIB = 2**20
SEMS = 96
ALPHA = 1.0


def dot(a, b):
    return lax.dot_general(a, b, (((1,), (0,)), ((), ())), preferred_element_type=F32)


def dot_nt(a, b):
    return lax.dot_general(a, b, (((1,), (1,)), ((), ())), preferred_element_type=F32)


def dot_tn(a, b):
    return lax.dot_general(a, b, (((0,), (0,)), ((), ())), preferred_element_type=F32)


def gelu_parts(x, want_slope):
    share = 0.5 + 0.5 * lax.erf(x * 0.7071067811865476)
    if not want_slope:
        return x * share, None
    return x * share, share + (0.3989422804014327 * x) * jnp.exp(-0.5 * (x * x))


def norm_parts(z):
    mean = jnp.mean(z, axis=-1, keepdims=True)
    c = z - mean
    var = jnp.mean(c * c, axis=-1, keepdims=True)
    r = lax.rsqrt(var + 1e-12)
    return c * r, r


def head_masks(scale):
    lane = lax.broadcasted_iota(jnp.int32, (1, 128), 1)
    low = jnp.where(lane < 64, scale, 0.0).astype(BF)
    high = jnp.where(lane < 64, 0.0, scale).astype(BF)
    return low, high


def stack_heads(pair, scale):
    low, high = head_masks(scale)
    return jnp.concatenate([pair * low, pair * high], axis=0)


def side_by_side(stacked):
    half = stacked.shape[0] // 2
    return jnp.concatenate([stacked[:half], stacked[half:]], axis=1)


class Copies:
    def __init__(self, sems):
        self.sems, self.used, self.open = sems, 0, []

    def make(self, src, dst):
        self.used += 1
        return pltpu.make_async_copy(src, dst, self.sems.at[self.used - 1])

    def fetch(self, src, dst):
        cp = self.make(src, dst)
        cp.start()
        return cp

    def pick(self, by_section, dst):
        if by_section[0] is by_section[1]:
            return self.fetch(by_section[0], dst)
        sem = self.sems.at[self.used]
        self.used += 1
        here = lax.axis_index("section")

        @pl.when(here == 0)
        def _():
            pltpu.make_async_copy(by_section[0], dst, sem).start()

        @pl.when(here != 0)
        def _():
            pltpu.make_async_copy(by_section[1], dst, sem).start()

        return pltpu.make_async_copy(by_section[0], dst, sem)

    def send(self, src, dst):
        self.open.append(self.fetch(src, dst))

    def drain(self):
        for cp in self.open:
            cp.wait()


def only_on(section, run):
    if section is None:
        run()
    else:
        pl.when(lax.axis_index("section") == section)(run)


VMEM = pl.BlockSpec(memory_space=pltpu.VMEM)
ANY = pl.BlockSpec(memory_space=pl.ANY)
SMEM = pl.BlockSpec(memory_space=pltpu.SMEM)
sd = jax.ShapeDtypeStruct


def call(kernel, name, outs, out_specs, ins, in_specs, scratch, micros, limit=56):
    return pl.pallas_call(
        kernel,
        out_shape=[sd(*o) for o in outs],
        in_specs=in_specs,
        out_specs=out_specs,
        scratch_shapes=[pltpu.VMEM(*s) for s in scratch] + [pltpu.SemaphoreType.DMA((SEMS,))],
        compiler_params=pltpu.CompilerParams(vmem_limit_bytes=limit * MIB),
        cost_estimate=pl.CostEstimate(flops=int(micros * ALPHA * 1.15e9), bytes_accessed=1000, transcendentals=0),
        name=name,
    )(*ins)


def saved_shapes(rows):
    crops = rows // SLOTS
    return [
        ((rows, 3 * D), BF),
        ((PAIRS * crops, 2 * SLOTS, SLOTS), BF),
        ((2 * SLOTS, 128), F32),
        ((rows, D), BF),
        ((rows, D), BF),
        ((rows, 128), F32),
        ((rows, D), BF),
        ((rows, FF), BF),
        ((rows, FF), BF),
        ((rows, D), BF),
        ((rows, 128), F32),
    ]


def fetch_rows(copies, refs, kinds, x):
    waits = []
    half = refs[0].shape[1] if "halves" in kinds else SLOTS // 2
    for c in range(x.shape[0] // SLOTS):
        for h in range(SLOTS // half):
            at = slice(SLOTS * c + half * h, SLOTS * c + half * (h + 1))
            options = []
            if "halves" in kinds:
                options.append(refs[h].at[c])
            if "whole" in kinds:
                options.append(refs[-1].at[at, :])
            waits.append(copies.pick((options[0], options[-1]), x.at[at, :]))
    return waits


def read_vectors(refs, key):
    if key:
        b, g, up = refs
        rows = b[0].astype(F32)
        rows = [rows[i : i + 1] for i in range(6)]
    else:
        b, g, up, q = refs
        rows = b[0].astype(F32)
        rows = [q[...].astype(F32)] + [rows[i : i + 1] for i in range(5)]
    gains = g[0].astype(F32)
    return rows + [gains[0:1], gains[1:2]], up[...].astype(F32)


def load_vectors(refs, kinds, vec, bup):
    sets = []
    for kind in kinds:
        n = 3 if kind == "key" else 4
        sets.append(read_vectors(refs[:n], kind == "key"))
        refs = refs[n:]
    here = lax.axis_index("section")
    for i in range(8):
        row = sets[0][0][i]
        if len(sets) == 2:
            row = jnp.where(here == 0, row, sets[1][0][i])
        vec[i : i + 1, :] = row
    up = sets[0][1]
    if len(sets) == 2:
        up = jnp.where(here == 0, up, sets[1][1])
    bup[...] = up


def forward_kernel(rows, active, save, x_kinds, sets, *refs):
    def run():
        forward_body(rows, save, x_kinds, sets, *refs)

    only_on(active, run)


def forward_body(rows, save, x_kinds, sets, *refs):
    crops = rows // SLOTS
    lens_refs, refs = refs[: len(sets)], refs[len(sets) :]
    here = lax.axis_index("section")
    if len(sets) == 2:
        lens = [jnp.where(here == 0, lens_refs[0][c], lens_refs[1][c]) for c in range(crops)]
    else:
        lens = [lens_refs[0][c] for c in range(crops)]
    n_x = (2 if "halves" in x_kinds else 0) + (1 if "whole" in x_kinds else 0)
    x_refs, refs = refs[:n_x], refs[n_x:]
    w_refs, refs = refs[: 4 * len(sets)], refs[4 * len(sets) :]
    n_v = sum(3 if k == "key" else 4 for k in sets)
    v_refs, refs = refs[:n_v], refs[n_v:]
    y_ref, pool_ref = refs[:2]
    refs = refs[2:]
    if save:
        (qkv_o, prob_o, inv_o, ctx_o, n1_o, r1_o, first_o, hid_o, slope_o, n2_o, r2_o) = refs[:11]
        refs = refs[11:]
    (x, wqkv, wout, wup, wdown, ctx, zbuf, first, hid, vec, bup) = refs[:11]
    refs = refs[11:]
    if save:
        (qkv, prob, inv_all, n1, r1, slope, n2, r2) = refs[:8]
        refs = refs[8:]
        inv_all[...] = jnp.zeros_like(inv_all)
    copies = Copies(refs[0])
    got_x = fetch_rows(copies, x_refs, x_kinds, x)
    pairs = [(w_refs[i], w_refs[4 + i] if len(sets) == 2 else w_refs[i]) for i in range(4)]
    got_qkv = copies.pick(pairs[0], wqkv)
    load_vectors(v_refs, sets, vec, bup)
    for cp in got_x:
        cp.wait()
    got_qkv.wait()
    got_out = copies.pick(pairs[1], wout)
    got_up = copies.pick(pairs[2], wup)
    got_down = copies.pick(pairs[3], wdown)
    keycol = lax.broadcasted_iota(jnp.int32, (1, SLOTS), 1)
    lane = lax.broadcasted_iota(jnp.int32, (1, 128), 1)
    gain1, gain2 = vec[6:7], vec[7:8]

    def heads(i, carry):
        thirds = []
        for j in range(3):
            cols = pl.ds(pl.multiple_of(D * j + 256 * i, 256), 256)
            part = dot(x[...], wqkv[:, cols])
            if j != 1:
                at = pl.ds(pl.multiple_of(256 * i, 256), 256)
                part = part + vec[j // 2 : j // 2 + 1, at]
            part = part.astype(BF)
            if save:
                qkv[:, cols] = part
            thirds.append(part)
        for c in range(crops):
            crop = slice(SLOTS * c, SLOTS * (c + 1))
            for pr in range(2):
                qp, kp, vp = [t[crop, 128 * pr : 128 * (pr + 1)] for t in thirds]
                scores = jnp.where(keycol < lens[c], dot_nt(stack_heads(qp, 0.125), kp), MASKED)
                e = jnp.exp(scores - jnp.max(scores, axis=-1, keepdims=True))
                inv = pl.reciprocal(jnp.sum(e, axis=-1, keepdims=True))
                e = e.astype(BF)
                if save:
                    unit = PAIRS * c + 2 * i + pr
                    prob[unit] = e
                    inv_all[...] = jnp.where(lane == unit, inv, inv_all[...])
                at = pl.ds(pl.multiple_of(256 * i + 128 * pr, 128), 128)
                both = dot(e, vp) * inv
                ctx[crop, at] = jnp.where(lane < 64, both[:SLOTS], both[SLOTS:]).astype(BF)
        return carry

    lax.fori_loop(0, 3, heads, 0)
    if save:
        copies.send(qkv, qkv_o)
        copies.send(prob, prob_o)
        copies.send(inv_all, inv_o)
        copies.send(ctx, ctx_o)
    got_out.wait()
    for j in range(3):
        cols = slice(256 * j, 256 * (j + 1))
        zbuf[:, cols] = x[:, cols].astype(F32) + dot(ctx[...], wout[:, cols]) + vec[2:3, cols]
    block = 64
    steps = rows // block

    def first_norm(i, carry):
        at = pl.ds(pl.multiple_of(i * block, block), block)
        n, r = norm_parts(zbuf[at, :])
        f = (n * gain1 + vec[3:4]).astype(BF)
        first[at, :] = f
        zbuf[at, :] = f.astype(F32) + vec[4:5]
        if save:
            n1[at, :] = n.astype(BF)
            r1[at, :] = jnp.broadcast_to(r, (block, 128))
        return carry

    lax.fori_loop(0, steps, first_norm, 0, unroll=True)
    if save:
        copies.send(n1, n1_o)
        copies.send(r1, r1_o)
        copies.send(first, first_o)
    got_up.wait()
    got_down.wait()

    def down_part(k):
        cols = slice(512 * k, 512 * (k + 1))
        zbuf[...] += dot(hid[:, cols], wdown[cols, :])

    for i in range(12):
        cols = slice(256 * i, 256 * (i + 1))
        g, slope_part = gelu_parts(dot(first[...], wup[:, cols]) + bup[:, cols], save)
        hid[:, cols] = g.astype(BF)
        if save:
            slope[:, cols] = slope_part.astype(BF)
        if i % 2 and i > 2:
            down_part(i // 2 - 1)
    if save:
        copies.send(hid, hid_o)
        copies.send(slope, slope_o)
    down_part(5)
    pool_ref[...] = jnp.zeros_like(pool_ref)
    per_crop = SLOTS // block
    for i in range(steps):
        at = slice(i * block, (i + 1) * block)
        n, r = norm_parts(zbuf[at, :])
        f = n * gain2 + vec[5:6]
        y_ref[at, :] = f.astype(BF)
        if save:
            n2[at, :] = n.astype(BF)
            r2[at, :] = jnp.broadcast_to(r, (block, 128))
        c = i // per_crop
        token = lax.broadcasted_iota(jnp.int32, (block, 1), 0) + (i % per_crop) * block
        part = jnp.sum(jnp.where(token < lens[c], f, 0.0), axis=0, keepdims=True)
        pool_ref[c : c + 1, :] += part / lens[c].astype(F32)
    pooled = pool_ref[:crops]
    pool_ref[crops : 2 * crops] = pooled * lax.rsqrt(jnp.sum(pooled * pooled, axis=-1, keepdims=True) + 1e-6)
    if save:
        copies.send(n2, n2_o)
        copies.send(r2, r2_o)
    copies.drain()


def forward(rows, active, save, halves, whole, encoders):
    x_kinds = (("halves",) if halves else ()) + (("whole",) if whole is not None else ())
    xs = list(halves or ()) + ([whole] if whole is not None else [])
    lens = [e[1] for e in encoders]
    weights = [w for e in encoders for w in e[2]]
    vectors = [v for e in encoders for v in e[3]]
    outs = [((rows, D), BF), ((8, D), F32)]
    out_specs = [VMEM, VMEM]
    scratch = [
        ((rows, D), BF),
        ((D, 3 * D), BF),
        ((D, D), BF),
        ((D, FF), BF),
        ((FF, D), BF),
        ((rows, D), BF),
        ((rows, D), F32),
        ((rows, D), BF),
        ((rows, FF), BF),
        ((8, D), F32),
        ((1, FF), F32),
    ]
    if save:
        kept = saved_shapes(rows)
        outs += kept
        out_specs += [ANY] * len(kept)
        scratch += [kept[i] for i in (0, 1, 2, 4, 5, 8, 9, 10)]
    return call(
        functools.partial(forward_kernel, rows, active, save, x_kinds, [e[0] for e in encoders]),
        "layer_forward",
        outs,
        out_specs,
        [*lens, *xs, *weights, *vectors],
        [SMEM] * len(lens) + [ANY] * (len(xs) + len(weights)) + [VMEM] * len(vectors),
        scratch,
        20 if save else 18,
    )


def split3(v):
    hi = v.astype(BF)
    rest = v - hi.astype(F32)
    mid = rest.astype(BF)
    lo = (rest - mid.astype(F32)).astype(BF)
    return hi, mid, lo


def stack3(v):
    parts = split3(v)
    return jnp.concatenate(list(parts) + [jnp.zeros_like(parts[0])] * 5, axis=0)


def unstack3(rows, n):
    return rows[:n] + rows[n : 2 * n] + rows[2 * n : 3 * n]


def queue_norm_kernel(active, queue_h, inv_ref, queue, sems):
    def run():
        Copies(sems).fetch(queue_h, queue).wait()

        def step(i, carry):
            at = pl.ds(pl.multiple_of(i * 512, 512), 512)
            v = queue[at, :].astype(F32)
            sq = v * v
            hi = sq.astype(BF)
            lo = (sq - hi.astype(F32)).astype(BF)
            ones = jnp.ones((8, D), BF)
            total = dot_nt(ones, hi) + dot_nt(ones, lo)
            inv_ref[:, at] = lax.rsqrt(total + 1e-6)
            return carry

        lax.fori_loop(0, queue.shape[0] // 512, step, 0)

    only_on(active, run)


def loss_kernel(active, crops, count, pooled, matched, queue, inv, grad_ref, loss_ref, sems):
    def run():
        v = pooled[:crops]
        r = lax.rsqrt(jnp.sum(v * v, axis=-1, keepdims=True) + 1e-6)
        u = v * r
        k = matched[:crops]
        near = jnp.sum(u * k, axis=-1, keepdims=True) * 20.0
        inv_row = inv[0:1]
        far = unstack3(dot_nt(stack3(u), queue[...]), crops) * (inv_row * 20.0)
        top = jnp.maximum(near, jnp.max(far, axis=-1, keepdims=True))
        e_near = jnp.exp(near - top)
        e_far = jnp.exp(far - top)
        total = e_near + jnp.sum(e_far, axis=-1, keepdims=True)
        share = 20.0 / (total * count)
        d_u = unstack3(dot(stack3(e_far * inv_row * share), queue[...]), crops)
        d_u = d_u + (e_near - total) * share * k
        grad = r * (d_u - u * jnp.sum(u * d_u, axis=-1, keepdims=True))
        grad_ref[...] = jnp.zeros_like(grad_ref)
        grad_ref[:crops] = grad
        lost = jnp.sum(top + jnp.log(total) - near, axis=0, keepdims=True) / count
        loss_ref[...] = jnp.broadcast_to(lost, loss_ref.shape)

    only_on(active, run)


def norm_back(dy, gain, n, r):
    dn = dy * gain
    return r * (dn - jnp.mean(dn, axis=-1, keepdims=True) - n * jnp.mean(dn * n, axis=-1, keepdims=True))


def column_sum(v):
    return jnp.sum(v, axis=0, keepdims=True)


def fast_mesh():
    return lax.axis_size("dp") == 8 and lax.axis_size("rep") == 2


def place_bits():
    dp, rep = lax.axis_index("dp"), lax.axis_index("rep")
    return dp // 2, dp % 2, rep


CHUNK = 512


def data_backward_kernel(rows, active, pooled, lens, dy, gains, *refs):
    def run():
        n2_h, r2_h, wdown_h, slope_h, wup_h, n1_h, r1_h, wout_h, qkv_h, prob_h, inv_h, wqkv_h = refs[:12]
        vec, bup, ddown_o, dup_o, datt_o, dqkv_o, dx_o = refs[12:19]
        n2, r2, wdown, slope, wup, n1, r1, wout, qkv, prob, inv, wqkv = refs[19:31]
        acc, ddown, dup, datt, dqkv, dx, sems = refs[31:]
        copies = Copies(sems)
        got_n2, got_r2 = copies.fetch(n2_h, n2), copies.fetch(r2_h, r2)
        got = []
        for i in range(FF // CHUNK):
            cols = slice(CHUNK * i, CHUNK * (i + 1))
            got.append(
                [
                    copies.fetch(wdown_h.at[cols, :], wdown.at[cols, :]),
                    copies.fetch(slope_h.at[:, cols], slope.at[:, cols]),
                    copies.fetch(wup_h.at[:, cols], wup.at[:, cols]),
                ]
            )
        got_n1 = [copies.fetch(n1_h, n1), copies.fetch(r1_h, r1), copies.fetch(wout_h, wout)]
        got_qkv = [copies.fetch(qkv_h, qkv), copies.fetch(prob_h, prob), copies.fetch(inv_h, inv)]
        got_w = copies.fetch(wqkv_h, wqkv)
        vec[...] = jnp.zeros_like(vec)
        gain1, gain2 = gains[0].astype(F32)[0:1], gains[0].astype(F32)[1:2]
        block = 64
        per_crop = SLOTS // block
        got_n2.wait()
        got_r2.wait()
        for i in range(rows // block):
            at = slice(block * i, block * (i + 1))
            c = i // per_crop
            if pooled:
                token = lax.broadcasted_iota(jnp.int32, (block, 1), 0) + (i % per_crop) * block
                grow = jnp.where(token < lens[c], 1.0 / lens[c].astype(F32), 0.0) * dy[c : c + 1]
            else:
                grow = dy[at].astype(F32)
            n = n2[at].astype(F32)
            ds = norm_back(grow, gain2, n, r2[at, 0:1])
            low_ds = ds.astype(BF)
            acc[at] = ds
            ddown[at] = low_ds
            vec[0:1] += column_sum(grow * n)
            vec[1:2] += column_sum(grow)
            vec[2:3] += column_sum(low_ds.astype(F32))
        copies.send(ddown, ddown_o)
        for i in range(FF // CHUNK):
            cols = slice(CHUNK * i, CHUNK * (i + 1))
            for cp in got[i]:
                cp.wait()
            up = (dot_nt(ddown[...], wdown[cols, :]) * slope[:, cols].astype(F32)).astype(BF)
            dup[:, cols] = up
            copies.send(dup.at[:, cols], dup_o.at[:, cols])
            bup[:, cols] = jnp.broadcast_to(column_sum(up.astype(F32)), (8, CHUNK))
            acc[...] += dot_nt(up, wup[:, cols])
        for cp in got_n1:
            cp.wait()
        for i in range(rows // block):
            at = slice(block * i, block * (i + 1))
            n = n1[at].astype(F32)
            dfirst = acc[at]
            ds = norm_back(dfirst, gain1, n, r1[at, 0:1])
            low_ds = ds.astype(BF)
            acc[at] = ds
            datt[at] = low_ds
            vec[3:4] += column_sum(dfirst * n)
            vec[4:5] += column_sum(dfirst)
            vec[5:6] += column_sum(low_ds.astype(F32))
        copies.send(datt, datt_o)
        dctx = dot_nt(datt[...], wout[...]).astype(BF)
        for cp in got_qkv:
            cp.wait()
        for c in range(rows // SLOTS):
            crop = slice(SLOTS * c, SLOTS * (c + 1))
            for pr in range(PAIRS):
                cols = [slice(D * j + 128 * pr, D * j + 128 * (pr + 1)) for j in range(3)]
                unit = PAIRS * c + pr
                qp, kp, vp = [qkv[crop, t] for t in cols]
                dcs = stack_heads(dctx[crop, 128 * pr : 128 * (pr + 1)], 1.0)
                scale = inv[:, unit : unit + 1]
                e = prob[unit]
                pf = e.astype(F32) * scale
                weighted = pf * dot_nt(dcs, vp)
                ds = (weighted - pf * jnp.sum(weighted, axis=-1, keepdims=True)).astype(BF)
                dqkv[crop, cols[0]] = dot(side_by_side(ds), stack_heads(kp, 0.125)).astype(BF)
                dqkv[crop, cols[1]] = dot_tn(ds, stack_heads(qp, 0.125)).astype(BF)
                dqkv[crop, cols[2]] = dot_tn(e, (dcs * scale).astype(BF)).astype(BF)
        got_w.wait()
        for j in range(3):
            cols = slice(256 * j, 256 * (j + 1))
            dx[:, cols] = (dot_nt(dqkv[...], wqkv[cols, :]) + acc[:, cols]).astype(BF)
        copies.send(dx, dx_o)
        copies.send(dqkv, dqkv_o)
        vec[6:7] = column_sum(dqkv[:, :D].astype(F32))
        vec[7:8] = column_sum(dqkv[:, 2 * D :].astype(F32))
        copies.drain()

    only_on(active, run)


def data_backward(active, pooled, lens, dy, gains, n2, r2, wdown, slope, wup, n1, r1, wout, qkv, prob, inv, wqkv):
    rows = n1.shape[0]
    held = [n2, r2, wdown, slope, wup, n1, r1, wout, qkv, prob, inv, wqkv]
    wide_rows = ((rows, D), BF)
    return call(
        functools.partial(data_backward_kernel, rows, active, pooled),
        "data_backward",
        [((8, D), F32), ((8, FF), F32), wide_rows, ((rows, FF), BF), wide_rows, ((rows, 3 * D), BF), wide_rows],
        [VMEM] * 2 + [ANY] * 5,
        [lens, dy, gains, *held],
        [SMEM, VMEM, VMEM] + [ANY] * len(held),
        [(h.shape, h.dtype) for h in held]
        + [((rows, D), F32), wide_rows, ((rows, FF), BF), wide_rows, ((rows, 3 * D), BF), wide_rows],
        26,
    )


def ffn_weights_kernel(rows, active, fast, *refs):
    def run():
        if fast:
            first_h, first_p, ddown_h, ddown_p, hid_h, dup_h, wup_h, wdown_h, bup_h, send, keep = refs[:11]
            first, ddown, hid, dup, gup, gdown, wup, wdown, bup, sems = refs[11:]
        else:
            first_h, ddown_h, hid_h, dup_h, up_o, down_o = refs[:6]
            first, ddown, hid, dup, gup, gdown, sems = refs[6:]
        copies = Copies(sems)
        own = slice(0, rows)
        got = [copies.fetch(first_h, first.at[own, :]), copies.fetch(ddown_h, ddown.at[own, :])]
        z, x, y = place_bits()
        parts = 4 if fast else FF // 384
        if fast:
            peer = slice(rows, 2 * rows)
            got += [copies.fetch(first_p, first.at[peer, :]), copies.fetch(ddown_p, ddown.at[peer, :])]
            got.append(copies.fetch(bup_h, bup))
        blocks = []
        for i in range(parts):
            here = slice(384 * i, 384 * (i + 1))
            there = pl.ds(pl.multiple_of(768 * i + 384 * x, 128), 384) if fast else here
            block = [
                copies.fetch(hid_h.at[:, there], hid.at[own, here]),
                copies.fetch(dup_h.at[:, there], dup.at[own, here]),
            ]
            if fast:
                block.append(copies.fetch(wup_h.at[:, there], wup.at[:, here]))
                block.append(copies.fetch(wdown_h.at[there, :], wdown.at[here, :]))
            blocks.append(block)
        for cp in got:
            cp.wait()
        for i in range(parts):
            here = slice(384 * i, 384 * (i + 1))
            for cp in blocks[i]:
                cp.wait()
            if fast:
                there = pl.ds(pl.multiple_of(768 * i + 384 * x, 128), 384)
                bias = bup[:, there].astype(F32)
                g, slope = gelu_parts(dot(first[peer, :], wup[:, here]) + bias, True)
                hid[peer, here] = g.astype(BF)
                dup[peer, here] = (dot_nt(ddown[peer, :], wdown[here, :]) * slope).astype(BF)
            gdown[here, :] = dot_tn(hid[:, here], ddown[...]).astype(BF)
            if fast:
                for jy, out in ((1, send), (0, keep)):
                    at = pl.ds(pl.multiple_of(384 * i + 192 * jnp.bitwise_xor(y, jy), 64), 192)
                    copies.send(gdown.at[at, :], out.at[jnp.bitwise_xor(z, i), 192:384, :])
            gup[:, here] = dot_tn(first[...], dup[:, here]).astype(BF)
            if fast and i % 2:
                half = i // 2
                for jy, out in ((1, send), (0, keep)):
                    for jz in range(4):
                        for jx in range(2):
                            owner = (jnp.bitwise_xor(z, jz) * 2 + jnp.bitwise_xor(x, jx)) * 2 + jnp.bitwise_xor(y, jy)
                            at = pl.ds(pl.multiple_of(48 * owner, 16), 48)
                            to = slice(96 * jx + 48 * half, 96 * jx + 48 * (half + 1))
                            copies.send(gup.at[at, slice(D * half, D * (half + 1))], out.at[jz, to, :])
        if not fast:
            copies.send(gup, up_o)
            copies.send(gdown, down_o)
        copies.drain()

    only_on(active, run)


def ffn_weights(active, first, first_peer, ddown, ddown_peer, hid, dup, wup, wdown, bup):
    rows = first.shape[0]
    fast = fast_mesh()
    if fast:
        ins = [first, first_peer, ddown, ddown_peer, hid, dup, wup, wdown, bup]
        outs = [((4, 384, D), BF)] * 2
        tokens, units = 2 * rows, FF // 2
        extra = [((D, units), BF), ((units, D), BF), ((1, FF), BF)]
    else:
        ins = [first, ddown, hid, dup]
        outs = [((D, FF), BF), ((FF, D), BF)]
        tokens, units, extra = rows, FF, []
    return call(
        functools.partial(ffn_weights_kernel, rows, active, fast),
        "ffn_weights",
        outs,
        [ANY] * 2,
        ins,
        [ANY] * len(ins),
        [
            ((tokens, D), BF),
            ((tokens, D), BF),
            ((tokens, units), BF),
            ((tokens, units), BF),
            ((D, units), BF),
            ((units, D), BF),
        ]
        + extra,
        15,
    )


VECTOR_ROWS = (7, 5, 4, 2, 1, 3, 0, 6)


def attention_weights_kernel(rows, active, fast, x_kinds, *refs):
    def run():
        n_x = len(x_kinds) + 1
        x_refs = refs[:n_x]
        if fast:
            vec, bup, lost, *refs_ = refs[n_x:]
            ctx_h, datt_h, dqkv_h, out_a, out_b, x, ctx, datt, dqkv, gqkv, gout, tail, sems = refs_
        else:
            ctx_h, datt_h, dqkv_h, out_a, out_b, x, ctx, datt, dqkv, gqkv, gout, sems = refs[n_x:]
        copies = Copies(sems)
        got = [copies.fetch(ctx_h, ctx), copies.fetch(datt_h, datt)]
        got_x = fetch_rows(copies, x_refs, x_kinds, x)
        got_x.append(copies.fetch(dqkv_h, dqkv))
        if fast:
            z, xx, y = place_bits()
            small = jnp.concatenate([vec[k : k + 1] for k in VECTOR_ROWS], axis=0)
            row = lax.broadcasted_iota(jnp.int32, (8, D), 0)
            lane = lax.broadcasted_iota(jnp.int32, (8, D), 1) - 3 * ((z * 2 + xx) * 2 + y)
            terms = [jnp.broadcast_to(t.astype(F32)[0:1, 0:1], (8, D)) for t in split3(lost[...])]
            lost_row = sum(jnp.where(lane == i, t, 0.0) for i, t in enumerate(terms))

        def ship(part, to):
            for j in range(15, -1, -1):
                jx, jy, jz = j // 8, j // 4 % 2, j % 4
                owner = (jnp.bitwise_xor(z, jz) * 2 + jnp.bitwise_xor(xx, jx)) * 2 + jnp.bitwise_xor(y, jy)
                at = pl.ds(pl.multiple_of(48 * owner, 16), 48)
                copies.send(part.at[at, :], (out_b if jx else out_a).at[j % 8, to : to + 48, :])

        for cp in got:
            cp.wait()
        gout[...] = dot_tn(ctx[...], datt[...]).astype(BF)
        if fast:
            ship(gout, 144)
            for j in range(16):
                jx, jy, jz = j // 8, j // 4 % 2, j % 4
                owner = (jnp.bitwise_xor(z, jz) * 2 + jnp.bitwise_xor(xx, jx)) * 2 + jnp.bitwise_xor(y, jy)
                head = pltpu.roll(small, D - 48 * owner, 1)
                ups = pltpu.roll(bup[...], FF - 192 * owner, 1)[:, :D]
                other = jnp.where(row == 0, ups, jnp.where(row == 1, lost_row, 0.0))
                tail[j] = jnp.concatenate([head, other], axis=0).astype(BF)
                copies.send(tail.at[j], (out_b if jx else out_a).at[j % 8, 192:208, :])
        for cp in got_x:
            cp.wait()
        for t in range(3):
            for k in range(2):
                cols = slice(D * t + 384 * k, D * t + 384 * (k + 1))
                gqkv[:, cols] = dot_tn(x[...], dqkv[:, cols]).astype(BF)
            if fast:
                ship(gqkv.at[:, slice(D * t, D * (t + 1))], 48 * t)
        if not fast:
            copies.send(gqkv, out_a)
            copies.send(gout, out_b)
        copies.drain()

    only_on(active, run)


def attention_weights(active, halves, whole, ctx, datt, dqkv, small):
    rows = ctx.shape[0]
    fast = fast_mesh()
    x_kinds = ("halves", "whole")
    outs = [((8, 208, D), BF)] * 2 if fast else [((D, 3 * D), BF), ((D, D), BF)]
    ins = [*halves, whole, *(small if fast else ()), ctx, datt, dqkv]
    in_specs = [ANY] * 3 + [VMEM] * (3 if fast else 0) + [ANY] * 3
    return call(
        functools.partial(attention_weights_kernel, rows, active, fast, x_kinds),
        "attention_weights",
        outs,
        [ANY] * 2,
        ins,
        in_specs,
        [((rows, D), BF)] * 3
        + [((rows, 3 * D), BF), ((D, 3 * D), BF), ((D, D), BF)]
        + ([((16, 16, D), BF)] if fast else []),
        8,
    )


AXES = ("section", "dp", "rep")


def swap(block, section, dp_flip, rep_flip):
    dps, reps = lax.axis_size("dp"), lax.axis_size("rep")
    sections = range(lax.axis_size("section")) if section is None else [section]
    route = [
        ((s * dps + d) * reps + r, (s * dps + (d ^ dp_flip)) * reps + (r ^ rep_flip))
        for s in sections
        for d in range(dps)
        for r in range(reps)
    ]
    return lax.ppermute(block, AXES, route)


def flips():
    out, bit = [], 1
    while bit < lax.axis_size("rep"):
        out.append((0, bit))
        bit *= 2
    bit = 1
    while bit < lax.axis_size("dp"):
        out.append((bit, 0))
        bit *= 2
    return out


def add_rows(pieces, dst, at, count):
    def step(i, carry):
        here = pl.ds(pl.multiple_of(i * 16, 16), 16)
        total = pieces[0][here, :].astype(F32)
        for p in pieces[1:]:
            total = total + p[here, :].astype(F32)
        dst[pl.ds(pl.multiple_of(at + i * 16, 16), 16), :] = total.astype(dst.dtype)
        return carry

    lax.fori_loop(0, count // 16, step, 0, unroll=2 if count % 32 == 0 else 1)


def half_sums_kernel(active, rows, kept, received, out, held, made, sems):
    def run():
        copies = Copies(sems)
        got = [copies.fetch(kept.at[4 + i], held.at[i]) for i in range(4)]
        for i in range(4):
            got[i].wait()
            add_rows([held.at[i], received.at[4 + i]], made.at[i], 0, rows)
            copies.send(made.at[i], out.at[i])
        copies.drain()

    only_on(active, run)


def half_sums(kept, received, section):
    shape = kept.shape[1:]
    held = ((4, *shape), BF)
    return call(
        functools.partial(half_sums_kernel, section, shape[0]),
        "half_sums",
        [held],
        [ANY],
        [kept, received],
        [ANY, VMEM],
        [held, held],
        3,
        20,
    )[0]


def slot_sums_kernel(active, counts, sizes, *refs):
    def run():
        groups, at = [], 0
        for n in counts:
            groups.append(refs[at : at + n])
            at += n
        own_o, kept_o, send_o = refs[at : at + 3]
        helds = refs[at + 3 : at + 3 + len(counts)]
        own, made, sems = refs[-3:]
        copies = Copies(sems)
        order = (1, 3, 2, 0)
        got = {k: [copies.fetch(g[0].at[k], h.at[k]) for g, h in zip(groups, helds)] for k in order}
        for k, out in zip(order, (send_o.at[0], send_o.at[1], kept_o, own_o)):
            to, base = made.at[k - 1] if k else own, 0
            for g, h, cp, size in zip(groups, helds, got[k], sizes):
                cp.wait()
                add_rows([h.at[k]] + [r.at[k] for r in g[1:]], to, base, size)
                base += size
            copies.send(to, out)
        copies.drain()

    only_on(active, run)


def slot_sums(section, *groups):
    sizes = [g[0].shape[1] for g in groups]
    shape = (sum(sizes), D)
    return call(
        functools.partial(slot_sums_kernel, section, [len(g) for g in groups], sizes),
        "slot_sums",
        [(shape, F32), (shape, BF), ((2, *shape), BF)],
        [ANY] * 3,
        [t for g in groups for t in g],
        [spec for g in groups for spec in [ANY] + [VMEM] * (len(g) - 1)],
        [((4, size, D), BF) for size in sizes] + [(shape, F32), ((3, *shape), BF)],
        3 * len(groups),
        24,
    )


def second_sum_kernel(active, rows, kept, received, out, held, made, sems):
    def run():
        copies = Copies(sems)
        copies.fetch(kept, held).wait()
        add_rows([held, received.at[1]], made, 0, rows)
        copies.send(made, out)
        copies.drain()

    only_on(active, run)


def second_sum(section, kept, received):
    held = (kept.shape, BF)
    return call(
        functools.partial(second_sum_kernel, section, kept.shape[0]),
        "second_sum",
        [held],
        [ANY],
        [kept, received],
        [ANY, VMEM],
        [held, held],
        2,
        16,
    )[0]


def add_terms(copies, first, last, at, count, own, total):
    rows = pl.ds(at, count)
    copies.pick((first[0], last[0].at[rows, :]), own).wait()

    @pl.when(lax.axis_index("section") == 0)
    def _():
        add_rows([own, first[1].at[0], first[2]], total, 0, count)

    @pl.when(lax.axis_index("section") != 0)
    def _():
        add_rows([own, last[1].at[0, rows, :], last[2].at[rows, :]], total, 0, count)


def attention_total_kernel(*refs):
    qkv_o, out_o, bias_o, gain_o, query_o, up_o, loss_o, own, total, sems = refs[6:]
    add_terms(Copies(sems), refs[:3], refs[3:6], 384, 208, own, total)
    for t in range(3):
        qkv_o[:, D * t : D * (t + 1)] = total[48 * t : 48 * (t + 1), :]
    out_o[...] = total[144:192, :]
    bias_o[...] = total[192:197, :48]
    gain_o[...] = total[197:199, :48]
    query_o[...] = total[199:200, :48]
    up_o[...] = total[200:201, :192]
    loss_o[...] = jnp.broadcast_to(jnp.sum(total[201:202, :], axis=-1, keepdims=True), loss_o.shape)


def ffn_total_kernel(*refs):
    down_o, own_o, peer_o, own, total, sems = refs[6:]
    add_terms(Copies(sems), refs[:3], refs[3:6], 0, 384, own, total)
    own_o[...] = total[0:96, :]
    peer_o[...] = total[96:192, :].astype(BF)
    down_o[...] = total[192:384, :]


def up_total_kernel(own, peer, up_o, sems):
    x = lax.axis_index("dp") % 2
    for c in range(2):
        for k in range(2):
            cols = slice(384 * k, 384 * (k + 1))
            at = 768 * (2 * c + k)
            up_o[:, pl.ds(pl.multiple_of(at + 384 * x, 128), 384)] = own[48 * c : 48 * (c + 1), cols]
            up_o[:, pl.ds(pl.multiple_of(at + 384 * (1 - x), 128), 384)] = peer[48 * c : 48 * (c + 1), cols].astype(F32)


def totals(kernel, name, ins, rows, outs):
    specs = ([ANY] + [VMEM] * 2) * 2 if rows else [VMEM] * len(ins)
    scratch = [((rows, D), F32)] * 2 if rows else []
    return call(kernel, name, outs, [VMEM] * len(outs), ins, specs, scratch, 3, 20)


def after(value, *others):
    return lax.optimization_barrier((value, others))[0]


def near_z(parts, section):
    return swap(parts[2], section, 2, 0)


def far_z(parts, near, section):
    return [parts[0], near, swap(second_sum(section, parts[1], near), section, 4, 0)]


def chip_totals(ffn, attention, both):
    down, own, peer = totals(
        ffn_total_kernel, "ffn_total", ffn + both, 384, [((192, D), F32), ((96, D), F32), ((96, D), BF)]
    )
    peer = swap(peer, None, 1, 0)
    attention[0] = after(attention[0], down)
    qkv, out, bias, gain, query, up_bias, loss = totals(
        attention_total_kernel,
        "attention_total",
        attention + both,
        208,
        [((48, 3 * D), F32), ((48, D), F32), ((5, 48), F32), ((2, 48), F32), ((1, 48), F32), ((1, 192), F32), ((8, 128), F32)],
    )
    (up,) = totals(up_total_kernel, "up_total", [after(own, qkv), peer], 0, [((48, FF), F32)])
    return qkv, out, up, down, bias, gain, up_bias, query, loss


def body(
    query_crops,
    key_crops,
    query_lengths,
    key_lengths,
    positive,
    queue,
    qkv_weight,
    out_weight,
    up_weight,
    down_weight,
    biases,
    gains,
    up_biases,
    query_bias,
    key_qkv_weight,
    key_out_weight,
    key_up_weight,
    key_down_weight,
    key_biases,
    key_gains,
    key_up_biases,
):
    crops = query_crops.shape[0]
    rows = crops * SLOTS
    sections, dps, reps = [lax.axis_size(a) for a in AXES]
    fast = fast_mesh()
    crop_all = crops * dps * reps
    on_first = lax.axis_index("section") == 0
    dp, rep = lax.axis_index("dp"), lax.axis_index("rep")
    last = sections - 1

    def relay(block, distance):
        return lax.ppermute(block, "section", [(0, 1)] if distance > 0 else [(1, 0)])

    key_half, query_half = lax.optimization_barrier((relay(key_crops, -1), relay(query_crops, -1)))
    key_halves = (key_crops, key_half)
    query_halves = (query_crops, query_half)
    query_weights = [w[0] for w in (qkv_weight, out_weight, up_weight, down_weight)]
    key_weights = [w[0] for w in (key_qkv_weight, key_out_weight, key_up_weight, key_down_weight)]
    query_encoder = ("query", query_lengths, query_weights, (biases, gains, up_biases, query_bias))
    key_encoder = ("key", key_lengths, key_weights, (key_biases, key_gains, key_up_biases))

    key_middle, _ = forward(rows, 0, False, key_halves, None, [key_encoder])
    inv = call(
        functools.partial(queue_norm_kernel, last),
        "queue_norm",
        [((8, queue.shape[0]), F32)],
        [VMEM],
        [queue],
        [ANY],
        [(queue.shape, BF)],
        4,
    )[0]
    key_middle, inv = lax.optimization_barrier((key_middle, inv))
    key_middle = relay(key_middle, 1)
    query_middle, key_pooled = forward(rows, None, False, query_halves, key_middle, [query_encoder, key_encoder])
    query_middle = relay(query_middle, 1)

    every_key = key_pooled[crops : 2 * crops]
    near_flips = [(0, 1), (1, 0), (1, 1)]
    if fast:
        near_keys = [swap(every_key, None, *f) for f in near_flips]
    step = forward(rows, None, True, query_halves, query_middle, [query_encoder])
    query_pooled = step[1]
    qkv, prob, row_scale, ctx, n1, r1, first, hid, slope, n2, r2 = step[2:]

    if fast:
        near_keys, query_pooled = lax.optimization_barrier((near_keys, query_pooled))
        every_key = jnp.concatenate([every_key, *near_keys], axis=0)
        every_key = jnp.concatenate([every_key] + [swap(every_key, None, 2 * k, 0) for k in range(1, 4)], axis=0)
    else:
        for flip in flips():
            every_key = jnp.concatenate([every_key, swap(every_key, None, *flip)], axis=0)
    place = dp * reps + rep
    matched = jnp.take(every_key, jnp.bitwise_xor(positive // crops, place) * crops + positive % crops, axis=0)
    matched = jnp.concatenate([matched, jnp.zeros((8 - crops, D), F32)], axis=0)
    first_peer = swap(first, None, 1, 0) if fast else None

    pooled_grad, lost = call(
        functools.partial(loss_kernel, last, crops, crop_all),
        "contrast",
        [((8, D), F32), ((8, 128), F32)],
        [VMEM] * 2,
        [query_pooled, matched, queue, inv],
        [VMEM] * 4,
        [],
        8,
    )

    def data_part(active, pooled, dy):
        wqkv, wout, wup, wdown = query_weights
        vec, grad_bup, ddown, dup, datt, dqkv, dx = data_backward(
            active, pooled, query_lengths, dy, gains, n2, r2, wdown, slope, wup, n1, r1, wout, qkv, prob, row_scale, wqkv
        )
        ddown_peer = swap(ddown, active, 1, 0) if fast else None
        return vec, grad_bup, ddown, ddown_peer, dup, datt, dqkv, dx

    def attention_part(active, vec, grad_bup, datt, dqkv, term):
        return attention_weights(active, query_halves, query_middle, ctx, datt, dqkv, (vec, grad_bup, term))

    def ffn_part(active, first_rows, ddown, ddown_peer, dup):
        _, _, wup, wdown = query_weights
        return ffn_weights(active, first_rows, first_peer, ddown, ddown_peer, hid, dup, wup, wdown, up_biases)

    def small_rows(vec, grad_bup, term):
        picked = [vec[k : k + 1] for k in VECTOR_ROWS]
        lost_row = jnp.concatenate([term[0:1]] * (D // 128), axis=1)
        return jnp.concatenate(picked + [grad_bup[0:1].reshape(FF // D, D), lost_row], axis=0)

    vec1, bup1, ddown, ddown_peer, dup, datt, dqkv, dmiddle = data_part(last, True, pooled_grad)
    dmiddle = relay(dmiddle, -1)
    lost_first = relay(lost, -1)
    if fast:
        datt = after(datt, dmiddle, lost_first, first_peer)
    ka1, sa1 = attention_part(last, vec1, bup1, datt, dqkv, lost)
    a1 = swap(sa1, last, 1, 0) if fast else sa1
    sf1, kf1 = ffn_part(last, after(first, sa1), ddown, ddown_peer, dup)
    f1 = swap(sf1, last, 0, 1) if fast else sf1
    if fast:
        s1 = half_sums(ka1, after(a1, sf1), last)
        b1 = swap(s1, last, 0, 1)
        dmiddle = after(dmiddle, f1, b1)
    vec0, bup0, ddown, ddown_peer, dup, datt, dqkv, dx = data_part(0, False, dmiddle)
    half = SLOTS // sections
    dx = dx.reshape(crops, SLOTS, D)
    dx_half = dx[:, half:]
    if fast:
        p1 = slot_sums(last, [kf1, after(f1, dx)], [ka1, a1, b1])
        z1 = far_z(p1, near_z(p1, last), last)
        datt = after(datt, *z1)
    ka0, sa0 = attention_part(0, vec0, bup0, datt, dqkv, lost_first)
    sf0, kf0 = ffn_part(0, after(first, sa0), ddown, ddown_peer, dup)

    if fast:
        a0 = swap(sa0, 0, 1, 0)
        f0 = swap(sf0, 0, 0, 1)
        s0 = half_sums(ka0, after(a0, kf0), 0)
        b0 = swap(s0, 0, 0, 1)
        p0 = slot_sums(0, [kf0, after(f0, s0)])
        near_f = near_z(p0, 0)
        q0 = slot_sums(0, [ka0, a0, after(b0, *p0)])
        near_a = near_z(q0, 0)
        g0 = far_z(p0, after(near_f, *q0), 0)
        h0 = far_z(q0, near_a, 0)
        summed = chip_totals(g0, h0, z1)
        grad_qkv, grad_out, grad_up, grad_down, bias, gain, up_part, query_part, loss_row = summed
        loss_row = loss_row[0]
        dx_half = after(dx_half, grad_down)
    else:
        grad_up, grad_down, grad_qkv, grad_out = [
            lax.psum_scatter(jnp.where(on_first, a, b).astype(F32), ("dp", "rep"), scatter_dimension=0, tiled=True)
            for a, b in zip([sf0, kf0, ka0, sa0], [sf1, kf1, ka1, sa1])
        ]
        small = jnp.where(on_first, small_rows(vec0, bup0, lost_first), small_rows(vec1, bup1, lost))
        for flip in flips():
            small = small + swap(small, None, *flip)
        width, up_width = D // (dps * reps), FF // (dps * reps)
        mine = lax.dynamic_slice(small[:8], (0, place * width), (8, width))
        bias, gain, query_part = mine[:5], mine[5:7], mine[7:]
        up_part = lax.dynamic_slice(small[8:12].reshape(1, FF), (0, place * up_width), (1, up_width))
        loss_row = small[12, :128]
    crops_grad = jnp.where(on_first, dx[:, :half], relay(dx_half, 1)).astype(F32)
    return (
        loss_row[:1],
        crops_grad,
        grad_qkv[None],
        grad_out[None],
        grad_up[None],
        grad_down[None],
        bias[None],
        gain[None],
        up_part,
        query_part,
    )


def solution(mesh):
    crop = P(("dp", "rep"), "section", None)
    per_crop = P(("dp", "rep"))
    layer3 = P("section", None, None)
    layer2 = P("section", None)
    placed = (
        (crop, crop, per_crop, per_crop, per_crop, P())
        + (layer3,) * 6
        + (layer2,) * 2
        + (layer3,) * 6
        + (layer2,)
    )
    shared3 = P("section", ("dp", "rep"), None)
    return jax.shard_map(
        body,
        mesh=mesh,
        in_specs=placed,
        out_specs=(
            P(),
            crop,
            shared3,
            shared3,
            shared3,
            shared3,
            P("section", None, ("dp", "rep")),
            P("section", None, ("dp", "rep")),
            P("section", ("dp", "rep")),
            P("section", ("dp", "rep")),
        ),
        check_vma=False,
    )
```

```python
import functools

import jax
import jax.numpy as jnp
from jax import lax
from jax.experimental import pallas as pl
from jax.experimental.pallas import tpu as pltpu
from jax.sharding import PartitionSpec as P

F32 = jnp.float32
BF = jnp.bfloat16
MASKED = -1e30
D = 768
FF = 3072
SLOTS = 256
PAIRS = 6
MIB = 2**20
SEMS = 112
ALPHA = 1.0


def dot(a, b):
    return lax.dot_general(a, b, (((1,), (0,)), ((), ())), preferred_element_type=F32)


def dot_nt(a, b):
    return lax.dot_general(a, b, (((1,), (1,)), ((), ())), preferred_element_type=F32)


def dot_tn(a, b):
    return lax.dot_general(a, b, (((0,), (0,)), ((), ())), preferred_element_type=F32)


def gelu_parts(x, want_slope):
    share = 0.5 + 0.5 * lax.erf(x * 0.7071067811865476)
    if not want_slope:
        return x * share, None
    return x * share, share + (0.3989422804014327 * x) * jnp.exp(-0.5 * (x * x))


def norm_parts(z):
    mean = jnp.mean(z, axis=-1, keepdims=True)
    c = z - mean
    var = jnp.mean(c * c, axis=-1, keepdims=True)
    r = lax.rsqrt(var + 1e-12)
    return c * r, r


def head_masks(scale):
    lane = lax.broadcasted_iota(jnp.int32, (1, 128), 1)
    low = jnp.where(lane < 64, scale, 0.0).astype(BF)
    high = jnp.where(lane < 64, 0.0, scale).astype(BF)
    return low, high


def stack_heads(pair, scale):
    low, high = head_masks(scale)
    return jnp.concatenate([pair * low, pair * high], axis=0)


def side_by_side(stacked):
    half = stacked.shape[0] // 2
    return jnp.concatenate([stacked[:half], stacked[half:]], axis=1)


class Copies:
    def __init__(self, sems):
        self.sems, self.used, self.open = sems, 0, []

    def make(self, src, dst):
        self.used += 1
        return pltpu.make_async_copy(src, dst, self.sems.at[self.used - 1])

    def fetch(self, src, dst):
        cp = self.make(src, dst)
        cp.start()
        return cp

    def pick(self, by_section, dst):
        if by_section[0] is by_section[1]:
            return self.fetch(by_section[0], dst)
        sem = self.sems.at[self.used]
        self.used += 1
        here = lax.axis_index("section")

        @pl.when(here == 0)
        def _():
            pltpu.make_async_copy(by_section[0], dst, sem).start()

        @pl.when(here != 0)
        def _():
            pltpu.make_async_copy(by_section[1], dst, sem).start()

        return pltpu.make_async_copy(by_section[0], dst, sem)

    def send(self, src, dst):
        self.open.append(self.fetch(src, dst))

    def drain(self):
        for cp in self.open:
            cp.wait()


def only_on(section, run):
    if section is None:
        run()
    else:
        pl.when(lax.axis_index("section") == section)(run)


VMEM = pl.BlockSpec(memory_space=pltpu.VMEM)
ANY = pl.BlockSpec(memory_space=pl.ANY)
SMEM = pl.BlockSpec(memory_space=pltpu.SMEM)
sd = jax.ShapeDtypeStruct


def call(kernel, name, outs, out_specs, ins, in_specs, scratch, micros, limit=56):
    return pl.pallas_call(
        kernel,
        out_shape=[sd(*o) for o in outs],
        in_specs=in_specs,
        out_specs=out_specs,
        scratch_shapes=[pltpu.VMEM(*s) for s in scratch] + [pltpu.SemaphoreType.DMA((SEMS,))],
        compiler_params=pltpu.CompilerParams(vmem_limit_bytes=limit * MIB),
        cost_estimate=pl.CostEstimate(flops=int(micros * ALPHA * 1.15e9), bytes_accessed=1000, transcendentals=0),
        name=name,
    )(*ins)


def saved_shapes(rows):
    crops = rows // SLOTS
    return [
        ((rows, 3 * D), BF),
        ((PAIRS * crops, 2 * SLOTS, SLOTS), BF),
        ((2 * SLOTS, 128), F32),
        ((rows, D), BF),
        ((rows, D), BF),
        ((rows, 128), F32),
        ((rows, D), BF),
        ((rows, FF), BF),
        ((rows, FF), BF),
        ((rows, D), BF),
        ((rows, 128), F32),
    ]


def fetch_rows(copies, refs, kinds, x):
    waits = []
    half = refs[0].shape[1] if "halves" in kinds else SLOTS // 2
    for c in range(x.shape[0] // SLOTS):
        for h in range(SLOTS // half):
            at = slice(SLOTS * c + half * h, SLOTS * c + half * (h + 1))
            options = []
            if "halves" in kinds:
                options.append(refs[h].at[c])
            if "whole" in kinds:
                options.append(refs[-1].at[at, :])
            waits.append(copies.pick((options[0], options[-1]), x.at[at, :]))
    return waits


def read_vectors(refs, key):
    if key:
        b, g, up = refs
        rows = b[0].astype(F32)
        rows = [rows[i : i + 1] for i in range(6)]
    else:
        b, g, up, q = refs
        rows = b[0].astype(F32)
        rows = [q[...].astype(F32)] + [rows[i : i + 1] for i in range(5)]
    gains = g[0].astype(F32)
    return rows + [gains[0:1], gains[1:2]], up[...].astype(F32)


def load_vectors(refs, kinds, vec, bup):
    sets = []
    for kind in kinds:
        n = 3 if kind == "key" else 4
        sets.append(read_vectors(refs[:n], kind == "key"))
        refs = refs[n:]
    here = lax.axis_index("section")
    for i in range(8):
        row = sets[0][0][i]
        if len(sets) == 2:
            row = jnp.where(here == 0, row, sets[1][0][i])
        vec[i : i + 1, :] = row
    up = sets[0][1]
    if len(sets) == 2:
        up = jnp.where(here == 0, up, sets[1][1])
    bup[...] = up


def forward_kernel(rows, active, save, x_kinds, sets, *refs):
    def run():
        forward_body(rows, save, x_kinds, sets, *refs)

    only_on(active, run)


def forward_body(rows, save, x_kinds, sets, *refs):
    crops = rows // SLOTS
    lens_refs, refs = refs[: len(sets)], refs[len(sets) :]
    here = lax.axis_index("section")
    if len(sets) == 2:
        lens = [jnp.where(here == 0, lens_refs[0][c], lens_refs[1][c]) for c in range(crops)]
    else:
        lens = [lens_refs[0][c] for c in range(crops)]
    n_x = (2 if "halves" in x_kinds else 0) + (1 if "whole" in x_kinds else 0)
    x_refs, refs = refs[:n_x], refs[n_x:]
    w_refs, refs = refs[: 4 * len(sets)], refs[4 * len(sets) :]
    n_v = sum(3 if k == "key" else 4 for k in sets)
    v_refs, refs = refs[:n_v], refs[n_v:]
    y_ref, pool_ref = refs[:2]
    refs = refs[2:]
    if save:
        (qkv_o, prob_o, inv_o, ctx_o, n1_o, r1_o, first_o, hid_o, slope_o, n2_o, r2_o) = refs[:11]
        refs = refs[11:]
    (x, wqkv, wout, wup, wdown, ctx, zbuf, first, hid, vec, bup) = refs[:11]
    refs = refs[11:]
    if save:
        (qkv, prob, inv_all, n1, r1, slope, n2, r2) = refs[:8]
        refs = refs[8:]
        inv_all[...] = jnp.zeros_like(inv_all)
    copies = Copies(refs[0])
    got_x = fetch_rows(copies, x_refs, x_kinds, x)
    pairs = [(w_refs[i], w_refs[4 + i] if len(sets) == 2 else w_refs[i]) for i in range(4)]
    got_qkv = copies.pick(pairs[0], wqkv)
    load_vectors(v_refs, sets, vec, bup)
    for cp in got_x:
        cp.wait()
    got_qkv.wait()
    got_out = copies.pick(pairs[1], wout)
    got_up = copies.pick(pairs[2], wup)
    got_down = copies.pick(pairs[3], wdown)
    keycol = lax.broadcasted_iota(jnp.int32, (1, SLOTS), 1)
    lane = lax.broadcasted_iota(jnp.int32, (1, 128), 1)
    gain1, gain2 = vec[6:7], vec[7:8]

    def heads(i, carry):
        thirds = []
        for j in range(3):
            cols = pl.ds(pl.multiple_of(D * j + 256 * i, 256), 256)
            part = dot(x[...], wqkv[:, cols])
            if j != 1:
                at = pl.ds(pl.multiple_of(256 * i, 256), 256)
                part = part + vec[j // 2 : j // 2 + 1, at]
            part = part.astype(BF)
            if save:
                qkv[:, cols] = part
            thirds.append(part)
        for c in range(crops):
            crop = slice(SLOTS * c, SLOTS * (c + 1))
            for pr in range(2):
                qp, kp, vp = [t[crop, 128 * pr : 128 * (pr + 1)] for t in thirds]
                scores = jnp.where(keycol < lens[c], dot_nt(stack_heads(qp, 0.125), kp), MASKED)
                e = jnp.exp(scores - jnp.max(scores, axis=-1, keepdims=True))
                inv = pl.reciprocal(jnp.sum(e, axis=-1, keepdims=True))
                e = e.astype(BF)
                if save:
                    unit = PAIRS * c + 2 * i + pr
                    prob[unit] = e
                    inv_all[...] = jnp.where(lane == unit, inv, inv_all[...])
                at = pl.ds(pl.multiple_of(256 * i + 128 * pr, 128), 128)
                both = dot(e, vp) * inv
                ctx[crop, at] = jnp.where(lane < 64, both[:SLOTS], both[SLOTS:]).astype(BF)
        return carry

    lax.fori_loop(0, 3, heads, 0)
    if save:
        copies.send(qkv, qkv_o)
        copies.send(prob, prob_o)
        copies.send(inv_all, inv_o)
        copies.send(ctx, ctx_o)
    got_out.wait()
    for j in range(3):
        cols = slice(256 * j, 256 * (j + 1))
        zbuf[:, cols] = x[:, cols].astype(F32) + dot(ctx[...], wout[:, cols]) + vec[2:3, cols]
    block = 64
    steps = rows // block

    def first_norm(i, carry):
        at = pl.ds(pl.multiple_of(i * block, block), block)
        n, r = norm_parts(zbuf[at, :])
        f = (n * gain1 + vec[3:4]).astype(BF)
        first[at, :] = f
        zbuf[at, :] = f.astype(F32) + vec[4:5]
        if save:
            n1[at, :] = n.astype(BF)
            r1[at, :] = jnp.broadcast_to(r, (block, 128))
        return carry

    lax.fori_loop(0, steps, first_norm, 0, unroll=True)
    if save:
        copies.send(n1, n1_o)
        copies.send(r1, r1_o)
        copies.send(first, first_o)
    got_up.wait()
    got_down.wait()

    def down_part(k):
        cols = slice(512 * k, 512 * (k + 1))
        zbuf[...] += dot(hid[:, cols], wdown[cols, :])

    for i in range(12):
        cols = slice(256 * i, 256 * (i + 1))
        g, slope_part = gelu_parts(dot(first[...], wup[:, cols]) + bup[:, cols], save)
        hid[:, cols] = g.astype(BF)
        if save:
            slope[:, cols] = slope_part.astype(BF)
        if i % 2 and i > 2:
            down_part(i // 2 - 1)
    if save:
        copies.send(hid, hid_o)
        copies.send(slope, slope_o)
    down_part(5)
    pool_ref[...] = jnp.zeros_like(pool_ref)
    per_crop = SLOTS // block
    for i in range(steps):
        at = slice(i * block, (i + 1) * block)
        n, r = norm_parts(zbuf[at, :])
        f = n * gain2 + vec[5:6]
        y_ref[at, :] = f.astype(BF)
        if save:
            n2[at, :] = n.astype(BF)
            r2[at, :] = jnp.broadcast_to(r, (block, 128))
        c = i // per_crop
        token = lax.broadcasted_iota(jnp.int32, (block, 1), 0) + (i % per_crop) * block
        part = jnp.sum(jnp.where(token < lens[c], f, 0.0), axis=0, keepdims=True)
        pool_ref[c : c + 1, :] += part / lens[c].astype(F32)
    pooled = pool_ref[:crops]
    pool_ref[crops : 2 * crops] = pooled * lax.rsqrt(jnp.sum(pooled * pooled, axis=-1, keepdims=True) + 1e-6)
    if save:
        copies.send(n2, n2_o)
        copies.send(r2, r2_o)
    copies.drain()


def forward(rows, active, save, halves, whole, encoders):
    x_kinds = (("halves",) if halves else ()) + (("whole",) if whole is not None else ())
    xs = list(halves or ()) + ([whole] if whole is not None else [])
    lens = [e[1] for e in encoders]
    weights = [w for e in encoders for w in e[2]]
    vectors = [v for e in encoders for v in e[3]]
    outs = [((rows, D), BF), ((8, D), F32)]
    out_specs = [VMEM, VMEM]
    scratch = [
        ((rows, D), BF),
        ((D, 3 * D), BF),
        ((D, D), BF),
        ((D, FF), BF),
        ((FF, D), BF),
        ((rows, D), BF),
        ((rows, D), F32),
        ((rows, D), BF),
        ((rows, FF), BF),
        ((8, D), F32),
        ((1, FF), F32),
    ]
    if save:
        kept = saved_shapes(rows)
        outs += kept
        out_specs += [ANY] * len(kept)
        scratch += [kept[i] for i in (0, 1, 2, 4, 5, 8, 9, 10)]
    return call(
        functools.partial(forward_kernel, rows, active, save, x_kinds, [e[0] for e in encoders]),
        "layer_forward",
        outs,
        out_specs,
        [*lens, *xs, *weights, *vectors],
        [SMEM] * len(lens) + [ANY] * (len(xs) + len(weights)) + [VMEM] * len(vectors),
        scratch,
        20 if save else 18,
    )


def split3(v):
    hi = v.astype(BF)
    rest = v - hi.astype(F32)
    mid = rest.astype(BF)
    lo = (rest - mid.astype(F32)).astype(BF)
    return hi, mid, lo


def stack3(v):
    parts = split3(v)
    return jnp.concatenate(list(parts) + [jnp.zeros_like(parts[0])] * 5, axis=0)


def unstack3(rows, n):
    return rows[:n] + rows[n : 2 * n] + rows[2 * n : 3 * n]


def queue_norm_kernel(active, queue_h, inv_ref, queue, sems):
    def run():
        Copies(sems).fetch(queue_h, queue).wait()

        def step(i, carry):
            at = pl.ds(pl.multiple_of(i * 512, 512), 512)
            v = queue[at, :].astype(F32)
            sq = v * v
            hi = sq.astype(BF)
            lo = (sq - hi.astype(F32)).astype(BF)
            ones = jnp.ones((8, D), BF)
            total = dot_nt(ones, hi) + dot_nt(ones, lo)
            inv_ref[:, at] = lax.rsqrt(total + 1e-6)
            return carry

        lax.fori_loop(0, queue.shape[0] // 512, step, 0)

    only_on(active, run)


def loss_kernel(active, crops, count, pooled, matched, queue, inv, grad_ref, loss_ref, sems):
    def run():
        v = pooled[:crops]
        r = lax.rsqrt(jnp.sum(v * v, axis=-1, keepdims=True) + 1e-6)
        u = v * r
        k = matched[:crops]
        near = jnp.sum(u * k, axis=-1, keepdims=True) * 20.0
        inv_row = inv[0:1]
        far = unstack3(dot_nt(stack3(u), queue[...]), crops) * (inv_row * 20.0)
        top = jnp.maximum(near, jnp.max(far, axis=-1, keepdims=True))
        e_near = jnp.exp(near - top)
        e_far = jnp.exp(far - top)
        total = e_near + jnp.sum(e_far, axis=-1, keepdims=True)
        share = 20.0 / (total * count)
        d_u = unstack3(dot(stack3(e_far * inv_row * share), queue[...]), crops)
        d_u = d_u + (e_near - total) * share * k
        grad = r * (d_u - u * jnp.sum(u * d_u, axis=-1, keepdims=True))
        grad_ref[...] = jnp.zeros_like(grad_ref)
        grad_ref[:crops] = grad
        lost = jnp.sum(top + jnp.log(total) - near, axis=0, keepdims=True) / count
        loss_ref[...] = jnp.broadcast_to(lost, loss_ref.shape)

    only_on(active, run)


def norm_back(dy, gain, n, r):
    dn = dy * gain
    return r * (dn - jnp.mean(dn, axis=-1, keepdims=True) - n * jnp.mean(dn * n, axis=-1, keepdims=True))


def column_sum(v):
    return jnp.sum(v, axis=0, keepdims=True)


def fast_mesh():
    return lax.axis_size("dp") == 8 and lax.axis_size("rep") == 2


def place_bits():
    dp, rep = lax.axis_index("dp"), lax.axis_index("rep")
    return dp // 2, dp % 2, rep


CHUNK = 512


def data_backward_kernel(rows, active, pooled, lens, dy, gains, *refs):
    def run():
        n2_h, r2_h, wdown_h, slope_h, wup_h, n1_h, r1_h, wout_h, qkv_h, prob_h, inv_h, wqkv_h = refs[:12]
        vec, bup, ddown_o, dup_o, datt_o, dqkv_o, dx_o = refs[12:19]
        n2, r2, wdown, slope, wup, n1, r1, wout, qkv, prob, inv, wqkv = refs[19:31]
        acc, ddown, dup, datt, dqkv, dx, sems = refs[31:]
        copies = Copies(sems)
        got_n2, got_r2 = copies.fetch(n2_h, n2), copies.fetch(r2_h, r2)
        got = []
        for i in range(FF // CHUNK):
            cols = slice(CHUNK * i, CHUNK * (i + 1))
            got.append(
                [
                    copies.fetch(wdown_h.at[cols, :], wdown.at[cols, :]),
                    copies.fetch(slope_h.at[:, cols], slope.at[:, cols]),
                    copies.fetch(wup_h.at[:, cols], wup.at[:, cols]),
                ]
            )
        got_n1 = [copies.fetch(n1_h, n1), copies.fetch(r1_h, r1), copies.fetch(wout_h, wout)]
        got_qkv = [copies.fetch(qkv_h, qkv), copies.fetch(prob_h, prob), copies.fetch(inv_h, inv)]
        got_w = copies.fetch(wqkv_h, wqkv)
        vec[...] = jnp.zeros_like(vec)
        gain1, gain2 = gains[0].astype(F32)[0:1], gains[0].astype(F32)[1:2]
        block = 64
        per_crop = SLOTS // block
        got_n2.wait()
        got_r2.wait()
        for i in range(rows // block):
            at = slice(block * i, block * (i + 1))
            c = i // per_crop
            if pooled:
                token = lax.broadcasted_iota(jnp.int32, (block, 1), 0) + (i % per_crop) * block
                grow = jnp.where(token < lens[c], 1.0 / lens[c].astype(F32), 0.0) * dy[c : c + 1]
            else:
                grow = dy[at].astype(F32)
            n = n2[at].astype(F32)
            ds = norm_back(grow, gain2, n, r2[at, 0:1])
            low_ds = ds.astype(BF)
            acc[at] = ds
            ddown[at] = low_ds
            vec[0:1] += column_sum(grow * n)
            vec[1:2] += column_sum(grow)
            vec[2:3] += column_sum(low_ds.astype(F32))
        copies.send(ddown, ddown_o)
        for i in range(FF // CHUNK):
            cols = slice(CHUNK * i, CHUNK * (i + 1))
            for cp in got[i]:
                cp.wait()
            up = (dot_nt(ddown[...], wdown[cols, :]) * slope[:, cols].astype(F32)).astype(BF)
            dup[:, cols] = up
            copies.send(dup.at[:, cols], dup_o.at[:, cols])
            bup[:, cols] = jnp.broadcast_to(column_sum(up.astype(F32)), (8, CHUNK))
            acc[...] += dot_nt(up, wup[:, cols])
        for cp in got_n1:
            cp.wait()
        for i in range(rows // block):
            at = slice(block * i, block * (i + 1))
            n = n1[at].astype(F32)
            dfirst = acc[at]
            ds = norm_back(dfirst, gain1, n, r1[at, 0:1])
            low_ds = ds.astype(BF)
            acc[at] = ds
            datt[at] = low_ds
            vec[3:4] += column_sum(dfirst * n)
            vec[4:5] += column_sum(dfirst)
            vec[5:6] += column_sum(low_ds.astype(F32))
        copies.send(datt, datt_o)
        dctx = dot_nt(datt[...], wout[...]).astype(BF)
        for cp in got_qkv:
            cp.wait()
        for c in range(rows // SLOTS):
            crop = slice(SLOTS * c, SLOTS * (c + 1))
            for pr in range(PAIRS):
                cols = [slice(D * j + 128 * pr, D * j + 128 * (pr + 1)) for j in range(3)]
                unit = PAIRS * c + pr
                qp, kp, vp = [qkv[crop, t] for t in cols]
                dcs = stack_heads(dctx[crop, 128 * pr : 128 * (pr + 1)], 1.0)
                scale = inv[:, unit : unit + 1]
                e = prob[unit]
                pf = e.astype(F32) * scale
                weighted = pf * dot_nt(dcs, vp)
                ds = (weighted - pf * jnp.sum(weighted, axis=-1, keepdims=True)).astype(BF)
                dqkv[crop, cols[0]] = dot(side_by_side(ds), stack_heads(kp, 0.125)).astype(BF)
                dqkv[crop, cols[1]] = dot_tn(ds, stack_heads(qp, 0.125)).astype(BF)
                dqkv[crop, cols[2]] = dot_tn(e, (dcs * scale).astype(BF)).astype(BF)
        got_w.wait()
        for j in range(3):
            cols = slice(256 * j, 256 * (j + 1))
            dx[:, cols] = (dot_nt(dqkv[...], wqkv[cols, :]) + acc[:, cols]).astype(BF)
        copies.send(dx, dx_o)
        copies.send(dqkv, dqkv_o)
        vec[6:7] = column_sum(dqkv[:, :D].astype(F32))
        vec[7:8] = column_sum(dqkv[:, 2 * D :].astype(F32))
        copies.drain()

    only_on(active, run)


def data_backward(active, pooled, lens, dy, gains, n2, r2, wdown, slope, wup, n1, r1, wout, qkv, prob, inv, wqkv):
    rows = n1.shape[0]
    held = [n2, r2, wdown, slope, wup, n1, r1, wout, qkv, prob, inv, wqkv]
    wide_rows = ((rows, D), BF)
    return call(
        functools.partial(data_backward_kernel, rows, active, pooled),
        "data_backward",
        [((8, D), F32), ((8, FF), F32), wide_rows, ((rows, FF), BF), wide_rows, ((rows, 3 * D), BF), wide_rows],
        [VMEM] * 2 + [ANY] * 5,
        [lens, dy, gains, *held],
        [SMEM, VMEM, VMEM] + [ANY] * len(held),
        [(h.shape, h.dtype) for h in held]
        + [((rows, D), F32), wide_rows, ((rows, FF), BF), wide_rows, ((rows, 3 * D), BF), wide_rows],
        26,
    )


def ffn_weights_kernel(rows, active, fast, *refs):
    def run():
        if fast:
            first_h, first_p, ddown_h, ddown_p, hid_h, dup_h, wup_h, wdown_h, bup_h = refs[:9]
            up_keep, up_send, down_keep, down_send = refs[9:13]
            first, ddown, hid, dup, gup, gdown, wup, wdown, bup, sems = refs[13:]
        else:
            first_h, ddown_h, hid_h, dup_h, up_o, down_o = refs[:6]
            first, ddown, hid, dup, gup, gdown, sems = refs[6:]
        copies = Copies(sems)
        own = slice(0, rows)
        got = [copies.fetch(first_h, first.at[own, :]), copies.fetch(ddown_h, ddown.at[own, :])]
        z, x, y = place_bits()
        parts = 4 if fast else FF // 384
        if fast:
            peer = slice(rows, 2 * rows)
            got += [copies.fetch(first_p, first.at[peer, :]), copies.fetch(ddown_p, ddown.at[peer, :])]
            got.append(copies.fetch(bup_h, bup))
        order = (1, 3, 0, 2) if fast else range(parts)
        blocks = {}
        for i in order:
            here = slice(384 * i, 384 * (i + 1))
            there = pl.ds(pl.multiple_of(768 * jnp.bitwise_xor(z, i) + 384 * x, 128), 384) if fast else here
            block = [
                copies.fetch(hid_h.at[:, there], hid.at[own, here]),
                copies.fetch(dup_h.at[:, there], dup.at[own, here]),
            ]
            if fast:
                block.append(copies.fetch(wup_h.at[:, there], wup.at[:, here]))
                block.append(copies.fetch(wdown_h.at[there, :], wdown.at[here, :]))
            blocks[i] = block
        for cp in got:
            cp.wait()
        for i in order:
            here = slice(384 * i, 384 * (i + 1))
            for cp in blocks[i]:
                cp.wait()
            if fast:
                zz = jnp.bitwise_xor(z, i)
                bias = bup[:, pl.ds(pl.multiple_of(768 * zz + 384 * x, 128), 384)].astype(F32)
                g, slope = gelu_parts(dot(first[peer, :], wup[:, here]) + bias, True)
                hid[peer, here] = g.astype(BF)
                dup[peer, here] = (dot_nt(ddown[peer, :], wdown[here, :]) * slope).astype(BF)
            gdown[here, :] = dot_tn(hid[:, here], ddown[...]).astype(BF)
            if fast:
                out = (down_send if i % 2 else down_keep).at[i // 2]
                for jy in range(2):
                    at = pl.ds(pl.multiple_of(384 * i + 192 * jnp.bitwise_xor(y, jy), 64), 192)
                    copies.send(gdown.at[at, :], out.at[192 * jy : 192 * (jy + 1), :])
            gup[:, here] = dot_tn(first[...], dup[:, here]).astype(BF)
            if fast:
                to_cols = pl.ds(pl.multiple_of(384 * (zz % 2), 128), 384)
                for jy, out in ((1, up_send), (0, up_keep)):
                    for jz in range(4):
                        for jx in range(2):
                            owner = (jnp.bitwise_xor(z, jz) * 2 + jnp.bitwise_xor(x, jx)) * 2 + jnp.bitwise_xor(y, jy)
                            at = pl.ds(pl.multiple_of(48 * owner, 16), 48)
                            to = pl.ds(pl.multiple_of(96 * jx + 48 * (zz // 2), 16), 48)
                            copies.send(gup.at[at, here], out.at[jz, to, to_cols])
        if not fast:
            copies.send(gup, up_o)
            copies.send(gdown, down_o)
        copies.drain()

    only_on(active, run)


def ffn_weights(active, first, first_peer, ddown, ddown_peer, hid, dup, wup, wdown, bup):
    rows = first.shape[0]
    fast = fast_mesh()
    if fast:
        ins = [first, first_peer, ddown, ddown_peer, hid, dup, wup, wdown, bup]
        outs = [((4, 192, D), BF)] * 2 + [((2, 384, D), BF)] * 2
        tokens, units = 2 * rows, FF // 2
        extra = [((D, units), BF), ((units, D), BF), ((1, FF), BF)]
    else:
        ins = [first, ddown, hid, dup]
        outs = [((D, FF), BF), ((FF, D), BF)]
        tokens, units, extra = rows, FF, []
    return call(
        functools.partial(ffn_weights_kernel, rows, active, fast),
        "ffn_weights",
        outs,
        [ANY] * len(outs),
        ins,
        [ANY] * len(ins),
        [
            ((tokens, D), BF),
            ((tokens, D), BF),
            ((tokens, units), BF),
            ((tokens, units), BF),
            ((D, units), BF),
            ((units, D), BF),
        ]
        + extra,
        15,
    )


VECTOR_ROWS = (7, 5, 4, 2, 1, 3, 0, 6)


def attention_weights_kernel(rows, active, fast, x_kinds, *refs):
    def run():
        n_x = len(x_kinds) + 1
        x_refs = refs[:n_x]
        if fast:
            vec, bup, lost, *refs_ = refs[n_x:]
            ctx_h, datt_h, dqkv_h, out_a, out_b, x, ctx, datt, dqkv, gqkv, gout, tail, sems = refs_
        else:
            ctx_h, datt_h, dqkv_h, out_a, out_b, x, ctx, datt, dqkv, gqkv, gout, sems = refs[n_x:]
        copies = Copies(sems)
        got = [copies.fetch(ctx_h, ctx), copies.fetch(datt_h, datt)]
        got_x = fetch_rows(copies, x_refs, x_kinds, x)
        got_x.append(copies.fetch(dqkv_h, dqkv))
        if fast:
            z, xx, y = place_bits()
            small = jnp.concatenate([vec[k : k + 1] for k in VECTOR_ROWS], axis=0)
            row = lax.broadcasted_iota(jnp.int32, (8, D), 0)
            lane = lax.broadcasted_iota(jnp.int32, (8, D), 1) - 3 * ((z * 2 + xx) * 2 + y)
            terms = [jnp.broadcast_to(t.astype(F32)[0:1, 0:1], (8, D)) for t in split3(lost[...])]
            lost_row = sum(jnp.where(lane == i, t, 0.0) for i, t in enumerate(terms))

        def ship(part, to):
            for j in range(15, -1, -1):
                jx, jy, jz = j // 8, j // 4 % 2, j % 4
                owner = (jnp.bitwise_xor(z, jz) * 2 + jnp.bitwise_xor(xx, jx)) * 2 + jnp.bitwise_xor(y, jy)
                at = pl.ds(pl.multiple_of(48 * owner, 16), 48)
                copies.send(part.at[at, :], (out_b if jx else out_a).at[j % 8, to : to + 48, :])

        for cp in got:
            cp.wait()
        gout[...] = dot_tn(ctx[...], datt[...]).astype(BF)
        if fast:
            ship(gout, 144)
            for j in range(16):
                jx, jy, jz = j // 8, j // 4 % 2, j % 4
                owner = (jnp.bitwise_xor(z, jz) * 2 + jnp.bitwise_xor(xx, jx)) * 2 + jnp.bitwise_xor(y, jy)
                head = pltpu.roll(small, D - 48 * owner, 1)
                ups = pltpu.roll(bup[...], FF - 192 * owner, 1)[:, :D]
                other = jnp.where(row == 0, ups, jnp.where(row == 1, lost_row, 0.0))
                tail[j] = jnp.concatenate([head, other], axis=0).astype(BF)
                copies.send(tail.at[j], (out_b if jx else out_a).at[j % 8, 192:208, :])
        for cp in got_x:
            cp.wait()
        for t in range(3):
            for k in range(2):
                cols = slice(D * t + 384 * k, D * t + 384 * (k + 1))
                gqkv[:, cols] = dot_tn(x[...], dqkv[:, cols]).astype(BF)
            if fast:
                ship(gqkv.at[:, slice(D * t, D * (t + 1))], 48 * t)
        if not fast:
            copies.send(gqkv, out_a)
            copies.send(gout, out_b)
        copies.drain()

    only_on(active, run)


def attention_weights(active, halves, whole, ctx, datt, dqkv, small):
    rows = ctx.shape[0]
    fast = fast_mesh()
    x_kinds = ("halves", "whole")
    outs = [((8, 208, D), BF)] * 2 if fast else [((D, 3 * D), BF), ((D, D), BF)]
    ins = [*halves, whole, *(small if fast else ()), ctx, datt, dqkv]
    in_specs = [ANY] * 3 + [VMEM] * (3 if fast else 0) + [ANY] * 3
    return call(
        functools.partial(attention_weights_kernel, rows, active, fast, x_kinds),
        "attention_weights",
        outs,
        [ANY] * 2,
        ins,
        in_specs,
        [((rows, D), BF)] * 3
        + [((rows, 3 * D), BF), ((D, 3 * D), BF), ((D, D), BF)]
        + ([((16, 16, D), BF)] if fast else []),
        8,
    )


AXES = ("section", "dp", "rep")


def swap(block, section, dp_flip, rep_flip):
    dps, reps = lax.axis_size("dp"), lax.axis_size("rep")
    sections = range(lax.axis_size("section")) if section is None else [section]
    route = [
        ((s * dps + d) * reps + r, (s * dps + (d ^ dp_flip)) * reps + (r ^ rep_flip))
        for s in sections
        for d in range(dps)
        for r in range(reps)
    ]
    return lax.ppermute(block, AXES, route)


def flips():
    out, bit = [], 1
    while bit < lax.axis_size("rep"):
        out.append((0, bit))
        bit *= 2
    bit = 1
    while bit < lax.axis_size("dp"):
        out.append((bit, 0))
        bit *= 2
    return out


def add_rows(pieces, dst, at, count):
    def step(i, carry):
        here = pl.ds(pl.multiple_of(i * 16, 16), 16)
        total = pieces[0][here, :].astype(F32)
        for p in pieces[1:]:
            total = total + p[here, :].astype(F32)
        dst[pl.ds(pl.multiple_of(at + i * 16, 16), 16), :] = total.astype(dst.dtype)
        return carry

    lax.fori_loop(0, count // 16, step, 0, unroll=2 if count % 32 == 0 else 1)


def half_sums_kernel(active, rows, kept, received, near, far, held, made, sems):
    def run():
        copies = Copies(sems)
        order = (4, 5, 6, 7, 0, 1, 2, 3)
        got = {i: copies.fetch(kept.at[i], held.at[i]) for i in order}
        for i in order:
            got[i].wait()
            add_rows([held.at[i], received.at[i]], made.at[i], 0, rows)
            copies.send(made.at[i], (far if i > 3 else near).at[i % 4])
        copies.drain()

    only_on(active, run)


def half_sums(kept, received, section):
    shape = kept.shape[1:]
    return call(
        functools.partial(half_sums_kernel, section, shape[0]),
        "half_sums",
        [((4, *shape), BF)] * 2,
        [ANY] * 2,
        [kept, received],
        [ANY, VMEM],
        [((8, *shape), BF)] * 2,
        4,
        24,
    )


def slot_sums_kernel(active, counts, sizes, *refs):
    def run():
        groups, at = [], 0
        for n in counts:
            groups.append(refs[at : at + n])
            at += n
        own_o, kept_o, send_o = refs[at : at + 3]
        helds = refs[at + 3 : at + 3 + len(counts)]
        own, made, sems = refs[-3:]
        copies = Copies(sems)
        order = (1, 3, 2, 0)
        got = {k: [copies.fetch(g[0].at[k], h.at[k]) for g, h in zip(groups, helds)] for k in order}
        for k, out in zip(order, (send_o.at[0], send_o.at[1], kept_o, own_o)):
            to, base = made.at[k - 1] if k else own, 0
            for g, h, cp, size in zip(groups, helds, got[k], sizes):
                cp.wait()
                add_rows([h.at[k]] + [r.at[k] for r in g[1:]], to, base, size)
                base += size
            copies.send(to, out)
        copies.drain()

    only_on(active, run)


def slot_sums(section, *groups):
    sizes = [g[0].shape[1] for g in groups]
    shape = (sum(sizes), D)
    return call(
        functools.partial(slot_sums_kernel, section, [len(g) for g in groups], sizes),
        "slot_sums",
        [(shape, F32), (shape, BF), ((2, *shape), BF)],
        [ANY] * 3,
        [t for g in groups for t in g],
        [spec for g in groups for spec in [ANY] + [VMEM] * (len(g) - 1)],
        [((4, size, D), BF) for size in sizes] + [(shape, F32), ((3, *shape), BF)],
        3 * len(groups),
        24,
    )


def second_sum_kernel(active, rows, kept, received, out, held, made, sems):
    def run():
        copies = Copies(sems)
        copies.fetch(kept if len(kept.shape) == 2 else kept.at[1], held).wait()
        add_rows([held, received.at[1]], made, 0, rows)
        copies.send(made, out)
        copies.drain()

    only_on(active, run)


def second_sum(section, kept, received):
    held = (kept.shape[-2:], BF)
    return call(
        functools.partial(second_sum_kernel, section, kept.shape[-2]),
        "second_sum",
        [held],
        [ANY],
        [kept, received],
        [ANY, VMEM],
        [held, held],
        2,
        16,
    )[0]


def third_sum_kernel(active, kept, near, far, own_o, send_o, held, own, made, sems):
    def run():
        copies = Copies(sems)
        copies.fetch(kept.at[0], held).wait()
        first, second = pl.ds(0, 192), pl.ds(192, 192)
        add_rows([held.at[second, :], near.at[0, second, :], far.at[second, :]], made, 0, 192)
        copies.send(made, send_o)
        add_rows([held.at[first, :], near.at[0, first, :], far.at[first, :]], own, 0, 192)
        copies.send(own, own_o)
        copies.drain()

    only_on(active, run)


def third_sum(section, kept, near, far):
    return call(
        functools.partial(third_sum_kernel, section),
        "third_sum",
        [((192, D), F32), ((192, D), BF)],
        [ANY] * 2,
        [kept, near, far],
        [ANY, VMEM, VMEM],
        [((384, D), BF), ((192, D), F32), ((192, D), BF)],
        2,
        16,
    )


def last_section_kernel(active, own_h, near, far, down_h, down_far, sums_o, down_o, own, down, total, down_total, sems):
    def run():
        copies = Copies(sems)
        got = [copies.fetch(own_h, own), copies.fetch(down_h, down)]
        for cp in got:
            cp.wait()
        add_rows([own, near.at[0], far], total, 0, 400)
        copies.send(total, sums_o)
        add_rows([down, down_far], down_total, 0, 192)
        copies.send(down_total, down_o)
        copies.drain()

    only_on(active, run)


def last_section(section, own, near, far, down, down_far):
    shapes = [((400, D), F32), ((192, D), F32)]
    return call(
        functools.partial(last_section_kernel, section),
        "last_section_sums",
        shapes,
        [ANY] * 2,
        [own, near, far, down, down_far],
        [ANY, VMEM, VMEM, ANY, VMEM],
        shapes * 2,
        3,
        20,
    )


def add_terms(copies, first, done, own, total, base=0):
    count = own.shape[0]
    here = lax.axis_index("section")

    @pl.when(here == 0)
    def _():
        copies.fetch(first[0], own).wait()
        add_rows([own, *first[1:]], total, 0, count)

    @pl.when(here != 0)
    def _():
        copies.fetch(done.at[pl.ds(base, count), :], total).wait()


def up_total_kernel(own_h, near, far, done, own_o, peer_o, own, total, sems):
    add_terms(Copies(sems), (own_h, near.at[0], far), done, own, total)
    own_o[...] = total[0:96, :]
    peer_o[...] = total[96:192, :].astype(BF)


def last_totals_kernel(own_h, near, far, done, down_h, down_far, down_done, up_own, up_peer, *refs):
    qkv_o, out_o, up_o, down_o, bias_o, gain_o, query_o, up_bias_o, loss_o = refs[:9]
    own, total, down, sems = refs[9:]
    copies = Copies(sems)
    x = lax.axis_index("dp") % 2
    for c in range(2):
        for k in range(2):
            cols = slice(384 * k, 384 * (k + 1))
            at = 768 * (2 * c + k)
            here, there = pl.multiple_of(at + 384 * x, 128), pl.multiple_of(at + 384 * (1 - x), 128)
            up_o[:, pl.ds(here, 384)] = up_own[48 * c : 48 * (c + 1), cols]
            up_o[:, pl.ds(there, 384)] = up_peer[48 * c : 48 * (c + 1), cols].astype(F32)
    add_terms(copies, (down_h, down_far), down_done, down, down_o)
    add_terms(copies, (own_h, near.at[0], far), done, own, total, 192)
    for t in range(3):
        qkv_o[:, D * t : D * (t + 1)] = total[48 * t : 48 * (t + 1), :]
    out_o[...] = total[144:192, :]
    bias_o[...] = total[192:197, :48]
    gain_o[...] = total[197:199, :48]
    query_o[...] = total[199:200, :48]
    up_bias_o[...] = total[200:201, :192]
    loss_o[...] = jnp.broadcast_to(jnp.sum(total[201:202, :], axis=-1, keepdims=True), loss_o.shape)


def after(value, *others):
    return lax.optimization_barrier((value, others))[0]


def near_z(block, section):
    return swap(block, section, 2, 0)


def far_z(block, section):
    return swap(block, section, 4, 0)


def chip_totals(up, attention, down, sums_last, down_last):
    own, peer = call(
        up_total_kernel,
        "up_total",
        [((96, D), F32), ((96, D), BF)],
        [VMEM] * 2,
        [*up, sums_last],
        [ANY, VMEM, VMEM, ANY],
        [((192, D), F32)] * 2,
        2,
        16,
    )
    peer = swap(peer, None, 1, 0)
    outs = [(48, 3 * D), (48, D), (48, FF), (192, D), (5, 48), (2, 48), (1, 48), (1, 192), (8, 128)]
    return call(
        last_totals_kernel,
        "last_totals",
        [(shape, F32) for shape in outs],
        [VMEM] * len(outs),
        [*attention, sums_last, *down, down_last, own, peer],
        [ANY, VMEM, VMEM, ANY, ANY, VMEM, ANY, VMEM, VMEM],
        [((208, D), F32)] * 2 + [((192, D), F32)],
        4,
        24,
    )


def body(
    query_crops,
    key_crops,
    query_lengths,
    key_lengths,
    positive,
    queue,
    qkv_weight,
    out_weight,
    up_weight,
    down_weight,
    biases,
    gains,
    up_biases,
    query_bias,
    key_qkv_weight,
    key_out_weight,
    key_up_weight,
    key_down_weight,
    key_biases,
    key_gains,
    key_up_biases,
):
    crops = query_crops.shape[0]
    rows = crops * SLOTS
    sections, dps, reps = [lax.axis_size(a) for a in AXES]
    fast = fast_mesh()
    crop_all = crops * dps * reps
    on_first = lax.axis_index("section") == 0
    dp, rep = lax.axis_index("dp"), lax.axis_index("rep")
    last = sections - 1

    def relay(block, distance):
        return lax.ppermute(block, "section", [(0, 1)] if distance > 0 else [(1, 0)])

    key_half, query_half = lax.optimization_barrier((relay(key_crops, -1), relay(query_crops, -1)))
    key_halves = (key_crops, key_half)
    query_halves = (query_crops, query_half)
    query_weights = [w[0] for w in (qkv_weight, out_weight, up_weight, down_weight)]
    key_weights = [w[0] for w in (key_qkv_weight, key_out_weight, key_up_weight, key_down_weight)]
    query_encoder = ("query", query_lengths, query_weights, (biases, gains, up_biases, query_bias))
    key_encoder = ("key", key_lengths, key_weights, (key_biases, key_gains, key_up_biases))

    key_middle, _ = forward(rows, 0, False, key_halves, None, [key_encoder])
    inv = call(
        functools.partial(queue_norm_kernel, last),
        "queue_norm",
        [((8, queue.shape[0]), F32)],
        [VMEM],
        [queue],
        [ANY],
        [(queue.shape, BF)],
        4,
    )[0]
    key_middle, inv = lax.optimization_barrier((key_middle, inv))
    key_middle = relay(key_middle, 1)
    query_middle, key_pooled = forward(rows, None, False, query_halves, key_middle, [query_encoder, key_encoder])
    query_middle = relay(query_middle, 1)

    every_key = key_pooled[crops : 2 * crops]
    near_flips = [(0, 1), (1, 0), (1, 1)]
    if fast:
        near_keys = [swap(every_key, None, *f) for f in near_flips]
    step = forward(rows, None, True, query_halves, query_middle, [query_encoder])
    query_pooled = step[1]
    qkv, prob, row_scale, ctx, n1, r1, first, hid, slope, n2, r2 = step[2:]

    if fast:
        near_keys, query_pooled = lax.optimization_barrier((near_keys, query_pooled))
        every_key = jnp.concatenate([every_key, *near_keys], axis=0)
        every_key = jnp.concatenate([every_key] + [swap(every_key, None, 2 * k, 0) for k in range(1, 4)], axis=0)
    else:
        for flip in flips():
            every_key = jnp.concatenate([every_key, swap(every_key, None, *flip)], axis=0)
    place = dp * reps + rep
    matched = jnp.take(every_key, jnp.bitwise_xor(positive // crops, place) * crops + positive % crops, axis=0)
    matched = jnp.concatenate([matched, jnp.zeros((8 - crops, D), F32)], axis=0)
    first_peer = swap(first, None, 1, 0) if fast else None

    pooled_grad, lost = call(
        functools.partial(loss_kernel, last, crops, crop_all),
        "contrast",
        [((8, D), F32), ((8, 128), F32)],
        [VMEM] * 2,
        [query_pooled, matched, queue, inv],
        [VMEM] * 4,
        [],
        8,
    )

    def data_part(active, pooled, dy):
        wqkv, wout, wup, wdown = query_weights
        vec, grad_bup, ddown, dup, datt, dqkv, dx = data_backward(
            active, pooled, query_lengths, dy, gains, n2, r2, wdown, slope, wup, n1, r1, wout, qkv, prob, row_scale, wqkv
        )
        ddown_peer = swap(ddown, active, 1, 0) if fast else None
        return vec, grad_bup, ddown, ddown_peer, dup, datt, dqkv, dx

    def attention_part(active, vec, grad_bup, datt, dqkv, term):
        return attention_weights(active, query_halves, query_middle, ctx, datt, dqkv, (vec, grad_bup, term))

    def ffn_part(active, first_rows, ddown, ddown_peer, dup):
        _, _, wup, wdown = query_weights
        return ffn_weights(active, first_rows, first_peer, ddown, ddown_peer, hid, dup, wup, wdown, up_biases)

    def small_rows(vec, grad_bup, term):
        picked = [vec[k : k + 1] for k in VECTOR_ROWS]
        lost_row = jnp.concatenate([term[0:1]] * (D // 128), axis=1)
        return jnp.concatenate(picked + [grad_bup[0:1].reshape(FF // D, D), lost_row], axis=0)

    vec1, bup1, ddown, ddown_peer, dup, datt, dqkv, dmiddle = data_part(last, True, pooled_grad)
    dmiddle = relay(dmiddle, -1)
    lost_first = relay(lost, -1)
    if fast:
        datt = after(datt, dmiddle, lost_first, first_peer)
    ka1, sa1 = attention_part(last, vec1, bup1, datt, dqkv, lost)
    a1 = swap(after(sa1, ddown_peer), last, 1, 0) if fast else sa1
    wide1 = ffn_part(last, after(first, sa1), ddown, ddown_peer, dup)
    if fast:
        ku1, su1, kd1, sd1 = wide1
        u1 = swap(su1, last, 0, 1)
        d1 = near_z(sd1, last)
        ka1, s1 = half_sums(ka1, after(a1, u1), last)
        b1 = swap(s1, last, 0, 1)
        e1 = second_sum(last, kd1, after(d1, s1))
        p1 = slot_sums(last, [ku1, u1], [ka1, after(b1, e1)])
        dmiddle = after(dmiddle, e1, *p1)
    vec0, bup0, ddown, ddown_peer, dup, datt, dqkv, dx = data_part(0, False, dmiddle)
    half = SLOTS // sections
    dx = dx.reshape(crops, SLOTS, D)
    dx_half = dx[:, half:]
    if fast:
        e1 = far_z(e1, last)
        n1z = near_z(p1[2], last)
        datt = after(datt, e1, n1z)
    ka0, sa0 = attention_part(0, vec0, bup0, datt, dqkv, lost_first)
    wide0 = ffn_part(0, after(first, sa0), ddown, ddown_peer, dup)

    if fast:
        a0 = swap(after(sa0, ddown_peer), 0, 1, 0)
        ku0, su0, kd0, sd0 = wide0
        u0 = swap(su0, 0, 0, 1)
        d0 = near_z(sd0, 0)
        ka0, s0 = half_sums(ka0, after(a0, ku0), 0)
        b0 = swap(s0, 0, 0, 1)
        w1, t1 = third_sum(last, kd1, d1, after(e1, s0))
        t1 = swap(t1, last, 0, 1)
        m1 = second_sum(last, p1[1], after(n1z, w1))
        sums_last, down_last = last_section(last, p1[0], n1z, far_z(m1, last), w1, t1)
        e0 = second_sum(0, kd0, after(d0, m1))
        p0 = slot_sums(0, [ku0, after(u0, e0)])
        e0 = far_z(e0, 0)
        n0z = near_z(p0[2], 0)
        q0 = slot_sums(0, [ka0, after(b0, *p0)])
        l0z = near_z(q0[2], 0)
        m0 = second_sum(0, p0[1], after(n0z, *q0))
        w0, t0 = third_sum(0, kd0, d0, after(e0, m0))
        t0 = swap(t0, 0, 0, 1)
        g0 = [p0[0], n0z, far_z(m0, 0)]
        m0 = second_sum(0, q0[1], after(l0z, w0))
        dx_half = after(dx_half, m0)
        h0 = [q0[0], l0z, far_z(m0, 0)]
        summed = chip_totals(g0, h0, [w0, t0], sums_last, down_last)
        grad_qkv, grad_out, grad_up, grad_down, bias, gain, query_part, up_part, loss_row = summed
        loss_row = loss_row[0]
    else:
        grad_up, grad_down, grad_qkv, grad_out = [
            lax.psum_scatter(jnp.where(on_first, a, b).astype(F32), ("dp", "rep"), scatter_dimension=0, tiled=True)
            for a, b in zip([*wide0, ka0, sa0], [*wide1, ka1, sa1])
        ]
        small = jnp.where(on_first, small_rows(vec0, bup0, lost_first), small_rows(vec1, bup1, lost))
        for flip in flips():
            small = small + swap(small, None, *flip)
        width, up_width = D // (dps * reps), FF // (dps * reps)
        mine = lax.dynamic_slice(small[:8], (0, place * width), (8, width))
        bias, gain, query_part = mine[:5], mine[5:7], mine[7:]
        up_part = lax.dynamic_slice(small[8:12].reshape(1, FF), (0, place * up_width), (1, up_width))
        loss_row = small[12, :128]
    crops_grad = jnp.where(on_first, dx[:, :half], relay(dx_half, 1)).astype(F32)
    return (
        loss_row[:1],
        crops_grad,
        grad_qkv[None],
        grad_out[None],
        grad_up[None],
        grad_down[None],
        bias[None],
        gain[None],
        up_part,
        query_part,
    )


def solution(mesh):
    crop = P(("dp", "rep"), "section", None)
    per_crop = P(("dp", "rep"))
    layer3 = P("section", None, None)
    layer2 = P("section", None)
    placed = (
        (crop, crop, per_crop, per_crop, per_crop, P())
        + (layer3,) * 6
        + (layer2,) * 2
        + (layer3,) * 6
        + (layer2,)
    )
    shared3 = P("section", ("dp", "rep"), None)
    return jax.shard_map(
        body,
        mesh=mesh,
        in_specs=placed,
        out_specs=(
            P(),
            crop,
            shared3,
            shared3,
            shared3,
            shared3,
            P("section", None, ("dp", "rep")),
            P("section", None, ("dp", "rep")),
            P("section", ("dp", "rep")),
            P("section", ("dp", "rep")),
        ),
        check_vma=False,
    )
```

```python
import functools

import jax
import jax.numpy as jnp
from jax import lax
from jax.experimental import pallas as pl
from jax.experimental.pallas import tpu as pltpu
from jax.sharding import PartitionSpec as P

F32 = jnp.float32
BF = jnp.bfloat16
MASKED = -1e30
D = 768
FF = 3072
SLOTS = 256
PAIRS = 6
MIB = 2**20
SEMS = 112
P_ROWS, Q_ROWS = 96, 112
ALPHA = 1.0


def dot(a, b):
    return lax.dot_general(a, b, (((1,), (0,)), ((), ())), preferred_element_type=F32)


def dot_nt(a, b):
    return lax.dot_general(a, b, (((1,), (1,)), ((), ())), preferred_element_type=F32)


def dot_tn(a, b):
    return lax.dot_general(a, b, (((0,), (0,)), ((), ())), preferred_element_type=F32)


def gelu_parts(x, want_slope):
    share = 0.5 + 0.5 * lax.erf(x * 0.7071067811865476)
    if not want_slope:
        return x * share, None
    return x * share, share + (0.3989422804014327 * x) * jnp.exp(-0.5 * (x * x))


def norm_parts(z):
    mean = jnp.mean(z, axis=-1, keepdims=True)
    c = z - mean
    var = jnp.mean(c * c, axis=-1, keepdims=True)
    r = lax.rsqrt(var + 1e-12)
    return c * r, r


def head_masks(scale):
    lane = lax.broadcasted_iota(jnp.int32, (1, 128), 1)
    low = jnp.where(lane < 64, scale, 0.0).astype(BF)
    high = jnp.where(lane < 64, 0.0, scale).astype(BF)
    return low, high


def stack_heads(pair, scale):
    low, high = head_masks(scale)
    return jnp.concatenate([pair * low, pair * high], axis=0)


def side_by_side(stacked):
    half = stacked.shape[0] // 2
    return jnp.concatenate([stacked[:half], stacked[half:]], axis=1)


class Copies:
    def __init__(self, sems):
        self.sems, self.used, self.open = sems, 0, []

    def make(self, src, dst):
        self.used += 1
        return pltpu.make_async_copy(src, dst, self.sems.at[self.used - 1])

    def fetch(self, src, dst):
        cp = self.make(src, dst)
        cp.start()
        return cp

    def pick(self, by_section, dst):
        if by_section[0] is by_section[1]:
            return self.fetch(by_section[0], dst)
        sem = self.sems.at[self.used]
        self.used += 1
        here = lax.axis_index("section")

        @pl.when(here == 0)
        def _():
            pltpu.make_async_copy(by_section[0], dst, sem).start()

        @pl.when(here != 0)
        def _():
            pltpu.make_async_copy(by_section[1], dst, sem).start()

        return pltpu.make_async_copy(by_section[0], dst, sem)

    def send(self, src, dst):
        self.open.append(self.fetch(src, dst))

    def drain(self):
        for cp in self.open:
            cp.wait()


def only_on(section, run):
    if section is None:
        run()
    else:
        pl.when(lax.axis_index("section") == section)(run)


VMEM = pl.BlockSpec(memory_space=pltpu.VMEM)
ANY = pl.BlockSpec(memory_space=pl.ANY)
HBM = pl.BlockSpec(memory_space=pltpu.HBM)
SMEM = pl.BlockSpec(memory_space=pltpu.SMEM)
sd = jax.ShapeDtypeStruct


def call(kernel, name, outs, out_specs, ins, in_specs, scratch, micros, limit=56):
    return pl.pallas_call(
        kernel,
        out_shape=[sd(*o) for o in outs],
        in_specs=in_specs,
        out_specs=out_specs,
        scratch_shapes=[pltpu.VMEM(*s) for s in scratch] + [pltpu.SemaphoreType.DMA((SEMS,))],
        compiler_params=pltpu.CompilerParams(vmem_limit_bytes=limit * MIB),
        cost_estimate=pl.CostEstimate(flops=int(micros * ALPHA * 1.15e9), bytes_accessed=1000, transcendentals=0),
        name=name,
    )(*ins)


def saved_shapes(rows):
    crops = rows // SLOTS
    return [
        ((rows, 3 * D), BF),
        ((PAIRS * crops, 2 * SLOTS, SLOTS), BF),
        ((2 * SLOTS, 128), F32),
        ((rows, D), BF),
        ((rows, D), BF),
        ((rows, 128), F32),
        ((rows, D), BF),
        ((rows, FF), BF),
        ((rows, FF), BF),
        ((rows, D), BF),
        ((rows, 128), F32),
    ]


def fetch_rows(copies, refs, kinds, x):
    waits = []
    half = refs[0].shape[1] if "halves" in kinds else SLOTS // 2
    for c in range(x.shape[0] // SLOTS):
        for h in range(SLOTS // half):
            at = slice(SLOTS * c + half * h, SLOTS * c + half * (h + 1))
            options = []
            if "halves" in kinds:
                options.append(refs[h].at[c])
            if "whole" in kinds:
                options.append(refs[-1].at[at, :])
            waits.append(copies.pick((options[0], options[-1]), x.at[at, :]))
    return waits


def read_vectors(refs, key):
    if key:
        b, g, up = refs
        rows = b[0].astype(F32)
        rows = [rows[i : i + 1] for i in range(6)]
    else:
        b, g, up, q = refs
        rows = b[0].astype(F32)
        rows = [q[...].astype(F32)] + [rows[i : i + 1] for i in range(5)]
    gains = g[0].astype(F32)
    return rows + [gains[0:1], gains[1:2]], up[...].astype(F32)


def load_vectors(refs, kinds, vec, bup):
    sets = []
    for kind in kinds:
        n = 3 if kind == "key" else 4
        sets.append(read_vectors(refs[:n], kind == "key"))
        refs = refs[n:]
    here = lax.axis_index("section")
    for i in range(8):
        row = sets[0][0][i]
        if len(sets) == 2:
            row = jnp.where(here == 0, row, sets[1][0][i])
        vec[i : i + 1, :] = row
    up = sets[0][1]
    if len(sets) == 2:
        up = jnp.where(here == 0, up, sets[1][1])
    bup[...] = up


def forward_kernel(rows, active, save, x_kinds, sets, *refs):
    def run():
        forward_body(rows, save, x_kinds, sets, *refs)

    only_on(active, run)


def forward_body(rows, save, x_kinds, sets, *refs):
    crops = rows // SLOTS
    lens_refs, refs = refs[: len(sets)], refs[len(sets) :]
    here = lax.axis_index("section")
    if len(sets) == 2:
        lens = [jnp.where(here == 0, lens_refs[0][c], lens_refs[1][c]) for c in range(crops)]
    else:
        lens = [lens_refs[0][c] for c in range(crops)]
    n_x = (2 if "halves" in x_kinds else 0) + (1 if "whole" in x_kinds else 0)
    x_refs, refs = refs[:n_x], refs[n_x:]
    w_refs, refs = refs[: 4 * len(sets)], refs[4 * len(sets) :]
    n_v = sum(3 if k == "key" else 4 for k in sets)
    v_refs, refs = refs[:n_v], refs[n_v:]
    y_ref, pool_ref, unit_ref = refs[:3]
    refs = refs[3:]
    if save:
        (qkv_o, prob_o, inv_o, ctx_o, n1_o, r1_o, first_o, hid_o, slope_o, n2_o, r2_o) = refs[:11]
        refs = refs[11:]
    (x, wqkv, wout, wup, wdown, ctx, zbuf, first, hid, vec, bup) = refs[:11]
    refs = refs[11:]
    if save:
        (qkv, prob, inv_all, n1, r1, slope, n2, r2) = refs[:8]
        refs = refs[8:]
        inv_all[...] = jnp.zeros_like(inv_all)
    copies = Copies(refs[0])
    got_x = fetch_rows(copies, x_refs, x_kinds, x)
    pairs = [(w_refs[i], w_refs[4 + i] if len(sets) == 2 else w_refs[i]) for i in range(4)]
    got_qkv = copies.pick(pairs[0], wqkv)
    load_vectors(v_refs, sets, vec, bup)
    for cp in got_x:
        cp.wait()
    got_qkv.wait()
    got_out = copies.pick(pairs[1], wout)
    got_up = copies.pick(pairs[2], wup)
    got_down = copies.pick(pairs[3], wdown)
    keycol = lax.broadcasted_iota(jnp.int32, (1, SLOTS), 1)
    lane = lax.broadcasted_iota(jnp.int32, (1, 128), 1)
    gain1, gain2 = vec[6:7], vec[7:8]

    def heads(i, carry):
        thirds = []
        for j in range(3):
            cols = pl.ds(pl.multiple_of(D * j + 256 * i, 256), 256)
            part = dot(x[...], wqkv[:, cols])
            if j != 1:
                at = pl.ds(pl.multiple_of(256 * i, 256), 256)
                part = part + vec[j // 2 : j // 2 + 1, at]
            part = part.astype(BF)
            if save:
                qkv[:, cols] = part
            thirds.append(part)
        for c in range(crops):
            crop = slice(SLOTS * c, SLOTS * (c + 1))
            for pr in range(2):
                qp, kp, vp = [t[crop, 128 * pr : 128 * (pr + 1)] for t in thirds]
                scores = jnp.where(keycol < lens[c], dot_nt(stack_heads(qp, 0.125), kp), MASKED)
                e = jnp.exp(scores - jnp.max(scores, axis=-1, keepdims=True))
                inv = pl.reciprocal(jnp.sum(e, axis=-1, keepdims=True))
                e = e.astype(BF)
                if save:
                    unit = PAIRS * c + 2 * i + pr
                    prob[unit] = e
                    inv_all[...] = jnp.where(lane == unit, inv, inv_all[...])
                at = pl.ds(pl.multiple_of(256 * i + 128 * pr, 128), 128)
                both = dot(e, vp) * inv
                ctx[crop, at] = jnp.where(lane < 64, both[:SLOTS], both[SLOTS:]).astype(BF)
        return carry

    lax.fori_loop(0, 3, heads, 0)
    if save:
        copies.send(qkv, qkv_o)
        copies.send(prob, prob_o)
        copies.send(inv_all, inv_o)
        copies.send(ctx, ctx_o)
    got_out.wait()
    for j in range(3):
        cols = slice(256 * j, 256 * (j + 1))
        zbuf[:, cols] = x[:, cols].astype(F32) + dot(ctx[...], wout[:, cols]) + vec[2:3, cols]
    block = 64
    steps = rows // block

    def first_norm(i, carry):
        at = pl.ds(pl.multiple_of(i * block, block), block)
        n, r = norm_parts(zbuf[at, :])
        f = (n * gain1 + vec[3:4]).astype(BF)
        first[at, :] = f
        zbuf[at, :] = f.astype(F32) + vec[4:5]
        if save:
            n1[at, :] = n.astype(BF)
            r1[at, :] = jnp.broadcast_to(r, (block, 128))
        return carry

    lax.fori_loop(0, steps, first_norm, 0, unroll=True)
    if save:
        copies.send(n1, n1_o)
        copies.send(r1, r1_o)
        copies.send(first, first_o)
    got_up.wait()
    got_down.wait()

    def down_part(k):
        cols = slice(512 * k, 512 * (k + 1))
        zbuf[...] += dot(hid[:, cols], wdown[cols, :])

    for i in range(12):
        cols = slice(256 * i, 256 * (i + 1))
        g, slope_part = gelu_parts(dot(first[...], wup[:, cols]) + bup[:, cols], save)
        hid[:, cols] = g.astype(BF)
        if save:
            slope[:, cols] = slope_part.astype(BF)
        if i % 2 and i > 2:
            down_part(i // 2 - 1)
    if save:
        copies.send(hid, hid_o)
        copies.send(slope, slope_o)
    down_part(5)
    pool_ref[...] = jnp.zeros_like(pool_ref)
    per_crop = SLOTS // block
    for i in range(steps):
        at = slice(i * block, (i + 1) * block)
        n, r = norm_parts(zbuf[at, :])
        f = n * gain2 + vec[5:6]
        y_ref[at, :] = f.astype(BF)
        if save:
            n2[at, :] = n.astype(BF)
            r2[at, :] = jnp.broadcast_to(r, (block, 128))
        c = i // per_crop
        token = lax.broadcasted_iota(jnp.int32, (block, 1), 0) + (i % per_crop) * block
        part = jnp.sum(jnp.where(token < lens[c], f, 0.0), axis=0, keepdims=True)
        pool_ref[c : c + 1, :] += part / lens[c].astype(F32)
    pooled = pool_ref[:crops]
    unit_ref[...] = pooled * lax.rsqrt(jnp.sum(pooled * pooled, axis=-1, keepdims=True) + 1e-6)
    if save:
        copies.send(n2, n2_o)
        copies.send(r2, r2_o)
    copies.drain()


def forward(rows, active, save, halves, whole, encoders):
    x_kinds = (("halves",) if halves else ()) + (("whole",) if whole is not None else ())
    xs = list(halves or ()) + ([whole] if whole is not None else [])
    lens = [e[1] for e in encoders]
    weights = [w for e in encoders for w in e[2]]
    vectors = [v for e in encoders for v in e[3]]
    outs = [((rows, D), BF), ((8, D), F32), ((rows // SLOTS, D), F32)]
    out_specs = [VMEM] * 3
    scratch = [
        ((rows, D), BF),
        ((D, 3 * D), BF),
        ((D, D), BF),
        ((D, FF), BF),
        ((FF, D), BF),
        ((rows, D), BF),
        ((rows, D), F32),
        ((rows, D), BF),
        ((rows, FF), BF),
        ((8, D), F32),
        ((1, FF), F32),
    ]
    if save:
        kept = saved_shapes(rows)
        outs += kept
        out_specs += [ANY] * len(kept)
        scratch += [kept[i] for i in (0, 1, 2, 4, 5, 8, 9, 10)]
    return call(
        functools.partial(forward_kernel, rows, active, save, x_kinds, [e[0] for e in encoders]),
        "layer_forward",
        outs,
        out_specs,
        [*lens, *xs, *weights, *vectors],
        [SMEM] * len(lens) + [ANY] * (len(xs) + len(weights)) + [VMEM] * len(vectors),
        scratch,
        20 if save else 18,
    )


def split3(v):
    hi = v.astype(BF)
    rest = v - hi.astype(F32)
    mid = rest.astype(BF)
    lo = (rest - mid.astype(F32)).astype(BF)
    return hi, mid, lo


def stack3(v):
    parts = split3(v)
    return jnp.concatenate(list(parts) + [jnp.zeros_like(parts[0])] * 5, axis=0)


def unstack3(rows, n):
    return rows[:n] + rows[n : 2 * n] + rows[2 * n : 3 * n]


def queue_norm_kernel(active, queue_h, inv_ref, queue, sems):
    def run():
        Copies(sems).fetch(queue_h, queue).wait()

        def step(i, carry):
            at = pl.ds(pl.multiple_of(i * 512, 512), 512)
            v = queue[at, :].astype(F32)
            sq = v * v
            hi = sq.astype(BF)
            lo = (sq - hi.astype(F32)).astype(BF)
            ones = jnp.ones((8, D), BF)
            total = dot_nt(ones, hi) + dot_nt(ones, lo)
            inv_ref[:, at] = lax.rsqrt(total + 1e-6)
            return carry

        lax.fori_loop(0, queue.shape[0] // 512, step, 0)

    only_on(active, run)


def loss_kernel(active, crops, count, positive, pooled, inv, queue, *refs):
    *key_refs, grad_ref, loss_ref, keys, sems = refs

    def run():
        at = 0
        for r in key_refs:
            keys[at : at + r.shape[0], :] = r[...]
            at += r.shape[0]
        place = lax.axis_index("dp") * lax.axis_size("rep") + lax.axis_index("rep")
        picked = []
        for c in range(crops):
            index = positive[c]
            row = jnp.bitwise_xor(index // crops, place) * crops + index % crops
            picked.append(keys[pl.ds(row, 1), :])
        v = pooled[:crops]
        r = lax.rsqrt(jnp.sum(v * v, axis=-1, keepdims=True) + 1e-6)
        u = v * r
        k = jnp.concatenate(picked, axis=0)
        near = jnp.sum(u * k, axis=-1, keepdims=True) * 20.0
        inv_row = inv[0:1]
        far = unstack3(dot_nt(stack3(u), queue[...]), crops) * (inv_row * 20.0)
        top = jnp.maximum(near, jnp.max(far, axis=-1, keepdims=True))
        e_near = jnp.exp(near - top)
        e_far = jnp.exp(far - top)
        total = e_near + jnp.sum(e_far, axis=-1, keepdims=True)
        share = 20.0 / (total * count)
        d_u = unstack3(dot(stack3(e_far * inv_row * share), queue[...]), crops)
        d_u = d_u + (e_near - total) * share * k
        grad = r * (d_u - u * jnp.sum(u * d_u, axis=-1, keepdims=True))
        grad_ref[...] = jnp.zeros_like(grad_ref)
        grad_ref[:crops] = grad
        lost = jnp.sum(top + jnp.log(total) - near, axis=0, keepdims=True) / count
        loss_ref[...] = jnp.broadcast_to(lost, loss_ref.shape)

    only_on(active, run)


def norm_back(dy, gain, n, r):
    dn = dy * gain
    return r * (dn - jnp.mean(dn, axis=-1, keepdims=True) - n * jnp.mean(dn * n, axis=-1, keepdims=True))


def column_sum(v):
    return jnp.sum(v, axis=0, keepdims=True)


def fast_mesh():
    return lax.axis_size("dp") == 8 and lax.axis_size("rep") == 2


def place_bits():
    dp, rep = lax.axis_index("dp"), lax.axis_index("rep")
    return dp // 2, dp % 2, rep


CHUNK = 512


def early_down_kernel(rows, active, dy, n2, r2, gains, ddown_o):
    def run():
        gain = gains[0].astype(F32)[1:2]
        for i in range(rows // 64):
            at = slice(64 * i, 64 * (i + 1))
            ddown_o[at] = norm_back(dy[at].astype(F32), gain, n2[at].astype(F32), r2[at, 0:1]).astype(BF)

    only_on(active, run)


def early_down(active, dy, n2, r2, gains):
    return call(
        lambda *refs: early_down_kernel(n2.shape[0], active, *refs[:-1]),
        "early_down",
        [(n2.shape, BF)],
        [VMEM],
        [dy, n2, r2, gains],
        [VMEM] * 4,
        [],
        3,
    )[0]


def data_backward_kernel(rows, active, pooled, lens, dy, gains, *refs):
    def run():
        n2_h, r2_h, wdown_h, slope_h, wup_h, n1_h, r1_h, wout_h, qkv_h, prob_h, inv_h, wqkv_h = refs[:12]
        vec, bup, ddown_o, dup_o, datt_o, dqkv_o, dx_o = refs[12:19]
        n2, r2, wdown, slope, wup, n1, r1, wout, qkv, prob, inv, wqkv = refs[19:31]
        acc, ddown, dup, datt, dqkv, dx, sems = refs[31:]
        copies = Copies(sems)
        got_n2, got_r2 = copies.fetch(n2_h, n2), copies.fetch(r2_h, r2)
        got = []
        for i in range(FF // CHUNK):
            cols = slice(CHUNK * i, CHUNK * (i + 1))
            got.append(
                [
                    copies.fetch(wdown_h.at[cols, :], wdown.at[cols, :]),
                    copies.fetch(slope_h.at[:, cols], slope.at[:, cols]),
                    copies.fetch(wup_h.at[:, cols], wup.at[:, cols]),
                ]
            )
        got_n1 = [copies.fetch(n1_h, n1), copies.fetch(r1_h, r1), copies.fetch(wout_h, wout)]
        got_qkv = [copies.fetch(qkv_h, qkv), copies.fetch(prob_h, prob), copies.fetch(inv_h, inv)]
        got_w = copies.fetch(wqkv_h, wqkv)
        vec[...] = jnp.zeros_like(vec)
        gain1, gain2 = gains[0].astype(F32)[0:1], gains[0].astype(F32)[1:2]
        block = 64
        per_crop = SLOTS // block
        got_n2.wait()
        got_r2.wait()
        for i in range(rows // block):
            at = slice(block * i, block * (i + 1))
            c = i // per_crop
            if pooled:
                token = lax.broadcasted_iota(jnp.int32, (block, 1), 0) + (i % per_crop) * block
                grow = jnp.where(token < lens[c], 1.0 / lens[c].astype(F32), 0.0) * dy[c : c + 1]
            else:
                grow = dy[at].astype(F32)
            n = n2[at].astype(F32)
            ds = norm_back(grow, gain2, n, r2[at, 0:1])
            low_ds = ds.astype(BF)
            acc[at] = ds
            ddown[at] = low_ds
            vec[0:1] += column_sum(grow * n)
            vec[1:2] += column_sum(grow)
            vec[2:3] += column_sum(low_ds.astype(F32))
        copies.send(ddown, ddown_o)
        for i in range(FF // CHUNK):
            cols = slice(CHUNK * i, CHUNK * (i + 1))
            for cp in got[i]:
                cp.wait()
            up = (dot_nt(ddown[...], wdown[cols, :]) * slope[:, cols].astype(F32)).astype(BF)
            dup[:, cols] = up
            copies.send(dup.at[:, cols], dup_o.at[:, cols])
            bup[:, cols] = jnp.broadcast_to(column_sum(up.astype(F32)), (8, CHUNK))
            acc[...] += dot_nt(up, wup[:, cols])
        for cp in got_n1:
            cp.wait()
        for i in range(rows // block):
            at = slice(block * i, block * (i + 1))
            n = n1[at].astype(F32)
            dfirst = acc[at]
            ds = norm_back(dfirst, gain1, n, r1[at, 0:1])
            low_ds = ds.astype(BF)
            acc[at] = ds
            datt[at] = low_ds
            vec[3:4] += column_sum(dfirst * n)
            vec[4:5] += column_sum(dfirst)
            vec[5:6] += column_sum(low_ds.astype(F32))
        copies.send(datt, datt_o)
        dctx = dot_nt(datt[...], wout[...]).astype(BF)
        for cp in got_qkv:
            cp.wait()
        for c in range(rows // SLOTS):
            crop = slice(SLOTS * c, SLOTS * (c + 1))
            for pr in range(PAIRS):
                cols = [slice(D * j + 128 * pr, D * j + 128 * (pr + 1)) for j in range(3)]
                unit = PAIRS * c + pr
                qp, kp, vp = [qkv[crop, t] for t in cols]
                dcs = stack_heads(dctx[crop, 128 * pr : 128 * (pr + 1)], 1.0)
                scale = inv[:, unit : unit + 1]
                e = prob[unit]
                pf = e.astype(F32) * scale
                weighted = pf * dot_nt(dcs, vp)
                ds = (weighted - pf * jnp.sum(weighted, axis=-1, keepdims=True)).astype(BF)
                dqkv[crop, cols[0]] = dot(side_by_side(ds), stack_heads(kp, 0.125)).astype(BF)
                dqkv[crop, cols[1]] = dot_tn(ds, stack_heads(qp, 0.125)).astype(BF)
                dqkv[crop, cols[2]] = dot_tn(e, (dcs * scale).astype(BF)).astype(BF)
        got_w.wait()
        for j in range(3):
            cols = slice(256 * j, 256 * (j + 1))
            dx[:, cols] = (dot_nt(dqkv[...], wqkv[cols, :]) + acc[:, cols]).astype(BF)
        copies.send(dx, dx_o)
        copies.send(dqkv, dqkv_o)
        vec[6:7] = column_sum(dqkv[:, :D].astype(F32))
        vec[7:8] = column_sum(dqkv[:, 2 * D :].astype(F32))
        copies.drain()

    only_on(active, run)


def data_backward(active, pooled, lens, dy, gains, n2, r2, wdown, slope, wup, n1, r1, wout, qkv, prob, inv, wqkv):
    rows = n1.shape[0]
    held = [n2, r2, wdown, slope, wup, n1, r1, wout, qkv, prob, inv, wqkv]
    wide_rows = ((rows, D), BF)
    return call(
        functools.partial(data_backward_kernel, rows, active, pooled),
        "data_backward",
        [((8, D), F32), ((8, FF), F32), wide_rows, ((rows, FF), BF), wide_rows, ((rows, 3 * D), BF), wide_rows],
        [VMEM] * 2 + [ANY] * 5,
        [lens, dy, gains, *held],
        [SMEM, VMEM, VMEM] + [ANY] * len(held),
        [(h.shape, h.dtype) for h in held]
        + [((rows, D), F32), wide_rows, ((rows, FF), BF), wide_rows, ((rows, 3 * D), BF), wide_rows],
        26,
    )


def ffn_weights_kernel(rows, active, fast, *refs):
    def run():
        groups = 4 if fast else 1
        firsts, refs_ = refs[:groups], refs[groups:]
        ddowns, refs_ = refs_[:groups], refs_[groups:]
        hid_h, dup_h, *refs_ = refs_
        if fast:
            wup_h, wdown_h, bup_h, keep, send, *refs_ = refs_
            first, ddown, hid, dup, gup, gdown, wup, wdown, bup, sems = refs_
        else:
            up_o, down_o, first, ddown, hid, dup, gup, gdown, sems = refs_
        copies = Copies(sems)
        own = slice(0, rows)
        at = [slice(rows * k, rows * (k + 1)) for k in range(groups)]
        got_first = [copies.fetch(h, first.at[r, :]) for h, r in zip(firsts, at)]
        parts = range(FF // 384)
        if fast:
            z, x, y = place_bits()
            parts = (1, 0)
            got_first.append(copies.fetch(bup_h, bup))
        blocks = {}
        for i in parts:
            here = slice(384 * i, 384 * (i + 1))
            there = pl.ds(pl.multiple_of(768 * jnp.bitwise_xor(z, 2 * i) + 384 * x, 128), 384) if fast else here
            block = [copies.fetch(wup_h.at[:, there], wup.at[:, here])] if fast else []
            if i == parts[0]:
                got_ddown = [copies.fetch(h, ddown.at[r, :]) for h, r in zip(ddowns, at)]
            if fast:
                block.append(copies.fetch(wdown_h.at[there, :], wdown.at[here, :]))
            block.append(copies.fetch(hid_h.at[:, there], hid.at[own, here]))
            block.append(copies.fetch(dup_h.at[:, there], dup.at[own, here]))
            blocks[i] = block
        for cp in got_first:
            cp.wait()
        for i in parts:
            here = slice(384 * i, 384 * (i + 1))
            for cp in blocks[i]:
                cp.wait()
            if i == parts[0]:
                for cp in got_ddown:
                    cp.wait()
            if fast:
                zz = jnp.bitwise_xor(z, 2 * i)
                bias = bup[:, pl.ds(pl.multiple_of(768 * zz + 384 * x, 128), 384)].astype(F32)
                for r in at[1:]:
                    g, slope = gelu_parts(dot(first[r, :], wup[:, here]) + bias, True)
                    hid[r, here] = g.astype(BF)
                    dup[r, here] = (dot_nt(ddown[r, :], wdown[here, :]) * slope).astype(BF)
            gdown[here, :] = dot_tn(hid[:, here], ddown[...]).astype(BF)
            if fast:
                for jy, out in ((1, send), (0, keep)):
                    units = pl.ds(pl.multiple_of(384 * i + 192 * jnp.bitwise_xor(y, jy), 64), 192)
                    copies.send(gdown.at[units, :], out.at[i, 192:384, :])
            gup[:, here] = dot_tn(first[...], dup[:, here]).astype(BF)
            if fast:
                to_cols = pl.ds(pl.multiple_of(384 * (zz // 2), 128), 384)
                for jy, out in ((1, send), (0, keep)):
                    for jh in (1, 0):
                        for jx in range(2):
                            for jn in range(2):
                                oz = jnp.bitwise_xor(z, jn + 2 * jh)
                                owner = (oz * 2 + jnp.bitwise_xor(x, jx)) * 2 + jnp.bitwise_xor(y, jy)
                                rows48 = pl.ds(pl.multiple_of(48 * owner, 16), 48)
                                k = 2 * jx + jn
                                copies.send(gup.at[rows48, here], out.at[jh, 48 * k : 48 * (k + 1), to_cols])
        if not fast:
            copies.send(gup, up_o)
            copies.send(gdown, down_o)
        copies.drain()

    only_on(active, run)


def ffn_weights(active, firsts, ddowns, hid, dup, wup, wdown, bup):
    rows = hid.shape[0]
    fast = fast_mesh()
    ins = [*firsts, *ddowns, hid, dup]
    if fast:
        ins += [wup, wdown, bup]
        outs = [((2, 384, D), BF)] * 2
        tokens, units = 4 * rows, FF // 4
        extra = [((D, units), BF), ((units, D), BF), ((1, FF), BF)]
    else:
        outs = [((D, FF), BF), ((FF, D), BF)]
        tokens, units, extra = rows, FF, []
    return call(
        functools.partial(ffn_weights_kernel, rows, active, fast),
        "ffn_weights",
        outs,
        [ANY] * len(outs),
        ins,
        [ANY] * len(ins),
        [
            ((tokens, D), BF),
            ((tokens, D), BF),
            ((tokens, units), BF),
            ((tokens, units), BF),
            ((D, units), BF),
            ((units, D), BF),
        ]
        + extra,
        15,
    )


VECTOR_ROWS = (7, 5, 4, 2, 1, 3, 0, 6)


def attention_weights_kernel(rows, active, fast, x_kinds, *refs):
    def run():
        n_x = len(x_kinds) + 1
        x_refs = refs[:n_x]
        if fast:
            vec_h, bup_h, lost_h, *refs_ = refs[n_x:]
            ctx_h, datt_h, dqkv_h, p_keep, p_send, q_keep, q_send, x, ctx, datt, dqkv, gqkv, gout, tail, vec, bup, lost, sems = refs_
        else:
            ctx_h, datt_h, dqkv_h, out_qkv, out_out, x, ctx, datt, dqkv, gqkv, gout, sems = refs[n_x:]
        copies = Copies(sems)
        got = [copies.fetch(ctx_h, ctx), copies.fetch(datt_h, datt)]
        got_small = [copies.fetch(vec_h, vec), copies.fetch(bup_h, bup), copies.fetch(lost_h, lost)] if fast else []
        got_x = fetch_rows(copies, x_refs, x_kinds, x)
        got_x.append(copies.fetch(dqkv_h, dqkv))
        for cp in got_small:
            cp.wait()
        if fast:
            z, xx, y = place_bits()
            small = jnp.concatenate([vec[k : k + 1] for k in VECTOR_ROWS], axis=0)
            row = lax.broadcasted_iota(jnp.int32, (8, D), 0)
            lane = lax.broadcasted_iota(jnp.int32, (8, D), 1) - 3 * ((z * 2 + xx) * 2 + y)
            terms = [jnp.broadcast_to(t.astype(F32)[0:1, 0:1], (8, D)) for t in split3(lost[...])]
            lost_row = sum(jnp.where(lane == i, t, 0.0) for i, t in enumerate(terms))

        def slots():
            for j in range(15, -1, -1):
                jx, jy, jz = j // 8, j // 4 % 2, j % 4
                owner = (jnp.bitwise_xor(z, jz) * 2 + jnp.bitwise_xor(xx, jx)) * 2 + jnp.bitwise_xor(y, jy)
                p_out = (p_send if jx else p_keep).at[jy * 4 + jz]
                q_out = (q_send if jy else q_keep).at[jx * 4 + jz]
                yield j, owner, p_out, q_out

        def ship(part, third):
            for _, owner, p_out, q_out in slots():
                at = pl.ds(pl.multiple_of(48 * owner, 16), 48)
                to = (p_out.at[0:48, :], p_out.at[48:96, :], q_out.at[0:48, :], q_out.at[48:96, :])[third]
                copies.send(part.at[at, :], to)

        for cp in got:
            cp.wait()
        gout[...] = dot_tn(ctx[...], datt[...]).astype(BF)
        if fast:
            ship(gout, 3)
            for j, owner, _, q_out in slots():
                head = pltpu.roll(small, D - 48 * owner, 1)
                ups = pltpu.roll(bup[...], FF - 192 * owner, 1)[:, :D]
                other = jnp.where(row == 0, ups, jnp.where(row == 1, lost_row, 0.0))
                tail[j] = jnp.concatenate([head, other], axis=0).astype(BF)
                copies.send(tail.at[j], q_out.at[96:112, :])
        for cp in got_x:
            cp.wait()
        for t in range(3):
            for k in range(2):
                cols = slice(D * t + 384 * k, D * t + 384 * (k + 1))
                gqkv[:, cols] = dot_tn(x[...], dqkv[:, cols]).astype(BF)
            if fast:
                ship(gqkv.at[:, slice(D * t, D * (t + 1))], t)
        if not fast:
            copies.send(gqkv, out_qkv)
            copies.send(gout, out_out)
        copies.drain()

    only_on(active, run)


def attention_weights(active, halves, whole, ctx, datt, dqkv, small):
    rows = ctx.shape[0]
    fast = fast_mesh()
    x_kinds = ("halves", "whole")
    outs = [((8, n, D), BF) for n in (P_ROWS, P_ROWS, Q_ROWS, Q_ROWS)] if fast else [((D, 3 * D), BF), ((D, D), BF)]
    ins = [*halves, whole, *(small if fast else ()), ctx, datt, dqkv]
    in_specs = [ANY] * (9 if fast else 6)
    return call(
        functools.partial(attention_weights_kernel, rows, active, fast, x_kinds),
        "attention_weights",
        outs,
        [HBM] * len(outs),
        ins,
        in_specs,
        [((rows, D), BF)] * 3
        + [((rows, 3 * D), BF), ((D, 3 * D), BF), ((D, D), BF)]
        + ([((16, 16, D), BF), ((8, D), F32), ((8, FF), F32), ((8, 128), F32)] if fast else []),
        8,
    )


AXES = ("section", "dp", "rep")


def swap(block, section, dp_flip, rep_flip):
    dps, reps = lax.axis_size("dp"), lax.axis_size("rep")
    sections = range(lax.axis_size("section")) if section is None else [section]
    route = [
        ((s * dps + d) * reps + r, (s * dps + (d ^ dp_flip)) * reps + (r ^ rep_flip))
        for s in sections
        for d in range(dps)
        for r in range(reps)
    ]
    return lax.ppermute(block, AXES, route)


def flips():
    out, bit = [], 1
    while bit < lax.axis_size("rep"):
        out.append((0, bit))
        bit *= 2
    bit = 1
    while bit < lax.axis_size("dp"):
        out.append((bit, 0))
        bit *= 2
    return out


def add_rows(pieces, dst, at, count):
    def step(i, carry):
        here = pl.ds(pl.multiple_of(i * 16, 16), 16)
        total = pieces[0][here, :].astype(F32)
        for p in pieces[1:]:
            total = total + p[here, :].astype(F32)
        dst[pl.ds(pl.multiple_of(at + i * 16, 16), 16), :] = total.astype(dst.dtype)
        return carry

    tiles = count // 16
    lax.fori_loop(0, tiles, step, 0, unroll=next(u for u in (6, 5, 4, 7, 3, 2, 1) if tiles % u == 0))


def add_slots(kept, received, dst, first, rows):
    def step(i, carry):
        for t in range(rows // 16):
            here = slice(16 * t, 16 * (t + 1))
            total = kept[first + i, here, :].astype(F32) + received[first + i, here, :].astype(F32)
            dst[first + i, here, :] = total.astype(BF)
        return carry

    lax.fori_loop(0, 4, step, 0)


def half_sums_kernel(active, p_kept, p_received, q_kept, q_received, *refs):
    def run():
        p_near, p_far, q_near, q_far, p_held, q_held, p_made, q_made, sems = refs
        groups = (
            (p_kept, p_received, p_near, p_far, p_held, p_made, P_ROWS),
            (q_kept, q_received, q_near, q_far, q_held, q_made, Q_ROWS),
        )
        copies = Copies(sems)
        half = {True: pl.ds(4, 4), False: pl.ds(0, 4)}
        got = [(g, f, copies.fetch(g[0].at[half[f]], g[4].at[half[f]])) for f in (True, False) for g in groups]
        for (_, received, near, far, held, made, rows), is_far, cp in got:
            cp.wait()
            add_slots(held, received, made, 4 if is_far else 0, rows)
            copies.send(made.at[half[is_far]], far if is_far else near)
        copies.drain()

    only_on(active, run)


def half_sums(section, p_kept, p_received, q_kept, q_received):
    p, q = [((4, n, D), BF) for n in (P_ROWS, Q_ROWS)]
    p_all, q_all = [((8, n, D), BF) for n in (P_ROWS, Q_ROWS)]
    return call(
        functools.partial(half_sums_kernel, section),
        "half_sums",
        [p, p, q, q],
        [HBM] * 4,
        [p_kept, p_received, q_kept, q_received],
        [HBM, VMEM] * 2,
        [p_all, q_all, p_all, q_all],
        4,
        24,
    )


def slot_sums_kernel(active, counts, sizes, *refs):
    def run():
        groups, at = [], 0
        for n in counts:
            groups.append(refs[at : at + n])
            at += n
        own_o, kept_o, send_o = refs[at : at + 3]
        helds = refs[at + 3 : at + 3 + len(counts)]
        own, made, sems = refs[-3:]
        copies = Copies(sems)
        order = (1, 3, 2, 0)
        got = {k: [copies.fetch(g[0].at[k], h.at[k]) for g, h in zip(groups, helds)] for k in order}
        for k, out in zip(order, (send_o.at[0], send_o.at[1], kept_o, own_o)):
            to, base = made.at[k - 1] if k else own, 0
            for g, h, cp, size in zip(groups, helds, got[k], sizes):
                cp.wait()
                add_rows([h.at[k]] + [r.at[k] for r in g[1:]], to, base, size)
                base += size
            copies.send(to, out)
        copies.drain()

    only_on(active, run)


def slot_sums(section, *groups):
    sizes = [g[0].shape[1] for g in groups]
    shape = (sum(sizes), D)
    return call(
        functools.partial(slot_sums_kernel, section, [len(g) for g in groups], sizes),
        "slot_sums",
        [(shape, F32), (shape, BF), ((2, *shape), BF)],
        [ANY] * 3,
        [t for g in groups for t in g],
        [spec for g in groups for spec in [HBM] + [VMEM] * (len(g) - 1)],
        [((4, size, D), BF) for size in sizes] + [(shape, F32), ((3, *shape), BF)],
        3 * len(groups),
        24,
    )


def second_sum_kernel(active, rows, kept, received, out, held, made, sems):
    def run():
        copies = Copies(sems)
        copies.fetch(kept if len(kept.shape) == 2 else kept.at[1], held).wait()
        add_rows([held, received.at[1]], made, 0, rows)
        copies.send(made, out)
        copies.drain()

    only_on(active, run)


def second_sum(section, kept, received):
    held = (kept.shape[-2:], BF)
    return call(
        functools.partial(second_sum_kernel, section, kept.shape[-2]),
        "second_sum",
        [held],
        [ANY],
        [kept, received],
        [HBM, VMEM],
        [held, held],
        2,
        16,
    )[0]


def far_sums_kernel(active, kept, received, own_o, far_o, held, own, made, sems):
    def run():
        copies = Copies(sems)
        got = {k: copies.fetch(kept.at[k], held.at[k]) for k in (1, 0)}
        got[1].wait()
        add_rows([held.at[1], received.at[1]], made, 0, 384)
        copies.send(made, far_o)
        got[0].wait()
        add_rows([held.at[0], received.at[0]], own, 0, 384)
        copies.send(own, own_o)
        copies.drain()

    only_on(active, run)


def far_sums(section, kept, received):
    shape = kept.shape[1:]
    return call(
        functools.partial(far_sums_kernel, section),
        "far_sums",
        [(shape, F32), (shape, BF)],
        [ANY] * 2,
        [kept, received],
        [ANY, VMEM],
        [((2, *shape), BF), (shape, F32), (shape, BF)],
        3,
        16,
    )


def last_section_kernel(active, own_h, near, far, ffn_h, ffn_far, sums_o, ffn_o, own, ffn, total, ffn_total, sems):
    def run():
        copies = Copies(sems)
        got = [copies.fetch(own_h, own), copies.fetch(ffn_h, ffn)]
        for cp in got:
            cp.wait()
        add_rows([own, near.at[0], far], total, 0, 208)
        copies.send(total, sums_o)
        add_rows([ffn, ffn_far], ffn_total, 0, 384)
        copies.send(ffn_total, ffn_o)
        copies.drain()

    only_on(active, run)


def last_section(section, own, near, far, ffn, ffn_far):
    shapes = [((208, D), F32), ((384, D), F32)]
    return call(
        functools.partial(last_section_kernel, section),
        "last_section_sums",
        shapes,
        [ANY] * 2,
        [own, near, far, ffn, ffn_far],
        [ANY, VMEM, VMEM, ANY, VMEM],
        shapes * 2,
        3,
        20,
    )


def add_terms(copies, first, done, own, total, base=0):
    count = own.shape[0]
    here = lax.axis_index("section")

    @pl.when(here == 0)
    def _():
        copies.fetch(first[0], own).wait()
        add_rows([own, *first[1:]], total, 0, count)

    @pl.when(here != 0)
    def _():
        copies.fetch(done.at[pl.ds(base, count), :], total).wait()


def ffn_total_kernel(own_h, far, done, down_o, own_o, x_o, near_o, both_o, own, total, sems):
    add_terms(Copies(sems), (own_h, far), done, own, total)
    own_o[...] = total[0:48, :]
    near_o[...] = total[48:96, :].astype(BF)
    x_o[...] = total[96:144, :].astype(BF)
    both_o[...] = total[144:192, :].astype(BF)
    down_o[...] = total[192:384, :]


def last_totals_kernel(own_h, near, far, done, up_own, up_x, up_near, up_both, *refs):
    qkv_o, out_o, up_o, bias_o, gain_o, query_o, up_bias_o, loss_o = refs[:8]
    own, total, sems = refs[8:]
    copies = Copies(sems)
    z, x, _ = place_bits()
    for jx, jn, part in ((0, 0, up_own), (1, 0, up_x), (0, 1, up_near), (1, 1, up_both)):
        for h in range(2):
            units = 768 * (jnp.bitwise_xor(z % 2, jn) + 2 * h) + 384 * jnp.bitwise_xor(x, jx)
            up_o[:, pl.ds(pl.multiple_of(units, 128), 384)] = part[:, 384 * h : 384 * (h + 1)].astype(F32)
    add_terms(copies, (own_h, near.at[0], far), done, own, total)
    for t in range(3):
        qkv_o[:, D * t : D * (t + 1)] = total[48 * t : 48 * (t + 1), :]
    out_o[...] = total[144:192, :]
    bias_o[...] = total[192:197, :48]
    gain_o[...] = total[197:199, :48]
    query_o[...] = total[199:200, :48]
    up_bias_o[...] = total[200:201, :192]
    loss_o[...] = jnp.broadcast_to(jnp.sum(total[201:202, :], axis=-1, keepdims=True), loss_o.shape)


def after(value, *others):
    return lax.optimization_barrier((value, others))[0]


def near_z(block, section):
    return swap(block, section, 2, 0)


def far_z(block, section):
    return swap(block, section, 4, 0)


def ffn_totals(own, far, done):
    down, up_own, up_x, up_near, up_both = call(
        ffn_total_kernel,
        "ffn_total",
        [((192, D), F32), ((48, D), F32)] + [((48, D), BF)] * 3,
        [VMEM] * 5,
        [own, far, done],
        [ANY, VMEM, ANY],
        [((384, D), F32)] * 2,
        3,
        16,
    )
    return down, [up_own, swap(up_x, None, 1, 0), swap(up_near, None, 2, 0), swap(up_both, None, 3, 0)]


def last_totals(attention, done, up):
    outs = [(48, 3 * D), (48, D), (48, FF), (5, 48), (2, 48), (1, 48), (1, 192), (8, 128)]
    return call(
        last_totals_kernel,
        "last_totals",
        [(shape, F32) for shape in outs],
        [VMEM] * len(outs),
        [*attention, done, *up],
        [ANY, VMEM, VMEM, ANY] + [VMEM] * 4,
        [((208, D), F32)] * 2,
        4,
        16,
    )


def to_partners(block, section):
    by_x, by_z = swap(block, section, 1, 0), swap(block, section, 2, 0)
    return [by_x, by_z, swap(by_x, section, 2, 0)]


def body(
    query_crops,
    key_crops,
    query_lengths,
    key_lengths,
    positive,
    queue,
    qkv_weight,
    out_weight,
    up_weight,
    down_weight,
    biases,
    gains,
    up_biases,
    query_bias,
    key_qkv_weight,
    key_out_weight,
    key_up_weight,
    key_down_weight,
    key_biases,
    key_gains,
    key_up_biases,
):
    crops = query_crops.shape[0]
    rows = crops * SLOTS
    sections, dps, reps = [lax.axis_size(a) for a in AXES]
    fast = fast_mesh()
    crop_all = crops * dps * reps
    on_first = lax.axis_index("section") == 0
    dp, rep = lax.axis_index("dp"), lax.axis_index("rep")
    last = sections - 1

    def relay(block, distance):
        return lax.ppermute(block, "section", [(0, 1)] if distance > 0 else [(1, 0)])

    key_half, query_half = lax.optimization_barrier((relay(key_crops, -1), relay(query_crops, -1)))
    key_halves = (key_crops, key_half)
    query_halves = (query_crops, query_half)
    query_weights = [w[0] for w in (qkv_weight, out_weight, up_weight, down_weight)]
    key_weights = [w[0] for w in (key_qkv_weight, key_out_weight, key_up_weight, key_down_weight)]
    query_encoder = ("query", query_lengths, query_weights, (biases, gains, up_biases, query_bias))
    key_encoder = ("key", key_lengths, key_weights, (key_biases, key_gains, key_up_biases))

    key_middle, _, _ = forward(rows, 0, False, key_halves, None, [key_encoder])
    inv = call(
        functools.partial(queue_norm_kernel, last),
        "queue_norm",
        [((8, queue.shape[0]), F32)],
        [VMEM],
        [queue],
        [ANY],
        [(queue.shape, BF)],
        4,
    )[0]
    key_middle, inv = lax.optimization_barrier((key_middle, inv))
    key_middle = relay(key_middle, 1)
    query_middle, _, every_key = forward(rows, None, False, query_halves, key_middle, [query_encoder, key_encoder])
    query_middle = relay(query_middle, 1)

    near_flips = [(0, 1), (1, 0), (1, 1)]
    if fast:
        near_keys = [swap(every_key, None, *f) for f in near_flips]
    step = forward(rows, None, True, query_halves, query_middle, [query_encoder])
    query_pooled = step[1]
    qkv, prob, row_scale, ctx, n1, r1, first, hid, slope, n2, r2 = step[3:]

    if fast:
        near_keys, query_pooled = lax.optimization_barrier((near_keys, query_pooled))
        every_key = jnp.concatenate([every_key, *near_keys], axis=0)
        keys = [every_key] + [swap(every_key, None, 2 * k, 0) for k in range(1, 4)]
    else:
        for flip in flips():
            every_key = jnp.concatenate([every_key, swap(every_key, None, *flip)], axis=0)
        keys = [every_key]
    firsts = [first] + (to_partners(first, None) if fast else [])

    pooled_grad, lost = call(
        functools.partial(loss_kernel, last, crops, crop_all),
        "contrast",
        [((8, D), F32), ((8, 128), F32)],
        [VMEM] * 2,
        [positive, query_pooled, inv, queue, *keys],
        [SMEM] + [VMEM] * (3 + len(keys)),
        [((crops * dps * reps, D), F32)],
        8,
        16,
    )

    def data_part(active, pooled, dy):
        wqkv, wout, wup, wdown = query_weights
        return data_backward(
            active, pooled, query_lengths, dy, gains, n2, r2, wdown, slope, wup, n1, r1, wout, qkv, prob, row_scale, wqkv
        )

    def attention_part(active, vec, grad_bup, datt, dqkv, term):
        return attention_weights(active, query_halves, query_middle, ctx, datt, dqkv, (vec, grad_bup, term))

    def ffn_part(active, hid_rows, ddowns, dup):
        _, _, wup, wdown = query_weights
        return ffn_weights(active, firsts, ddowns, hid_rows, dup, wup, wdown, up_biases)

    def small_rows(vec, grad_bup, term):
        picked = [vec[k : k + 1] for k in VECTOR_ROWS]
        lost_row = jnp.concatenate([term[0:1]] * (D // 128), axis=1)
        return jnp.concatenate(picked + [grad_bup[0:1].reshape(FF // D, D), lost_row], axis=0)

    vec1, bup1, ddown, dup, datt, dqkv, dmiddle = data_part(last, True, pooled_grad)
    ddowns = [ddown] + (to_partners(ddown, last) if fast else [])
    dmiddle = relay(dmiddle, -1)
    lost_first = relay(lost, -1)
    if fast:
        datt = after(datt, dmiddle, lost_first, *firsts[1:])
    attention1 = attention_part(last, vec1, bup1, datt, dqkv, lost)
    if fast:
        kp1, sp1, kq1, sq1 = attention1
        ap1 = swap(after(sp1, ddowns[1]), last, 1, 0)
        aq1 = swap(sq1, last, 0, 1)
    ffn1 = ffn_part(last, after(hid, *attention1), ddowns, dup)
    if fast:
        kf1, sf1 = ffn1
        f1 = swap(sf1, last, 0, 1)
        kp1, fp1, kq1, fq1 = half_sums(last, kp1, ap1, kq1, after(aq1, sf1))
        bp1 = swap(fp1, last, 0, 1)
        bq1 = swap(fq1, last, 1, 0)
        own1, far1 = far_sums(last, kf1, after(f1, fp1))
        p1 = slot_sums(last, [kp1, after(bp1, far1)], [kq1, bq1])
        dmiddle = after(dmiddle, far1, *p1)
        ddown = early_down(0, dmiddle, n2, r2, gains)
        partners = [swap(ddown, 0, 1, 0), swap(ddown, 0, 2, 0)]
        dmiddle = after(dmiddle, ddown)
    vec0, bup0, ddown, dup, datt, dqkv, dx = data_part(0, False, dmiddle)
    half = SLOTS // sections
    dx = dx.reshape(crops, SLOTS, D)
    dx_half = dx[:, half:]
    if fast:
        far1 = far_z(far1, last)
        n1z = near_z(p1[2], last)
        datt = after(datt, far1, n1z, *partners)
        partners.append(swap(after(partners[0], dx), 0, 2, 0))
    attention0 = attention_part(0, vec0, bup0, datt, dqkv, lost_first)
    ffn0 = ffn_part(0, after(hid, *attention0), [ddown] + (partners if fast else []), dup)

    if fast:
        kp0, sp0, kq0, sq0 = attention0
        ap0 = swap(after(sp0, partners[2]), 0, 1, 0)
        aq0 = swap(sq0, 0, 0, 1)
        kf0, sf0 = ffn0
        f0 = swap(sf0, 0, 0, 1)
        kp0, fp0, kq0, fq0 = half_sums(0, kp0, ap0, kq0, after(aq0, kf0))
        bp0 = swap(fp0, 0, 0, 1)
        bq0 = swap(fq0, 0, 1, 0)
        m1 = second_sum(last, p1[1], after(n1z, fp0))
        sums_last, ffn_last = last_section(last, p1[0], n1z, far_z(m1, last), own1, far1)
        own0, far0 = far_sums(0, kf0, after(f0, m1))
        far0 = far_z(far0, 0)
        q0 = slot_sums(0, [kp0, after(bp0, own0)], [kq0, bq0])
        l0z = near_z(q0[2], 0)
        grad_down, up = ffn_totals(after(own0, *q0), far0, ffn_last)
        m0 = second_sum(0, q0[1], after(l0z, grad_down))
        dx_half = after(dx_half, m0)
        summed = last_totals([q0[0], l0z, far_z(m0, 0)], sums_last, up)
        grad_qkv, grad_out, grad_up, bias, gain, query_part, up_part, loss_row = summed
        loss_row = loss_row[0]
    else:
        grad_up, grad_down, grad_qkv, grad_out = [
            lax.psum_scatter(jnp.where(on_first, a, b).astype(F32), ("dp", "rep"), scatter_dimension=0, tiled=True)
            for a, b in zip([*ffn0, *attention0], [*ffn1, *attention1])
        ]
        small = jnp.where(on_first, small_rows(vec0, bup0, lost_first), small_rows(vec1, bup1, lost))
        for flip in flips():
            small = small + swap(small, None, *flip)
        place = dp * reps + rep
        width, up_width = D // (dps * reps), FF // (dps * reps)
        mine = lax.dynamic_slice(small[:8], (0, place * width), (8, width))
        bias, gain, query_part = mine[:5], mine[5:7], mine[7:]
        up_part = lax.dynamic_slice(small[8:12].reshape(1, FF), (0, place * up_width), (1, up_width))
        loss_row = small[12, :128]
    crops_grad = jnp.where(on_first, dx[:, :half], relay(dx_half, 1)).astype(F32)
    return (
        loss_row[:1],
        crops_grad,
        grad_qkv[None],
        grad_out[None],
        grad_up[None],
        grad_down[None],
        bias[None],
        gain[None],
        up_part,
        query_part,
    )


def solution(mesh):
    crop = P(("dp", "rep"), "section", None)
    per_crop = P(("dp", "rep"))
    layer3 = P("section", None, None)
    layer2 = P("section", None)
    placed = (
        (crop, crop, per_crop, per_crop, per_crop, P())
        + (layer3,) * 6
        + (layer2,) * 2
        + (layer3,) * 6
        + (layer2,)
    )
    shared3 = P("section", ("dp", "rep"), None)
    return jax.shard_map(
        body,
        mesh=mesh,
        in_specs=placed,
        out_specs=(
            P(),
            crop,
            shared3,
            shared3,
            shared3,
            shared3,
            P("section", None, ("dp", "rep")),
            P("section", None, ("dp", "rep")),
            P("section", ("dp", "rep")),
            P("section", ("dp", "rep")),
        ),
        check_vma=False,
    )
```

```python
import functools

import jax
import jax.numpy as jnp
from jax import lax
from jax.experimental import pallas as pl
from jax.experimental.pallas import tpu as pltpu
from jax.sharding import PartitionSpec as P

F32 = jnp.float32
BF = jnp.bfloat16
MASKED = -1e30
D = 768
FF = 3072
SLOTS = 256
PAIRS = 6
MIB = 2**20
SEMS = 112
P_ROWS, Q_ROWS = 96, 112
ALPHA = 1.0


def dot(a, b):
    return lax.dot_general(a, b, (((1,), (0,)), ((), ())), preferred_element_type=F32)


def dot_nt(a, b):
    return lax.dot_general(a, b, (((1,), (1,)), ((), ())), preferred_element_type=F32)


def dot_tn(a, b):
    return lax.dot_general(a, b, (((0,), (0,)), ((), ())), preferred_element_type=F32)


def gelu_parts(x, want_slope):
    share = 0.5 + 0.5 * lax.erf(x * 0.7071067811865476)
    if not want_slope:
        return x * share, None
    return x * share, share + (0.3989422804014327 * x) * jnp.exp(-0.5 * (x * x))


def norm_parts(z):
    mean = jnp.mean(z, axis=-1, keepdims=True)
    c = z - mean
    var = jnp.mean(c * c, axis=-1, keepdims=True)
    r = lax.rsqrt(var + 1e-12)
    return c * r, r


def head_masks(scale):
    lane = lax.broadcasted_iota(jnp.int32, (1, 128), 1)
    low = jnp.where(lane < 64, scale, 0.0).astype(BF)
    high = jnp.where(lane < 64, 0.0, scale).astype(BF)
    return low, high


def stack_heads(pair, scale):
    low, high = head_masks(scale)
    return jnp.concatenate([pair * low, pair * high], axis=0)


def side_by_side(stacked):
    half = stacked.shape[0] // 2
    return jnp.concatenate([stacked[:half], stacked[half:]], axis=1)


class Copies:
    def __init__(self, sems):
        self.sems, self.used, self.open = sems, 0, []

    def make(self, src, dst):
        self.used += 1
        return pltpu.make_async_copy(src, dst, self.sems.at[self.used - 1])

    def fetch(self, src, dst):
        cp = self.make(src, dst)
        cp.start()
        return cp

    def pick(self, by_section, dst):
        if by_section[0] is by_section[1]:
            return self.fetch(by_section[0], dst)
        sem = self.sems.at[self.used]
        self.used += 1
        here = lax.axis_index("section")

        @pl.when(here == 0)
        def _():
            pltpu.make_async_copy(by_section[0], dst, sem).start()

        @pl.when(here != 0)
        def _():
            pltpu.make_async_copy(by_section[1], dst, sem).start()

        return pltpu.make_async_copy(by_section[0], dst, sem)

    def send(self, src, dst):
        self.open.append(self.fetch(src, dst))

    def drain(self):
        for cp in self.open:
            cp.wait()


def only_on(section, run):
    if section is None:
        run()
    else:
        pl.when(lax.axis_index("section") == section)(run)


VMEM = pl.BlockSpec(memory_space=pltpu.VMEM)
ANY = pl.BlockSpec(memory_space=pl.ANY)
HBM = pl.BlockSpec(memory_space=pltpu.HBM)
SMEM = pl.BlockSpec(memory_space=pltpu.SMEM)
sd = jax.ShapeDtypeStruct


def call(kernel, name, outs, out_specs, ins, in_specs, scratch, micros, limit=56):
    return pl.pallas_call(
        kernel,
        out_shape=[sd(*o) for o in outs],
        in_specs=in_specs,
        out_specs=out_specs,
        scratch_shapes=[pltpu.VMEM(*s) for s in scratch] + [pltpu.SemaphoreType.DMA((SEMS,))],
        compiler_params=pltpu.CompilerParams(vmem_limit_bytes=limit * MIB),
        cost_estimate=pl.CostEstimate(flops=int(micros * ALPHA * 1.15e9), bytes_accessed=1000, transcendentals=0),
        name=name,
    )(*ins)


def saved_shapes(rows):
    crops = rows // SLOTS
    return [
        ((rows, 3 * D), BF),
        ((PAIRS * crops, 2 * SLOTS, SLOTS), BF),
        ((2 * SLOTS, 128), F32),
        ((rows, D), BF),
        ((rows, D), BF),
        ((rows, 128), F32),
        ((rows, D), BF),
        ((rows, FF), BF),
        ((rows, FF), BF),
        ((rows, D), BF),
        ((rows, 128), F32),
    ]


def fetch_rows(copies, refs, kinds, x):
    waits = []
    half = refs[0].shape[1] if "halves" in kinds else SLOTS // 2
    for c in range(x.shape[0] // SLOTS):
        for h in range(SLOTS // half):
            at = slice(SLOTS * c + half * h, SLOTS * c + half * (h + 1))
            options = []
            if "halves" in kinds:
                options.append(refs[h].at[c])
            if "whole" in kinds:
                options.append(refs[-1].at[at, :])
            waits.append(copies.pick((options[0], options[-1]), x.at[at, :]))
    return waits


def read_vectors(refs, key):
    if key:
        b, g, up = refs
        rows = b[0].astype(F32)
        rows = [rows[i : i + 1] for i in range(6)]
    else:
        b, g, up, q = refs
        rows = b[0].astype(F32)
        rows = [q[...].astype(F32)] + [rows[i : i + 1] for i in range(5)]
    gains = g[0].astype(F32)
    return rows + [gains[0:1], gains[1:2]], up[...].astype(F32)


def load_vectors(refs, kinds, vec, bup):
    sets = []
    for kind in kinds:
        n = 3 if kind == "key" else 4
        sets.append(read_vectors(refs[:n], kind == "key"))
        refs = refs[n:]
    here = lax.axis_index("section")
    for i in range(8):
        row = sets[0][0][i]
        if len(sets) == 2:
            row = jnp.where(here == 0, row, sets[1][0][i])
        vec[i : i + 1, :] = row
    up = sets[0][1]
    if len(sets) == 2:
        up = jnp.where(here == 0, up, sets[1][1])
    bup[...] = up


def forward_kernel(rows, active, save, x_kinds, sets, *refs):
    def run():
        forward_body(rows, save, x_kinds, sets, *refs)

    only_on(active, run)


def forward_body(rows, save, x_kinds, sets, *refs):
    crops = rows // SLOTS
    lens_refs, refs = refs[: len(sets)], refs[len(sets) :]
    here = lax.axis_index("section")
    if len(sets) == 2:
        lens = [jnp.where(here == 0, lens_refs[0][c], lens_refs[1][c]) for c in range(crops)]
    else:
        lens = [lens_refs[0][c] for c in range(crops)]
    n_x = (2 if "halves" in x_kinds else 0) + (1 if "whole" in x_kinds else 0)
    x_refs, refs = refs[:n_x], refs[n_x:]
    w_refs, refs = refs[: 4 * len(sets)], refs[4 * len(sets) :]
    n_v = sum(3 if k == "key" else 4 for k in sets)
    v_refs, refs = refs[:n_v], refs[n_v:]
    y_ref, pool_ref, unit_ref = refs[:3]
    refs = refs[3:]
    if save:
        (qkv_o, prob_o, inv_o, ctx_o, n1_o, r1_o, first_o, hid_o, slope_o, n2_o, r2_o) = refs[:11]
        refs = refs[11:]
    (x, wqkv, wout, wup, wdown, ctx, zbuf, first, hid, vec, bup) = refs[:11]
    refs = refs[11:]
    if save:
        (qkv, prob, inv_all, n1, r1, slope, n2, r2) = refs[:8]
        refs = refs[8:]
        inv_all[...] = jnp.zeros_like(inv_all)
    copies = Copies(refs[0])
    got_x = fetch_rows(copies, x_refs, x_kinds, x)
    pairs = [(w_refs[i], w_refs[4 + i] if len(sets) == 2 else w_refs[i]) for i in range(4)]
    got_qkv = copies.pick(pairs[0], wqkv)
    load_vectors(v_refs, sets, vec, bup)
    for cp in got_x:
        cp.wait()
    got_qkv.wait()
    got_out = copies.pick(pairs[1], wout)
    got_up = copies.pick(pairs[2], wup)
    got_down = copies.pick(pairs[3], wdown)
    keycol = lax.broadcasted_iota(jnp.int32, (1, SLOTS), 1)
    lane = lax.broadcasted_iota(jnp.int32, (1, 128), 1)
    gain1, gain2 = vec[6:7], vec[7:8]

    def heads(i, carry):
        thirds = []
        for j in range(3):
            cols = pl.ds(pl.multiple_of(D * j + 256 * i, 256), 256)
            part = dot(x[...], wqkv[:, cols])
            if j != 1:
                at = pl.ds(pl.multiple_of(256 * i, 256), 256)
                part = part + vec[j // 2 : j // 2 + 1, at]
            part = part.astype(BF)
            if save:
                qkv[:, cols] = part
            thirds.append(part)
        for c in range(crops):
            crop = slice(SLOTS * c, SLOTS * (c + 1))
            for pr in range(2):
                qp, kp, vp = [t[crop, 128 * pr : 128 * (pr + 1)] for t in thirds]
                scores = jnp.where(keycol < lens[c], dot_nt(stack_heads(qp, 0.125), kp), MASKED)
                e = jnp.exp(scores - jnp.max(scores, axis=-1, keepdims=True))
                inv = pl.reciprocal(jnp.sum(e, axis=-1, keepdims=True))
                e = e.astype(BF)
                if save:
                    unit = PAIRS * c + 2 * i + pr
                    prob[unit] = e
                    inv_all[...] = jnp.where(lane == unit, inv, inv_all[...])
                at = pl.ds(pl.multiple_of(256 * i + 128 * pr, 128), 128)
                both = dot(e, vp) * inv
                ctx[crop, at] = jnp.where(lane < 64, both[:SLOTS], both[SLOTS:]).astype(BF)
        return carry

    lax.fori_loop(0, 3, heads, 0)
    if save:
        copies.send(qkv, qkv_o)
        copies.send(prob, prob_o)
        copies.send(inv_all, inv_o)
        copies.send(ctx, ctx_o)
    got_out.wait()
    for j in range(3):
        cols = slice(256 * j, 256 * (j + 1))
        zbuf[:, cols] = x[:, cols].astype(F32) + dot(ctx[...], wout[:, cols]) + vec[2:3, cols]
    block = 64
    steps = rows // block

    def first_norm(i, carry):
        at = pl.ds(pl.multiple_of(i * block, block), block)
        n, r = norm_parts(zbuf[at, :])
        f = (n * gain1 + vec[3:4]).astype(BF)
        first[at, :] = f
        zbuf[at, :] = f.astype(F32) + vec[4:5]
        if save:
            n1[at, :] = n.astype(BF)
            r1[at, :] = jnp.broadcast_to(r, (block, 128))
        return carry

    lax.fori_loop(0, steps, first_norm, 0, unroll=True)
    if save:
        copies.send(n1, n1_o)
        copies.send(r1, r1_o)
        copies.send(first, first_o)
    got_up.wait()
    got_down.wait()

    def down_part(k):
        cols = slice(512 * k, 512 * (k + 1))
        zbuf[...] += dot(hid[:, cols], wdown[cols, :])

    for i in range(12):
        cols = slice(256 * i, 256 * (i + 1))
        g, slope_part = gelu_parts(dot(first[...], wup[:, cols]) + bup[:, cols], save)
        hid[:, cols] = g.astype(BF)
        if save:
            slope[:, cols] = slope_part.astype(BF)
        if i % 2 and i > 2:
            down_part(i // 2 - 1)
    if save:
        copies.send(hid, hid_o)
        copies.send(slope, slope_o)
    down_part(5)
    pool_ref[...] = jnp.zeros_like(pool_ref)
    per_crop = SLOTS // block
    for i in range(steps):
        at = slice(i * block, (i + 1) * block)
        n, r = norm_parts(zbuf[at, :])
        f = n * gain2 + vec[5:6]
        y_ref[at, :] = f.astype(BF)
        if save:
            n2[at, :] = n.astype(BF)
            r2[at, :] = jnp.broadcast_to(r, (block, 128))
        c = i // per_crop
        token = lax.broadcasted_iota(jnp.int32, (block, 1), 0) + (i % per_crop) * block
        part = jnp.sum(jnp.where(token < lens[c], f, 0.0), axis=0, keepdims=True)
        pool_ref[c : c + 1, :] += part / lens[c].astype(F32)
    pooled = pool_ref[:crops]
    unit_ref[...] = pooled * lax.rsqrt(jnp.sum(pooled * pooled, axis=-1, keepdims=True) + 1e-6)
    if save:
        copies.send(n2, n2_o)
        copies.send(r2, r2_o)
    copies.drain()


def forward(rows, active, save, halves, whole, encoders):
    x_kinds = (("halves",) if halves else ()) + (("whole",) if whole is not None else ())
    xs = list(halves or ()) + ([whole] if whole is not None else [])
    lens = [e[1] for e in encoders]
    weights = [w for e in encoders for w in e[2]]
    vectors = [v for e in encoders for v in e[3]]
    outs = [((rows, D), BF), ((8, D), F32), ((rows // SLOTS, D), F32)]
    out_specs = [VMEM] * 3
    scratch = [
        ((rows, D), BF),
        ((D, 3 * D), BF),
        ((D, D), BF),
        ((D, FF), BF),
        ((FF, D), BF),
        ((rows, D), BF),
        ((rows, D), F32),
        ((rows, D), BF),
        ((rows, FF), BF),
        ((8, D), F32),
        ((1, FF), F32),
    ]
    if save:
        kept = saved_shapes(rows)
        outs += kept
        out_specs += [ANY] * len(kept)
        scratch += [kept[i] for i in (0, 1, 2, 4, 5, 8, 9, 10)]
    return call(
        functools.partial(forward_kernel, rows, active, save, x_kinds, [e[0] for e in encoders]),
        "layer_forward",
        outs,
        out_specs,
        [*lens, *xs, *weights, *vectors],
        [SMEM] * len(lens) + [ANY] * (len(xs) + len(weights)) + [VMEM] * len(vectors),
        scratch,
        20 if save else 18,
    )


def split3(v):
    hi = v.astype(BF)
    rest = v - hi.astype(F32)
    mid = rest.astype(BF)
    lo = (rest - mid.astype(F32)).astype(BF)
    return hi, mid, lo


def stack3(v):
    parts = split3(v)
    return jnp.concatenate(list(parts) + [jnp.zeros_like(parts[0])] * 5, axis=0)


def unstack3(rows, n):
    return rows[:n] + rows[n : 2 * n] + rows[2 * n : 3 * n]


def queue_norm_kernel(active, queue_h, inv_ref, queue, sems):
    def run():
        Copies(sems).fetch(queue_h, queue).wait()

        def step(i, carry):
            at = pl.ds(pl.multiple_of(i * 512, 512), 512)
            v = queue[at, :].astype(F32)
            sq = v * v
            hi = sq.astype(BF)
            lo = (sq - hi.astype(F32)).astype(BF)
            ones = jnp.ones((8, D), BF)
            total = dot_nt(ones, hi) + dot_nt(ones, lo)
            inv_ref[:, at] = lax.rsqrt(total + 1e-6)
            return carry

        lax.fori_loop(0, queue.shape[0] // 512, step, 0)

    only_on(active, run)


def loss_kernel(active, crops, count, positive, pooled, inv, queue, *refs):
    *key_refs, grad_ref, loss_ref, keys, sems = refs

    def run():
        at = 0
        for r in key_refs:
            keys[at : at + r.shape[0], :] = r[...]
            at += r.shape[0]
        place = lax.axis_index("dp") * lax.axis_size("rep") + lax.axis_index("rep")
        picked = []
        for c in range(crops):
            index = positive[c]
            row = jnp.bitwise_xor(index // crops, place) * crops + index % crops
            picked.append(keys[pl.ds(row, 1), :])
        v = pooled[:crops]
        r = lax.rsqrt(jnp.sum(v * v, axis=-1, keepdims=True) + 1e-6)
        u = v * r
        k = jnp.concatenate(picked, axis=0)
        near = jnp.sum(u * k, axis=-1, keepdims=True) * 20.0
        inv_row = inv[0:1]
        far = unstack3(dot_nt(stack3(u), queue[...]), crops) * (inv_row * 20.0)
        top = jnp.maximum(near, jnp.max(far, axis=-1, keepdims=True))
        e_near = jnp.exp(near - top)
        e_far = jnp.exp(far - top)
        total = e_near + jnp.sum(e_far, axis=-1, keepdims=True)
        share = 20.0 / (total * count)
        d_u = unstack3(dot(stack3(e_far * inv_row * share), queue[...]), crops)
        d_u = d_u + (e_near - total) * share * k
        grad = r * (d_u - u * jnp.sum(u * d_u, axis=-1, keepdims=True))
        grad_ref[...] = jnp.zeros_like(grad_ref)
        grad_ref[:crops] = grad
        lost = jnp.sum(top + jnp.log(total) - near, axis=0, keepdims=True) / count
        loss_ref[...] = jnp.broadcast_to(lost, loss_ref.shape)

    only_on(active, run)


def norm_back(dy, gain, n, r):
    dn = dy * gain
    return r * (dn - jnp.mean(dn, axis=-1, keepdims=True) - n * jnp.mean(dn * n, axis=-1, keepdims=True))


def column_sum(v):
    return jnp.sum(v, axis=0, keepdims=True)


def fast_mesh():
    return lax.axis_size("dp") == 8 and lax.axis_size("rep") == 2


def place_bits():
    dp, rep = lax.axis_index("dp"), lax.axis_index("rep")
    return dp // 2, dp % 2, rep


CHUNK = 512


def early_down_kernel(rows, active, dy, n2, r2, gains, ddown_o):
    def run():
        gain = gains[0].astype(F32)[1:2]
        for i in range(rows // 64):
            at = slice(64 * i, 64 * (i + 1))
            ddown_o[at] = norm_back(dy[at].astype(F32), gain, n2[at].astype(F32), r2[at, 0:1]).astype(BF)

    only_on(active, run)


def early_down(active, dy, n2, r2, gains):
    return call(
        lambda *refs: early_down_kernel(n2.shape[0], active, *refs[:-1]),
        "early_down",
        [(n2.shape, BF)],
        [VMEM],
        [dy, n2, r2, gains],
        [VMEM] * 4,
        [],
        3,
    )[0]


def data_backward_kernel(rows, active, pooled, halves, lens, dy, gains, *refs):
    def run():
        n2_h, r2_h, wdown_h, slope_h, wup_h, n1_h, r1_h, wout_h, qkv_h, prob_h, inv_h, wqkv_h = refs[:12]
        vec, bup, ddown_o, dup_o, datt_o, dqkv_o, *dx_o = refs[12 : 19 + halves]
        refs_ = refs[19 + halves :]
        n2, r2, wdown, slope, wup, n1, r1, wout, qkv, prob, inv, wqkv = refs_[:12]
        acc, ddown, dup, datt, dqkv, dx, sems = refs_[12:]
        copies = Copies(sems)
        got_n2, got_r2 = copies.fetch(n2_h, n2), copies.fetch(r2_h, r2)
        got = []
        for i in range(FF // CHUNK):
            cols = slice(CHUNK * i, CHUNK * (i + 1))
            got.append(
                [
                    copies.fetch(wdown_h.at[cols, :], wdown.at[cols, :]),
                    copies.fetch(slope_h.at[:, cols], slope.at[:, cols]),
                    copies.fetch(wup_h.at[:, cols], wup.at[:, cols]),
                ]
            )
        got_n1 = [copies.fetch(n1_h, n1), copies.fetch(r1_h, r1), copies.fetch(wout_h, wout)]
        got_qkv = [copies.fetch(qkv_h, qkv), copies.fetch(prob_h, prob), copies.fetch(inv_h, inv)]
        got_w = copies.fetch(wqkv_h, wqkv)
        vec[...] = jnp.zeros_like(vec)
        gain1, gain2 = gains[0].astype(F32)[0:1], gains[0].astype(F32)[1:2]
        block = 64
        per_crop = SLOTS // block
        got_n2.wait()
        got_r2.wait()
        for i in range(rows // block):
            at = slice(block * i, block * (i + 1))
            c = i // per_crop
            if pooled:
                token = lax.broadcasted_iota(jnp.int32, (block, 1), 0) + (i % per_crop) * block
                grow = jnp.where(token < lens[c], 1.0 / lens[c].astype(F32), 0.0) * dy[c : c + 1]
            else:
                grow = dy[at].astype(F32)
            n = n2[at].astype(F32)
            ds = norm_back(grow, gain2, n, r2[at, 0:1])
            low_ds = ds.astype(BF)
            acc[at] = ds
            ddown[at] = low_ds
            vec[0:1] += column_sum(grow * n)
            vec[1:2] += column_sum(grow)
            vec[2:3] += column_sum(low_ds.astype(F32))
        copies.send(ddown, ddown_o)
        for i in range(FF // CHUNK):
            cols = slice(CHUNK * i, CHUNK * (i + 1))
            for cp in got[i]:
                cp.wait()
            up = (dot_nt(ddown[...], wdown[cols, :]) * slope[:, cols].astype(F32)).astype(BF)
            dup[:, cols] = up
            copies.send(dup.at[:, cols], dup_o.at[:, cols])
            bup[:, cols] = jnp.broadcast_to(column_sum(up.astype(F32)), (8, CHUNK))
            for r in range(2):
                at = slice(rows // 2 * r, rows // 2 * (r + 1))
                acc[at, :] += dot_nt(up[at], wup[:, cols])
        for cp in got_n1:
            cp.wait()
        for i in range(rows // block):
            at = slice(block * i, block * (i + 1))
            n = n1[at].astype(F32)
            dfirst = acc[at]
            ds = norm_back(dfirst, gain1, n, r1[at, 0:1])
            low_ds = ds.astype(BF)
            acc[at] = ds
            datt[at] = low_ds
            vec[3:4] += column_sum(dfirst * n)
            vec[4:5] += column_sum(dfirst)
            vec[5:6] += column_sum(low_ds.astype(F32))
        copies.send(datt, datt_o)
        dctx = dot_nt(datt[...], wout[...]).astype(BF)
        for cp in got_qkv:
            cp.wait()
        for c in range(rows // SLOTS):
            crop = slice(SLOTS * c, SLOTS * (c + 1))
            for pr in range(PAIRS):
                cols = [slice(D * j + 128 * pr, D * j + 128 * (pr + 1)) for j in range(3)]
                unit = PAIRS * c + pr
                qp, kp, vp = [qkv[crop, t] for t in cols]
                dcs = stack_heads(dctx[crop, 128 * pr : 128 * (pr + 1)], 1.0)
                scale = inv[:, unit : unit + 1]
                e = prob[unit]
                pf = e.astype(F32) * scale
                weighted = pf * dot_nt(dcs, vp)
                ds = (weighted - pf * jnp.sum(weighted, axis=-1, keepdims=True)).astype(BF)
                dqkv[crop, cols[0]] = dot(side_by_side(ds), stack_heads(kp, 0.125)).astype(BF)
                dqkv[crop, cols[1]] = dot_tn(ds, stack_heads(qp, 0.125)).astype(BF)
                dqkv[crop, cols[2]] = dot_tn(e, (dcs * scale).astype(BF)).astype(BF)
        got_w.wait()
        for j in range(3):
            cols = slice(256 * j, 256 * (j + 1))
            dx[:, cols] = (dot_nt(dqkv[...], wqkv[cols, :]) + acc[:, cols]).astype(BF)
        if halves:
            for c in range(rows // SLOTS):
                for h, out in enumerate(dx_o):
                    size = SLOTS // 2
                    copies.send(dx.at[pl.ds(SLOTS * c + size * h, size), :], out.at[c])
        else:
            copies.send(dx, dx_o[0])
        copies.send(dqkv, dqkv_o)
        vec[6:7] = column_sum(dqkv[:, :D].astype(F32))
        vec[7:8] = column_sum(dqkv[:, 2 * D :].astype(F32))
        copies.drain()

    only_on(active, run)


def data_backward(active, pooled, halves, lens, dy, gains, n2, r2, wdown, slope, wup, n1, r1, wout, qkv, prob, inv, wqkv):
    rows = n1.shape[0]
    held = [n2, r2, wdown, slope, wup, n1, r1, wout, qkv, prob, inv, wqkv]
    wide_rows = ((rows, D), BF)
    dx_shapes = [((rows // SLOTS, SLOTS // 2, D), BF)] * 2 if halves else [wide_rows]
    return call(
        functools.partial(data_backward_kernel, rows, active, pooled, halves),
        "data_backward",
        [((8, D), F32), ((8, FF), F32), wide_rows, ((rows, FF), BF), wide_rows, ((rows, 3 * D), BF)] + dx_shapes,
        [VMEM] * 2 + [ANY] * (4 + len(dx_shapes)),
        [lens, dy, gains, *held],
        [SMEM, VMEM, VMEM] + [ANY] * len(held),
        [(h.shape, h.dtype) for h in held]
        + [((rows, D), F32), wide_rows, ((rows, FF), BF), wide_rows, ((rows, 3 * D), BF), wide_rows],
        26,
    )


def ffn_weights_kernel(rows, active, fast, *refs):
    def run():
        groups = 4 if fast else 1
        firsts, refs_ = refs[:groups], refs[groups:]
        ddowns, refs_ = refs_[:groups], refs_[groups:]
        hid_h, dup_h, *refs_ = refs_
        if fast:
            wup_h, wdown_h, bup_h, keep, send, *refs_ = refs_
            first, ddown, hid, dup, gup, gdown, wup, wdown, bup, sems = refs_
        else:
            up_o, down_o, first, ddown, hid, dup, gup, gdown, sems = refs_
        copies = Copies(sems)
        own = slice(0, rows)
        at = [slice(rows * k, rows * (k + 1)) for k in range(groups)]
        got_first = [copies.fetch(h, first.at[r, :]) for h, r in zip(firsts, at)]
        parts = range(FF // 384)
        if fast:
            z, x, y = place_bits()
            parts = (1, 0)
            got_first.append(copies.fetch(bup_h, bup))
        blocks = {}
        for i in parts:
            here = slice(384 * i, 384 * (i + 1))
            there = pl.ds(pl.multiple_of(768 * jnp.bitwise_xor(z, 2 * i) + 384 * x, 128), 384) if fast else here
            block = [copies.fetch(wup_h.at[:, there], wup.at[:, here])] if fast else []
            if i == parts[0]:
                got_ddown = [copies.fetch(h, ddown.at[r, :]) for h, r in zip(ddowns, at)]
            if fast:
                block.append(copies.fetch(wdown_h.at[there, :], wdown.at[here, :]))
            block.append(copies.fetch(hid_h.at[:, there], hid.at[own, here]))
            block.append(copies.fetch(dup_h.at[:, there], dup.at[own, here]))
            blocks[i] = block
        for cp in got_first:
            cp.wait()
        for i in parts:
            here = slice(384 * i, 384 * (i + 1))
            for cp in blocks[i]:
                cp.wait()
            if i == parts[0]:
                for cp in got_ddown:
                    cp.wait()
            if fast:
                zz = jnp.bitwise_xor(z, 2 * i)
                bias = bup[:, pl.ds(pl.multiple_of(768 * zz + 384 * x, 128), 384)].astype(F32)
                for r in at[1:]:
                    g, slope = gelu_parts(dot(first[r, :], wup[:, here]) + bias, True)
                    hid[r, here] = g.astype(BF)
                    dup[r, here] = (dot_nt(ddown[r, :], wdown[here, :]) * slope).astype(BF)
            gdown[here, :] = dot_tn(hid[:, here], ddown[...]).astype(BF)
            if fast:
                for jy, out in ((1, send), (0, keep)):
                    units = pl.ds(pl.multiple_of(384 * i + 192 * jnp.bitwise_xor(y, jy), 64), 192)
                    copies.send(gdown.at[units, :], out.at[i, 192:384, :])
            gup[:, here] = dot_tn(first[...], dup[:, here]).astype(BF)
            if fast:
                to_cols = pl.ds(pl.multiple_of(384 * (zz // 2), 128), 384)
                for jy, out in ((1, send), (0, keep)):
                    for jh in (1, 0):
                        for jx in range(2):
                            for jn in range(2):
                                oz = jnp.bitwise_xor(z, jn + 2 * jh)
                                owner = (oz * 2 + jnp.bitwise_xor(x, jx)) * 2 + jnp.bitwise_xor(y, jy)
                                rows48 = pl.ds(pl.multiple_of(48 * owner, 16), 48)
                                k = 2 * jx + jn
                                copies.send(gup.at[rows48, here], out.at[jh, 48 * k : 48 * (k + 1), to_cols])
        if not fast:
            copies.send(gup, up_o)
            copies.send(gdown, down_o)
        copies.drain()

    only_on(active, run)


def ffn_weights(active, firsts, ddowns, hid, dup, wup, wdown, bup):
    rows = hid.shape[0]
    fast = fast_mesh()
    ins = [*firsts, *ddowns, hid, dup]
    if fast:
        ins += [wup, wdown, bup]
        outs = [((2, 384, D), BF)] * 2
        tokens, units = 4 * rows, FF // 4
        extra = [((D, units), BF), ((units, D), BF), ((1, FF), BF)]
    else:
        outs = [((D, FF), BF), ((FF, D), BF)]
        tokens, units, extra = rows, FF, []
    return call(
        functools.partial(ffn_weights_kernel, rows, active, fast),
        "ffn_weights",
        outs,
        [ANY] * len(outs),
        ins,
        [ANY] * len(ins),
        [
            ((tokens, D), BF),
            ((tokens, D), BF),
            ((tokens, units), BF),
            ((tokens, units), BF),
            ((D, units), BF),
            ((units, D), BF),
        ]
        + extra,
        15,
    )


VECTOR_ROWS = (7, 5, 4, 2, 1, 3, 0, 6)


def attention_weights_kernel(rows, active, fast, x_kinds, *refs):
    def run():
        n_x = len(x_kinds) + 1
        x_refs = refs[:n_x]
        if fast:
            vec_h, bup_h, lost_h, *refs_ = refs[n_x:]
            ctx_h, datt_h, dqkv_h, p_keep, p_send, q_keep, q_send, x, ctx, datt, dqkv, gqkv, gout, tail, vec, bup, lost, sems = refs_
        else:
            ctx_h, datt_h, dqkv_h, out_qkv, out_out, x, ctx, datt, dqkv, gqkv, gout, sems = refs[n_x:]
        copies = Copies(sems)
        got = [copies.fetch(ctx_h, ctx), copies.fetch(datt_h, datt)]
        got_small = [copies.fetch(vec_h, vec), copies.fetch(bup_h, bup), copies.fetch(lost_h, lost)] if fast else []
        got_x = fetch_rows(copies, x_refs, x_kinds, x)
        got_x.append(copies.fetch(dqkv_h, dqkv))
        for cp in got_small:
            cp.wait()
        if fast:
            z, xx, y = place_bits()
            small = jnp.concatenate([vec[k : k + 1] for k in VECTOR_ROWS], axis=0)
            row = lax.broadcasted_iota(jnp.int32, (8, D), 0)
            lane = lax.broadcasted_iota(jnp.int32, (8, D), 1) - 3 * ((z * 2 + xx) * 2 + y)
            terms = [jnp.broadcast_to(t.astype(F32)[0:1, 0:1], (8, D)) for t in split3(lost[...])]
            lost_row = sum(jnp.where(lane == i, t, 0.0) for i, t in enumerate(terms))

        def slots():
            for j in range(15, -1, -1):
                jx, jy, jz = j // 8, j // 4 % 2, j % 4
                owner = (jnp.bitwise_xor(z, jz) * 2 + jnp.bitwise_xor(xx, jx)) * 2 + jnp.bitwise_xor(y, jy)
                p_out = (p_send if jx else p_keep).at[jy * 4 + jz]
                q_out = (q_send if jy else q_keep).at[jx * 4 + jz]
                yield j, owner, p_out, q_out

        def ship(part, third):
            for _, owner, p_out, q_out in slots():
                at = pl.ds(pl.multiple_of(48 * owner, 16), 48)
                to = (p_out.at[0:48, :], p_out.at[48:96, :], q_out.at[0:48, :], q_out.at[48:96, :])[third]
                copies.send(part.at[at, :], to)

        for cp in got:
            cp.wait()
        gout[...] = dot_tn(ctx[...], datt[...]).astype(BF)
        if fast:
            ship(gout, 3)
            for j, owner, _, q_out in slots():
                head = pltpu.roll(small, D - 48 * owner, 1)
                ups = pltpu.roll(bup[...], FF - 192 * owner, 1)[:, :D]
                other = jnp.where(row == 0, ups, jnp.where(row == 1, lost_row, 0.0))
                tail[j] = jnp.concatenate([head, other], axis=0).astype(BF)
                copies.send(tail.at[j], q_out.at[96:112, :])
        for cp in got_x:
            cp.wait()
        for t in range(3):
            for k in range(2):
                cols = slice(D * t + 384 * k, D * t + 384 * (k + 1))
                gqkv[:, cols] = dot_tn(x[...], dqkv[:, cols]).astype(BF)
            if fast:
                ship(gqkv.at[:, slice(D * t, D * (t + 1))], t)
        if not fast:
            copies.send(gqkv, out_qkv)
            copies.send(gout, out_out)
        copies.drain()

    only_on(active, run)


def attention_weights(active, halves, whole, ctx, datt, dqkv, small):
    rows = ctx.shape[0]
    fast = fast_mesh()
    x_kinds = ("halves", "whole")
    outs = [((8, n, D), BF) for n in (P_ROWS, P_ROWS, Q_ROWS, Q_ROWS)] if fast else [((D, 3 * D), BF), ((D, D), BF)]
    ins = [*halves, whole, *(small if fast else ()), ctx, datt, dqkv]
    in_specs = [ANY] * (9 if fast else 6)
    return call(
        functools.partial(attention_weights_kernel, rows, active, fast, x_kinds),
        "attention_weights",
        outs,
        [HBM] * len(outs),
        ins,
        in_specs,
        [((rows, D), BF)] * 3
        + [((rows, 3 * D), BF), ((D, 3 * D), BF), ((D, D), BF)]
        + ([((16, 16, D), BF), ((8, D), F32), ((8, FF), F32), ((8, 128), F32)] if fast else []),
        8,
    )


AXES = ("section", "dp", "rep")


def swap(block, section, dp_flip, rep_flip):
    dps, reps = lax.axis_size("dp"), lax.axis_size("rep")
    sections = range(lax.axis_size("section")) if section is None else [section]
    route = [
        ((s * dps + d) * reps + r, (s * dps + (d ^ dp_flip)) * reps + (r ^ rep_flip))
        for s in sections
        for d in range(dps)
        for r in range(reps)
    ]
    return lax.ppermute(block, AXES, route)


def flips():
    out, bit = [], 1
    while bit < lax.axis_size("rep"):
        out.append((0, bit))
        bit *= 2
    bit = 1
    while bit < lax.axis_size("dp"):
        out.append((bit, 0))
        bit *= 2
    return out


def add_rows(pieces, dst, at, count):
    def step(i, carry):
        here = pl.ds(pl.multiple_of(i * 16, 16), 16)
        total = pieces[0][here, :].astype(F32)
        for p in pieces[1:]:
            total = total + p[here, :].astype(F32)
        dst[pl.ds(pl.multiple_of(at + i * 16, 16), 16), :] = total.astype(dst.dtype)
        return carry

    tiles = count // 16
    lax.fori_loop(0, tiles, step, 0, unroll=next(u for u in (6, 5, 4, 7, 3, 2, 1) if tiles % u == 0))


def add_slots(kept, received, dst, first, rows):
    def step(i, carry):
        for t in range(rows // 16):
            here = slice(16 * t, 16 * (t + 1))
            total = kept[first + i, here, :].astype(F32) + received[first + i, here, :].astype(F32)
            dst[first + i, here, :] = total.astype(BF)
        return carry

    lax.fori_loop(0, 4, step, 0)


def half_sums_kernel(active, p_kept, p_received, q_kept, q_received, *refs):
    def run():
        p_near, p_far, q_near, q_far, p_held, q_held, p_made, q_made, sems = refs
        groups = (
            (p_kept, p_received, p_near, p_far, p_held, p_made, P_ROWS),
            (q_kept, q_received, q_near, q_far, q_held, q_made, Q_ROWS),
        )
        copies = Copies(sems)
        half = {True: pl.ds(4, 4), False: pl.ds(0, 4)}
        got = [(g, f, copies.fetch(g[0].at[half[f]], g[4].at[half[f]])) for f in (True, False) for g in groups]
        for (_, received, near, far, held, made, rows), is_far, cp in got:
            cp.wait()
            add_slots(held, received, made, 4 if is_far else 0, rows)
            copies.send(made.at[half[is_far]], far if is_far else near)
        copies.drain()

    only_on(active, run)


def half_sums(section, p_kept, p_received, q_kept, q_received):
    p, q = [((4, n, D), BF) for n in (P_ROWS, Q_ROWS)]
    p_all, q_all = [((8, n, D), BF) for n in (P_ROWS, Q_ROWS)]
    return call(
        functools.partial(half_sums_kernel, section),
        "half_sums",
        [p, p, q, q],
        [HBM] * 4,
        [p_kept, p_received, q_kept, q_received],
        [HBM, VMEM] * 2,
        [p_all, q_all, p_all, q_all],
        4,
        24,
    )


def slot_sums_kernel(active, counts, sizes, *refs):
    def run():
        groups, at = [], 0
        for n in counts:
            groups.append(refs[at : at + n])
            at += n
        own_o, kept_o, send_o = refs[at : at + 3]
        helds = refs[at + 3 : at + 3 + len(counts)]
        own, made, sems = refs[-3:]
        copies = Copies(sems)
        order = (1, 3, 2, 0)
        got = {k: [copies.fetch(g[0].at[k], h.at[k]) for g, h in zip(groups, helds)] for k in order}
        for k, out in zip(order, (send_o.at[0], send_o.at[1], kept_o, own_o)):
            to, base = made.at[k - 1] if k else own, 0
            for g, h, cp, size in zip(groups, helds, got[k], sizes):
                cp.wait()
                add_rows([h.at[k]] + [r.at[k] for r in g[1:]], to, base, size)
                base += size
            copies.send(to, out)
        copies.drain()

    only_on(active, run)


def slot_sums(section, *groups):
    sizes = [g[0].shape[1] for g in groups]
    shape = (sum(sizes), D)
    return call(
        functools.partial(slot_sums_kernel, section, [len(g) for g in groups], sizes),
        "slot_sums",
        [(shape, F32), (shape, BF), ((2, *shape), BF)],
        [ANY] * 3,
        [t for g in groups for t in g],
        [spec for g in groups for spec in [HBM] + [VMEM] * (len(g) - 1)],
        [((4, size, D), BF) for size in sizes] + [(shape, F32), ((3, *shape), BF)],
        3 * len(groups),
        24,
    )


def second_sum_kernel(active, rows, kept, received, out, held, made, sems):
    def run():
        copies = Copies(sems)
        copies.fetch(kept if len(kept.shape) == 2 else kept.at[1], held).wait()
        add_rows([held, received.at[1]], made, 0, rows)
        copies.send(made, out)
        copies.drain()

    only_on(active, run)


def second_sum(section, kept, received):
    held = (kept.shape[-2:], BF)
    return call(
        functools.partial(second_sum_kernel, section, kept.shape[-2]),
        "second_sum",
        [held],
        [ANY],
        [kept, received],
        [HBM, VMEM],
        [held, held],
        2,
        16,
    )[0]


def far_sums_kernel(active, kept, received, own_o, far_o, held, own, made, sems):
    def run():
        copies = Copies(sems)
        got = {k: copies.fetch(kept.at[k], held.at[k]) for k in (1, 0)}
        got[1].wait()
        add_rows([held.at[1], received.at[1]], made, 0, 384)
        copies.send(made, far_o)
        got[0].wait()
        add_rows([held.at[0], received.at[0]], own, 0, 384)
        copies.send(own, own_o)
        copies.drain()

    only_on(active, run)


def far_sums(section, kept, received):
    shape = kept.shape[1:]
    return call(
        functools.partial(far_sums_kernel, section),
        "far_sums",
        [(shape, F32), (shape, BF)],
        [ANY] * 2,
        [kept, received],
        [ANY, VMEM],
        [((2, *shape), BF), (shape, F32), (shape, BF)],
        3,
        16,
    )


def last_section_kernel(active, own_h, near, far, ffn_h, ffn_far, sums_o, ffn_o, own, ffn, total, ffn_total, sems):
    def run():
        copies = Copies(sems)
        got = [copies.fetch(own_h, own), copies.fetch(ffn_h, ffn)]
        for cp in got:
            cp.wait()
        add_rows([own, near.at[0], far], total, 0, 208)
        copies.send(total, sums_o)
        add_rows([ffn, ffn_far], ffn_total, 0, 384)
        copies.send(ffn_total, ffn_o)
        copies.drain()

    only_on(active, run)


def last_section(section, own, near, far, ffn, ffn_far):
    shapes = [((208, D), F32), ((384, D), F32)]
    return call(
        functools.partial(last_section_kernel, section),
        "last_section_sums",
        shapes,
        [ANY] * 2,
        [own, near, far, ffn, ffn_far],
        [ANY, VMEM, VMEM, ANY, VMEM],
        shapes * 2,
        3,
        20,
    )


def add_terms(copies, first, done, own, total, base=0):
    count = own.shape[0]
    here = lax.axis_index("section")

    @pl.when(here == 0)
    def _():
        copies.fetch(first[0], own).wait()
        add_rows([own, *first[1:]], total, 0, count)

    @pl.when(here != 0)
    def _():
        copies.fetch(done.at[pl.ds(base, count), :], total).wait()


def ffn_total_kernel(own_h, far, done, down_o, own_o, x_o, near_o, both_o, own, total, sems):
    add_terms(Copies(sems), (own_h, far), done, own, total)
    own_o[...] = total[0:48, :]
    near_o[...] = total[48:96, :].astype(BF)
    x_o[...] = total[96:144, :].astype(BF)
    both_o[...] = total[144:192, :].astype(BF)
    down_o[...] = total[192:384, :]


def last_totals_kernel(own_h, near, far, done, dx_h, dx_other, up_own, up_x, up_near, up_both, *refs):
    qkv_o, out_o, up_o, bias_o, gain_o, query_o, up_bias_o, loss_o, crops_o = refs[:9]
    own, total, dx, sems = refs[9:]
    copies = Copies(sems)
    got_dx = copies.pick((dx_h, dx_other), dx)
    z, x, _ = place_bits()
    for jx, jn, part in ((0, 0, up_own), (1, 0, up_x), (0, 1, up_near), (1, 1, up_both)):
        for h in range(2):
            units = 768 * (jnp.bitwise_xor(z % 2, jn) + 2 * h) + 384 * jnp.bitwise_xor(x, jx)
            up_o[:, pl.ds(pl.multiple_of(units, 128), 384)] = part[:, 384 * h : 384 * (h + 1)].astype(F32)
    add_terms(copies, (own_h, near.at[0], far), done, own, total)
    for t in range(3):
        qkv_o[:, D * t : D * (t + 1)] = total[48 * t : 48 * (t + 1), :]
    out_o[...] = total[144:192, :]
    bias_o[...] = total[192:197, :48]
    gain_o[...] = total[197:199, :48]
    query_o[...] = total[199:200, :48]
    up_bias_o[...] = total[200:201, :192]
    loss_o[...] = jnp.broadcast_to(jnp.sum(total[201:202, :], axis=-1, keepdims=True), loss_o.shape)
    got_dx.wait()
    for c in range(dx.shape[0]):
        crops_o[c] = dx[c].astype(F32)


def after(value, *others):
    return lax.optimization_barrier((value, others))[0]


def near_z(block, section):
    return swap(block, section, 2, 0)


def far_z(block, section):
    return swap(block, section, 4, 0)


def ffn_totals(own, far, done):
    down, up_own, up_x, up_near, up_both = call(
        ffn_total_kernel,
        "ffn_total",
        [((192, D), F32), ((48, D), F32)] + [((48, D), BF)] * 3,
        [VMEM] * 5,
        [own, far, done],
        [ANY, VMEM, ANY],
        [((384, D), F32)] * 2,
        3,
        16,
    )
    return down, [up_own, swap(up_x, None, 1, 0), swap(up_near, None, 2, 0), swap(up_both, None, 3, 0)]


def last_totals(attention, done, dx, dx_other, up):
    outs = [(48, 3 * D), (48, D), (48, FF), (5, 48), (2, 48), (1, 48), (1, 192), (8, 128), dx.shape]
    return call(
        last_totals_kernel,
        "last_totals",
        [(shape, F32) for shape in outs],
        [VMEM] * len(outs),
        [*attention, done, dx, dx_other, *up],
        [ANY, VMEM, VMEM] + [ANY] * 3 + [VMEM] * 4,
        [((208, D), F32)] * 2 + [(dx.shape, BF)],
        4,
        16,
    )


def to_partners(block, section):
    by_x, by_z = swap(block, section, 1, 0), swap(block, section, 2, 0)
    return [by_x, by_z, swap(by_x, section, 2, 0)]


def body(
    query_crops,
    key_crops,
    query_lengths,
    key_lengths,
    positive,
    queue,
    qkv_weight,
    out_weight,
    up_weight,
    down_weight,
    biases,
    gains,
    up_biases,
    query_bias,
    key_qkv_weight,
    key_out_weight,
    key_up_weight,
    key_down_weight,
    key_biases,
    key_gains,
    key_up_biases,
):
    crops = query_crops.shape[0]
    rows = crops * SLOTS
    sections, dps, reps = [lax.axis_size(a) for a in AXES]
    fast = fast_mesh()
    crop_all = crops * dps * reps
    on_first = lax.axis_index("section") == 0
    dp, rep = lax.axis_index("dp"), lax.axis_index("rep")
    last = sections - 1

    def relay(block, distance):
        return lax.ppermute(block, "section", [(0, 1)] if distance > 0 else [(1, 0)])

    key_half, query_half = lax.optimization_barrier((relay(key_crops, -1), relay(query_crops, -1)))
    key_halves = (key_crops, key_half)
    query_halves = (query_crops, query_half)
    query_weights = [w[0] for w in (qkv_weight, out_weight, up_weight, down_weight)]
    key_weights = [w[0] for w in (key_qkv_weight, key_out_weight, key_up_weight, key_down_weight)]
    query_encoder = ("query", query_lengths, query_weights, (biases, gains, up_biases, query_bias))
    key_encoder = ("key", key_lengths, key_weights, (key_biases, key_gains, key_up_biases))

    key_middle, _, _ = forward(rows, 0, False, key_halves, None, [key_encoder])
    inv = call(
        functools.partial(queue_norm_kernel, last),
        "queue_norm",
        [((8, queue.shape[0]), F32)],
        [VMEM],
        [queue],
        [ANY],
        [(queue.shape, BF)],
        4,
    )[0]
    key_middle, inv = lax.optimization_barrier((key_middle, inv))
    key_middle = relay(key_middle, 1)
    query_middle, _, every_key = forward(rows, None, False, query_halves, key_middle, [query_encoder, key_encoder])
    query_middle = relay(query_middle, 1)

    near_flips = [(0, 1), (1, 0), (1, 1)]
    if fast:
        near_keys = [swap(every_key, None, *f) for f in near_flips]
    step = forward(rows, None, True, query_halves, query_middle, [query_encoder])
    query_pooled = step[1]
    qkv, prob, row_scale, ctx, n1, r1, first, hid, slope, n2, r2 = step[3:]

    if fast:
        near_keys, query_pooled = lax.optimization_barrier((near_keys, query_pooled))
        every_key = jnp.concatenate([every_key, *near_keys], axis=0)
        keys = [every_key] + [swap(every_key, None, 2 * k, 0) for k in range(1, 4)]
    else:
        for flip in flips():
            every_key = jnp.concatenate([every_key, swap(every_key, None, *flip)], axis=0)
        keys = [every_key]
    firsts = [first] + (to_partners(first, None) if fast else [])

    pooled_grad, lost = call(
        functools.partial(loss_kernel, last, crops, crop_all),
        "contrast",
        [((8, D), F32), ((8, 128), F32)],
        [VMEM] * 2,
        [positive, query_pooled, inv, queue, *keys],
        [SMEM] + [VMEM] * (3 + len(keys)),
        [((crops * dps * reps, D), F32)],
        8,
        16,
    )

    def data_part(active, pooled, dy, halves=False):
        wqkv, wout, wup, wdown = query_weights
        return data_backward(
            active, pooled, halves, query_lengths, dy, gains, n2, r2, wdown, slope, wup, n1, r1, wout, qkv, prob, row_scale, wqkv
        )

    def attention_part(active, vec, grad_bup, datt, dqkv, term):
        return attention_weights(active, query_halves, query_middle, ctx, datt, dqkv, (vec, grad_bup, term))

    def ffn_part(active, hid_rows, ddowns, dup):
        _, _, wup, wdown = query_weights
        return ffn_weights(active, firsts, ddowns, hid_rows, dup, wup, wdown, up_biases)

    def small_rows(vec, grad_bup, term):
        picked = [vec[k : k + 1] for k in VECTOR_ROWS]
        lost_row = jnp.concatenate([term[0:1]] * (D // 128), axis=1)
        return jnp.concatenate(picked + [grad_bup[0:1].reshape(FF // D, D), lost_row], axis=0)

    vec1, bup1, ddown, dup, datt, dqkv, dmiddle = data_part(last, True, pooled_grad)
    ddowns = [ddown] + (to_partners(ddown, last) if fast else [])
    dmiddle = relay(dmiddle, -1)
    lost_first = relay(lost, -1)
    if fast:
        datt = after(datt, dmiddle, lost_first, *firsts[1:])
    attention1 = attention_part(last, vec1, bup1, datt, dqkv, lost)
    if fast:
        kp1, sp1, kq1, sq1 = attention1
        ap1 = swap(after(sp1, ddowns[1]), last, 1, 0)
        aq1 = swap(sq1, last, 0, 1)
    ffn1 = ffn_part(last, after(hid, *attention1), ddowns, dup)
    if fast:
        kf1, sf1 = ffn1
        f1 = swap(sf1, last, 0, 1)
        kp1, fp1, kq1, fq1 = half_sums(last, kp1, ap1, kq1, after(aq1, sf1))
        bp1 = swap(fp1, last, 0, 1)
        bq1 = swap(fq1, last, 1, 0)
        own1, far1 = far_sums(last, kf1, after(f1, fp1))
        p1 = slot_sums(last, [kp1, after(bp1, far1)], [kq1, bq1])
        dmiddle = after(dmiddle, far1, *p1)
        ddown = early_down(0, dmiddle, n2, r2, gains)
        partners = [swap(ddown, 0, 1, 0), swap(ddown, 0, 2, 0)]
        dmiddle = after(dmiddle, ddown)
    vec0, bup0, ddown, dup, datt, dqkv, dx, dx_half = data_part(0, False, dmiddle, True)
    if fast:
        far1 = far_z(far1, last)
        n1z = near_z(p1[2], last)
        datt = after(datt, far1, n1z, *partners)
        partners.append(swap(after(partners[0], dx), 0, 2, 0))
    attention0 = attention_part(0, vec0, bup0, datt, dqkv, lost_first)
    ffn0 = ffn_part(0, after(hid, *attention0), [ddown] + (partners if fast else []), dup)

    if fast:
        kp0, sp0, kq0, sq0 = attention0
        ap0 = swap(after(sp0, partners[2]), 0, 1, 0)
        aq0 = swap(sq0, 0, 0, 1)
        kf0, sf0 = ffn0
        f0 = swap(sf0, 0, 0, 1)
        kp0, fp0, kq0, fq0 = half_sums(0, kp0, ap0, kq0, after(aq0, kf0))
        bp0 = swap(fp0, 0, 0, 1)
        bq0 = swap(fq0, 0, 1, 0)
        m1 = second_sum(last, p1[1], after(n1z, fp0))
        own0, far0 = far_sums(0, kf0, after(f0, m1))
        far0 = far_z(far0, 0)
        q0 = slot_sums(0, [kp0, after(bp0, own0)], [kq0, bq0])
        l0z = near_z(q0[2], 0)
        sums_last, ffn_last = last_section(last, after(p1[0], far0), n1z, far_z(m1, last), own1, far1)
        m0 = second_sum(0, q0[1], after(l0z, ffn_last))
        h0 = far_z(m0, 0)
        grad_down, up = ffn_totals(after(own0, m0), far0, ffn_last)
        dx_half = relay(after(dx_half, m0), 1)
        summed = last_totals([q0[0], l0z, h0], sums_last, dx, dx_half, up)
        grad_qkv, grad_out, grad_up, bias, gain, query_part, up_part, loss_row, crops_grad = summed
        loss_row = loss_row[0]
    else:
        grad_up, grad_down, grad_qkv, grad_out = [
            lax.psum_scatter(jnp.where(on_first, a, b).astype(F32), ("dp", "rep"), scatter_dimension=0, tiled=True)
            for a, b in zip([*ffn0, *attention0], [*ffn1, *attention1])
        ]
        small = jnp.where(on_first, small_rows(vec0, bup0, lost_first), small_rows(vec1, bup1, lost))
        for flip in flips():
            small = small + swap(small, None, *flip)
        place = dp * reps + rep
        width, up_width = D // (dps * reps), FF // (dps * reps)
        mine = lax.dynamic_slice(small[:8], (0, place * width), (8, width))
        bias, gain, query_part = mine[:5], mine[5:7], mine[7:]
        up_part = lax.dynamic_slice(small[8:12].reshape(1, FF), (0, place * up_width), (1, up_width))
        loss_row = small[12, :128]
        crops_grad = jnp.where(on_first, dx, relay(dx_half, 1)).astype(F32)
    return (
        loss_row[:1],
        crops_grad,
        grad_qkv[None],
        grad_out[None],
        grad_up[None],
        grad_down[None],
        bias[None],
        gain[None],
        up_part,
        query_part,
    )


def solution(mesh):
    crop = P(("dp", "rep"), "section", None)
    per_crop = P(("dp", "rep"))
    layer3 = P("section", None, None)
    layer2 = P("section", None)
    placed = (
        (crop, crop, per_crop, per_crop, per_crop, P())
        + (layer3,) * 6
        + (layer2,) * 2
        + (layer3,) * 6
        + (layer2,)
    )
    shared3 = P("section", ("dp", "rep"), None)
    return jax.shard_map(
        body,
        mesh=mesh,
        in_specs=placed,
        out_specs=(
            P(),
            crop,
            shared3,
            shared3,
            shared3,
            shared3,
            P("section", None, ("dp", "rep")),
            P("section", None, ("dp", "rep")),
            P("section", ("dp", "rep")),
            P("section", ("dp", "rep")),
        ),
        check_vma=False,
    )
```

```python
import functools

import jax
import jax.numpy as jnp
from jax import lax
from jax.experimental import pallas as pl
from jax.experimental.pallas import tpu as pltpu
from jax.sharding import PartitionSpec as P

F32 = jnp.float32
BF = jnp.bfloat16
MASKED = -1e30
D = 768
FF = 3072
SLOTS = 256
PAIRS = 6
MIB = 2**20
SEMS = 112
P_ROWS, Q_ROWS = 96, 112
ALPHA = 1.0


def dot(a, b):
    return lax.dot_general(a, b, (((1,), (0,)), ((), ())), preferred_element_type=F32)


def dot_nt(a, b):
    return lax.dot_general(a, b, (((1,), (1,)), ((), ())), preferred_element_type=F32)


def dot_tn(a, b):
    return lax.dot_general(a, b, (((0,), (0,)), ((), ())), preferred_element_type=F32)


def gelu_parts(x, want_slope):
    share = 0.5 + 0.5 * lax.erf(x * 0.7071067811865476)
    if not want_slope:
        return x * share, None
    return x * share, share + (0.3989422804014327 * x) * jnp.exp(-0.5 * (x * x))


def norm_parts(z):
    mean = jnp.mean(z, axis=-1, keepdims=True)
    c = z - mean
    var = jnp.mean(c * c, axis=-1, keepdims=True)
    r = lax.rsqrt(var + 1e-12)
    return c * r, r


def head_masks(scale):
    lane = lax.broadcasted_iota(jnp.int32, (1, 128), 1)
    low = jnp.where(lane < 64, scale, 0.0).astype(BF)
    high = jnp.where(lane < 64, 0.0, scale).astype(BF)
    return low, high


def stack_heads(pair, scale):
    low, high = head_masks(scale)
    return jnp.concatenate([pair * low, pair * high], axis=0)


def side_by_side(stacked):
    half = stacked.shape[0] // 2
    return jnp.concatenate([stacked[:half], stacked[half:]], axis=1)


class Copies:
    def __init__(self, sems):
        self.sems, self.used, self.open = sems, 0, []

    def make(self, src, dst):
        self.used += 1
        return pltpu.make_async_copy(src, dst, self.sems.at[self.used - 1])

    def fetch(self, src, dst):
        cp = self.make(src, dst)
        cp.start()
        return cp

    def pick(self, by_section, dst):
        if by_section[0] is by_section[1]:
            return self.fetch(by_section[0], dst)
        sem = self.sems.at[self.used]
        self.used += 1
        here = lax.axis_index("section")

        @pl.when(here == 0)
        def _():
            pltpu.make_async_copy(by_section[0], dst, sem).start()

        @pl.when(here != 0)
        def _():
            pltpu.make_async_copy(by_section[1], dst, sem).start()

        return pltpu.make_async_copy(by_section[0], dst, sem)

    def send(self, src, dst):
        self.open.append(self.fetch(src, dst))

    def drain(self):
        for cp in self.open:
            cp.wait()


def only_on(section, run):
    if section is None:
        run()
    else:
        pl.when(lax.axis_index("section") == section)(run)


VMEM = pl.BlockSpec(memory_space=pltpu.VMEM)
ANY = pl.BlockSpec(memory_space=pl.ANY)
HBM = pl.BlockSpec(memory_space=pltpu.HBM)
SMEM = pl.BlockSpec(memory_space=pltpu.SMEM)
sd = jax.ShapeDtypeStruct


def call(kernel, name, outs, out_specs, ins, in_specs, scratch, micros, limit=56):
    return pl.pallas_call(
        kernel,
        out_shape=[sd(*o) for o in outs],
        in_specs=in_specs,
        out_specs=out_specs,
        scratch_shapes=[pltpu.VMEM(*s) for s in scratch] + [pltpu.SemaphoreType.DMA((SEMS,))],
        compiler_params=pltpu.CompilerParams(vmem_limit_bytes=limit * MIB),
        cost_estimate=pl.CostEstimate(flops=int(micros * ALPHA * 1.15e9), bytes_accessed=1000, transcendentals=0),
        name=name,
    )(*ins)


def saved_shapes(rows):
    crops = rows // SLOTS
    return [
        ((rows, 3 * D), BF),
        ((PAIRS * crops, 2 * SLOTS, SLOTS), BF),
        ((2 * SLOTS, 128), F32),
        ((rows, D), BF),
        ((rows, D), BF),
        ((rows, 128), F32),
        ((rows, D), BF),
        ((rows, FF), BF),
        ((rows, FF), BF),
        ((rows, D), BF),
        ((rows, 128), F32),
    ]


def fetch_rows(copies, refs, kinds, x):
    waits = []
    half = refs[0].shape[1] if "halves" in kinds else SLOTS // 2
    for c in range(x.shape[0] // SLOTS):
        for h in range(SLOTS // half):
            at = slice(SLOTS * c + half * h, SLOTS * c + half * (h + 1))
            options = []
            if "halves" in kinds:
                options.append(refs[h].at[c])
            if "whole" in kinds:
                options.append(refs[-1].at[at, :])
            waits.append(copies.pick((options[0], options[-1]), x.at[at, :]))
    return waits


def read_vectors(refs, key):
    if key:
        b, g, up = refs
        rows = b[0].astype(F32)
        rows = [rows[i : i + 1] for i in range(6)]
    else:
        b, g, up, q = refs
        rows = b[0].astype(F32)
        rows = [q[...].astype(F32)] + [rows[i : i + 1] for i in range(5)]
    gains = g[0].astype(F32)
    return rows + [gains[0:1], gains[1:2]], up[...].astype(F32)


def load_vectors(refs, kinds, vec, bup):
    sets = []
    for kind in kinds:
        n = 3 if kind == "key" else 4
        sets.append(read_vectors(refs[:n], kind == "key"))
        refs = refs[n:]
    here = lax.axis_index("section")
    for i in range(8):
        row = sets[0][0][i]
        if len(sets) == 2:
            row = jnp.where(here == 0, row, sets[1][0][i])
        vec[i : i + 1, :] = row
    up = sets[0][1]
    if len(sets) == 2:
        up = jnp.where(here == 0, up, sets[1][1])
    bup[...] = up


def forward_kernel(rows, active, save, x_kinds, sets, *refs):
    def run():
        forward_body(rows, save, x_kinds, sets, *refs)

    only_on(active, run)


def forward_body(rows, save, x_kinds, sets, *refs):
    crops = rows // SLOTS
    lens_refs, refs = refs[: len(sets)], refs[len(sets) :]
    here = lax.axis_index("section")
    if len(sets) == 2:
        lens = [jnp.where(here == 0, lens_refs[0][c], lens_refs[1][c]) for c in range(crops)]
    else:
        lens = [lens_refs[0][c] for c in range(crops)]
    n_x = (2 if "halves" in x_kinds else 0) + (1 if "whole" in x_kinds else 0)
    x_refs, refs = refs[:n_x], refs[n_x:]
    w_refs, refs = refs[: 4 * len(sets)], refs[4 * len(sets) :]
    n_v = sum(3 if k == "key" else 4 for k in sets)
    v_refs, refs = refs[:n_v], refs[n_v:]
    y_ref, pool_ref, unit_ref = refs[:3]
    refs = refs[3:]
    if save:
        (qkv_o, prob_o, inv_o, ctx_o, n1_o, r1_o, first_o, hid_o, slope_o, n2_o, r2_o) = refs[:11]
        refs = refs[11:]
    (x, wqkv, wout, wup, wdown, ctx, zbuf, first, hid, vec, bup) = refs[:11]
    refs = refs[11:]
    if save:
        (qkv, prob, inv_all, n1, r1, slope, n2, r2) = refs[:8]
        refs = refs[8:]
        inv_all[...] = jnp.zeros_like(inv_all)
    copies = Copies(refs[0])
    got_x = fetch_rows(copies, x_refs, x_kinds, x)
    pairs = [(w_refs[i], w_refs[4 + i] if len(sets) == 2 else w_refs[i]) for i in range(4)]
    got_qkv = copies.pick(pairs[0], wqkv)
    load_vectors(v_refs, sets, vec, bup)
    for cp in got_x:
        cp.wait()
    got_qkv.wait()
    got_out = copies.pick(pairs[1], wout)
    got_up = copies.pick(pairs[2], wup)
    got_down = copies.pick(pairs[3], wdown)
    keycol = lax.broadcasted_iota(jnp.int32, (1, SLOTS), 1)
    lane = lax.broadcasted_iota(jnp.int32, (1, 128), 1)
    gain1, gain2 = vec[6:7], vec[7:8]

    def heads(i, carry):
        thirds = []
        for j in range(3):
            cols = pl.ds(pl.multiple_of(D * j + 256 * i, 256), 256)
            part = dot(x[...], wqkv[:, cols])
            if j != 1:
                at = pl.ds(pl.multiple_of(256 * i, 256), 256)
                part = part + vec[j // 2 : j // 2 + 1, at]
            part = part.astype(BF)
            if save:
                qkv[:, cols] = part
            thirds.append(part)
        for c in range(crops):
            crop = slice(SLOTS * c, SLOTS * (c + 1))
            for pr in range(2):
                qp, kp, vp = [t[crop, 128 * pr : 128 * (pr + 1)] for t in thirds]
                scores = jnp.where(keycol < lens[c], dot_nt(stack_heads(qp, 0.125), kp), MASKED)
                e = jnp.exp(scores - jnp.max(scores, axis=-1, keepdims=True))
                inv = pl.reciprocal(jnp.sum(e, axis=-1, keepdims=True))
                e = e.astype(BF)
                if save:
                    unit = PAIRS * c + 2 * i + pr
                    prob[unit] = e
                    inv_all[...] = jnp.where(lane == unit, inv, inv_all[...])
                at = pl.ds(pl.multiple_of(256 * i + 128 * pr, 128), 128)
                both = dot(e, vp) * inv
                ctx[crop, at] = jnp.where(lane < 64, both[:SLOTS], both[SLOTS:]).astype(BF)
        return carry

    lax.fori_loop(0, 3, heads, 0)
    if save:
        copies.send(qkv, qkv_o)
        copies.send(prob, prob_o)
        copies.send(inv_all, inv_o)
        copies.send(ctx, ctx_o)
    got_out.wait()
    for j in range(3):
        cols = slice(256 * j, 256 * (j + 1))
        zbuf[:, cols] = x[:, cols].astype(F32) + dot(ctx[...], wout[:, cols]) + vec[2:3, cols]
    block = 64
    steps = rows // block

    def first_norm(i, carry):
        at = pl.ds(pl.multiple_of(i * block, block), block)
        n, r = norm_parts(zbuf[at, :])
        f = (n * gain1 + vec[3:4]).astype(BF)
        first[at, :] = f
        zbuf[at, :] = f.astype(F32) + vec[4:5]
        if save:
            n1[at, :] = n.astype(BF)
            r1[at, :] = jnp.broadcast_to(r, (block, 128))
        return carry

    lax.fori_loop(0, steps, first_norm, 0, unroll=True)
    if save:
        copies.send(n1, n1_o)
        copies.send(r1, r1_o)
        copies.send(first, first_o)
    got_up.wait()
    got_down.wait()

    def down_part(k):
        cols = slice(512 * k, 512 * (k + 1))
        zbuf[...] += dot(hid[:, cols], wdown[cols, :])

    for i in range(12):
        cols = slice(256 * i, 256 * (i + 1))
        g, slope_part = gelu_parts(dot(first[...], wup[:, cols]) + bup[:, cols], save)
        hid[:, cols] = g.astype(BF)
        if save:
            slope[:, cols] = slope_part.astype(BF)
        if i % 2 and i > 2:
            down_part(i // 2 - 1)
    if save:
        copies.send(hid, hid_o)
        copies.send(slope, slope_o)
    down_part(5)
    pool_ref[...] = jnp.zeros_like(pool_ref)
    per_crop = SLOTS // block
    for i in range(steps):
        at = slice(i * block, (i + 1) * block)
        n, r = norm_parts(zbuf[at, :])
        f = n * gain2 + vec[5:6]
        y_ref[at, :] = f.astype(BF)
        if save:
            n2[at, :] = n.astype(BF)
            r2[at, :] = jnp.broadcast_to(r, (block, 128))
        c = i // per_crop
        token = lax.broadcasted_iota(jnp.int32, (block, 1), 0) + (i % per_crop) * block
        part = jnp.sum(jnp.where(token < lens[c], f, 0.0), axis=0, keepdims=True)
        pool_ref[c : c + 1, :] += part / lens[c].astype(F32)
    pooled = pool_ref[:crops]
    unit_ref[...] = pooled * lax.rsqrt(jnp.sum(pooled * pooled, axis=-1, keepdims=True) + 1e-6)
    if save:
        copies.send(n2, n2_o)
        copies.send(r2, r2_o)
    copies.drain()


def forward(rows, active, save, halves, whole, encoders):
    x_kinds = (("halves",) if halves else ()) + (("whole",) if whole is not None else ())
    xs = list(halves or ()) + ([whole] if whole is not None else [])
    lens = [e[1] for e in encoders]
    weights = [w for e in encoders for w in e[2]]
    vectors = [v for e in encoders for v in e[3]]
    outs = [((rows, D), BF), ((8, D), F32), ((rows // SLOTS, D), F32)]
    out_specs = [VMEM] * 3
    scratch = [
        ((rows, D), BF),
        ((D, 3 * D), BF),
        ((D, D), BF),
        ((D, FF), BF),
        ((FF, D), BF),
        ((rows, D), BF),
        ((rows, D), F32),
        ((rows, D), BF),
        ((rows, FF), BF),
        ((8, D), F32),
        ((1, FF), F32),
    ]
    if save:
        kept = saved_shapes(rows)
        outs += kept
        out_specs += [ANY] * len(kept)
        scratch += [kept[i] for i in (0, 1, 2, 4, 5, 8, 9, 10)]
    return call(
        functools.partial(forward_kernel, rows, active, save, x_kinds, [e[0] for e in encoders]),
        "layer_forward",
        outs,
        out_specs,
        [*lens, *xs, *weights, *vectors],
        [SMEM] * len(lens) + [ANY] * (len(xs) + len(weights)) + [VMEM] * len(vectors),
        scratch,
        20 if save else 18,
    )


def split3(v):
    hi = v.astype(BF)
    rest = v - hi.astype(F32)
    mid = rest.astype(BF)
    lo = (rest - mid.astype(F32)).astype(BF)
    return hi, mid, lo


def stack3(v):
    parts = split3(v)
    return jnp.concatenate(list(parts) + [jnp.zeros_like(parts[0])] * 5, axis=0)


def unstack3(rows, n):
    return rows[:n] + rows[n : 2 * n] + rows[2 * n : 3 * n]


def queue_norm_kernel(active, queue_h, inv_ref, queue, sems):
    def run():
        Copies(sems).fetch(queue_h, queue).wait()

        def step(i, carry):
            at = pl.ds(pl.multiple_of(i * 512, 512), 512)
            v = queue[at, :].astype(F32)
            sq = v * v
            hi = sq.astype(BF)
            lo = (sq - hi.astype(F32)).astype(BF)
            ones = jnp.ones((8, D), BF)
            total = dot_nt(ones, hi) + dot_nt(ones, lo)
            inv_ref[:, at] = lax.rsqrt(total + 1e-6)
            return carry

        lax.fori_loop(0, queue.shape[0] // 512, step, 0)

    only_on(active, run)


def loss_kernel(active, crops, count, positive, pooled, inv, queue, *refs):
    *key_refs, grad_ref, loss_ref, keys, sems = refs

    def run():
        at = 0
        for r in key_refs:
            keys[at : at + r.shape[0], :] = r[...]
            at += r.shape[0]
        place = lax.axis_index("dp") * lax.axis_size("rep") + lax.axis_index("rep")
        picked = []
        for c in range(crops):
            index = positive[c]
            row = jnp.bitwise_xor(index // crops, place) * crops + index % crops
            picked.append(keys[pl.ds(row, 1), :])
        v = pooled[:crops]
        r = lax.rsqrt(jnp.sum(v * v, axis=-1, keepdims=True) + 1e-6)
        u = v * r
        k = jnp.concatenate(picked, axis=0)
        near = jnp.sum(u * k, axis=-1, keepdims=True) * 20.0
        inv_row = inv[0:1]
        far = unstack3(dot_nt(stack3(u), queue[...]), crops) * (inv_row * 20.0)
        top = jnp.maximum(near, jnp.max(far, axis=-1, keepdims=True))
        e_near = jnp.exp(near - top)
        e_far = jnp.exp(far - top)
        total = e_near + jnp.sum(e_far, axis=-1, keepdims=True)
        share = 20.0 / (total * count)
        d_u = unstack3(dot(stack3(e_far * inv_row * share), queue[...]), crops)
        d_u = d_u + (e_near - total) * share * k
        grad = r * (d_u - u * jnp.sum(u * d_u, axis=-1, keepdims=True))
        grad_ref[...] = jnp.zeros_like(grad_ref)
        grad_ref[:crops] = grad
        lost = jnp.sum(top + jnp.log(total) - near, axis=0, keepdims=True) / count
        loss_ref[...] = jnp.broadcast_to(lost, loss_ref.shape)

    only_on(active, run)


def norm_back(dy, gain, n, r):
    dn = dy * gain
    return r * (dn - jnp.mean(dn, axis=-1, keepdims=True) - n * jnp.mean(dn * n, axis=-1, keepdims=True))


def column_sum(v):
    return jnp.sum(v, axis=0, keepdims=True)


def fast_mesh():
    return lax.axis_size("dp") == 8 and lax.axis_size("rep") == 2


def place_bits():
    dp, rep = lax.axis_index("dp"), lax.axis_index("rep")
    return dp // 2, dp % 2, rep


CHUNK = 768


def early_down_kernel(rows, active, dy, n2, r2, gains, ddown_o):
    def run():
        gain = gains[0].astype(F32)[1:2]
        for i in range(rows // 64):
            at = slice(64 * i, 64 * (i + 1))
            ddown_o[at] = norm_back(dy[at].astype(F32), gain, n2[at].astype(F32), r2[at, 0:1]).astype(BF)

    only_on(active, run)


def early_down(active, dy, n2, r2, gains):
    return call(
        lambda *refs: early_down_kernel(n2.shape[0], active, *refs[:-1]),
        "early_down",
        [(n2.shape, BF)],
        [VMEM],
        [dy, n2, r2, gains],
        [VMEM] * 4,
        [],
        3,
    )[0]


def data_backward_kernel(rows, active, pooled, halves, lens, dy, gains, *refs):
    def run():
        n2_h, r2_h, wdown_h, slope_h, wup_h, n1_h, r1_h, wout_h, qkv_h, prob_h, inv_h, wqkv_h = refs[:12]
        vec, bup, ddown_o, dup_o, datt_o, dqkv_o, *dx_o = refs[12 : 19 + halves]
        refs_ = refs[19 + halves :]
        n2, r2, wdown, slope, wup, n1, r1, wout, qkv, prob, inv, wqkv = refs_[:12]
        acc, ddown, dup, datt, dqkv, dx, sems = refs_[12:]
        copies = Copies(sems)
        got_n2, got_r2 = copies.fetch(n2_h, n2), copies.fetch(r2_h, r2)
        got = []
        for i in range(FF // CHUNK):
            cols = slice(CHUNK * i, CHUNK * (i + 1))
            got.append(
                [
                    copies.fetch(wdown_h.at[cols, :], wdown.at[cols, :]),
                    copies.fetch(slope_h.at[:, cols], slope.at[:, cols]),
                    copies.fetch(wup_h.at[:, cols], wup.at[:, cols]),
                ]
            )
        got_n1 = [copies.fetch(n1_h, n1), copies.fetch(r1_h, r1), copies.fetch(wout_h, wout)]
        got_qkv = [copies.fetch(qkv_h, qkv), copies.fetch(prob_h, prob), copies.fetch(inv_h, inv)]
        got_w = copies.fetch(wqkv_h, wqkv)
        vec[...] = jnp.zeros_like(vec)
        gain1, gain2 = gains[0].astype(F32)[0:1], gains[0].astype(F32)[1:2]
        block = 64
        per_crop = SLOTS // block
        got_n2.wait()
        got_r2.wait()
        for i in range(rows // block):
            at = slice(block * i, block * (i + 1))
            c = i // per_crop
            if pooled:
                token = lax.broadcasted_iota(jnp.int32, (block, 1), 0) + (i % per_crop) * block
                grow = jnp.where(token < lens[c], 1.0 / lens[c].astype(F32), 0.0) * dy[c : c + 1]
            else:
                grow = dy[at].astype(F32)
            n = n2[at].astype(F32)
            ds = norm_back(grow, gain2, n, r2[at, 0:1])
            low_ds = ds.astype(BF)
            acc[at] = ds
            ddown[at] = low_ds
            vec[0:1] += column_sum(grow * n)
            vec[1:2] += column_sum(grow)
            vec[2:3] += column_sum(low_ds.astype(F32))
        copies.send(ddown, ddown_o)
        for i in range(FF // CHUNK):
            cols = slice(CHUNK * i, CHUNK * (i + 1))
            for cp in got[i]:
                cp.wait()
            up = (dot_nt(ddown[...], wdown[cols, :]) * slope[:, cols].astype(F32)).astype(BF)
            dup[:, cols] = up
            copies.send(dup.at[:, cols], dup_o.at[:, cols])
            bup[:, cols] = jnp.broadcast_to(column_sum(up.astype(F32)), (8, CHUNK))
            for r in range(2):
                at = slice(rows // 2 * r, rows // 2 * (r + 1))
                acc[at, :] += dot_nt(up[at], wup[:, cols])
        for cp in got_n1:
            cp.wait()
        for i in range(rows // block):
            at = slice(block * i, block * (i + 1))
            n = n1[at].astype(F32)
            dfirst = acc[at]
            ds = norm_back(dfirst, gain1, n, r1[at, 0:1])
            low_ds = ds.astype(BF)
            acc[at] = ds
            datt[at] = low_ds
            vec[3:4] += column_sum(dfirst * n)
            vec[4:5] += column_sum(dfirst)
            vec[5:6] += column_sum(low_ds.astype(F32))
        copies.send(datt, datt_o)
        dctx = dot_nt(datt[...], wout[...]).astype(BF)
        for cp in got_qkv:
            cp.wait()
        for c in range(rows // SLOTS):
            crop = slice(SLOTS * c, SLOTS * (c + 1))
            for pr in range(PAIRS):
                cols = [slice(D * j + 128 * pr, D * j + 128 * (pr + 1)) for j in range(3)]
                unit = PAIRS * c + pr
                qp, kp, vp = [qkv[crop, t] for t in cols]
                dcs = stack_heads(dctx[crop, 128 * pr : 128 * (pr + 1)], 1.0)
                scale = inv[:, unit : unit + 1]
                e = prob[unit]
                pf = e.astype(F32) * scale
                weighted = pf * dot_nt(dcs, vp)
                ds = (weighted - pf * jnp.sum(weighted, axis=-1, keepdims=True)).astype(BF)
                dqkv[crop, cols[0]] = dot(side_by_side(ds), stack_heads(kp, 0.125)).astype(BF)
                dqkv[crop, cols[1]] = dot_tn(ds, stack_heads(qp, 0.125)).astype(BF)
                dqkv[crop, cols[2]] = dot_tn(e, (dcs * scale).astype(BF)).astype(BF)
        got_w.wait()
        for j in range(3):
            cols = slice(256 * j, 256 * (j + 1))
            dx[:, cols] = (dot_nt(dqkv[...], wqkv[cols, :]) + acc[:, cols]).astype(BF)
        if halves:
            for c in range(rows // SLOTS):
                for h, out in enumerate(dx_o):
                    size = SLOTS // 2
                    copies.send(dx.at[pl.ds(SLOTS * c + size * h, size), :], out.at[c])
        else:
            copies.send(dx, dx_o[0])
        copies.send(dqkv, dqkv_o)
        vec[6:7] = column_sum(dqkv[:, :D].astype(F32))
        vec[7:8] = column_sum(dqkv[:, 2 * D :].astype(F32))
        copies.drain()

    only_on(active, run)


def data_backward(active, pooled, halves, lens, dy, gains, n2, r2, wdown, slope, wup, n1, r1, wout, qkv, prob, inv, wqkv):
    rows = n1.shape[0]
    held = [n2, r2, wdown, slope, wup, n1, r1, wout, qkv, prob, inv, wqkv]
    wide_rows = ((rows, D), BF)
    dx_shapes = [((rows // SLOTS, SLOTS // 2, D), BF)] * 2 if halves else [wide_rows]
    return call(
        functools.partial(data_backward_kernel, rows, active, pooled, halves),
        "data_backward",
        [((8, D), F32), ((8, FF), F32), wide_rows, ((rows, FF), BF), wide_rows, ((rows, 3 * D), BF)] + dx_shapes,
        [VMEM] * 2 + [ANY] * (4 + len(dx_shapes)),
        [lens, dy, gains, *held],
        [SMEM, VMEM, VMEM] + [ANY] * len(held),
        [(h.shape, h.dtype) for h in held]
        + [((rows, D), F32), wide_rows, ((rows, FF), BF), wide_rows, ((rows, 3 * D), BF), wide_rows],
        26,
    )


def ffn_weights_kernel(rows, active, fast, *refs):
    def run():
        groups = 4 if fast else 1
        firsts, refs_ = refs[:groups], refs[groups:]
        ddowns, refs_ = refs_[:groups], refs_[groups:]
        hid_h, dup_h, *refs_ = refs_
        if fast:
            wup_h, wdown_h, bup_h, keep, send, *refs_ = refs_
            first, ddown, hid, dup, gup, gdown, wup, wdown, bup, sems = refs_
        else:
            up_o, down_o, first, ddown, hid, dup, gup, gdown, sems = refs_
        copies = Copies(sems)
        own = slice(0, rows)
        at = [slice(rows * k, rows * (k + 1)) for k in range(groups)]
        got_first = [copies.fetch(h, first.at[r, :]) for h, r in zip(firsts, at)]
        parts = range(FF // 384)
        if fast:
            z, x, y = place_bits()
            parts = (1, 0)
            got_first.append(copies.fetch(bup_h, bup))
        blocks = {}
        for i in parts:
            here = slice(384 * i, 384 * (i + 1))
            there = pl.ds(pl.multiple_of(768 * jnp.bitwise_xor(z, 2 * i) + 384 * x, 128), 384) if fast else here
            block = [copies.fetch(wup_h.at[:, there], wup.at[:, here])] if fast else []
            if i == parts[0]:
                got_ddown = [copies.fetch(h, ddown.at[r, :]) for h, r in zip(ddowns, at)]
            if fast:
                block.append(copies.fetch(wdown_h.at[there, :], wdown.at[here, :]))
            block.append(copies.fetch(hid_h.at[:, there], hid.at[own, here]))
            block.append(copies.fetch(dup_h.at[:, there], dup.at[own, here]))
            blocks[i] = block
        for cp in got_first:
            cp.wait()
        for i in parts:
            here = slice(384 * i, 384 * (i + 1))
            for cp in blocks[i]:
                cp.wait()
            if i == parts[0]:
                for cp in got_ddown:
                    cp.wait()
            if fast:
                zz = jnp.bitwise_xor(z, 2 * i)
                bias = bup[:, pl.ds(pl.multiple_of(768 * zz + 384 * x, 128), 384)].astype(F32)
                for r in at[1:]:
                    g, slope = gelu_parts(dot(first[r, :], wup[:, here]) + bias, True)
                    hid[r, here] = g.astype(BF)
                    dup[r, here] = (dot_nt(ddown[r, :], wdown[here, :]) * slope).astype(BF)
            gdown[here, :] = dot_tn(hid[:, here], ddown[...]).astype(BF)
            if fast:
                for jy, out in ((1, send), (0, keep)):
                    units = pl.ds(pl.multiple_of(384 * i + 192 * jnp.bitwise_xor(y, jy), 64), 192)
                    copies.send(gdown.at[units, :], out.at[i, 192:384, :])
            gup[:, here] = dot_tn(first[...], dup[:, here]).astype(BF)
            if fast:
                to_cols = pl.ds(pl.multiple_of(384 * (zz // 2), 128), 384)
                for jy, out in ((1, send), (0, keep)):
                    for jh in (1, 0):
                        for jx in range(2):
                            for jn in range(2):
                                oz = jnp.bitwise_xor(z, jn + 2 * jh)
                                owner = (oz * 2 + jnp.bitwise_xor(x, jx)) * 2 + jnp.bitwise_xor(y, jy)
                                rows48 = pl.ds(pl.multiple_of(48 * owner, 16), 48)
                                k = 2 * jx + jn
                                copies.send(gup.at[rows48, here], out.at[jh, 48 * k : 48 * (k + 1), to_cols])
        if not fast:
            copies.send(gup, up_o)
            copies.send(gdown, down_o)
        copies.drain()

    only_on(active, run)


def ffn_weights(active, firsts, ddowns, hid, dup, wup, wdown, bup):
    rows = hid.shape[0]
    fast = fast_mesh()
    ins = [*firsts, *ddowns, hid, dup]
    if fast:
        ins += [wup, wdown, bup]
        outs = [((2, 384, D), BF)] * 2
        tokens, units = 4 * rows, FF // 4
        extra = [((D, units), BF), ((units, D), BF), ((1, FF), BF)]
    else:
        outs = [((D, FF), BF), ((FF, D), BF)]
        tokens, units, extra = rows, FF, []
    return call(
        functools.partial(ffn_weights_kernel, rows, active, fast),
        "ffn_weights",
        outs,
        [ANY] * len(outs),
        ins,
        [ANY] * len(ins),
        [
            ((tokens, D), BF),
            ((tokens, D), BF),
            ((tokens, units), BF),
            ((tokens, units), BF),
            ((D, units), BF),
            ((units, D), BF),
        ]
        + extra,
        15,
    )


VECTOR_ROWS = (7, 5, 4, 2, 1, 3, 0, 6)


def attention_weights_kernel(rows, active, fast, x_kinds, *refs):
    def run():
        n_x = len(x_kinds) + 1
        x_refs = refs[:n_x]
        if fast:
            vec_h, bup_h, lost_h, *refs_ = refs[n_x:]
            ctx_h, datt_h, dqkv_h, p_keep, p_send, q_keep, q_send, x, ctx, datt, dqkv, gqkv, gout, tail, vec, bup, lost, sems = refs_
        else:
            ctx_h, datt_h, dqkv_h, out_qkv, out_out, x, ctx, datt, dqkv, gqkv, gout, sems = refs[n_x:]
        copies = Copies(sems)
        got = [copies.fetch(ctx_h, ctx), copies.fetch(datt_h, datt)]
        got_small = [copies.fetch(vec_h, vec), copies.fetch(bup_h, bup), copies.fetch(lost_h, lost)] if fast else []
        got_x = fetch_rows(copies, x_refs, x_kinds, x)
        got_x.append(copies.fetch(dqkv_h, dqkv))
        for cp in got_small:
            cp.wait()
        if fast:
            z, xx, y = place_bits()
            small = jnp.concatenate([vec[k : k + 1] for k in VECTOR_ROWS], axis=0)
            row = lax.broadcasted_iota(jnp.int32, (8, D), 0)
            lane = lax.broadcasted_iota(jnp.int32, (8, D), 1) - 3 * ((z * 2 + xx) * 2 + y)
            terms = [jnp.broadcast_to(t.astype(F32)[0:1, 0:1], (8, D)) for t in split3(lost[...])]
            lost_row = sum(jnp.where(lane == i, t, 0.0) for i, t in enumerate(terms))

        def slots():
            for j in range(15, -1, -1):
                jx, jy, jz = j // 8, j // 4 % 2, j % 4
                owner = (jnp.bitwise_xor(z, jz) * 2 + jnp.bitwise_xor(xx, jx)) * 2 + jnp.bitwise_xor(y, jy)
                p_out = (p_send if jx else p_keep).at[jy * 4 + jz]
                q_out = (q_send if jy else q_keep).at[jx * 4 + jz]
                yield j, owner, p_out, q_out

        def ship(part, third):
            for _, owner, p_out, q_out in slots():
                at = pl.ds(pl.multiple_of(48 * owner, 16), 48)
                to = (p_out.at[0:48, :], p_out.at[48:96, :], q_out.at[0:48, :], q_out.at[48:96, :])[third]
                copies.send(part.at[at, :], to)

        for cp in got:
            cp.wait()
        gout[...] = dot_tn(ctx[...], datt[...]).astype(BF)
        if fast:
            ship(gout, 3)
            for j, owner, _, q_out in slots():
                head = pltpu.roll(small, D - 48 * owner, 1)
                ups = pltpu.roll(bup[...], FF - 192 * owner, 1)[:, :D]
                other = jnp.where(row == 0, ups, jnp.where(row == 1, lost_row, 0.0))
                tail[j] = jnp.concatenate([head, other], axis=0).astype(BF)
                copies.send(tail.at[j], q_out.at[96:112, :])
        for cp in got_x:
            cp.wait()
        for t in range(3):
            for k in range(2):
                cols = slice(D * t + 384 * k, D * t + 384 * (k + 1))
                gqkv[:, cols] = dot_tn(x[...], dqkv[:, cols]).astype(BF)
            if fast:
                ship(gqkv.at[:, slice(D * t, D * (t + 1))], t)
        if not fast:
            copies.send(gqkv, out_qkv)
            copies.send(gout, out_out)
        copies.drain()

    only_on(active, run)


def attention_weights(active, halves, whole, ctx, datt, dqkv, small):
    rows = ctx.shape[0]
    fast = fast_mesh()
    x_kinds = ("halves", "whole")
    outs = [((8, n, D), BF) for n in (P_ROWS, P_ROWS, Q_ROWS, Q_ROWS)] if fast else [((D, 3 * D), BF), ((D, D), BF)]
    ins = [*halves, whole, *(small if fast else ()), ctx, datt, dqkv]
    in_specs = [ANY] * (9 if fast else 6)
    return call(
        functools.partial(attention_weights_kernel, rows, active, fast, x_kinds),
        "attention_weights",
        outs,
        [HBM] * len(outs),
        ins,
        in_specs,
        [((rows, D), BF)] * 3
        + [((rows, 3 * D), BF), ((D, 3 * D), BF), ((D, D), BF)]
        + ([((16, 16, D), BF), ((8, D), F32), ((8, FF), F32), ((8, 128), F32)] if fast else []),
        8,
    )


AXES = ("section", "dp", "rep")


def swap(block, section, dp_flip, rep_flip):
    dps, reps = lax.axis_size("dp"), lax.axis_size("rep")
    sections = range(lax.axis_size("section")) if section is None else [section]
    route = [
        ((s * dps + d) * reps + r, (s * dps + (d ^ dp_flip)) * reps + (r ^ rep_flip))
        for s in sections
        for d in range(dps)
        for r in range(reps)
    ]
    return lax.ppermute(block, AXES, route)


def flips():
    out, bit = [], 1
    while bit < lax.axis_size("rep"):
        out.append((0, bit))
        bit *= 2
    bit = 1
    while bit < lax.axis_size("dp"):
        out.append((bit, 0))
        bit *= 2
    return out


def add_rows(pieces, dst, at, count):
    def step(i, carry):
        here = pl.ds(pl.multiple_of(i * 16, 16), 16)
        total = pieces[0][here, :].astype(F32)
        for p in pieces[1:]:
            total = total + p[here, :].astype(F32)
        dst[pl.ds(pl.multiple_of(at + i * 16, 16), 16), :] = total.astype(dst.dtype)
        return carry

    tiles = count // 16
    lax.fori_loop(0, tiles, step, 0, unroll=next(u for u in (6, 5, 4, 7, 3, 2, 1) if tiles % u == 0))


def add_slots(kept, received, dst, first, rows):
    def step(i, carry):
        for t in range(rows // 16):
            here = slice(16 * t, 16 * (t + 1))
            total = kept[first + i, here, :].astype(F32) + received[first + i, here, :].astype(F32)
            dst[first + i, here, :] = total.astype(BF)
        return carry

    lax.fori_loop(0, 4, step, 0)


def half_sums_kernel(active, p_kept, p_received, q_kept, q_received, *refs):
    def run():
        p_near, p_far, q_near, q_far, p_held, q_held, p_made, q_made, sems = refs
        groups = (
            (p_kept, p_received, p_near, p_far, p_held, p_made, P_ROWS),
            (q_kept, q_received, q_near, q_far, q_held, q_made, Q_ROWS),
        )
        copies = Copies(sems)
        half = {True: pl.ds(4, 4), False: pl.ds(0, 4)}
        got = [(g, f, copies.fetch(g[0].at[half[f]], g[4].at[half[f]])) for f in (True, False) for g in groups]
        for (_, received, near, far, held, made, rows), is_far, cp in got:
            cp.wait()
            add_slots(held, received, made, 4 if is_far else 0, rows)
            copies.send(made.at[half[is_far]], far if is_far else near)
        copies.drain()

    only_on(active, run)


def half_sums(section, p_kept, p_received, q_kept, q_received):
    p, q = [((4, n, D), BF) for n in (P_ROWS, Q_ROWS)]
    p_all, q_all = [((8, n, D), BF) for n in (P_ROWS, Q_ROWS)]
    return call(
        functools.partial(half_sums_kernel, section),
        "half_sums",
        [p, p, q, q],
        [HBM] * 4,
        [p_kept, p_received, q_kept, q_received],
        [HBM, VMEM] * 2,
        [p_all, q_all, p_all, q_all],
        4,
        24,
    )


def slot_sums_kernel(active, counts, sizes, *refs):
    def run():
        groups, at = [], 0
        for n in counts:
            groups.append(refs[at : at + n])
            at += n
        own_o, kept_o, send_o = refs[at : at + 3]
        helds = refs[at + 3 : at + 3 + len(counts)]
        own, made, sems = refs[-3:]
        copies = Copies(sems)
        order = (1, 3, 2, 0)
        got = {k: [copies.fetch(g[0].at[k], h.at[k]) for g, h in zip(groups, helds)] for k in order}
        for k, out in zip(order, (send_o.at[0], send_o.at[1], kept_o, own_o)):
            to, base = made.at[k - 1] if k else own, 0
            for g, h, cp, size in zip(groups, helds, got[k], sizes):
                cp.wait()
                add_rows([h.at[k]] + [r.at[k] for r in g[1:]], to, base, size)
                base += size
            copies.send(to, out)
        copies.drain()

    only_on(active, run)


def slot_sums(section, *groups):
    sizes = [g[0].shape[1] for g in groups]
    shape = (sum(sizes), D)
    return call(
        functools.partial(slot_sums_kernel, section, [len(g) for g in groups], sizes),
        "slot_sums",
        [(shape, F32), (shape, BF), ((2, *shape), BF)],
        [ANY] * 3,
        [t for g in groups for t in g],
        [spec for g in groups for spec in [HBM] + [VMEM] * (len(g) - 1)],
        [((4, size, D), BF) for size in sizes] + [(shape, F32), ((3, *shape), BF)],
        3 * len(groups),
        24,
    )


def second_sum_kernel(active, rows, kept, received, out, held, made, sems):
    def run():
        copies = Copies(sems)
        copies.fetch(kept if len(kept.shape) == 2 else kept.at[1], held).wait()
        add_rows([held, received.at[1]], made, 0, rows)
        copies.send(made, out)
        copies.drain()

    only_on(active, run)


def second_sum(section, kept, received):
    held = (kept.shape[-2:], BF)
    return call(
        functools.partial(second_sum_kernel, section, kept.shape[-2]),
        "second_sum",
        [held],
        [ANY],
        [kept, received],
        [HBM, VMEM],
        [held, held],
        2,
        16,
    )[0]


def far_sums_kernel(active, kept, received, own_o, far_o, held, own, made, sems):
    def run():
        copies = Copies(sems)
        got = {k: copies.fetch(kept.at[k], held.at[k]) for k in (1, 0)}
        got[1].wait()
        add_rows([held.at[1], received.at[1]], made, 0, 384)
        copies.send(made, far_o)
        got[0].wait()
        add_rows([held.at[0], received.at[0]], own, 0, 384)
        copies.send(own, own_o)
        copies.drain()

    only_on(active, run)


def far_sums(section, kept, received):
    shape = kept.shape[1:]
    return call(
        functools.partial(far_sums_kernel, section),
        "far_sums",
        [(shape, F32), (shape, BF)],
        [ANY] * 2,
        [kept, received],
        [ANY, VMEM],
        [((2, *shape), BF), (shape, F32), (shape, BF)],
        3,
        16,
    )


def last_section_kernel(active, own_h, near, far, ffn_h, ffn_far, sums_o, ffn_o, own, ffn, total, ffn_total, sems):
    def run():
        copies = Copies(sems)
        got = [copies.fetch(own_h, own), copies.fetch(ffn_h, ffn)]
        for cp in got:
            cp.wait()
        add_rows([own, near.at[0], far], total, 0, 208)
        copies.send(total, sums_o)
        add_rows([ffn, ffn_far], ffn_total, 0, 384)
        copies.send(ffn_total, ffn_o)
        copies.drain()

    only_on(active, run)


def last_section(section, own, near, far, ffn, ffn_far):
    shapes = [((208, D), F32), ((384, D), F32)]
    return call(
        functools.partial(last_section_kernel, section),
        "last_section_sums",
        shapes,
        [ANY] * 2,
        [own, near, far, ffn, ffn_far],
        [ANY, VMEM, VMEM, ANY, VMEM],
        shapes * 2,
        3,
        20,
    )


def add_terms(copies, first, done, own, total, base=0):
    count = own.shape[0]
    here = lax.axis_index("section")

    @pl.when(here == 0)
    def _():
        copies.fetch(first[0], own).wait()
        add_rows([own, *first[1:]], total, 0, count)

    @pl.when(here != 0)
    def _():
        copies.fetch(done.at[pl.ds(base, count), :], total).wait()


def ffn_total_kernel(own_h, far, done, down_o, own_o, x_o, near_o, both_o, own, total, sems):
    add_terms(Copies(sems), (own_h, far), done, own, total)
    own_o[...] = total[0:48, :]
    near_o[...] = total[48:96, :].astype(BF)
    x_o[...] = total[96:144, :].astype(BF)
    both_o[...] = total[144:192, :].astype(BF)
    down_o[...] = total[192:384, :]


def last_totals_kernel(own_h, near, far, done, dx_h, dx_other, up_own, up_x, up_near, up_both, *refs):
    qkv_o, out_o, up_o, bias_o, gain_o, query_o, up_bias_o, loss_o, crops_o = refs[:9]
    own, total, dx, sems = refs[9:]
    copies = Copies(sems)
    got_dx = copies.pick((dx_h, dx_other), dx)
    z, x, _ = place_bits()
    for jx, jn, part in ((0, 0, up_own), (1, 0, up_x), (0, 1, up_near), (1, 1, up_both)):
        for h in range(2):
            units = 768 * (jnp.bitwise_xor(z % 2, jn) + 2 * h) + 384 * jnp.bitwise_xor(x, jx)
            up_o[:, pl.ds(pl.multiple_of(units, 128), 384)] = part[:, 384 * h : 384 * (h + 1)].astype(F32)
    add_terms(copies, (own_h, near.at[0], far), done, own, total)
    for t in range(3):
        qkv_o[:, D * t : D * (t + 1)] = total[48 * t : 48 * (t + 1), :]
    out_o[...] = total[144:192, :]
    bias_o[...] = total[192:197, :48]
    gain_o[...] = total[197:199, :48]
    query_o[...] = total[199:200, :48]
    up_bias_o[...] = total[200:201, :192]
    loss_o[...] = jnp.broadcast_to(jnp.sum(total[201:202, :], axis=-1, keepdims=True), loss_o.shape)
    got_dx.wait()
    for c in range(dx.shape[0]):
        crops_o[c] = dx[c].astype(F32)


def after(value, *others):
    return lax.optimization_barrier((value, others))[0]


def near_z(block, section):
    return swap(block, section, 2, 0)


def far_z(block, section):
    return swap(block, section, 4, 0)


def ffn_totals(own, far, done):
    down, up_own, up_x, up_near, up_both = call(
        ffn_total_kernel,
        "ffn_total",
        [((192, D), F32), ((48, D), F32)] + [((48, D), BF)] * 3,
        [VMEM] * 5,
        [own, far, done],
        [ANY, VMEM, ANY],
        [((384, D), F32)] * 2,
        3,
        16,
    )
    return down, [up_own, swap(up_x, None, 1, 0), swap(up_near, None, 2, 0), swap(up_both, None, 3, 0)]


def last_totals(attention, done, dx, dx_other, up):
    outs = [(48, 3 * D), (48, D), (48, FF), (5, 48), (2, 48), (1, 48), (1, 192), (8, 128), dx.shape]
    return call(
        last_totals_kernel,
        "last_totals",
        [(shape, F32) for shape in outs],
        [VMEM] * len(outs),
        [*attention, done, dx, dx_other, *up],
        [ANY, VMEM, VMEM] + [ANY] * 3 + [VMEM] * 4,
        [((208, D), F32)] * 2 + [(dx.shape, BF)],
        4,
        16,
    )


def to_partners(block, section):
    by_x, by_z = swap(block, section, 1, 0), swap(block, section, 2, 0)
    return [by_x, by_z, swap(by_x, section, 2, 0)]


def body(
    query_crops,
    key_crops,
    query_lengths,
    key_lengths,
    positive,
    queue,
    qkv_weight,
    out_weight,
    up_weight,
    down_weight,
    biases,
    gains,
    up_biases,
    query_bias,
    key_qkv_weight,
    key_out_weight,
    key_up_weight,
    key_down_weight,
    key_biases,
    key_gains,
    key_up_biases,
):
    crops = query_crops.shape[0]
    rows = crops * SLOTS
    sections, dps, reps = [lax.axis_size(a) for a in AXES]
    fast = fast_mesh()
    crop_all = crops * dps * reps
    on_first = lax.axis_index("section") == 0
    dp, rep = lax.axis_index("dp"), lax.axis_index("rep")
    last = sections - 1

    def relay(block, distance):
        return lax.ppermute(block, "section", [(0, 1)] if distance > 0 else [(1, 0)])

    key_half, query_half = lax.optimization_barrier((relay(key_crops, -1), relay(query_crops, -1)))
    key_halves = (key_crops, key_half)
    query_halves = (query_crops, query_half)
    query_weights = [w[0] for w in (qkv_weight, out_weight, up_weight, down_weight)]
    key_weights = [w[0] for w in (key_qkv_weight, key_out_weight, key_up_weight, key_down_weight)]
    query_encoder = ("query", query_lengths, query_weights, (biases, gains, up_biases, query_bias))
    key_encoder = ("key", key_lengths, key_weights, (key_biases, key_gains, key_up_biases))

    key_middle, _, _ = forward(rows, 0, False, key_halves, None, [key_encoder])
    inv = call(
        functools.partial(queue_norm_kernel, last),
        "queue_norm",
        [((8, queue.shape[0]), F32)],
        [VMEM],
        [queue],
        [ANY],
        [(queue.shape, BF)],
        4,
    )[0]
    key_middle, inv = lax.optimization_barrier((key_middle, inv))
    key_middle = relay(key_middle, 1)
    query_middle, _, every_key = forward(rows, None, False, query_halves, key_middle, [query_encoder, key_encoder])
    query_middle = relay(query_middle, 1)

    near_flips = [(0, 1), (1, 0), (1, 1)]
    if fast:
        near_keys = [swap(every_key, None, *f) for f in near_flips]
    step = forward(rows, None, True, query_halves, query_middle, [query_encoder])
    query_pooled = step[1]
    qkv, prob, row_scale, ctx, n1, r1, first, hid, slope, n2, r2 = step[3:]

    if fast:
        near_keys, query_pooled = lax.optimization_barrier((near_keys, query_pooled))
        every_key = jnp.concatenate([every_key, *near_keys], axis=0)
        keys = [every_key] + [swap(every_key, None, 2 * k, 0) for k in range(1, 4)]
    else:
        for flip in flips():
            every_key = jnp.concatenate([every_key, swap(every_key, None, *flip)], axis=0)
        keys = [every_key]
    firsts = [first] + (to_partners(first, None) if fast else [])

    pooled_grad, lost = call(
        functools.partial(loss_kernel, last, crops, crop_all),
        "contrast",
        [((8, D), F32), ((8, 128), F32)],
        [VMEM] * 2,
        [positive, query_pooled, inv, queue, *keys],
        [SMEM] + [VMEM] * (3 + len(keys)),
        [((crops * dps * reps, D), F32)],
        8,
        16,
    )

    def data_part(active, pooled, dy, halves=False):
        wqkv, wout, wup, wdown = query_weights
        return data_backward(
            active, pooled, halves, query_lengths, dy, gains, n2, r2, wdown, slope, wup, n1, r1, wout, qkv, prob, row_scale, wqkv
        )

    def attention_part(active, vec, grad_bup, datt, dqkv, term):
        return attention_weights(active, query_halves, query_middle, ctx, datt, dqkv, (vec, grad_bup, term))

    def ffn_part(active, hid_rows, ddowns, dup):
        _, _, wup, wdown = query_weights
        return ffn_weights(active, firsts, ddowns, hid_rows, dup, wup, wdown, up_biases)

    def small_rows(vec, grad_bup, term):
        picked = [vec[k : k + 1] for k in VECTOR_ROWS]
        lost_row = jnp.concatenate([term[0:1]] * (D // 128), axis=1)
        return jnp.concatenate(picked + [grad_bup[0:1].reshape(FF // D, D), lost_row], axis=0)

    vec1, bup1, ddown, dup, datt, dqkv, dmiddle = data_part(last, True, pooled_grad)
    ddowns = [ddown] + (to_partners(ddown, last) if fast else [])
    dmiddle = relay(dmiddle, -1)
    lost_first = relay(lost, -1)
    if fast:
        datt = after(datt, dmiddle, lost_first, *firsts[1:])
    attention1 = attention_part(last, vec1, bup1, datt, dqkv, lost)
    if fast:
        kp1, sp1, kq1, sq1 = attention1
        ap1 = swap(after(sp1, ddowns[1]), last, 1, 0)
        aq1 = swap(sq1, last, 0, 1)
    ffn1 = ffn_part(last, after(hid, *attention1), ddowns, dup)
    if fast:
        kf1, sf1 = ffn1
        f1 = swap(sf1, last, 0, 1)
        kp1, fp1, kq1, fq1 = half_sums(last, kp1, ap1, kq1, after(aq1, sf1))
        bp1 = swap(fp1, last, 0, 1)
        bq1 = swap(fq1, last, 1, 0)
        own1, far1 = far_sums(last, kf1, after(f1, fp1))
        p1 = slot_sums(last, [kp1, after(bp1, far1)], [kq1, bq1])
        dmiddle = after(dmiddle, far1, *p1)
        ddown = early_down(0, dmiddle, n2, r2, gains)
        partners = [swap(ddown, 0, 1, 0), swap(ddown, 0, 2, 0)]
        dmiddle = after(dmiddle, ddown)
    vec0, bup0, ddown, dup, datt, dqkv, dx, dx_half = data_part(0, False, dmiddle, True)
    if fast:
        far1 = far_z(far1, last)
        n1z = near_z(p1[2], last)
        datt = after(datt, far1, n1z, *partners)
        partners.append(swap(after(partners[0], dx), 0, 2, 0))
    attention0 = attention_part(0, vec0, bup0, datt, dqkv, lost_first)
    ffn0 = ffn_part(0, after(hid, *attention0), [ddown] + (partners if fast else []), dup)

    if fast:
        kp0, sp0, kq0, sq0 = attention0
        ap0 = swap(after(sp0, partners[2]), 0, 1, 0)
        aq0 = swap(sq0, 0, 0, 1)
        kf0, sf0 = ffn0
        f0 = swap(sf0, 0, 0, 1)
        kp0, fp0, kq0, fq0 = half_sums(0, kp0, ap0, kq0, after(aq0, kf0))
        bp0 = swap(fp0, 0, 0, 1)
        bq0 = swap(fq0, 0, 1, 0)
        m1 = second_sum(last, p1[1], after(n1z, fp0))
        own0, far0 = far_sums(0, kf0, after(f0, m1))
        far0 = far_z(far0, 0)
        q0 = slot_sums(0, [kp0, after(bp0, own0)], [kq0, bq0])
        l0z = near_z(q0[2], 0)
        sums_last, ffn_last = last_section(last, after(p1[0], far0), n1z, far_z(m1, last), own1, far1)
        m0 = second_sum(0, q0[1], after(l0z, ffn_last))
        h0 = far_z(m0, 0)
        grad_down, up = ffn_totals(after(own0, m0), far0, ffn_last)
        dx_half = relay(after(dx_half, m0), 1)
        summed = last_totals([q0[0], l0z, h0], sums_last, dx, dx_half, up)
        grad_qkv, grad_out, grad_up, bias, gain, query_part, up_part, loss_row, crops_grad = summed
        loss_row = loss_row[0]
    else:
        grad_up, grad_down, grad_qkv, grad_out = [
            lax.psum_scatter(jnp.where(on_first, a, b).astype(F32), ("dp", "rep"), scatter_dimension=0, tiled=True)
            for a, b in zip([*ffn0, *attention0], [*ffn1, *attention1])
        ]
        small = jnp.where(on_first, small_rows(vec0, bup0, lost_first), small_rows(vec1, bup1, lost))
        for flip in flips():
            small = small + swap(small, None, *flip)
        place = dp * reps + rep
        width, up_width = D // (dps * reps), FF // (dps * reps)
        mine = lax.dynamic_slice(small[:8], (0, place * width), (8, width))
        bias, gain, query_part = mine[:5], mine[5:7], mine[7:]
        up_part = lax.dynamic_slice(small[8:12].reshape(1, FF), (0, place * up_width), (1, up_width))
        loss_row = small[12, :128]
        crops_grad = jnp.where(on_first, dx, relay(dx_half, 1)).astype(F32)
    return (
        loss_row[:1],
        crops_grad,
        grad_qkv[None],
        grad_out[None],
        grad_up[None],
        grad_down[None],
        bias[None],
        gain[None],
        up_part,
        query_part,
    )


def solution(mesh):
    crop = P(("dp", "rep"), "section", None)
    per_crop = P(("dp", "rep"))
    layer3 = P("section", None, None)
    layer2 = P("section", None)
    placed = (
        (crop, crop, per_crop, per_crop, per_crop, P())
        + (layer3,) * 6
        + (layer2,) * 2
        + (layer3,) * 6
        + (layer2,)
    )
    shared3 = P("section", ("dp", "rep"), None)
    return jax.shard_map(
        body,
        mesh=mesh,
        in_specs=placed,
        out_specs=(
            P(),
            crop,
            shared3,
            shared3,
            shared3,
            shared3,
            P("section", None, ("dp", "rep")),
            P("section", None, ("dp", "rep")),
            P("section", ("dp", "rep")),
            P("section", ("dp", "rep")),
        ),
        check_vma=False,
    )
```
